32 devices in a mesh: dp: 4 (over z), ctx: 2 (over x), tensor: 4 (over y, core).
Axes of the slice: x: 2, y: 2, z: 4, core: 2. Of those that a mesh axis runs over, the one named last changes fastest.
Arguments:
- inputs: bfloat16 [8, 1024, 768], P('dp', 'ctx'), may hold values from -6 to 6
- lengths: int32 [8], P('dp'), may hold values from 256 to 1024, as said below
- expert_ids: int32 [8, 1024], P('dp', 'ctx'), may hold values from 0 to 3, as said below
- slot_rows: int32 [8, 2, 4, 256], P('dp', 'ctx'), may hold values from 0 to 512, as said below
- attn_gain: bfloat16 [768], P(('dp', 'ctx')), may hold values from 0.5 to 1.5
- qkv_weight: bfloat16 [3, 768, 768], P(None, ('dp', 'ctx'), 'tensor'), may hold values from -0.21875 to 0.21875
- out_weight: bfloat16 [768, 768], P('tensor', ('dp', 'ctx')), may hold values from -1.75 to 1.75
- position_bias: float32 [32, 12], P(None, 'tensor'), may hold values from -3 to 3
- ffn_gain: bfloat16 [768], P(('dp', 'ctx')), may hold values from 0.5 to 1.5
- router_weight: bfloat16 [768, 4], P(('dp', 'ctx')), may hold values from -0.125 to 0.125
- up_weight: bfloat16 [4, 768, 3072], P(None, ('dp', 'ctx'), 'tensor'), may hold values from -0.21875 to 0.21875
- down_weight: bfloat16 [4, 3072, 768], P(None, 'tensor', ('dp', 'ctx')), may hold values from -0.875 to 0.875
- cotangent: bfloat16 [8, 1024, 768], P('dp', 'ctx'), may hold values from -6 to 6
Outputs:
- outputs: bfloat16 [8, 1024, 768], P('dp', 'ctx')
- input_grad: bfloat16 [8, 1024, 768], P('dp', 'ctx')
- attn_gain_grad: float32 [768], P(('dp', 'ctx'))
- qkv_grad: float32 [3, 768, 768], P(None, ('dp', 'ctx'), 'tensor')
- out_proj_grad: float32 [768, 768], P('tensor', ('dp', 'ctx'))
- bias_table_grad: float32 [32, 12], P(None, 'tensor')
- ffn_gain_grad: float32 [768], P(('dp', 'ctx'))
- router_grad: float32 [768, 4], P(('dp', 'ctx'))
- up_grad: float32 [4, 768, 3072], P(None, ('dp', 'ctx'), 'tensor')
- down_grad: float32 [4, 3072, 768], P(None, 'tensor', ('dp', 'ctx'))
The draws below stay inside these ranges and needn't reach their ends.
Inputs may be any that keep to these rules, and one draw needn't show every extreme that they name: `lengths`: in each group of 2 sequences that one index of dp holds, one has length 1024; some sequence has length 256. `expert_ids`: position t's expert is the expert in whose slots of t's segment it stands in slot_rows. `slot_rows`: entries are positions within the segment; 512 marks an empty slot. Every position of a segment stands in exactly one slot, and in every segment one expert fills all 256 of its slots.
All inputs are finite; a program needn't handle non-finite values.
Results may differ from the reference program's by a relative error of at most 0.025.
Values may be sent and summed in bfloat16 or wider, within the bound.
A program may use at most 384 MiB of HBM per device.

```python
import jax
import jax.numpy as jnp
import numpy as np
from jax import lax

D = 768
HEADS = 12
HD = 64
FF = 3072
BUCKETS = 32
EXPERTS = 4
MICRO = 2
SEG = 512
LEN = 1024
SEQS = 8
CAP = 256


def route_tables(key):
    blocks = SEQS * (LEN // SEG)

    def one_block(block_key):
        key_order, key_full, key_rest = jax.random.split(block_key, 3)
        token_order = jax.random.permutation(key_order, SEG)
        full_expert = jax.random.randint(key_full, (), 0, EXPERTS)
        others = jax.random.permutation(key_rest, (EXPERTS - 1) * CAP)[:SEG - CAP]
        shifted = others // CAP
        expert_other = shifted + (shifted >= full_expert).astype(jnp.int32)
        slot_other = expert_other * CAP + others % CAP
        slot_full = full_expert * CAP + jnp.arange(CAP, dtype=jnp.int32)
        ordered = jnp.concatenate([slot_full, slot_other]).astype(jnp.int32)
        slot_of = jnp.zeros((SEG,), jnp.int32).at[token_order].set(ordered)
        slot_table = jnp.full((EXPERTS * CAP,), SEG, jnp.int32).at[slot_of].set(jnp.arange(SEG, dtype=jnp.int32))
        return ((slot_of // CAP).astype(jnp.int32), slot_table.reshape(EXPERTS, CAP))
    experts, tables = jax.vmap(one_block)(jax.random.split(jax.random.fold_in(key, 11), blocks))
    return (experts.reshape(SEQS, LEN), tables.reshape(SEQS, LEN // SEG, EXPERTS, CAP))


def draw_lengths(key, part):
    key_len, key_pick, key_short = jax.random.split(jax.random.fold_in(key, 5), 3)
    groups = SEQS // MICRO
    drawn_lengths = jax.random.randint(key_len, (SEQS,), LEN // 4, LEN + 1)
    picked = jax.random.randint(key_pick, (groups,), 0, MICRO)
    longest = jnp.arange(groups, dtype=jnp.int32) * MICRO + picked
    drawn_lengths = drawn_lengths.at[longest].set(LEN)
    short_group = jax.random.randint(key_short, (), 0, groups)
    shortest = short_group * MICRO + (picked[short_group] + 1) % MICRO
    return drawn_lengths.at[shortest].set(LEN // 4).astype(jnp.int32)


def draw_expert_ids(key, part):
    return route_tables(key)[0]


def draw_slot_rows(key, part):
    return route_tables(key)[1]


def steps_of(rng, extent, shards, least, high):
    gain = 1.0
    for axis_at, parts in shards:
        draws = jax.random.uniform(jax.random.fold_in(jax.random.fold_in(rng, 6), axis_at), (parts,), jnp.float32, least / len(shards), high / len(shards))
        gain = gain * jnp.repeat(jnp.exp(draws), extent[axis_at] // parts).reshape((-1,) + (1,) * (len(extent) - 1 - axis_at))
    return gain


def normal_values(own_key, extent, spread, bound, shards=(), held_as=jnp.bfloat16):
    array = spread * jax.random.normal(own_key, extent, jnp.float32)
    if shards:
        array = array * steps_of(own_key, extent, shards, -0.22, 0.18)
    return jnp.clip(array, -bound, bound).astype(held_as)


def setup_inputs(seed: int = 0) -> dict:
    seeds = jax.random.split(jax.random.key(seed), 14)
    return {
        "inputs": normal_values(seeds[0], (SEQS, LEN, D), 1.0, 6.0, ((0, 4), (1, 2))),
        "lengths": draw_lengths(jax.random.fold_in(seeds[13], 71), 0),
        "expert_ids": draw_expert_ids(jax.random.fold_in(seeds[13], 71), 0),
        "slot_rows": draw_slot_rows(jax.random.fold_in(seeds[13], 71), 0),
        "attn_gain": jnp.clip(1.0 + 0.1 * jax.random.normal(seeds[4], (D,), jnp.float32), 0.5, 1.5).astype(jnp.bfloat16),
        "qkv_weight": normal_values(seeds[5], (3, D, D), D ** -0.5, 0.21875, ((1, 8), (2, 4))),
        "out_weight": normal_values(seeds[6], (D, D), (D // 64) ** -0.5, 1.75, ((0, 4), (1, 8))),
        "position_bias": normal_values(seeds[7], (BUCKETS, HEADS), 0.5, 3.0, ((1, 4),), jnp.float32),
        "ffn_gain": jnp.clip(1.0 + 0.1 * jax.random.normal(seeds[8], (D,), jnp.float32), 0.5, 1.5).astype(jnp.bfloat16),
        "router_weight": normal_values(seeds[9], (D, EXPERTS), (3 * D) ** -0.5, 0.125, ((0, 8),)),
        "up_weight": normal_values(seeds[10], (EXPERTS, D, FF), D ** -0.5, 0.21875, ((1, 8), (2, 4))),
        "down_weight": normal_values(seeds[11], (EXPERTS, FF, D), (FF // 64) ** -0.5, 0.875, ((1, 4), (2, 8))),
        "cotangent": normal_values(seeds[12], (SEQS, LEN, D), 1.0, 6.0, ((0, 4), (1, 2))),
    }


@jax.custom_vjp
def low(v):
    return lax.optimization_barrier(v.astype(jnp.bfloat16)).astype(jnp.float32)

@jax.custom_vjp
def low_back(v):
    return v

def low_keep(v):
    return (low(v), None)

def low_pass(kept, grad):
    return (grad,)

def back_keep(v):
    return (v, None)

def back_low(kept, grad):
    return (low(grad),)
low.defvjp(low_keep, low_pass)
low_back.defvjp(back_keep, back_low)
bucket_edges = np.ceil(16.0 * 8.0 ** (np.arange(1, 16) / 16.0)).astype(np.int32)

def bucket_of(distance):
    clipped = jnp.maximum(distance, 0)
    edge_values = jnp.asarray(bucket_edges, dtype=jnp.int32)
    beyond = lax.optimization_barrier(jnp.sum((clipped[..., None] >= edge_values).astype(jnp.int32), axis=-1))
    return jnp.where(clipped < 16, clipped, jnp.minimum(16 + beyond, 31)).astype(jnp.int32)

def rms_norm(values, gain_vector):
    return values * lax.rsqrt(lax.optimization_barrier(jnp.mean(values * values, axis=-1, keepdims=True)) + 1e-06) * gain_vector

def reference(inputs, lengths, expert_ids, slot_rows, attn_gain, qkv_weight, out_weight, position_bias, ffn_gain, router_weight, up_weight, down_weight, cotangent):
    highest = lax.Precision.HIGHEST
    positions = jnp.arange(LEN, dtype=jnp.int32)
    block_rows = min(512, LEN)

    def forward(inputs_f, attn_gain_f, qkv_f, out_f, bias_f, ffn_gain_f, router_f, up_f, down_f):

        def one_sequence(packed):
            tokens, length, experts, slot_table = packed
            live_rows = (positions < length).astype(jnp.float32)
            normed = low(rms_norm(tokens, attn_gain_f))
            projected = low(low_back(jnp.einsum('td,cde->cte', normed, qkv_f, precision=highest)))
            queries = projected[0].reshape(LEN, HEADS, HD)
            keys = projected[1].reshape(LEN, HEADS, HD)
            values = projected[2].reshape(LEN, HEADS, HD)

            def attend(block_index):
                first_row = block_index * block_rows
                query_block = lax.dynamic_slice_in_dim(queries, first_row, block_rows, 0)
                query_pos = first_row + jnp.arange(block_rows, dtype=jnp.int32)
                distance = query_pos[:, None] - positions[None, :]
                scores = jnp.einsum('qhd,khd->hqk', query_block, keys, precision=highest) * 0.125
                scores = low_back(scores + jnp.transpose(bias_f[bucket_of(distance)], (2, 0, 1)))
                allowed = (distance >= 0) & (positions[None, :] < length)
                scores = jnp.where(allowed[None], scores, -1e+30)
                soft_weights = low(jax.nn.softmax(scores, axis=-1))
                return jnp.einsum('hqk,khd->qhd', soft_weights, values, precision=highest)
            attended = lax.map(jax.checkpoint(attend), jnp.arange(LEN // block_rows, dtype=jnp.int32))
            attended = low(low_back(attended.reshape(LEN, D)))
            branch = low_back(jnp.dot(attended, out_f, precision=highest))
            hidden = tokens + branch
            normed_two = low(rms_norm(hidden, ffn_gain_f))
            logits = low_back(jnp.dot(normed_two, router_f, precision=highest))
            router_probs = jax.nn.softmax(logits, axis=-1)
            chosen = (experts[:, None] == jnp.arange(EXPERTS, dtype=jnp.int32)[None, :]).astype(jnp.float32)
            gate_value = lax.optimization_barrier(jnp.sum(router_probs * chosen, axis=-1))
            offsets = (jnp.arange(LEN // SEG, dtype=jnp.int32) * SEG)[:, None, None]
            token_rows = jnp.where(slot_table < SEG, slot_table + offsets, LEN).astype(jnp.int32)
            padded = jnp.concatenate([normed_two, jnp.zeros((1, D), jnp.float32)], axis=0)
            picked = padded[token_rows]
            raised = low_back(jnp.einsum('cekd,edf->cekf', picked, up_f, precision=highest))
            activated = low(jax.nn.gelu(raised))
            lowered = jnp.einsum('cekf,efd->cekd', activated, down_f, precision=highest)
            expert_sum = jnp.zeros((LEN + 1, D), jnp.float32).at[token_rows.reshape(-1)].add(lowered.reshape(-1, D))[:LEN]
            expert_sum = low_back(expert_sum)
            return live_rows[:, None] * (hidden + gate_value[:, None] * expert_sum)
        return lax.map(jax.checkpoint(one_sequence), (inputs_f, lengths, expert_ids, slot_rows))
    floats = [array_in.astype(jnp.float32) for array_in in (inputs, attn_gain, qkv_weight, out_weight, position_bias, ffn_gain, router_weight, up_weight, down_weight)]
    result, pullback = jax.vjp(forward, *floats)
    gradients = pullback(cotangent.astype(jnp.float32))
    return (result.astype(jnp.bfloat16), gradients[0].astype(jnp.bfloat16), gradients[1], gradients[2], gradients[3], gradients[4], gradients[5], gradients[6], gradients[7], gradients[8])
```

```python
import functools

import jax
import jax.numpy as jnp
import numpy as np
from jax import lax
from jax.experimental import pallas as pl
from jax.experimental.pallas import tpu as pltpu
from jax.sharding import PartitionSpec as P

BUCKETS = 32
MESH = pl.DeviceIdType.MESH
BF = jnp.bfloat16
F32 = jnp.float32


bucket_edges = np.ceil(16.0 * 8.0 ** (np.arange(1, 16) / 16.0)).astype(np.int32)
bucket_starts = [int(n) for n in range(17)] + [int(n) for n in bucket_edges]


QT = 256
BAND = 128


def mm(a, b):
    return jnp.dot(a, b, preferred_element_type=F32)


def mm_nt(a, b):
    return lax.dot_general(a, b, (((1,), (1,)), ((), ())), preferred_element_type=F32)


def mm_tn(a, b):
    return lax.dot_general(a, b, (((0,), (0,)), ((), ())), preferred_element_type=F32)


class Group:
    def __init__(self, place, src, dst_at, zs, zr, xs, xr, local):
        self.dp, self.cx, self.t = place
        self.src, self.dst_at = src, dst_at
        self.zs, self.zr, self.xs, self.xr, self.local = zs, zr, xs, xr, local

    def slab(self, k, cx):
        return lax.rem(self.dp + 4 - k, 4) * 2 + cx

    def own(self):
        return pltpu.make_async_copy(self.src, self.dst_at(self.slab(0, self.cx)), self.local)

    def z_send(self, k):
        return pltpu.make_async_remote_copy(
            src_ref=self.src,
            dst_ref=self.dst_at(self.slab(0, self.cx)),
            send_sem=self.zs(k - 1),
            recv_sem=self.zr(k - 1),
            device_id=(lax.rem(self.dp + k, 4), self.cx, self.t),
            device_id_type=MESH,
        )

    def z_recv(self, k):
        return pltpu.make_async_remote_copy(
            src_ref=self.src,
            dst_ref=self.dst_at(self.slab(k, self.cx)),
            send_sem=self.zs(k - 1),
            recv_sem=self.zr(k - 1),
            device_id=(lax.rem(self.dp + k, 4), self.cx, self.t),
            device_id_type=MESH,
        )

    def x_send(self, k):
        spot = self.dst_at(self.slab(k, self.cx))
        return pltpu.make_async_remote_copy(
            src_ref=self.src if k == 0 else spot,
            dst_ref=spot,
            send_sem=self.xs(k),
            recv_sem=self.xr(k),
            device_id=(self.dp, 1 - self.cx, self.t),
            device_id_type=MESH,
        )

    def x_recv(self, k):
        spot = self.dst_at(self.slab(k, 1 - self.cx))
        return pltpu.make_async_remote_copy(
            src_ref=self.src,
            dst_ref=spot,
            send_sem=self.xs(k),
            recv_sem=self.xr(k),
            device_id=(self.dp, 1 - self.cx, self.t),
            device_id_type=MESH,
        )

    def begin(self):
        self.own().start()
        for k in (1, 3, 2):
            self.z_send(k).start()
        self.x_send(0).start()

    def hand_on(self):
        for k in (1, 3, 2):
            self.z_recv(k).wait_recv()
            self.x_send(k).start()

    def finish(self):
        self.own().wait()
        for k in range(4):
            self.x_recv(k).wait_recv()

    def drain(self):
        for k in (1, 2, 3):
            self.z_send(k).wait_send()
        for k in range(4):
            self.x_send(k).wait_send()


def lane_halves(shape):
    return lax.broadcasted_iota(jnp.int32, shape, len(shape) - 1) < 64


def head_cut(h):
    return (h // 2) * 128, h % 2 == 0


def head_tile(block, h, heads):
    if block.shape[-1] == 64:
        return block
    lower = lane_halves(block.shape)
    keep = lower if h % 2 == 0 else jnp.logical_not(lower)
    return jnp.where(keep, block, jnp.zeros_like(block))


def lanes_of(h, heads):
    first = (h // 2) * 128
    return slice(first, min(first + 128, heads * 64))


def fill_bias(bias_ref, band_ref, heads):
    rows = lax.broadcasted_iota(jnp.int32, (BAND, 2 * BAND), 0)
    cols = lax.broadcasted_iota(jnp.int32, (BAND, 2 * BAND), 1)
    away = rows + BAND - cols
    for h in range(heads):
        tile = jnp.full((BAND, 2 * BAND), bias_ref[0, h], F32)
        for b in range(1, BUCKETS):
            tile = jnp.where(away >= bucket_starts[b], bias_ref[b, h], tile)
        band_ref[h] = tile - bias_ref[BUCKETS - 1, h]


def masked_scores(q_tile, keys, band_ref, scores, h, first, length):
    count = keys.shape[0]
    scores[:, BAND:] = mm_nt(q_tile, keys) * 0.125
    for part in range(QT // BAND):
        spot = (
            pl.ds(part * BAND, BAND),
            pl.ds(pl.multiple_of(first + part * BAND, BAND), 2 * BAND),
        )
        scores[spot] = scores[spot] + band_ref[h]
    values = scores[:, BAND:]
    key_pos = lax.broadcasted_iota(jnp.int32, (QT, count), 1)
    query_pos = lax.broadcasted_iota(jnp.int32, (QT, count), 0) + first
    allowed = (key_pos <= query_pos) & (key_pos < length)
    return jnp.where(allowed, values, -1e30), allowed


def first_kernel(
    heads,
    len_ref,
    bias_ref,
    tok,
    small,
    wqkv,
    wo,
    w,
    hidden,
    ntwo,
    normed,
    q,
    kcat,
    vcat,
    lse,
    ab,
    wqkv_full,
    wo_own,
    gains,
    w_full,
    small_all,
    wo_full,
    ab_all,
    band,
    scores,
    sm_s,
    sm_r,
    q_s,
    q_r,
    o_s,
    o_r,
    ot_s,
    ot_r,
    kv_s,
    kv_r,
    ab_s,
    ab_r,
    w_s,
    w_r,
    local,
):
    dp, cx, t = lax.axis_index("dp"), lax.axis_index("ctx"), lax.axis_index("tensor")
    place = (dp, cx, t)
    seg = tok.shape[0] // 2
    experts = w.shape[0]
    group_peers = [
        (lax.rem(dp + k, 4), cx if c == 0 else 1 - cx, t)
        for k in range(4)
        for c in range(2)
        if (k, c) != (0, 0)
    ]
    group_from = [
        lax.rem(dp + 4 - k, 4) * 2 + (cx if c == 0 else 1 - cx)
        for k in range(4)
        for c in range(2)
        if (k, c) != (0, 0)
    ]
    tensor_peers = [(dp, cx, lax.rem(t + k, 4)) for k in (1, 2, 3)]
    own_slab = dp * 2 + cx

    barrier = pltpu.get_barrier_semaphore()
    for peer in group_peers + tensor_peers:
        pl.semaphore_signal(barrier, inc=1, device_id=peer, device_id_type=MESH)
    pl.semaphore_wait(barrier, len(group_peers) + len(tensor_peers))

    def small_send(i):
        return pltpu.make_async_remote_copy(
            src_ref=small,
            dst_ref=small_all.at[own_slab],
            send_sem=sm_s.at[i],
            recv_sem=sm_r.at[i],
            device_id=group_peers[i],
            device_id_type=MESH,
        )

    def small_recv(i):
        return pltpu.make_async_remote_copy(
            src_ref=small,
            dst_ref=small_all.at[group_from[i]],
            send_sem=sm_s.at[i],
            recv_sem=sm_r.at[i],
            device_id=group_peers[i],
            device_id_type=MESH,
        )

    small_own = pltpu.make_async_copy(small, small_all.at[own_slab], local.at[0])

    def rows96(s):
        return pl.ds(pl.multiple_of(s * 96, 32), 96)

    g_qkv = Group(
        place,
        wqkv,
        lambda s: wqkv_full.at[:, rows96(s), :],
        lambda i: q_s.at[i],
        lambda i: q_r.at[i],
        lambda i: q_s.at[3 + i],
        lambda i: q_r.at[3 + i],
        local.at[1],
    )
    g_out = Group(
        place,
        wo,
        lambda s: wo_full.at[t, rows96(s), :],
        lambda i: o_s.at[i],
        lambda i: o_r.at[i],
        lambda i: o_s.at[3 + i],
        lambda i: o_r.at[3 + i],
        local.at[2],
    )
    g_w = [
        Group(
            place,
            w.at[e],
            lambda s, e=e: w_full.at[e, :, rows96(s), :],
            lambda i, e=e: w_s.at[e, i],
            lambda i, e=e: w_r.at[e, i],
            lambda i, e=e: w_s.at[e, 3 + i],
            lambda i, e=e: w_r.at[e, 3 + i],
            local.at[3 + e],
        )
        for e in range(experts)
    ]

    small_own.start()
    for i in range(7):
        small_send(i).start()
    g_qkv.begin()
    g_out.begin()

    @pl.when(cx == 0)
    def _():
        for m in range(2):
            kcat[m, seg:, :] = jnp.zeros((seg, kcat.shape[2]), BF)
            vcat[m, seg:, :] = jnp.zeros((seg, kcat.shape[2]), BF)

    fill_bias(bias_ref, band, heads)

    small_own.wait()
    for i in range(7):
        small_recv(i).wait_recv()
    total = small_all[0].astype(F32)
    for i in range(1, 8):
        total = total + small_all[i].astype(F32)
    gains[...] = total

    def norm_rows(i, carry):
        rows = pl.ds(pl.multiple_of(i * 128, 128), 128)
        x = tok[rows, :].astype(F32)
        scale = lax.rsqrt(jnp.mean(x * x, axis=-1, keepdims=True) + 1e-06)
        normed[rows, :] = (x * scale * gains[0:1, :]).astype(BF)
        return carry

    lax.fori_loop(0, 2 * seg // 128, norm_rows, 0)

    g_qkv.hand_on()
    for e in range(experts):
        g_w[e].begin()
    g_out.hand_on()
    g_qkv.finish()

    def project(m):
        def step(i, carry):
            rows = pl.ds(pl.multiple_of(m * seg + i * 256, 256), 256)
            spots = pl.ds(pl.multiple_of(cx * seg + i * 256, 256), 256)
            x = normed[rows, :]
            q[rows, :] = mm(x, wqkv_full[0]).astype(BF)
            kcat[m, spots, :] = mm(x, wqkv_full[1]).astype(BF)
            vcat[m, spots, :] = mm(x, wqkv_full[2]).astype(BF)
            return carry

        lax.fori_loop(0, seg // 256, step, 0)

    def kv_copy(m, which):
        ref = (kcat, vcat)[which]
        return pltpu.make_async_remote_copy(
            src_ref=ref.at[m, pl.ds(0, seg), :],
            dst_ref=ref.at[m, pl.ds(0, seg), :],
            send_sem=kv_s.at[m * 2 + which],
            recv_sem=kv_r.at[m * 2 + which],
            device_id=(dp, 1 - cx, t),
            device_id_type=MESH,
        )

    for m in range(2):
        project(m)

        @pl.when(cx == 0)
        def _():
            kv_copy(m, 0).start()
            kv_copy(m, 1).start()

    g_out.finish()

    def wo_send(k):
        return pltpu.make_async_remote_copy(
            src_ref=wo_full.at[t],
            dst_ref=wo_full.at[t],
            send_sem=ot_s.at[k - 1],
            recv_sem=ot_r.at[k - 1],
            device_id=tensor_peers[k - 1],
            device_id_type=MESH,
        )

    def wo_recv(k):
        spot = wo_full.at[lax.rem(t + 4 - k, 4)]
        return pltpu.make_async_remote_copy(
            src_ref=spot,
            dst_ref=spot,
            send_sem=ot_s.at[k - 1],
            recv_sem=ot_r.at[k - 1],
            device_id=tensor_peers[k - 1],
            device_id_type=MESH,
        )

    for k in (1, 2, 3):
        wo_send(k).start()

    def ab_copy(m, k, source):
        spot = ab_all.at[source, pl.ds(m * seg, seg), :]
        return pltpu.make_async_remote_copy(
            src_ref=spot,
            dst_ref=spot,
            send_sem=ab_s.at[m * 3 + k - 1],
            recv_sem=ab_r.at[m * 3 + k - 1],
            device_id=tensor_peers[k - 1],
            device_id_type=MESH,
        )

    def attend(m):
        length = len_ref[m]

        def step(i, carry):
            rows = pl.ds(pl.multiple_of(m * seg + i * QT, QT), QT)
            first = cx * seg + i * QT
            lanes128 = lax.broadcasted_iota(jnp.int32, (QT, 128), 1)
            tops = jnp.zeros((QT, 128), F32)
            held = []
            for h in range(heads):
                cut = lanes_of(h, heads)
                q_tile = head_tile(q[rows, cut], h, heads)
                values, allowed = masked_scores(
                    q_tile, kcat[m, :, cut], band, scores, h, first, length
                )
                top = jnp.max(values, axis=-1, keepdims=True)
                raised = jnp.where(allowed, jnp.exp(values - top), 0.0)
                mass = jnp.sum(raised, axis=-1, keepdims=True)
                probs = (raised * (1.0 / mass)).astype(BF)
                held.append(mm(probs, vcat[m, :, cut]))
                tops = jnp.where(lanes128 == h, top + jnp.log(mass), tops)
                if h % 2 == 1:
                    both = jnp.where(lane_halves(held[0].shape), held[0], held[1])
                    ab_all[t, rows, cut] = both.astype(BF)
                    held = []
                elif h == heads - 1:
                    ab_all[t, rows, cut] = held[0].astype(BF)
            lse[rows, :] = tops
            return carry

        lax.fori_loop(0, seg // QT, step, 0)

    for m in range(2):

        @pl.when(cx == 1)
        def _():
            kv_copy(m, 0).wait_recv()
            kv_copy(m, 1).wait_recv()

        attend(m)
        for k in (1, 2, 3):
            ab_copy(m, k, t).start()
        if m == 0:
            g_w[0].hand_on()
    for k in (1, 2, 3):
        wo_recv(k).wait_recv()
    wo_own[...] = wo_full[t]
    ab[...] = ab_all[t]

    for m in range(2):
        for k in (1, 2, 3):
            ab_copy(m, k, lax.rem(t + 4 - k, 4)).wait_recv()

        def branch(i, carry):
            rows = pl.ds(pl.multiple_of(m * seg + i * 256, 256), 256)
            total = mm_nt(ab_all[0, rows, :], wo_full[0])
            for j in range(1, 4):
                total = total + mm_nt(ab_all[j, rows, :], wo_full[j])
            x = tok[rows, :].astype(F32) + total
            hidden[rows, :] = x
            scale = lax.rsqrt(jnp.mean(x * x, axis=-1, keepdims=True) + 1e-06)
            ntwo[rows, :] = (x * scale * gains[1:2, :]).astype(BF)
            return carry

        lax.fori_loop(0, seg // 256, branch, 0)
        if m == 0 and experts > 1:
            g_w[1].hand_on()

    for e in range(2, experts):
        g_w[e].hand_on()
    for e in range(experts):
        g_w[e].finish()

    for i in range(7):
        small_send(i).wait_send()
    g_qkv.drain()
    g_out.drain()
    for e in range(experts):
        g_w[e].drain()
    for k in (1, 2, 3):
        wo_send(k).wait_send()
    for m in range(2):
        for k in (1, 2, 3):
            ab_copy(m, k, t).wait_send()

        @pl.when(cx == 0)
        def _():
            kv_copy(m, 0).wait_send()
            kv_copy(m, 1).wait_send()


def first_call(lengths, bias, tok, small, wqkv, wo, w):
    heads = bias.shape[1]
    rows, width = tok.shape
    span = wqkv.shape[2]
    experts = w.shape[0]
    ff = w.shape[3]
    vm = pl.BlockSpec(memory_space=pltpu.VMEM)
    sm = pl.BlockSpec(memory_space=pltpu.SMEM)
    hbm = pl.BlockSpec(memory_space=pl.ANY)
    dma = pltpu.SemaphoreType.DMA
    return pl.pallas_call(
        functools.partial(first_kernel, heads),
        out_shape=(
            jax.ShapeDtypeStruct((rows, width), F32),
            jax.ShapeDtypeStruct((rows, width), BF),
            jax.ShapeDtypeStruct((rows, width), BF),
            jax.ShapeDtypeStruct((rows, span), BF),
            jax.ShapeDtypeStruct((2, rows, span), BF),
            jax.ShapeDtypeStruct((2, rows, span), BF),
            jax.ShapeDtypeStruct((rows, 128), F32),
            jax.ShapeDtypeStruct((rows, span), BF),
            jax.ShapeDtypeStruct((3, width, span), BF),
            jax.ShapeDtypeStruct((width, span), BF),
            jax.ShapeDtypeStruct((16, width), F32),
            jax.ShapeDtypeStruct((experts, 2, width, ff), BF),
        ),
        in_specs=[sm, sm, vm, hbm, hbm, hbm, hbm],
        out_specs=(vm,) * 11 + (hbm,),
        scratch_shapes=[
            pltpu.VMEM((8, 16, width), BF),
            pltpu.VMEM((4, width, span), BF),
            pltpu.VMEM((4, rows, span), BF),
            pltpu.VMEM((heads, BAND, 2 * BAND), F32),
            pltpu.VMEM((QT, rows + BAND), F32),
            dma((7,)),
            dma((7,)),
            dma((7,)),
            dma((7,)),
            dma((7,)),
            dma((7,)),
            dma((3,)),
            dma((3,)),
            dma((4,)),
            dma((4,)),
            dma((6,)),
            dma((6,)),
            dma((experts, 7)),
            dma((experts, 7)),
            dma((3 + experts,)),
        ],
        compiler_params=pltpu.CompilerParams(
            collective_id=0, has_side_effects=True, vmem_limit_bytes=56 << 20
        ),
    )(lengths, bias, tok, small, wqkv, wo, w)


def back_kernel(heads, len_ref, bias_ref, q, kcat, vcat, lse, grad, dq, dk, dv, dbias, band, scores, spread, band_sum, whole_sum):
    cx = lax.axis_index("ctx")
    seg = q.shape[0] // 2
    fill_bias(bias_ref, band, heads)
    dk[...] = jnp.zeros(dk.shape, F32)
    dv[...] = jnp.zeros(dv.shape, F32)
    spread[...] = jnp.zeros(spread.shape, F32)
    band_sum[...] = jnp.zeros(band_sum.shape, F32)
    whole_sum[...] = jnp.zeros(whole_sum.shape, F32)
    for m in range(2):
        length = len_ref[m]

        def step(i, carry):
            rows = pl.ds(pl.multiple_of(m * seg + i * QT, QT), QT)
            first = cx * seg + i * QT
            held = []
            for h in range(heads):
                cut = lanes_of(h, heads)
                q_tile = head_tile(q[rows, cut], h, heads)
                do_tile = head_tile(grad[rows, cut], h, heads)
                values, allowed = masked_scores(
                    q_tile, kcat[m, :, cut], band, scores, h, first, length
                )
                soft = jnp.where(allowed, jnp.exp(values - lse[rows, h : h + 1]), 0.0)
                soft_grad = mm_nt(do_tile, vcat[m, :, cut])
                dv[m, :, cut] += mm_tn(soft.astype(BF), do_tile)
                delta = jnp.sum(soft * soft_grad, axis=-1, keepdims=True)
                score_grad = (soft * (soft_grad - delta)).astype(BF)
                dk[m, :, cut] += mm_tn(score_grad, q_tile)
                held.append(mm(score_grad, kcat[m, :, cut]) * 0.125)
                spread[:, BAND:] = score_grad.astype(F32)
                for part in range(QT // BAND):
                    lanes = pl.ds(pl.multiple_of(first + part * BAND, BAND), 2 * BAND)
                    band_sum[h] += spread[part * BAND : (part + 1) * BAND, lanes]
                whole_sum[h : h + 1, :] += jnp.sum(spread[:, BAND:], axis=0, keepdims=True)
                if h % 2 == 1:
                    both = jnp.where(lane_halves(held[0].shape), held[0], held[1])
                    dq[rows, cut] = both.astype(BF)
                    held = []
                elif h == heads - 1:
                    dq[rows, cut] = held[0].astype(BF)
            return carry

        lax.fori_loop(0, seg // QT, step, 0)
    bucket_sums(heads, band_sum, whole_sum, dbias)


def bucket_sums(heads, band_sum, whole_sum, dbias):
    rows = lax.broadcasted_iota(jnp.int32, (BAND, 2 * BAND), 0)
    cols = lax.broadcasted_iota(jnp.int32, (BAND, 2 * BAND), 1)
    away = rows + BAND - cols
    bucket = lax.broadcasted_iota(jnp.int32, (BUCKETS, 2 * BAND), 0)
    lanes128 = lax.broadcasted_iota(jnp.int32, (BUCKETS, 128), 1)
    result = jnp.zeros((BUCKETS, 128), F32)
    for h in range(heads):
        tile = band_sum[h]
        sums = jnp.zeros((BUCKETS, 2 * BAND), F32)
        for b in range(BUCKETS - 1):
            inside = (away >= bucket_starts[b]) & (away < bucket_starts[b + 1])
            row = jnp.sum(jnp.where(inside, tile, 0.0), axis=0, keepdims=True)
            sums = jnp.where(bucket == b, row, sums)
        per_bucket = jnp.sum(sums, axis=1, keepdims=True)
        near = jnp.sum(per_bucket, axis=0, keepdims=True)
        total = jnp.sum(whole_sum[h : h + 1, :], axis=1, keepdims=True)
        last = lax.broadcasted_iota(jnp.int32, (BUCKETS, 1), 0) == BUCKETS - 1
        per_bucket = jnp.where(last, total - near, per_bucket)
        result = jnp.where(lanes128 == h, per_bucket, result)
    dbias[...] = result


def back_call(lengths, bias, q, kcat, vcat, lse, grad):
    heads = bias.shape[1]
    vm = pl.BlockSpec(memory_space=pltpu.VMEM)
    sm = pl.BlockSpec(memory_space=pltpu.SMEM)
    return pl.pallas_call(
        functools.partial(back_kernel, heads),
        out_shape=(
            jax.ShapeDtypeStruct(q.shape, BF),
            jax.ShapeDtypeStruct(kcat.shape, F32),
            jax.ShapeDtypeStruct(kcat.shape, F32),
            jax.ShapeDtypeStruct((BUCKETS, 128), F32),
        ),
        in_specs=[sm, sm] + [vm] * 5,
        out_specs=(vm,) * 4,
        scratch_shapes=[
            pltpu.VMEM((heads, BAND, 2 * BAND), F32),
            pltpu.VMEM((QT, q.shape[0] + BAND), F32),
            pltpu.VMEM((QT, q.shape[0] + BAND), F32),
            pltpu.VMEM((heads, BAND, 2 * BAND), F32),
            pltpu.VMEM((8, q.shape[0]), F32),
        ],
        compiler_params=pltpu.CompilerParams(vmem_limit_bytes=56 << 20),
    )(lengths, bias, q, kcat, vcat, lse, grad)


def body_fast(
    inputs, lengths, expert_ids, slot_rows, attn_gain, qkv_weight, out_weight, position_bias,
    ffn_gain, router_weight, up_weight, down_weight, cotangent,
):
    micro, seg, width = inputs.shape
    rows = micro * seg
    experts = up_weight.shape[0]
    cx = lax.axis_index("ctx")
    slab = lax.axis_index("dp") * 2 + cx
    shard = attn_gain.shape[0]
    small_own = jnp.concatenate(
        [attn_gain[None], ffn_gain[None], router_weight.T, jnp.zeros((10, shard), BF)], axis=0
    )
    small = lax.dynamic_update_slice(jnp.zeros((16, width), BF), small_own, (0, slab * shard))
    w = jnp.stack([up_weight, jnp.transpose(down_weight, (0, 2, 1))], axis=1)
    tok = inputs.reshape(rows, width)
    (hidden, ntwo, normed, q, kcat, vcat, lse, ab, wqkv, wo, gains, w_full) = first_call(
        lengths, position_bias, tok, small, qkv_weight, out_weight.T, w
    )
    gain_one, gain_two, router = gains[0], gains[1], gains[2 : 2 + experts].T.astype(BF)
    f32dot = functools.partial(jnp.einsum, preferred_element_type=F32)
    probs = jax.nn.softmax(f32dot("td,de->te", ntwo, router), axis=-1)
    chosen = (expert_ids.reshape(rows)[:, None] == jnp.arange(experts)[None, :]).astype(F32)
    gate = jnp.sum(probs * chosen, axis=-1)
    positions = cx * seg + jnp.arange(seg, dtype=jnp.int32)
    live = (positions[None, :] < lengths[:, None]).astype(F32).reshape(rows, 1)
    upstream = live * cotangent.reshape(rows, width).astype(F32)
    sum_grad = (gate[:, None] * upstream).astype(BF)
    slots = slot_rows[:, 0]
    place = jnp.where(slots < seg, slots + jnp.arange(micro)[:, None, None] * seg, rows)
    place = jnp.transpose(place, (1, 0, 2)).reshape(experts, -1)
    one_hot = (place[:, :, None] == jnp.arange(rows)[None, None, :]).astype(BF)
    picked = f32dot("ekt,td->ekd", one_hot, ntwo).astype(BF)
    slot_grad = f32dot("ekt,td->ekd", one_hot, sum_grad).astype(BF)
    up, dn = w_full[:, 0], w_full[:, 1]
    raised = f32dot("ekd,edf->ekf", picked, up)
    activated, gelu_back = jax.vjp(jax.nn.gelu, raised)
    activated = activated.astype(BF)
    lowered = f32dot("ekf,edf->ekd", activated, dn).astype(BF)
    spread = f32dot("ekt,ekd->td", one_hot, lowered).astype(BF)
    down_part = f32dot("ekd,ekf->edf", slot_grad, activated)
    act_grad = f32dot("ekd,edf->ekf", slot_grad, dn)
    raised_grad = gelu_back(act_grad)[0].astype(BF)
    up_part = f32dot("ekd,ekf->edf", picked, raised_grad)
    picked_grad = f32dot("ekf,edf->ekd", raised_grad, up).astype(BF)
    spread_grad = f32dot("ekt,ekd->td", one_hot, picked_grad).astype(BF)
    expert_sum = lax.psum(spread, "tensor").astype(F32)
    result = (live * (hidden + gate[:, None] * expert_sum)).astype(BF)
    gate_grad = jnp.sum(expert_sum * upstream, axis=-1)
    logit_grad = (probs * gate_grad[:, None] * (chosen - gate[:, None])).astype(BF)
    router_part = f32dot("td,te->de", ntwo, logit_grad)
    normed_two_grad = lax.psum(spread_grad, "tensor").astype(F32) + f32dot(
        "te,de->td", logit_grad, router
    )
    unused, second_back = jax.vjp(rms_norm, hidden, gain_two)
    hidden_grad, gain_two_part = second_back(normed_two_grad)
    hidden_grad = hidden_grad + upstream
    branch_grad = hidden_grad.astype(BF)
    out_part = f32dot("td,te->de", branch_grad, ab)
    attended_grad = f32dot("td,de->te", branch_grad, wo).astype(BF)
    dq, dk, dv, dbias = back_call(lengths, position_bias, q, kcat, vcat, lse, attended_grad)
    dkv = jnp.stack([dk * 0.125, dv], axis=0).astype(BF)
    other = lax.dynamic_slice_in_dim(dkv, (1 - cx) * seg, seg, axis=2)
    own = lax.dynamic_slice_in_dim(dkv, cx * seg, seg, axis=2)
    came = lax.ppermute(other, "ctx", [(0, 1), (1, 0)])
    own = (own.astype(F32) + came.astype(F32)).astype(BF).reshape(2, rows, -1)
    grads = jnp.stack([dq, own[0], own[1]], axis=0)
    qkv_part = f32dot("td,cte->dce", normed, grads)
    normed_grad = lax.psum(f32dot("cte,cde->td", grads, wqkv).astype(BF), "tensor").astype(F32)
    unused, first_back = jax.vjp(rms_norm, tok.astype(F32), gain_one)
    token_grad, gain_one_part = first_back(normed_grad)
    input_part = (token_grad + hidden_grad).astype(BF)
    both = ("dp", "ctx")

    def scatter(v, dim):
        return lax.psum_scatter(v, both, scatter_dimension=dim, tiled=True)

    up_grad = scatter(up_part.astype(BF), 1).astype(F32)
    down_grad = jnp.transpose(scatter(down_part.astype(BF), 1).astype(F32), (0, 2, 1))
    rest = scatter(
        jnp.concatenate([qkv_part.reshape(width, -1), out_part], axis=1).astype(BF), 0
    ).astype(F32)
    span = q.shape[1]
    qkv_grad = jnp.transpose(rest[:, : 3 * span].reshape(shard, 3, span), (1, 0, 2))
    out_grad = rest[:, 3 * span :].T
    tiny = scatter(
        jnp.concatenate([gain_one_part[:, None], gain_two_part[:, None], router_part], axis=1), 0
    )
    bias_grad = lax.psum(dbias, both)[:, : position_bias.shape[1]]
    return (
        result.reshape(inputs.shape),
        input_part.reshape(inputs.shape),
        tiny[:, 0],
        qkv_grad,
        out_grad,
        bias_grad,
        tiny[:, 1],
        tiny[:, 2:],
        up_grad,
        down_grad,
    )


def rms_norm(values, gain_vector):
    return (
        values * lax.rsqrt(jnp.mean(values * values, axis=-1, keepdims=True) + 1e-06) * gain_vector
    )


def bucket_of(distance):
    clipped = jnp.maximum(distance, 0)
    edge_values = jnp.asarray(bucket_edges, dtype=jnp.int32)
    beyond = jnp.sum((clipped[..., None] >= edge_values).astype(jnp.int32), axis=-1)
    return jnp.where(clipped < 16, clipped, jnp.minimum(16 + beyond, 31))


def toeplitz(diagonal, query_count, key_count):
    head_count = diagonal.shape[0]
    padded = jnp.pad(diagonal, ((0, 0), (0, 1)))
    row_width = query_count + key_count
    repeated = jnp.broadcast_to(padded[:, None, :], (head_count, query_count, row_width)).reshape(
        head_count, query_count * row_width
    )
    repeated = jnp.pad(repeated, ((0, 0), (0, query_count))).reshape(
        head_count, query_count, row_width + 1
    )[:, :, :key_count]
    return repeated[:, :, ::-1]


def diagonal_sums(gradient):
    head_count, query_count, key_count = gradient.shape
    offset_count = query_count + key_count - 1
    flipped = jnp.pad(gradient[:, :, ::-1], ((0, 0), (0, 0), (0, query_count)))
    skewed = flipped.reshape(head_count, query_count * (offset_count + 1))[
        :, : query_count * offset_count
    ]
    return jnp.sum(skewed.reshape(head_count, query_count, offset_count), axis=1)


def bucket_table(query_first, query_count, key_count):
    offsets = (
        query_first - (key_count - 1) + jnp.arange(query_count + key_count - 1, dtype=jnp.int32)
    )
    return (bucket_of(offsets)[:, None] == jnp.arange(BUCKETS, dtype=jnp.int32)[None, :]).astype(
        jnp.float32
    )


def body(
    inputs,
    lengths,
    expert_ids,
    slot_rows,
    attn_gain,
    qkv_weight,
    out_weight,
    position_bias,
    ffn_gain,
    router_weight,
    up_weight,
    down_weight,
    cotangent,
):
    highest = lax.Precision.HIGHEST
    micro_count, seg_rows, model_width = inputs.shape
    local_heads = position_bias.shape[1]
    head_size = qkv_weight.shape[2] // local_heads
    expert_count = up_weight.shape[0]
    query_first = lax.axis_index("ctx") * seg_rows
    query_pos = query_first + jnp.arange(seg_rows, dtype=jnp.int32)

    def pair_scores(query_heads, query_start, key_heads, length):
        query_count = query_heads.shape[0]
        key_count = key_heads.shape[0]
        scores = (
            jnp.einsum("qhd,khd->hqk", query_heads, key_heads, preferred_element_type=jnp.float32)
            * 0.125
        )
        diagonal = jnp.einsum(
            "rb,bh->hr",
            bucket_table(query_start, query_count, key_count),
            position_bias,
            precision=highest,
        )
        scores = scores + toeplitz(diagonal, query_count, key_count)
        query_place = query_start + jnp.arange(query_count, dtype=jnp.int32)
        key_place = jnp.arange(key_count, dtype=jnp.int32)
        allowed = (key_place[None, :] <= query_place[:, None]) & (key_place[None, :] < length)
        return (scores, allowed)

    def scores_for(query_heads, key_block, length):
        key_count = key_block.shape[0]
        key_heads = key_block.reshape(key_count, local_heads, head_size)
        scores, allowed = pair_scores(query_heads, query_first, key_heads, length)
        return (scores, allowed, key_heads)

    results = []
    input_parts = []
    grad_sums = None
    bias_total = jnp.zeros((local_heads, BUCKETS), jnp.float32)
    for micro_step in range(micro_count):
        forward_gain_one = lax.all_gather(attn_gain, ("dp", "ctx"), axis=0, tiled=True)
        forward_qkv_full = lax.all_gather(qkv_weight, ("dp", "ctx"), axis=1, tiled=True)
        forward_out_full = lax.all_gather(out_weight, ("dp", "ctx"), axis=1, tiled=True)
        forward_gain_two = lax.all_gather(ffn_gain, ("dp", "ctx"), axis=0, tiled=True)
        forward_router_full = lax.all_gather(router_weight, ("dp", "ctx"), axis=0, tiled=True)
        forward_up_full = lax.all_gather(up_weight, ("dp", "ctx"), axis=1, tiled=True)
        forward_down_full = lax.all_gather(down_weight, ("dp", "ctx"), axis=2, tiled=True)
        forward_tokens = inputs[micro_step].astype(jnp.float32)
        forward_length = lengths[micro_step]
        forward_normed = rms_norm(forward_tokens, forward_gain_one.astype(jnp.float32)).astype(
            jnp.bfloat16
        )
        forward_projected = jnp.einsum(
            "td,cde->cte", forward_normed, forward_qkv_full, preferred_element_type=jnp.float32
        ).astype(jnp.bfloat16)
        forward_query_heads = forward_projected[0].reshape(seg_rows, local_heads, head_size)
        row_top = jnp.full((local_heads, seg_rows), -1e30, jnp.float32)
        attend_scores, attend_allowed, attend_key_heads = scores_for(
            forward_query_heads,
            lax.all_gather(forward_projected[1], "ctx", axis=0, tiled=True),
            forward_length,
        )
        value_heads = lax.all_gather(forward_projected[2], "ctx", axis=0, tiled=True).reshape(
            attend_key_heads.shape
        )
        attend_scores = jnp.where(attend_allowed[None], attend_scores, -1e30)
        new_top = jnp.maximum(row_top, jnp.max(attend_scores, axis=-1))
        weights_exp = jnp.where(
            attend_allowed[None], jnp.exp(attend_scores - new_top[:, :, None]), 0.0
        )
        row_total = jnp.sum(weights_exp, axis=-1)
        summed = jnp.einsum(
            "hqk,khd->hqd",
            weights_exp.astype(jnp.bfloat16),
            value_heads,
            preferred_element_type=jnp.float32,
        )
        row_top, row_total, summed = (new_top, row_total, summed)
        forward_attended = summed / row_total[:, :, None]
        forward_log_total = row_top + jnp.log(row_total)
        forward_attended_low = (
            jnp.transpose(forward_attended, (1, 0, 2)).reshape(seg_rows, -1).astype(jnp.bfloat16)
        )
        branch = lax.psum(
            jnp.dot(
                forward_attended_low, forward_out_full, preferred_element_type=jnp.float32
            ).astype(jnp.bfloat16),
            "tensor",
        ).astype(jnp.float32)
        forward_hidden = forward_tokens + branch
        forward_normed_two = rms_norm(forward_hidden, forward_gain_two.astype(jnp.float32)).astype(
            jnp.bfloat16
        )
        logits = jnp.dot(
            forward_normed_two, forward_router_full, preferred_element_type=jnp.float32
        )
        forward_router_probs = jax.nn.softmax(logits, axis=-1)
        forward_chosen = (
            expert_ids[micro_step][:, None] == jnp.arange(expert_count, dtype=jnp.int32)[None, :]
        ).astype(jnp.float32)
        forward_gate_value = jnp.sum(forward_router_probs * forward_chosen, axis=-1)
        forward_slot_table = slot_rows[micro_step, 0]
        padded = jnp.concatenate(
            [forward_normed_two, jnp.zeros((1, model_width), jnp.bfloat16)], axis=0
        )
        forward_picked = padded[forward_slot_table]
        forward_raised = jnp.einsum(
            "ekd,edf->ekf", forward_picked, forward_up_full, preferred_element_type=jnp.float32
        )
        forward_activated = jax.nn.gelu(forward_raised).astype(jnp.bfloat16)
        lowered = jnp.einsum(
            "ekf,efd->ekd", forward_activated, forward_down_full, preferred_element_type=jnp.float32
        )
        spread = (
            jnp.zeros((seg_rows + 1, model_width), jnp.float32)
            .at[forward_slot_table.reshape(-1)]
            .add(lowered.reshape(-1, model_width))[:seg_rows]
        )
        forward_expert_sum = lax.psum(spread.astype(jnp.bfloat16), "tensor").astype(jnp.float32)
        forward_live_rows = (query_pos < forward_length).astype(jnp.float32)[:, None]
        result = (
            forward_live_rows * (forward_hidden + forward_gate_value[:, None] * forward_expert_sum)
        ).astype(jnp.bfloat16)
        forward_kept_state = (
            forward_tokens,
            forward_length,
            forward_normed,
            forward_projected,
            forward_attended,
            forward_log_total,
            forward_attended_low,
            forward_hidden,
            forward_normed_two,
            forward_router_probs,
            forward_chosen,
            forward_gate_value,
            forward_slot_table,
            forward_picked,
            forward_raised,
            forward_activated,
            forward_expert_sum,
            forward_live_rows,
        )
        result, kept_state = (result, forward_kept_state)
        gain_one = lax.all_gather(attn_gain, ("dp", "ctx"), axis=0, tiled=True)
        qkv_full = lax.all_gather(qkv_weight, ("dp", "ctx"), axis=1, tiled=True)
        out_full = lax.all_gather(out_weight, ("dp", "ctx"), axis=1, tiled=True)
        gain_two = lax.all_gather(ffn_gain, ("dp", "ctx"), axis=0, tiled=True)
        router_full = lax.all_gather(router_weight, ("dp", "ctx"), axis=0, tiled=True)
        up_full = lax.all_gather(up_weight, ("dp", "ctx"), axis=1, tiled=True)
        down_full = lax.all_gather(down_weight, ("dp", "ctx"), axis=2, tiled=True)
        (
            tokens,
            backward_length,
            normed,
            projected,
            attended,
            log_total,
            attended_low,
            hidden,
            normed_two,
            router_probs,
            chosen,
            gate_value,
            slot_table,
            picked,
            raised,
            activated,
            expert_sum,
            live_rows,
        ) = kept_state
        upstream = live_rows * cotangent[micro_step].astype(jnp.float32)
        sum_grad = (gate_value[:, None] * upstream).astype(jnp.bfloat16)
        gate_grad = jnp.sum(expert_sum * upstream, axis=-1)
        logit_grad = (router_probs * gate_grad[:, None] * (chosen - gate_value[:, None])).astype(
            jnp.bfloat16
        )
        router_part = jnp.einsum(
            "td,te->de", normed_two, logit_grad, preferred_element_type=jnp.float32
        )
        padded_grad = jnp.concatenate([sum_grad, jnp.zeros((1, model_width), jnp.bfloat16)], axis=0)
        slot_grad = padded_grad[slot_table]
        down_part = jnp.einsum(
            "ekf,ekd->efd", activated, slot_grad, preferred_element_type=jnp.float32
        )
        act_grad = jnp.einsum(
            "ekd,efd->ekf", slot_grad, down_full, preferred_element_type=jnp.float32
        )
        unused_value, gelu_back = jax.vjp(jax.nn.gelu, raised)
        raised_grad = gelu_back(act_grad)[0].astype(jnp.bfloat16)
        up_part = jnp.einsum(
            "ekd,ekf->edf", picked, raised_grad, preferred_element_type=jnp.float32
        )
        picked_grad = jnp.einsum(
            "ekf,edf->ekd", raised_grad, up_full, preferred_element_type=jnp.float32
        )
        spread_grad = (
            jnp.zeros((seg_rows + 1, model_width), jnp.float32)
            .at[slot_table.reshape(-1)]
            .add(picked_grad.reshape(-1, model_width))[:seg_rows]
        )
        normed_two_grad = lax.psum(spread_grad.astype(jnp.bfloat16), "tensor").astype(
            jnp.float32
        ) + jnp.einsum("te,de->td", logit_grad, router_full, preferred_element_type=jnp.float32)
        unused_norm, second_back = jax.vjp(rms_norm, hidden, gain_two.astype(jnp.float32))
        hidden_grad, gain_two_part = second_back(normed_two_grad)
        hidden_grad = hidden_grad + upstream
        branch_grad = hidden_grad.astype(jnp.bfloat16)
        out_part = jnp.einsum(
            "te,td->ed", attended_low, branch_grad, preferred_element_type=jnp.float32
        )
        attended_grad = jnp.einsum(
            "td,ed->te", branch_grad, out_full, preferred_element_type=jnp.float32
        ).astype(jnp.bfloat16)
        grad_heads = attended_grad.reshape(seg_rows, local_heads, head_size)
        row_delta = jnp.sum(
            jnp.transpose(grad_heads.astype(jnp.float32), (1, 0, 2)) * attended, axis=-1
        )
        backward_query_heads = projected[0].reshape(seg_rows, local_heads, head_size)
        bias_zero = jnp.zeros((local_heads, BUCKETS), jnp.float32)
        attend_bias_acc = bias_zero
        bias_acc = attend_bias_acc
        score_scores, score_allowed, score_key_heads = scores_for(
            backward_query_heads,
            lax.all_gather(projected[1], "ctx", axis=0, tiled=True),
            backward_length,
        )
        score_value_heads = lax.all_gather(projected[2], "ctx", axis=0, tiled=True).reshape(
            score_key_heads.shape
        )
        score_key_count = score_key_heads.shape[0]
        soft_weights = jnp.where(
            score_allowed[None], jnp.exp(score_scores - log_total[:, :, None]), 0.0
        )
        weight_grad = jnp.einsum(
            "qhd,khd->hqk", grad_heads, score_value_heads, preferred_element_type=jnp.float32
        )
        score_grad = (soft_weights * (weight_grad - row_delta[:, :, None])).astype(jnp.bfloat16)
        query_acc = jnp.einsum(
            "hqk,khd->qhd", score_grad, score_key_heads, preferred_element_type=jnp.float32
        )
        bias_acc = bias_acc + jnp.dot(
            diagonal_sums(score_grad.astype(jnp.float32)),
            bucket_table(query_first, seg_rows, score_key_count),
            precision=highest,
        )
        (
            (attend_query_acc, attend_bias_acc),
            attend_soft_weights,
            attend_score_grad,
            attend_key_count,
        ) = ((query_acc, bias_acc), soft_weights, score_grad, score_key_count)
        key_term = (
            jnp.einsum(
                "hqk,qhd->khd",
                attend_score_grad,
                backward_query_heads,
                preferred_element_type=jnp.float32,
            )
            * 0.125
        )
        value_term = jnp.einsum(
            "hqk,qhd->khd",
            attend_soft_weights.astype(jnp.bfloat16),
            grad_heads,
            preferred_element_type=jnp.float32,
        )
        grad_term = jnp.stack(
            [key_term.reshape(attend_key_count, -1), value_term.reshape(attend_key_count, -1)],
            axis=1,
        )
        key_value_acc = grad_term
        query_acc, key_value_acc, bias_part = (attend_query_acc, key_value_acc, attend_bias_acc)
        own_grads = lax.psum_scatter(
            key_value_acc.astype(jnp.bfloat16), "ctx", scatter_dimension=0, tiled=True
        ).astype(jnp.float32)
        query_grad = (query_acc * 0.125).reshape(seg_rows, -1).astype(jnp.bfloat16)
        qkv_grad = jnp.stack(
            [
                query_grad,
                own_grads[:, 0].astype(jnp.bfloat16),
                own_grads[:, 1].astype(jnp.bfloat16),
            ],
            axis=0,
        )
        qkv_part = jnp.einsum("td,cte->cde", normed, qkv_grad, preferred_element_type=jnp.float32)
        normed_grad = lax.psum(
            jnp.einsum(
                "cte,cde->td", qkv_grad, qkv_full, preferred_element_type=jnp.float32
            ).astype(jnp.bfloat16),
            "tensor",
        ).astype(jnp.float32)
        unused_first, first_back = jax.vjp(rms_norm, tokens, gain_one.astype(jnp.float32))
        token_grad, gain_one_part = first_back(normed_grad)
        input_part = (token_grad + hidden_grad).astype(jnp.bfloat16)
        weight_parts = (
            gain_one_part,
            qkv_part,
            out_part,
            gain_two_part,
            router_part,
            up_part,
            down_part,
        )
        input_part, weight_parts, bias_part = (input_part, weight_parts, bias_part)
        results.append(result)
        input_parts.append(input_part)
        grad_sums = (
            weight_parts
            if grad_sums is None
            else tuple((old_sum + new_part for old_sum, new_part in zip(grad_sums, weight_parts)))
        )
        bias_total = bias_total + bias_part
    reduced = (
        lax.psum_scatter(grad_sums[0], ("dp", "ctx"), scatter_dimension=0, tiled=True),
        lax.psum_scatter(grad_sums[1], ("dp", "ctx"), scatter_dimension=1, tiled=True),
        lax.psum_scatter(grad_sums[2], ("dp", "ctx"), scatter_dimension=1, tiled=True),
        lax.psum_scatter(grad_sums[3], ("dp", "ctx"), scatter_dimension=0, tiled=True),
        lax.psum_scatter(grad_sums[4], ("dp", "ctx"), scatter_dimension=0, tiled=True),
        lax.psum_scatter(grad_sums[5], ("dp", "ctx"), scatter_dimension=1, tiled=True),
        lax.psum_scatter(grad_sums[6], ("dp", "ctx"), scatter_dimension=2, tiled=True),
    )
    bias_grad_total = lax.psum(bias_total, ("dp", "ctx"))
    return (
        jnp.stack(results, axis=0),
        jnp.stack(input_parts, axis=0),
        reduced[0],
        reduced[1],
        reduced[2],
        jnp.transpose(bias_grad_total),
        reduced[3],
        reduced[4],
        reduced[5],
        reduced[6],
    )


def solution(mesh):
    small = mesh.shape["ctx"] == 2 and mesh.shape["dp"] == 4 and mesh.shape["tensor"] == 4
    return jax.shard_map(
        body_fast if small else body,
        mesh=mesh,
        in_specs=(
            P("dp", "ctx", None),
            P("dp"),
            P("dp", "ctx"),
            P("dp", "ctx", None, None),
            P(("dp", "ctx")),
            P(None, ("dp", "ctx"), "tensor"),
            P("tensor", ("dp", "ctx")),
            P(None, "tensor"),
            P(("dp", "ctx")),
            P(("dp", "ctx"), None),
            P(None, ("dp", "ctx"), "tensor"),
            P(None, "tensor", ("dp", "ctx")),
            P("dp", "ctx", None),
        ),
        out_specs=(
            P("dp", "ctx", None),
            P("dp", "ctx", None),
            P(("dp", "ctx")),
            P(None, ("dp", "ctx"), "tensor"),
            P("tensor", ("dp", "ctx")),
            P(None, "tensor"),
            P(("dp", "ctx")),
            P(("dp", "ctx"), None),
            P(None, ("dp", "ctx"), "tensor"),
            P(None, "tensor", ("dp", "ctx")),
        ),
        check_vma=False,
    )
```

```python
import functools

import jax
import jax.numpy as jnp
import numpy as np
from jax import lax
from jax.experimental import pallas as pl
from jax.experimental.pallas import tpu as pltpu
from jax.sharding import PartitionSpec as P

BUCKETS = 32
MESH = pl.DeviceIdType.MESH
BF = jnp.bfloat16
F32 = jnp.float32


bucket_edges = np.ceil(16.0 * 8.0 ** (np.arange(1, 16) / 16.0)).astype(np.int32)
bucket_starts = [int(n) for n in range(17)] + [int(n) for n in bucket_edges]


QT = 256
BAND = 128


def mm(a, b):
    return jnp.dot(a, b, preferred_element_type=F32)


def mm_nt(a, b):
    return lax.dot_general(a, b, (((1,), (1,)), ((), ())), preferred_element_type=F32)


def mm_tn(a, b):
    return lax.dot_general(a, b, (((0,), (0,)), ((), ())), preferred_element_type=F32)


class Group:
    def __init__(self, place, src, dst_at, zs, zr, xs, xr, local):
        self.dp, self.cx, self.t = place
        self.src, self.dst_at = src, dst_at
        self.zs, self.zr, self.xs, self.xr, self.local = zs, zr, xs, xr, local

    def slab(self, k, cx):
        return lax.rem(self.dp + 4 - k, 4) * 2 + cx

    def own(self):
        return pltpu.make_async_copy(self.src, self.dst_at(self.slab(0, self.cx)), self.local)

    def z_send(self, k):
        return pltpu.make_async_remote_copy(
            src_ref=self.src,
            dst_ref=self.dst_at(self.slab(0, self.cx)),
            send_sem=self.zs(k - 1),
            recv_sem=self.zr(k - 1),
            device_id=(lax.rem(self.dp + k, 4), self.cx, self.t),
            device_id_type=MESH,
        )

    def z_recv(self, k):
        return pltpu.make_async_remote_copy(
            src_ref=self.src,
            dst_ref=self.dst_at(self.slab(k, self.cx)),
            send_sem=self.zs(k - 1),
            recv_sem=self.zr(k - 1),
            device_id=(lax.rem(self.dp + k, 4), self.cx, self.t),
            device_id_type=MESH,
        )

    def x_send(self, k):
        spot = self.dst_at(self.slab(k, self.cx))
        return pltpu.make_async_remote_copy(
            src_ref=self.src if k == 0 else spot,
            dst_ref=spot,
            send_sem=self.xs(k),
            recv_sem=self.xr(k),
            device_id=(self.dp, 1 - self.cx, self.t),
            device_id_type=MESH,
        )

    def x_recv(self, k):
        spot = self.dst_at(self.slab(k, 1 - self.cx))
        return pltpu.make_async_remote_copy(
            src_ref=self.src,
            dst_ref=spot,
            send_sem=self.xs(k),
            recv_sem=self.xr(k),
            device_id=(self.dp, 1 - self.cx, self.t),
            device_id_type=MESH,
        )

    def begin(self):
        self.own().start()
        for k in (1, 3, 2):
            self.z_send(k).start()
        self.x_send(0).start()

    def hand_on(self):
        for k in (1, 3, 2):
            self.z_recv(k).wait_recv()
            self.x_send(k).start()

    def finish(self):
        self.own().wait()
        for k in range(4):
            self.x_recv(k).wait_recv()

    def drain(self):
        for k in (1, 2, 3):
            self.z_send(k).wait_send()
        for k in range(4):
            self.x_send(k).wait_send()


def lane_halves(shape):
    return lax.broadcasted_iota(jnp.int32, shape, len(shape) - 1) < 64


def head_cut(h):
    return (h // 2) * 128, h % 2 == 0


def head_tile(block, h, heads):
    if block.shape[-1] == 64:
        return block
    lower = lane_halves(block.shape)
    keep = lower if h % 2 == 0 else jnp.logical_not(lower)
    return jnp.where(keep, block, jnp.zeros_like(block))


def lanes_of(h, heads):
    first = (h // 2) * 128
    return slice(first, min(first + 128, heads * 64))


def fill_bias(bias_ref, band_ref, heads):
    rows = lax.broadcasted_iota(jnp.int32, (BAND, 2 * BAND), 0)
    cols = lax.broadcasted_iota(jnp.int32, (BAND, 2 * BAND), 1)
    away = rows + BAND - cols
    for h in range(heads):
        tile = jnp.full((BAND, 2 * BAND), bias_ref[0, h], F32)
        for b in range(1, BUCKETS):
            tile = jnp.where(away >= bucket_starts[b], bias_ref[b, h], tile)
        band_ref[h] = tile - bias_ref[BUCKETS - 1, h]


def masked_scores(q_tile, keys, band_ref, scores, h, first, length):
    count = keys.shape[0]
    scores[:, BAND:] = mm_nt(q_tile, keys) * 0.125
    for part in range(QT // BAND):
        spot = (
            pl.ds(part * BAND, BAND),
            pl.ds(pl.multiple_of(first + part * BAND, BAND), 2 * BAND),
        )
        scores[spot] = scores[spot] + band_ref[h]
    values = scores[:, BAND:]
    key_pos = lax.broadcasted_iota(jnp.int32, (QT, count), 1)
    query_pos = lax.broadcasted_iota(jnp.int32, (QT, count), 0) + first
    allowed = (key_pos <= query_pos) & (key_pos < length)
    return jnp.where(allowed, values, -1e30), allowed


def first_kernel(
    heads,
    len_ref,
    bias_ref,
    tok,
    small,
    wqkv,
    wo,
    w,
    hidden,
    ntwo,
    normed,
    q,
    kcat,
    vcat,
    lse,
    ab,
    wqkv_full,
    wo_own,
    gains,
    w_full,
    small_all,
    wo_full,
    ab_all,
    band,
    scores,
    sm_s,
    sm_r,
    q_s,
    q_r,
    o_s,
    o_r,
    ot_s,
    ot_r,
    kv_s,
    kv_r,
    ab_s,
    ab_r,
    w_s,
    w_r,
    local,
):
    dp, cx, t = lax.axis_index("dp"), lax.axis_index("ctx"), lax.axis_index("tensor")
    place = (dp, cx, t)
    seg = tok.shape[0] // 2
    experts = w.shape[0]
    group_peers = [
        (lax.rem(dp + k, 4), cx if c == 0 else 1 - cx, t)
        for k in range(4)
        for c in range(2)
        if (k, c) != (0, 0)
    ]
    group_from = [
        lax.rem(dp + 4 - k, 4) * 2 + (cx if c == 0 else 1 - cx)
        for k in range(4)
        for c in range(2)
        if (k, c) != (0, 0)
    ]
    tensor_peers = [(dp, cx, lax.rem(t + k, 4)) for k in (1, 2, 3)]
    own_slab = dp * 2 + cx

    barrier = pltpu.get_barrier_semaphore()
    for peer in group_peers + tensor_peers:
        pl.semaphore_signal(barrier, inc=1, device_id=peer, device_id_type=MESH)
    pl.semaphore_wait(barrier, len(group_peers) + len(tensor_peers))

    def small_send(i):
        return pltpu.make_async_remote_copy(
            src_ref=small,
            dst_ref=small_all.at[own_slab],
            send_sem=sm_s.at[i],
            recv_sem=sm_r.at[i],
            device_id=group_peers[i],
            device_id_type=MESH,
        )

    def small_recv(i):
        return pltpu.make_async_remote_copy(
            src_ref=small,
            dst_ref=small_all.at[group_from[i]],
            send_sem=sm_s.at[i],
            recv_sem=sm_r.at[i],
            device_id=group_peers[i],
            device_id_type=MESH,
        )

    small_own = pltpu.make_async_copy(small, small_all.at[own_slab], local.at[0])

    def rows96(s):
        return pl.ds(pl.multiple_of(s * 96, 32), 96)

    g_qkv = Group(
        place,
        wqkv,
        lambda s: wqkv_full.at[:, rows96(s), :],
        lambda i: q_s.at[i],
        lambda i: q_r.at[i],
        lambda i: q_s.at[3 + i],
        lambda i: q_r.at[3 + i],
        local.at[1],
    )
    g_out = Group(
        place,
        wo,
        lambda s: wo_full.at[t, rows96(s), :],
        lambda i: o_s.at[i],
        lambda i: o_r.at[i],
        lambda i: o_s.at[3 + i],
        lambda i: o_r.at[3 + i],
        local.at[2],
    )
    g_w = [
        Group(
            place,
            w.at[e],
            lambda s, e=e: w_full.at[e, :, s],
            lambda i, e=e: w_s.at[e, i],
            lambda i, e=e: w_r.at[e, i],
            lambda i, e=e: w_s.at[e, 3 + i],
            lambda i, e=e: w_r.at[e, 3 + i],
            local.at[3 + e],
        )
        for e in range(experts)
    ]

    small_own.start()
    for i in range(7):
        small_send(i).start()
    g_qkv.begin()
    g_out.begin()

    @pl.when(cx == 0)
    def _():
        for m in range(2):
            kcat[m, seg:, :] = jnp.zeros((seg, kcat.shape[2]), BF)
            vcat[m, seg:, :] = jnp.zeros((seg, kcat.shape[2]), BF)

    fill_bias(bias_ref, band, heads)

    small_own.wait()
    for i in range(7):
        small_recv(i).wait_recv()
    total = small_all[0].astype(F32)
    for i in range(1, 8):
        total = total + small_all[i].astype(F32)
    gains[...] = total

    def norm_rows(i, carry):
        rows = pl.ds(pl.multiple_of(i * 128, 128), 128)
        x = tok[rows, :].astype(F32)
        scale = lax.rsqrt(jnp.mean(x * x, axis=-1, keepdims=True) + 1e-06)
        normed[rows, :] = (x * scale * gains[0:1, :]).astype(BF)
        return carry

    lax.fori_loop(0, 2 * seg // 128, norm_rows, 0)

    g_qkv.hand_on()
    for e in range(experts):
        g_w[e].begin()
    g_out.hand_on()
    g_qkv.finish()

    def project(m):
        def step(i, carry):
            rows = pl.ds(pl.multiple_of(m * seg + i * 256, 256), 256)
            spots = pl.ds(pl.multiple_of(cx * seg + i * 256, 256), 256)
            x = normed[rows, :]
            q[rows, :] = mm(x, wqkv_full[0]).astype(BF)
            kcat[m, spots, :] = mm(x, wqkv_full[1]).astype(BF)
            vcat[m, spots, :] = mm(x, wqkv_full[2]).astype(BF)
            return carry

        lax.fori_loop(0, seg // 256, step, 0)

    def kv_copy(m, which):
        ref = (kcat, vcat)[which]
        return pltpu.make_async_remote_copy(
            src_ref=ref.at[m, pl.ds(0, seg), :],
            dst_ref=ref.at[m, pl.ds(0, seg), :],
            send_sem=kv_s.at[m * 2 + which],
            recv_sem=kv_r.at[m * 2 + which],
            device_id=(dp, 1 - cx, t),
            device_id_type=MESH,
        )

    for m in range(2):
        project(m)

        @pl.when(cx == 0)
        def _():
            kv_copy(m, 0).start()
            kv_copy(m, 1).start()

    g_out.finish()

    def wo_send(k):
        return pltpu.make_async_remote_copy(
            src_ref=wo_full.at[t],
            dst_ref=wo_full.at[t],
            send_sem=ot_s.at[k - 1],
            recv_sem=ot_r.at[k - 1],
            device_id=tensor_peers[k - 1],
            device_id_type=MESH,
        )

    def wo_recv(k):
        spot = wo_full.at[lax.rem(t + 4 - k, 4)]
        return pltpu.make_async_remote_copy(
            src_ref=spot,
            dst_ref=spot,
            send_sem=ot_s.at[k - 1],
            recv_sem=ot_r.at[k - 1],
            device_id=tensor_peers[k - 1],
            device_id_type=MESH,
        )

    for k in (1, 2, 3):
        wo_send(k).start()

    def ab_copy(m, k, source):
        spot = ab_all.at[source, pl.ds(m * seg, seg), :]
        return pltpu.make_async_remote_copy(
            src_ref=spot,
            dst_ref=spot,
            send_sem=ab_s.at[m * 3 + k - 1],
            recv_sem=ab_r.at[m * 3 + k - 1],
            device_id=tensor_peers[k - 1],
            device_id_type=MESH,
        )

    def attend(m):
        length = len_ref[m]

        def step(i, carry):
            rows = pl.ds(pl.multiple_of(m * seg + i * QT, QT), QT)
            first = cx * seg + i * QT
            lanes128 = lax.broadcasted_iota(jnp.int32, (QT, 128), 1)
            tops = jnp.zeros((QT, 128), F32)
            held = []
            for h in range(heads):
                cut = lanes_of(h, heads)
                q_tile = head_tile(q[rows, cut], h, heads)
                values, allowed = masked_scores(
                    q_tile, kcat[m, :, cut], band, scores, h, first, length
                )
                top = jnp.max(values, axis=-1, keepdims=True)
                raised = jnp.where(allowed, jnp.exp(values - top), 0.0)
                mass = jnp.sum(raised, axis=-1, keepdims=True)
                probs = (raised * (1.0 / mass)).astype(BF)
                held.append(mm(probs, vcat[m, :, cut]))
                tops = jnp.where(lanes128 == h, top + jnp.log(mass), tops)
                if h % 2 == 1:
                    both = jnp.where(lane_halves(held[0].shape), held[0], held[1])
                    ab_all[t, rows, cut] = both.astype(BF)
                    held = []
                elif h == heads - 1:
                    ab_all[t, rows, cut] = held[0].astype(BF)
            lse[rows, :] = tops
            return carry

        lax.fori_loop(0, seg // QT, step, 0)

    for m in range(2):

        @pl.when(cx == 1)
        def _():
            kv_copy(m, 0).wait_recv()
            kv_copy(m, 1).wait_recv()

        attend(m)
        for k in (1, 2, 3):
            ab_copy(m, k, t).start()
        if m == 0:
            g_w[0].hand_on()
    for k in (1, 2, 3):
        wo_recv(k).wait_recv()
    wo_own[...] = wo_full[t]
    ab[...] = ab_all[t]

    for m in range(2):
        for k in (1, 2, 3):
            ab_copy(m, k, lax.rem(t + 4 - k, 4)).wait_recv()

        def branch(i, carry):
            rows = pl.ds(pl.multiple_of(m * seg + i * 256, 256), 256)
            total = mm_nt(ab_all[0, rows, :], wo_full[0])
            for j in range(1, 4):
                total = total + mm_nt(ab_all[j, rows, :], wo_full[j])
            x = tok[rows, :].astype(F32) + total
            hidden[rows, :] = x
            scale = lax.rsqrt(jnp.mean(x * x, axis=-1, keepdims=True) + 1e-06)
            ntwo[rows, :] = (x * scale * gains[1:2, :]).astype(BF)
            return carry

        lax.fori_loop(0, seg // 256, branch, 0)
        if m == 0 and experts > 1:
            g_w[1].hand_on()

    for e in range(2, experts):
        g_w[e].hand_on()
    for e in range(experts):
        g_w[e].finish()

    for i in range(7):
        small_send(i).wait_send()
    g_qkv.drain()
    g_out.drain()
    for e in range(experts):
        g_w[e].drain()
    for k in (1, 2, 3):
        wo_send(k).wait_send()
    for m in range(2):
        for k in (1, 2, 3):
            ab_copy(m, k, t).wait_send()

        @pl.when(cx == 0)
        def _():
            kv_copy(m, 0).wait_send()
            kv_copy(m, 1).wait_send()


def first_call(lengths, bias, tok, small, wqkv, wo, w):
    heads = bias.shape[1]
    rows, width = tok.shape
    span = wqkv.shape[2]
    experts = w.shape[0]
    ff = w.shape[3]
    vm = pl.BlockSpec(memory_space=pltpu.VMEM)
    sm = pl.BlockSpec(memory_space=pltpu.SMEM)
    hbm = pl.BlockSpec(memory_space=pl.ANY)
    dma = pltpu.SemaphoreType.DMA
    return pl.pallas_call(
        functools.partial(first_kernel, heads),
        out_shape=(
            jax.ShapeDtypeStruct((rows, width), F32),
            jax.ShapeDtypeStruct((rows, width), BF),
            jax.ShapeDtypeStruct((rows, width), BF),
            jax.ShapeDtypeStruct((rows, span), BF),
            jax.ShapeDtypeStruct((2, rows, span), BF),
            jax.ShapeDtypeStruct((2, rows, span), BF),
            jax.ShapeDtypeStruct((rows, 128), F32),
            jax.ShapeDtypeStruct((rows, span), BF),
            jax.ShapeDtypeStruct((3, width, span), BF),
            jax.ShapeDtypeStruct((width, span), BF),
            jax.ShapeDtypeStruct((16, width), F32),
            jax.ShapeDtypeStruct((experts, 2, 8, width // 8, ff), BF),
        ),
        in_specs=[sm, sm, vm, hbm, hbm, hbm, hbm],
        out_specs=(vm,) * 11 + (hbm,),
        scratch_shapes=[
            pltpu.VMEM((8, 16, width), BF),
            pltpu.VMEM((4, width, span), BF),
            pltpu.VMEM((4, rows, span), BF),
            pltpu.VMEM((heads, BAND, 2 * BAND), F32),
            pltpu.VMEM((QT, rows + BAND), F32),
            dma((7,)),
            dma((7,)),
            dma((7,)),
            dma((7,)),
            dma((7,)),
            dma((7,)),
            dma((3,)),
            dma((3,)),
            dma((4,)),
            dma((4,)),
            dma((6,)),
            dma((6,)),
            dma((experts, 7)),
            dma((experts, 7)),
            dma((3 + experts,)),
        ],
        compiler_params=pltpu.CompilerParams(
            collective_id=0, has_side_effects=True, vmem_limit_bytes=56 << 20
        ),
    )(lengths, bias, tok, small, wqkv, wo, w)


C0 = float(np.sqrt(2.0 / np.pi))
C1 = 0.044715


def norm_back(x, gain, grad):
    scale = lax.rsqrt(jnp.mean(x * x, axis=-1, keepdims=True) + 1e-06)
    unit = x * scale
    pulled = grad * gain
    inner = jnp.mean(pulled * unit, axis=-1, keepdims=True)
    return scale * (pulled - unit * inner), grad * unit


def second_kernel(
    heads,
    len_ref,
    bias_ref,
    ids,
    slot_lanes,
    slot_subs,
    cot,
    ntwo,
    q,
    kcat,
    vcat,
    lse,
    ab,
    wqkv,
    wo,
    gains,
    normed_hbm,
    tok_hbm,
    hidden_hbm,
    w_full,
    result,
    input_grad,
    w_grad,
    small_grad,
    tiny_out,
    dbias_out,
    wbuf,
    gw,
    xbuf,
    gq,
    qx,
    qz,
    sum_grad,
    epart,
    npart,
    ffn,
    probs_ref,
    hidden,
    tok,
    cbuf,
    ysend,
    ybuf,
    kept,
    hgrad,
    bgrad,
    own_out,
    agrad,
    grads,
    dk,
    dv,
    dkv,
    band,
    scores,
    spread,
    band_sum,
    whole_sum,
    tiny_own,
    tiny_t,
    tiny_mid,
    tiny_g,
    dbias_own,
    dbias_g,
    load_sem,
    row_sem,
    out_sem,
    ready,
    wx_s,
    wx_r,
    wz_s,
    wz_r,
    c_s,
    c_r,
    y_s,
    y_r,
    a_s,
    a_r,
    kv_s,
    kv_r,
    qx_s,
    qx_r,
    qz_s,
    qz_r,
    tt_s,
    tt_r,
    tg_s,
    tg_r,
    db_s,
    db_r,
):
    dp, cx, t = lax.axis_index("dp"), lax.axis_index("ctx"), lax.axis_index("tensor")
    yy, core = t // 2, lax.rem(t, 2)
    seg = cot.shape[0] // 2
    width = cot.shape[1]
    experts = w_full.shape[0]
    cap = slot_subs.shape[0]
    half, quarter = seg // 2, seg // 4
    group_peers = [
        (lax.rem(dp + k, 4), cx if c == 0 else 1 - cx, t)
        for k in range(4)
        for c in range(2)
        if (k, c) != (0, 0)
    ]
    tensor_peers = [(dp, cx, lax.rem(t + k, 4)) for k in (1, 2, 3)]
    sibling = (dp, cx, t + 1 - 2 * core)
    across = (dp, cx, lax.rem(t + 2, 4))
    partner = (dp, 1 - cx, t)

    def z_peer(k):
        return (lax.rem(dp + k, 4), cx, t)

    barrier = pltpu.get_barrier_semaphore()
    for peer in group_peers + tensor_peers:
        pl.semaphore_signal(barrier, inc=1, device_id=peer, device_id_type=MESH)
    pl.semaphore_wait(barrier, len(group_peers) + len(tensor_peers))

    def remote(src, dst, send, recv, device):
        return pltpu.make_async_remote_copy(
            src_ref=src,
            dst_ref=dst,
            send_sem=send,
            recv_sem=recv,
            device_id=device,
            device_id_type=MESH,
        )

    def rows96(s):
        return pl.ds(pl.multiple_of(s * 96, 32), 96)

    def load(e, slot):
        return pltpu.make_async_copy(w_full.at[e], wbuf.at[pl.ds(slot * 2, 2)], load_sem.at[slot])

    def own_rows(m, size=None):
        return pl.ds(pl.multiple_of(m * seg + core * half + yy * quarter, 128), quarter)

    def fetch(m, which):
        ref, dst = ((hidden_hbm, hidden), (tok_hbm, tok))[which]
        return pltpu.make_async_copy(ref.at[own_rows(m)], dst.at[m], row_sem.at[m * 2 + which])

    load(0, 0).start()
    for m in range(2):
        fetch(m, 0).start()
        fetch(m, 1).start()

    router16 = gains[...].astype(BF)

    def upstream_of(rows, m, first):
        spot = lax.broadcasted_iota(jnp.int32, (rows.size, 1), 0) + (cx * seg + first)
        live = (spot < len_ref[m]).astype(F32)
        return live, live * cot[rows, :].astype(F32)

    def chosen_of(rows):
        lanes = lax.broadcasted_iota(jnp.int32, (rows.size, 16), 1)
        return (lanes == ids[rows, :] + 2).astype(F32)

    for m in range(2):

        def gates(i, carry):
            rows = pl.ds(pl.multiple_of(m * seg + i * 256, 256), 256)
            logits = mm_nt(ntwo[rows, :], router16)
            lanes = lax.broadcasted_iota(jnp.int32, (256, 16), 1)
            inside = (lanes >= 2) & (lanes < 2 + experts)
            logits = jnp.where(inside, logits, -1e30)
            top = jnp.max(logits, axis=-1, keepdims=True)
            raised = jnp.where(inside, jnp.exp(logits - top), 0.0)
            probs = raised / jnp.sum(raised, axis=-1, keepdims=True)
            probs_ref[rows, :] = probs
            gate = jnp.sum(probs * chosen_of(rows), axis=-1, keepdims=True)
            live, upstream = upstream_of(rows, m, i * 256)
            sum_grad[rows, :] = (gate * upstream).astype(BF)
            epart[rows, :] = jnp.zeros((256, width), BF)
            npart[rows, :] = jnp.zeros((256, width), BF)
            return carry

        lax.fori_loop(0, seg // 256, gates, 0)

    def wx_copy(e, k):
        d = lax.rem(dp + k, 4)
        return remote(
            gw.at[e, :, d * 2 + 1 - cx], xbuf.at[e, k], wx_s.at[e, k], wx_r.at[e, k], partner
        )

    def wz_copy(e, k):
        spot = wbuf.at[e, pl.ds(2 * (k - 1), 2)]
        return remote(xbuf.at[e, k], spot, wz_s.at[e, k - 1], wz_r.at[e, k - 1], z_peer(k))

    order = (2, 1, 3, 0)

    def weight(slot, which):
        return wbuf[slot * 2 + which].reshape(width, -1)

    picked, slot_grad, activated, raised_grad = (ffn.at[i] for i in range(4))

    def expert_step(e, carry):
        slot = lax.rem(e, 2)
        load(e, slot).wait()

        @pl.when(e + 1 < experts)
        def _():
            load(e + 1, 1 - slot).start()

        def one_micro(m, carry):
            rows = pl.ds(pl.multiple_of(m * seg, seg), seg)
            slots = pl.ds(pl.multiple_of(m * cap, cap), cap)
            lanes = lax.broadcasted_iota(jnp.int32, (cap, 8), 1)
            column = jnp.sum(
                jnp.where(lanes == m * experts + e, slot_subs[...], 0), axis=1, keepdims=True
            )
            pick = (column == lax.broadcasted_iota(jnp.int32, (cap, seg), 1)).astype(BF)
            row = slot_lanes[pl.ds(m * experts + e, 1), :]
            put = (row == lax.broadcasted_iota(jnp.int32, (seg, cap), 0)).astype(BF)
            chosen_rows = mm(pick, ntwo[rows, :]).astype(BF)
            picked[slots, :] = chosen_rows
            slot_part = mm(pick, sum_grad[rows, :]).astype(BF)
            slot_grad[slots, :] = slot_part
            raised = mm(chosen_rows, weight(slot, 0))
            square = raised * raised
            bent = jnp.tanh(C0 * raised * (1.0 + C1 * square))
            cdf = 0.5 * (1.0 + bent)
            act = (raised * cdf).astype(BF)
            activated[slots, :] = act
            slope = cdf + 0.5 * raised * (1.0 - bent * bent) * (C0 * (1.0 + 3.0 * C1 * square))
            act_grad = mm(slot_part, weight(slot, 1))
            back = (act_grad * slope).astype(BF)
            raised_grad[slots, :] = back
            lowered = mm_nt(act, weight(slot, 1)).astype(BF)
            epart[rows, :] += mm(put, lowered).astype(BF)
            pulled = mm_nt(back, weight(slot, 0)).astype(BF)
            npart[rows, :] += mm(put, pulled).astype(BF)
            return carry

        lax.fori_loop(0, 2, one_micro, 0)

        def weight_part(i, carry):
            lanes = pl.ds(pl.multiple_of(i * 384, 128), 384)
            slabs = pl.ds(i * 4, 4)
            part = mm_tn(picked[:, lanes], raised_grad[...]).astype(BF)
            gw[e, 0, slabs] = part.reshape(4, 96, -1)
            part = mm_tn(slot_grad[:, lanes], activated[...]).astype(BF)
            gw[e, 1, slabs] = part.reshape(4, 96, -1)
            return carry

        lax.fori_loop(0, width // 384, weight_part, 0)

        @pl.when(e < 2)
        def _():
            for k in order:
                wx_copy(e, k).start()

        return carry

    lax.fori_loop(0, experts, expert_step, 0)

    for k in (1, 2, 3):
        pl.semaphore_signal(ready, inc=1, device_id=z_peer(k), device_id_type=MESH)

    def fetch_normed(i):
        return pltpu.make_async_copy(
            normed_hbm.at[pl.ds(i * seg, seg)], ffn.at[i], load_sem.at[i]
        )

    fetch_normed(0).start()
    fetch_normed(1).start()

    def half_rows(m, c):
        return pl.ds(pl.multiple_of(m * seg + c * half, 128), half)

    parts = (epart, npart, None)

    def c_copy(m, j, src):
        return remote(
            src.at[half_rows(m, 1 - core)], cbuf.at[m, j % 2], c_s.at[m, j], c_r.at[m, j], sibling
        )

    def y_copy(m, j):
        return remote(ysend.at[m, j % 2], ybuf.at[m, j % 2], y_s.at[m, j], y_r.at[m, j], across)

    def to_quarters(m, j, src):
        c_copy(m, j, src).wait_recv()
        mine = pl.ds(pl.multiple_of(m * seg + core * half + yy * quarter, 128), quarter)
        other = pl.ds(pl.multiple_of(m * seg + core * half + (1 - yy) * quarter, 128), quarter)
        near = pl.ds(pl.multiple_of(yy * quarter, 128), quarter)
        far = pl.ds(pl.multiple_of((1 - yy) * quarter, 128), quarter)
        ysend[m, j % 2] = (src[other, :].astype(F32) + cbuf[m, j % 2, far, :].astype(F32)).astype(BF)
        y_copy(m, j).start()
        kept[m, j % 2] = src[mine, :].astype(F32) + cbuf[m, j % 2, near, :].astype(F32)

    def a_copy(m, j, ref, step):
        at = 1 - yy if step == 2 else yy
        spot = ref.at[pl.ds(pl.multiple_of(m * seg + core * half + at * quarter, 128), quarter)]
        source = spot if j == 0 or step == 2 else own_out.at[m, j - 1]
        return remote(
            source, spot, a_s.at[m, j, step], a_r.at[m, j, step], across if step == 0 else sibling
        )

    def a_recv(m, j, ref, step):
        c = core if step == 0 else 1 - core
        at = 1 - yy if step in (0, 2) else yy
        spot = ref.at[pl.ds(pl.multiple_of(m * seg + c * half + at * quarter, 128), quarter)]
        return remote(spot, spot, a_s.at[m, j, step], a_r.at[m, j, step], sibling)

    def own_copy(m, j, ref):
        return pltpu.make_async_copy(
            own_out.at[m, j - 1], ref.at[own_rows(m)], out_sem.at[m * 2 + j - 1]
        )

    def share(m, j, ref):
        a_copy(m, j, ref, 0).start()
        a_copy(m, j, ref, 1).start()
        if j > 0:
            own_copy(m, j, ref).start()

    def pass_on(m, j, ref):
        a_recv(m, j, ref, 0).wait_recv()
        a_copy(m, j, ref, 2).start()

    def shared(m, j, ref):
        a_recv(m, j, ref, 1).wait_recv()
        a_recv(m, j, ref, 2).wait_recv()

    def reduce_step(e):
        for k in order:
            wx_copy(e, k).wait_recv()
            mine = gw[e, :, lax.rem(dp + k, 4) * 2 + cx].astype(F32)
            total = mine + xbuf[e, k].astype(F32)
            if k == 0:
                w_grad[e] = total
            else:
                xbuf[e, k] = total.astype(BF)
                wz_copy(e, k).start()

    def reduce_end(e):
        total = w_grad[e]
        for k in (1, 2, 3):
            wz_copy(e, k).wait_recv()
            total = total + wbuf[e, 2 * (k - 1) : 2 * k].astype(F32)
        w_grad[e] = total

    for m in range(2):
        for j in range(2):
            c_copy(m, j, parts[j]).start()
    for m in range(2):
        for j in range(2):
            to_quarters(m, j, parts[j])

    fill_bias(bias_ref, band, heads)
    spread[...] = jnp.zeros(spread.shape, F32)
    band_sum[...] = jnp.zeros(band_sum.shape, F32)
    whole_sum[...] = jnp.zeros(whole_sum.shape, F32)
    tiny_own[...] = jnp.zeros(tiny_own.shape, F32)
    pl.semaphore_wait(ready, 3)
    reduce_step(0)

    for m in range(2):
        fetch(m, 0).wait()
        fetch(m, 1).wait()
        for j in range(2):
            y_copy(m, j).wait_recv()
        rows = own_rows(m)
        expert_sum = kept[m, 0] + ybuf[m, 0].astype(F32)
        live, upstream = upstream_of(rows, m, core * half + yy * quarter)
        probs, chosen = probs_ref[rows, :], chosen_of(rows)
        gate = jnp.sum(probs * chosen, axis=-1, keepdims=True)
        gate_grad = jnp.sum(expert_sum * upstream, axis=-1, keepdims=True)
        logit_grad = (probs * gate_grad * (chosen - gate)).astype(BF)
        x = hidden[m]
        down = kept[m, 1] + ybuf[m, 1].astype(F32) + mm(logit_grad, router16)
        through, gain_terms = norm_back(x, gains[1:2, :], down)
        full = through + upstream
        hgrad[m] = full
        bgrad[rows, :] = full.astype(BF)
        share(m, 0, bgrad)
        own_out[m, 0] = (live * (x + gate * expert_sum)).astype(BF)
        share(m, 1, result)
        tiny_own[1:2, :] += jnp.sum(gain_terms, axis=0, keepdims=True)
        tiny_own[...] += mm_tn(logit_grad, ntwo[rows, :])
    for m in range(2):
        pass_on(m, 0, bgrad)

    def dkv_copy(m):
        return remote(dkv.at[m], dkv.at[m], kv_s.at[m], kv_r.at[m], partner)

    def attend_back(m):
        length = len_ref[m]
        dk[...] = jnp.zeros(dk.shape, F32)
        dv[...] = jnp.zeros(dv.shape, F32)

        def lower(i, carry):
            rows = pl.ds(pl.multiple_of(m * seg + i * 256, 256), 256)
            agrad[pl.ds(pl.multiple_of(i * 256, 256), 256), :] = mm(bgrad[rows, :], wo[...]).astype(BF)
            return carry

        lax.fori_loop(0, seg // 256, lower, 0)

        def step(i, carry):
            rows = pl.ds(pl.multiple_of(m * seg + i * QT, QT), QT)
            local = pl.ds(pl.multiple_of(i * QT, QT), QT)
            first = cx * seg + i * QT
            held = []
            for h in range(heads):
                cut = lanes_of(h, heads)
                q_tile = head_tile(q[rows, cut], h, heads)
                do_tile = head_tile(agrad[local, cut], h, heads)
                values, allowed = masked_scores(
                    q_tile, kcat[m, :, cut], band, scores, h, first, length
                )
                soft = jnp.where(allowed, jnp.exp(values - lse[rows, h : h + 1]), 0.0)
                soft_grad = mm_nt(do_tile, vcat[m, :, cut])
                dv[:, cut] += mm_tn(soft.astype(BF), do_tile)
                delta = jnp.sum(soft * soft_grad, axis=-1, keepdims=True)
                score_grad = (soft * (soft_grad - delta)).astype(BF)
                dk[:, cut] += mm_tn(score_grad, q_tile)
                held.append(mm(score_grad, kcat[m, :, cut]) * 0.125)
                spread[:, BAND:] = score_grad.astype(F32)
                for part in range(QT // BAND):
                    lanes = pl.ds(pl.multiple_of(first + part * BAND, BAND), 2 * BAND)
                    band_sum[h] += spread[part * BAND : (part + 1) * BAND, lanes]
                whole_sum[h : h + 1, :] += jnp.sum(spread[:, BAND:], axis=0, keepdims=True)
                if h % 2 == 1:
                    both = jnp.where(lane_halves(held[0].shape), held[0], held[1])
                    grads[0, rows, cut] = both.astype(BF)
                    held = []
                elif h == heads - 1:
                    grads[0, rows, cut] = held[0].astype(BF)
            return carry

        lax.fori_loop(0, seg // QT, step, 0)

        @pl.when(cx == 1)
        def _():
            dkv[m, 0] = (dk[0:seg, :] * 0.125).astype(BF)
            dkv[m, 1] = dv[0:seg, :].astype(BF)
            dkv_copy(m).start()

        own = pl.ds(pl.multiple_of(cx * seg, seg), seg)
        rows = pl.ds(m * seg, seg)
        grads[1, rows, :] = (dk[own, :] * 0.125).astype(BF)
        grads[2, rows, :] = dv[own, :].astype(BF)

    def after_attend(m):
        rows = pl.ds(m * seg, seg)

        @pl.when(cx == 0)
        def _():
            dkv_copy(m).wait_recv()
            for i in range(2):
                total = grads[1 + i, rows, :].astype(F32) + dkv[m, i].astype(F32)
                grads[1 + i, rows, :] = total.astype(BF)

        def lower(i, carry):
            spot = pl.ds(pl.multiple_of(m * seg + i * 256, 256), 256)
            total = mm_nt(grads[0, spot, :], wqkv[0])
            for c in (1, 2):
                total = total + mm_nt(grads[c, spot, :], wqkv[c])
            npart[spot, :] = total.astype(BF)
            return carry

        lax.fori_loop(0, seg // 256, lower, 0)
        c_copy(m, 2, npart).start()

    for m in range(2):
        shared(m, 0, bgrad)
        attend_back(m)
        for k in order:
            wx_copy(2 + m, k).start()
        reduce_step(m) if m == 1 else None
        pass_on(m, 1, result)

    def out_part(i, carry):
        lanes = pl.ds(pl.multiple_of(i * 256, 256), 256)
        gq[3, lanes, :] = mm_tn(bgrad[:, lanes], ab[...]).astype(BF)
        return carry

    lax.fori_loop(0, width // 256, out_part, 0)
    bucket_sums(heads, band_sum, whole_sum, dbias_own)

    def db_copy(i):
        return remote(dbias_own, dbias_g.at[i], db_s.at[i], db_r.at[i], group_peers[i])

    for i in range(7):
        db_copy(i).start()

    for m in range(2):
        c_copy(m, 1, npart).wait_send()
        y_copy(m, 0).wait_send()
        after_attend(m)
    fetch_normed(0).wait()
    fetch_normed(1).wait()

    def qkv_part(i, carry):
        lanes = pl.ds(pl.multiple_of(i * 256, 256), 256)
        for c in range(3):
            part = mm_tn(ffn[0, :, lanes], grads[c, 0:seg, :])
            part = part + mm_tn(ffn[1, :, lanes], grads[c, seg:, :])
            gq[c, lanes, :] = part.astype(BF)
        return carry

    lax.fori_loop(0, width // 256, qkv_part, 0)

    def qx_copy(k):
        d = lax.rem(dp + k, 4)
        return remote(gq.at[:, rows96(d * 2 + 1 - cx), :], qx.at[k], qx_s.at[k], qx_r.at[k], partner)

    def qz_copy(k):
        return remote(qx.at[k], qz.at[k - 1], qz_s.at[k - 1], qz_r.at[k - 1], z_peer(k))

    for k in order:
        qx_copy(k).start()

    for m in range(2):
        to_quarters(m, 2, npart)
    reduce_step(2)

    for m in range(2):
        y_copy(m, 2).wait_recv()
        rows = own_rows(m)
        down = kept[m, 0] + ybuf[m, 0].astype(F32)
        through, gain_terms = norm_back(tok[m].astype(F32), gains[0:1, :], down)
        own_out[m, 1] = (through + hgrad[m]).astype(BF)
        share(m, 2, input_grad)
        tiny_own[0:1, :] += jnp.sum(gain_terms, axis=0, keepdims=True)

    def tt_copy(k):
        return remote(tiny_own, tiny_t.at[k - 1], tt_s.at[k - 1], tt_r.at[k - 1], tensor_peers[k - 1])

    for k in (1, 2, 3):
        tt_copy(k).start()
    for m in range(2):
        pass_on(m, 2, input_grad)
    for k in (1, 2, 3):
        tt_copy(k).wait_recv()
    tiny_mid[...] = tiny_own[...] + tiny_t[0] + tiny_t[1] + tiny_t[2]

    def tg_copy(i):
        return remote(tiny_mid, tiny_g.at[i], tg_s.at[i], tg_r.at[i], group_peers[i])

    for i in range(7):
        tg_copy(i).start()

    reduce_step(3)
    for k in order:
        qx_copy(k).wait_recv()
        total = gq[:, rows96(lax.rem(dp + k, 4) * 2 + cx), :].astype(F32) + qx[k].astype(F32)
        if k == 0:
            small_grad[...] = total
        else:
            qx[k] = total.astype(BF)
            qz_copy(k).start()

    total = dbias_own[...]
    for i in range(7):
        db_copy(i).wait_recv()
        total = total + dbias_g[i]
    dbias_out[...] = total
    total = tiny_mid[...]
    for i in range(7):
        tg_copy(i).wait_recv()
        total = total + tiny_g[i]
    tiny_out[...] = total
    for e in range(experts):
        reduce_end(e)
    total = small_grad[...]
    for k in (1, 2, 3):
        qz_copy(k).wait_recv()
        total = total + qz[k - 1].astype(F32)
    small_grad[...] = total
    for m in range(2):
        shared(m, 1, result)
        shared(m, 2, input_grad)

    for e in range(experts):
        for k in range(4):
            wx_copy(e, k).wait_send()
            if k > 0:
                wz_copy(e, k).wait_send()
    for k in range(4):
        qx_copy(k).wait_send()
        if k > 0:
            qz_copy(k).wait_send()
    for m in range(2):
        c_copy(m, 0, epart).wait_send()
        c_copy(m, 2, npart).wait_send()
        own_copy(m, 1, result).wait()
        own_copy(m, 2, input_grad).wait()
        for j in range(3):
            if j > 0:
                y_copy(m, j).wait_send()
            for step in range(3):
                a_copy(m, j, (bgrad, result, input_grad)[j], step).wait_send()

        @pl.when(cx == 1)
        def _():
            dkv_copy(m).wait_send()

    for k in (1, 2, 3):
        tt_copy(k).wait_send()
    for i in range(7):
        tg_copy(i).wait_send()
        db_copy(i).wait_send()


def second_call(
    lengths, bias, ids, slot_lanes, slot_subs, cot, ntwo, q, kcat, vcat, lse, ab, wqkv, wo, gains,
    normed, tok, hidden, w_full,
):
    heads = bias.shape[1]
    rows, width = cot.shape
    span = q.shape[1]
    experts, ff = w_full.shape[0], w_full.shape[4]
    seg = rows // 2
    quarter = seg // 4
    shard = width // 8
    slots = 2 * slot_subs.shape[0]
    vm = pl.BlockSpec(memory_space=pltpu.VMEM)
    sm = pl.BlockSpec(memory_space=pltpu.SMEM)
    hbm = pl.BlockSpec(memory_space=pl.ANY)
    dma = pltpu.SemaphoreType.DMA
    sds = jax.ShapeDtypeStruct
    return pl.pallas_call(
        functools.partial(second_kernel, heads),
        out_shape=(
            sds((rows, width), BF),
            sds((rows, width), BF),
            sds((experts, 2, shard, ff), F32),
            sds((4, shard, span), F32),
            sds((16, width), F32),
            sds((BUCKETS, 128), F32),
        ),
        in_specs=[sm, sm] + [vm] * 13 + [hbm] * 4,
        out_specs=(hbm,) * 2 + (vm,) * 4,
        scratch_shapes=[
            pltpu.VMEM((4, 8, shard, ff), BF),
            pltpu.VMEM((experts, 2, 8, shard, ff), BF),
            pltpu.VMEM((experts, 4, 2, shard, ff), BF),
            pltpu.VMEM((4, width, span), BF),
            pltpu.VMEM((4, 4, shard, span), BF),
            pltpu.VMEM((3, 4, shard, span), BF),
            pltpu.VMEM((rows, width), BF),
            pltpu.VMEM((rows, width), BF),
            pltpu.VMEM((rows, width), BF),
            pltpu.VMEM((4, slots, width), BF),
            pltpu.VMEM((rows, 16), F32),
            pltpu.VMEM((2, quarter, width), F32),
            pltpu.VMEM((2, quarter, width), BF),
            pltpu.VMEM((2, 2, 2 * quarter, width), BF),
            pltpu.VMEM((2, 2, quarter, width), BF),
            pltpu.VMEM((2, 2, quarter, width), BF),
            pltpu.VMEM((2, 2, quarter, width), F32),
            pltpu.VMEM((2, quarter, width), F32),
            pltpu.VMEM((rows, width), BF),
            pltpu.VMEM((2, 2, quarter, width), BF),
            pltpu.VMEM((seg, span), BF),
            pltpu.VMEM((3, rows, span), BF),
            pltpu.VMEM((rows, span), F32),
            pltpu.VMEM((rows, span), F32),
            pltpu.VMEM((2, 2, seg, span), BF),
            pltpu.VMEM((heads, BAND, 2 * BAND), F32),
            pltpu.VMEM((QT, rows + BAND), F32),
            pltpu.VMEM((QT, rows + BAND), F32),
            pltpu.VMEM((heads, BAND, 2 * BAND), F32),
            pltpu.VMEM((8, rows), F32),
            pltpu.VMEM((16, width), F32),
            pltpu.VMEM((3, 16, width), F32),
            pltpu.VMEM((16, width), F32),
            pltpu.VMEM((7, 16, width), F32),
            pltpu.VMEM((BUCKETS, 128), F32),
            pltpu.VMEM((7, BUCKETS, 128), F32),
            dma((2,)),
            dma((4,)),
            dma((4,)),
            pltpu.SemaphoreType.REGULAR,
            dma((experts, 4)),
            dma((experts, 4)),
            dma((experts, 3)),
            dma((experts, 3)),
            dma((2, 3)),
            dma((2, 3)),
            dma((2, 3)),
            dma((2, 3)),
            dma((2, 3, 3)),
            dma((2, 3, 3)),
            dma((2,)),
            dma((2,)),
            dma((4,)),
            dma((4,)),
            dma((3,)),
            dma((3,)),
            dma((3,)),
            dma((3,)),
            dma((7,)),
            dma((7,)),
            dma((7,)),
            dma((7,)),
        ],
        compiler_params=pltpu.CompilerParams(
            collective_id=1, has_side_effects=True, vmem_limit_bytes=63 << 20
        ),
    )(
        lengths, bias, ids, slot_lanes, slot_subs, cot, ntwo, q, kcat, vcat, lse, ab, wqkv, wo, gains,
        normed, tok, hidden, w_full,
    )


def bucket_sums(heads, band_sum, whole_sum, dbias):
    rows = lax.broadcasted_iota(jnp.int32, (BAND, 2 * BAND), 0)
    cols = lax.broadcasted_iota(jnp.int32, (BAND, 2 * BAND), 1)
    away = rows + BAND - cols
    bucket = lax.broadcasted_iota(jnp.int32, (BUCKETS, 2 * BAND), 0)
    lanes128 = lax.broadcasted_iota(jnp.int32, (BUCKETS, 128), 1)
    result = jnp.zeros((BUCKETS, 128), F32)
    for h in range(heads):
        tile = band_sum[h]
        sums = jnp.zeros((BUCKETS, 2 * BAND), F32)
        for b in range(BUCKETS - 1):
            inside = (away >= bucket_starts[b]) & (away < bucket_starts[b + 1])
            row = jnp.sum(jnp.where(inside, tile, 0.0), axis=0, keepdims=True)
            sums = jnp.where(bucket == b, row, sums)
        per_bucket = jnp.sum(sums, axis=1, keepdims=True)
        near = jnp.sum(per_bucket, axis=0, keepdims=True)
        total = jnp.sum(whole_sum[h : h + 1, :], axis=1, keepdims=True)
        last = lax.broadcasted_iota(jnp.int32, (BUCKETS, 1), 0) == BUCKETS - 1
        per_bucket = jnp.where(last, total - near, per_bucket)
        result = jnp.where(lanes128 == h, per_bucket, result)
    dbias[...] = result


def body_fast(
    inputs, lengths, expert_ids, slot_rows, attn_gain, qkv_weight, out_weight, position_bias,
    ffn_gain, router_weight, up_weight, down_weight, cotangent,
):
    micro, seg, width = inputs.shape
    rows = micro * seg
    experts = up_weight.shape[0]
    cx = lax.axis_index("ctx")
    slab = lax.axis_index("dp") * 2 + cx
    shard = attn_gain.shape[0]
    small_own = jnp.concatenate(
        [attn_gain[None], ffn_gain[None], router_weight.T, jnp.zeros((10, shard), BF)], axis=0
    )
    small = lax.dynamic_update_slice(jnp.zeros((16, width), BF), small_own, (0, slab * shard))
    w = jnp.stack([up_weight, jnp.transpose(down_weight, (0, 2, 1))], axis=1)
    tok = inputs.reshape(rows, width)
    (hidden, ntwo, normed, q, kcat, vcat, lse, ab, wqkv, wo, gains, w_full) = first_call(
        lengths, position_bias, tok, small, qkv_weight, out_weight.T, w
    )
    slots = slot_rows[:, 0].reshape(micro * experts, -1)
    result, input_part, w_grad, small_grad, tiny, dbias = second_call(
        lengths, position_bias, expert_ids.reshape(rows, 1), slots, slots.T,
        cotangent.reshape(rows, width), ntwo, q, kcat, vcat, lse, ab, wqkv, wo, gains, normed, tok,
        hidden, w_full,
    )
    tiny = lax.dynamic_slice_in_dim(tiny, slab * shard, shard, axis=1)
    return (
        result.reshape(inputs.shape),
        input_part.reshape(inputs.shape),
        tiny[0],
        small_grad[:3],
        small_grad[3].T,
        dbias[:, : position_bias.shape[1]],
        tiny[1],
        tiny[2 : 2 + experts].T,
        w_grad[:, 0],
        jnp.transpose(w_grad[:, 1], (0, 2, 1)),
    )


def rms_norm(values, gain_vector):
    return (
        values * lax.rsqrt(jnp.mean(values * values, axis=-1, keepdims=True) + 1e-06) * gain_vector
    )


def bucket_of(distance):
    clipped = jnp.maximum(distance, 0)
    edge_values = jnp.asarray(bucket_edges, dtype=jnp.int32)
    beyond = jnp.sum((clipped[..., None] >= edge_values).astype(jnp.int32), axis=-1)
    return jnp.where(clipped < 16, clipped, jnp.minimum(16 + beyond, 31))


def toeplitz(diagonal, query_count, key_count):
    head_count = diagonal.shape[0]
    padded = jnp.pad(diagonal, ((0, 0), (0, 1)))
    row_width = query_count + key_count
    repeated = jnp.broadcast_to(padded[:, None, :], (head_count, query_count, row_width)).reshape(
        head_count, query_count * row_width
    )
    repeated = jnp.pad(repeated, ((0, 0), (0, query_count))).reshape(
        head_count, query_count, row_width + 1
    )[:, :, :key_count]
    return repeated[:, :, ::-1]


def diagonal_sums(gradient):
    head_count, query_count, key_count = gradient.shape
    offset_count = query_count + key_count - 1
    flipped = jnp.pad(gradient[:, :, ::-1], ((0, 0), (0, 0), (0, query_count)))
    skewed = flipped.reshape(head_count, query_count * (offset_count + 1))[
        :, : query_count * offset_count
    ]
    return jnp.sum(skewed.reshape(head_count, query_count, offset_count), axis=1)


def bucket_table(query_first, query_count, key_count):
    offsets = (
        query_first - (key_count - 1) + jnp.arange(query_count + key_count - 1, dtype=jnp.int32)
    )
    return (bucket_of(offsets)[:, None] == jnp.arange(BUCKETS, dtype=jnp.int32)[None, :]).astype(
        jnp.float32
    )


def body(
    inputs,
    lengths,
    expert_ids,
    slot_rows,
    attn_gain,
    qkv_weight,
    out_weight,
    position_bias,
    ffn_gain,
    router_weight,
    up_weight,
    down_weight,
    cotangent,
):
    highest = lax.Precision.HIGHEST
    micro_count, seg_rows, model_width = inputs.shape
    local_heads = position_bias.shape[1]
    head_size = qkv_weight.shape[2] // local_heads
    expert_count = up_weight.shape[0]
    query_first = lax.axis_index("ctx") * seg_rows
    query_pos = query_first + jnp.arange(seg_rows, dtype=jnp.int32)

    def pair_scores(query_heads, query_start, key_heads, length):
        query_count = query_heads.shape[0]
        key_count = key_heads.shape[0]
        scores = (
            jnp.einsum("qhd,khd->hqk", query_heads, key_heads, preferred_element_type=jnp.float32)
            * 0.125
        )
        diagonal = jnp.einsum(
            "rb,bh->hr",
            bucket_table(query_start, query_count, key_count),
            position_bias,
            precision=highest,
        )
        scores = scores + toeplitz(diagonal, query_count, key_count)
        query_place = query_start + jnp.arange(query_count, dtype=jnp.int32)
        key_place = jnp.arange(key_count, dtype=jnp.int32)
        allowed = (key_place[None, :] <= query_place[:, None]) & (key_place[None, :] < length)
        return (scores, allowed)

    def scores_for(query_heads, key_block, length):
        key_count = key_block.shape[0]
        key_heads = key_block.reshape(key_count, local_heads, head_size)
        scores, allowed = pair_scores(query_heads, query_first, key_heads, length)
        return (scores, allowed, key_heads)

    results = []
    input_parts = []
    grad_sums = None
    bias_total = jnp.zeros((local_heads, BUCKETS), jnp.float32)
    for micro_step in range(micro_count):
        forward_gain_one = lax.all_gather(attn_gain, ("dp", "ctx"), axis=0, tiled=True)
        forward_qkv_full = lax.all_gather(qkv_weight, ("dp", "ctx"), axis=1, tiled=True)
        forward_out_full = lax.all_gather(out_weight, ("dp", "ctx"), axis=1, tiled=True)
        forward_gain_two = lax.all_gather(ffn_gain, ("dp", "ctx"), axis=0, tiled=True)
        forward_router_full = lax.all_gather(router_weight, ("dp", "ctx"), axis=0, tiled=True)
        forward_up_full = lax.all_gather(up_weight, ("dp", "ctx"), axis=1, tiled=True)
        forward_down_full = lax.all_gather(down_weight, ("dp", "ctx"), axis=2, tiled=True)
        forward_tokens = inputs[micro_step].astype(jnp.float32)
        forward_length = lengths[micro_step]
        forward_normed = rms_norm(forward_tokens, forward_gain_one.astype(jnp.float32)).astype(
            jnp.bfloat16
        )
        forward_projected = jnp.einsum(
            "td,cde->cte", forward_normed, forward_qkv_full, preferred_element_type=jnp.float32
        ).astype(jnp.bfloat16)
        forward_query_heads = forward_projected[0].reshape(seg_rows, local_heads, head_size)
        row_top = jnp.full((local_heads, seg_rows), -1e30, jnp.float32)
        attend_scores, attend_allowed, attend_key_heads = scores_for(
            forward_query_heads,
            lax.all_gather(forward_projected[1], "ctx", axis=0, tiled=True),
            forward_length,
        )
        value_heads = lax.all_gather(forward_projected[2], "ctx", axis=0, tiled=True).reshape(
            attend_key_heads.shape
        )
        attend_scores = jnp.where(attend_allowed[None], attend_scores, -1e30)
        new_top = jnp.maximum(row_top, jnp.max(attend_scores, axis=-1))
        weights_exp = jnp.where(
            attend_allowed[None], jnp.exp(attend_scores - new_top[:, :, None]), 0.0
        )
        row_total = jnp.sum(weights_exp, axis=-1)
        summed = jnp.einsum(
            "hqk,khd->hqd",
            weights_exp.astype(jnp.bfloat16),
            value_heads,
            preferred_element_type=jnp.float32,
        )
        row_top, row_total, summed = (new_top, row_total, summed)
        forward_attended = summed / row_total[:, :, None]
        forward_log_total = row_top + jnp.log(row_total)
        forward_attended_low = (
            jnp.transpose(forward_attended, (1, 0, 2)).reshape(seg_rows, -1).astype(jnp.bfloat16)
        )
        branch = lax.psum(
            jnp.dot(
                forward_attended_low, forward_out_full, preferred_element_type=jnp.float32
            ).astype(jnp.bfloat16),
            "tensor",
        ).astype(jnp.float32)
        forward_hidden = forward_tokens + branch
        forward_normed_two = rms_norm(forward_hidden, forward_gain_two.astype(jnp.float32)).astype(
            jnp.bfloat16
        )
        logits = jnp.dot(
            forward_normed_two, forward_router_full, preferred_element_type=jnp.float32
        )
        forward_router_probs = jax.nn.softmax(logits, axis=-1)
        forward_chosen = (
            expert_ids[micro_step][:, None] == jnp.arange(expert_count, dtype=jnp.int32)[None, :]
        ).astype(jnp.float32)
        forward_gate_value = jnp.sum(forward_router_probs * forward_chosen, axis=-1)
        forward_slot_table = slot_rows[micro_step, 0]
        padded = jnp.concatenate(
            [forward_normed_two, jnp.zeros((1, model_width), jnp.bfloat16)], axis=0
        )
        forward_picked = padded[forward_slot_table]
        forward_raised = jnp.einsum(
            "ekd,edf->ekf", forward_picked, forward_up_full, preferred_element_type=jnp.float32
        )
        forward_activated = jax.nn.gelu(forward_raised).astype(jnp.bfloat16)
        lowered = jnp.einsum(
            "ekf,efd->ekd", forward_activated, forward_down_full, preferred_element_type=jnp.float32
        )
        spread = (
            jnp.zeros((seg_rows + 1, model_width), jnp.float32)
            .at[forward_slot_table.reshape(-1)]
            .add(lowered.reshape(-1, model_width))[:seg_rows]
        )
        forward_expert_sum = lax.psum(spread.astype(jnp.bfloat16), "tensor").astype(jnp.float32)
        forward_live_rows = (query_pos < forward_length).astype(jnp.float32)[:, None]
        result = (
            forward_live_rows * (forward_hidden + forward_gate_value[:, None] * forward_expert_sum)
        ).astype(jnp.bfloat16)
        forward_kept_state = (
            forward_tokens,
            forward_length,
            forward_normed,
            forward_projected,
            forward_attended,
            forward_log_total,
            forward_attended_low,
            forward_hidden,
            forward_normed_two,
            forward_router_probs,
            forward_chosen,
            forward_gate_value,
            forward_slot_table,
            forward_picked,
            forward_raised,
            forward_activated,
            forward_expert_sum,
            forward_live_rows,
        )
        result, kept_state = (result, forward_kept_state)
        gain_one = lax.all_gather(attn_gain, ("dp", "ctx"), axis=0, tiled=True)
        qkv_full = lax.all_gather(qkv_weight, ("dp", "ctx"), axis=1, tiled=True)
        out_full = lax.all_gather(out_weight, ("dp", "ctx"), axis=1, tiled=True)
        gain_two = lax.all_gather(ffn_gain, ("dp", "ctx"), axis=0, tiled=True)
        router_full = lax.all_gather(router_weight, ("dp", "ctx"), axis=0, tiled=True)
        up_full = lax.all_gather(up_weight, ("dp", "ctx"), axis=1, tiled=True)
        down_full = lax.all_gather(down_weight, ("dp", "ctx"), axis=2, tiled=True)
        (
            tokens,
            backward_length,
            normed,
            projected,
            attended,
            log_total,
            attended_low,
            hidden,
            normed_two,
            router_probs,
            chosen,
            gate_value,
            slot_table,
            picked,
            raised,
            activated,
            expert_sum,
            live_rows,
        ) = kept_state
        upstream = live_rows * cotangent[micro_step].astype(jnp.float32)
        sum_grad = (gate_value[:, None] * upstream).astype(jnp.bfloat16)
        gate_grad = jnp.sum(expert_sum * upstream, axis=-1)
        logit_grad = (router_probs * gate_grad[:, None] * (chosen - gate_value[:, None])).astype(
            jnp.bfloat16
        )
        router_part = jnp.einsum(
            "td,te->de", normed_two, logit_grad, preferred_element_type=jnp.float32
        )
        padded_grad = jnp.concatenate([sum_grad, jnp.zeros((1, model_width), jnp.bfloat16)], axis=0)
        slot_grad = padded_grad[slot_table]
        down_part = jnp.einsum(
            "ekf,ekd->efd", activated, slot_grad, preferred_element_type=jnp.float32
        )
        act_grad = jnp.einsum(
            "ekd,efd->ekf", slot_grad, down_full, preferred_element_type=jnp.float32
        )
        unused_value, gelu_back = jax.vjp(jax.nn.gelu, raised)
        raised_grad = gelu_back(act_grad)[0].astype(jnp.bfloat16)
        up_part = jnp.einsum(
            "ekd,ekf->edf", picked, raised_grad, preferred_element_type=jnp.float32
        )
        picked_grad = jnp.einsum(
            "ekf,edf->ekd", raised_grad, up_full, preferred_element_type=jnp.float32
        )
        spread_grad = (
            jnp.zeros((seg_rows + 1, model_width), jnp.float32)
            .at[slot_table.reshape(-1)]
            .add(picked_grad.reshape(-1, model_width))[:seg_rows]
        )
        normed_two_grad = lax.psum(spread_grad.astype(jnp.bfloat16), "tensor").astype(
            jnp.float32
        ) + jnp.einsum("te,de->td", logit_grad, router_full, preferred_element_type=jnp.float32)
        unused_norm, second_back = jax.vjp(rms_norm, hidden, gain_two.astype(jnp.float32))
        hidden_grad, gain_two_part = second_back(normed_two_grad)
        hidden_grad = hidden_grad + upstream
        branch_grad = hidden_grad.astype(jnp.bfloat16)
        out_part = jnp.einsum(
            "te,td->ed", attended_low, branch_grad, preferred_element_type=jnp.float32
        )
        attended_grad = jnp.einsum(
            "td,ed->te", branch_grad, out_full, preferred_element_type=jnp.float32
        ).astype(jnp.bfloat16)
        grad_heads = attended_grad.reshape(seg_rows, local_heads, head_size)
        row_delta = jnp.sum(
            jnp.transpose(grad_heads.astype(jnp.float32), (1, 0, 2)) * attended, axis=-1
        )
        backward_query_heads = projected[0].reshape(seg_rows, local_heads, head_size)
        bias_zero = jnp.zeros((local_heads, BUCKETS), jnp.float32)
        attend_bias_acc = bias_zero
        bias_acc = attend_bias_acc
        score_scores, score_allowed, score_key_heads = scores_for(
            backward_query_heads,
            lax.all_gather(projected[1], "ctx", axis=0, tiled=True),
            backward_length,
        )
        score_value_heads = lax.all_gather(projected[2], "ctx", axis=0, tiled=True).reshape(
            score_key_heads.shape
        )
        score_key_count = score_key_heads.shape[0]
        soft_weights = jnp.where(
            score_allowed[None], jnp.exp(score_scores - log_total[:, :, None]), 0.0
        )
        weight_grad = jnp.einsum(
            "qhd,khd->hqk", grad_heads, score_value_heads, preferred_element_type=jnp.float32
        )
        score_grad = (soft_weights * (weight_grad - row_delta[:, :, None])).astype(jnp.bfloat16)
        query_acc = jnp.einsum(
            "hqk,khd->qhd", score_grad, score_key_heads, preferred_element_type=jnp.float32
        )
        bias_acc = bias_acc + jnp.dot(
            diagonal_sums(score_grad.astype(jnp.float32)),
            bucket_table(query_first, seg_rows, score_key_count),
            precision=highest,
        )
        (
            (attend_query_acc, attend_bias_acc),
            attend_soft_weights,
            attend_score_grad,
            attend_key_count,
        ) = ((query_acc, bias_acc), soft_weights, score_grad, score_key_count)
        key_term = (
            jnp.einsum(
                "hqk,qhd->khd",
                attend_score_grad,
                backward_query_heads,
                preferred_element_type=jnp.float32,
            )
            * 0.125
        )
        value_term = jnp.einsum(
            "hqk,qhd->khd",
            attend_soft_weights.astype(jnp.bfloat16),
            grad_heads,
            preferred_element_type=jnp.float32,
        )
        grad_term = jnp.stack(
            [key_term.reshape(attend_key_count, -1), value_term.reshape(attend_key_count, -1)],
            axis=1,
        )
        key_value_acc = grad_term
        query_acc, key_value_acc, bias_part = (attend_query_acc, key_value_acc, attend_bias_acc)
        own_grads = lax.psum_scatter(
            key_value_acc.astype(jnp.bfloat16), "ctx", scatter_dimension=0, tiled=True
        ).astype(jnp.float32)
        query_grad = (query_acc * 0.125).reshape(seg_rows, -1).astype(jnp.bfloat16)
        qkv_grad = jnp.stack(
            [
                query_grad,
                own_grads[:, 0].astype(jnp.bfloat16),
                own_grads[:, 1].astype(jnp.bfloat16),
            ],
            axis=0,
        )
        qkv_part = jnp.einsum("td,cte->cde", normed, qkv_grad, preferred_element_type=jnp.float32)
        normed_grad = lax.psum(
            jnp.einsum(
                "cte,cde->td", qkv_grad, qkv_full, preferred_element_type=jnp.float32
            ).astype(jnp.bfloat16),
            "tensor",
        ).astype(jnp.float32)
        unused_first, first_back = jax.vjp(rms_norm, tokens, gain_one.astype(jnp.float32))
        token_grad, gain_one_part = first_back(normed_grad)
        input_part = (token_grad + hidden_grad).astype(jnp.bfloat16)
        weight_parts = (
            gain_one_part,
            qkv_part,
            out_part,
            gain_two_part,
            router_part,
            up_part,
            down_part,
        )
        input_part, weight_parts, bias_part = (input_part, weight_parts, bias_part)
        results.append(result)
        input_parts.append(input_part)
        grad_sums = (
            weight_parts
            if grad_sums is None
            else tuple((old_sum + new_part for old_sum, new_part in zip(grad_sums, weight_parts)))
        )
        bias_total = bias_total + bias_part
    reduced = (
        lax.psum_scatter(grad_sums[0], ("dp", "ctx"), scatter_dimension=0, tiled=True),
        lax.psum_scatter(grad_sums[1], ("dp", "ctx"), scatter_dimension=1, tiled=True),
        lax.psum_scatter(grad_sums[2], ("dp", "ctx"), scatter_dimension=1, tiled=True),
        lax.psum_scatter(grad_sums[3], ("dp", "ctx"), scatter_dimension=0, tiled=True),
        lax.psum_scatter(grad_sums[4], ("dp", "ctx"), scatter_dimension=0, tiled=True),
        lax.psum_scatter(grad_sums[5], ("dp", "ctx"), scatter_dimension=1, tiled=True),
        lax.psum_scatter(grad_sums[6], ("dp", "ctx"), scatter_dimension=2, tiled=True),
    )
    bias_grad_total = lax.psum(bias_total, ("dp", "ctx"))
    return (
        jnp.stack(results, axis=0),
        jnp.stack(input_parts, axis=0),
        reduced[0],
        reduced[1],
        reduced[2],
        jnp.transpose(bias_grad_total),
        reduced[3],
        reduced[4],
        reduced[5],
        reduced[6],
    )


def solution(mesh):
    small = mesh.shape["ctx"] == 2 and mesh.shape["dp"] == 4 and mesh.shape["tensor"] == 4
    return jax.shard_map(
        body_fast if small else body,
        mesh=mesh,
        in_specs=(
            P("dp", "ctx", None),
            P("dp"),
            P("dp", "ctx"),
            P("dp", "ctx", None, None),
            P(("dp", "ctx")),
            P(None, ("dp", "ctx"), "tensor"),
            P("tensor", ("dp", "ctx")),
            P(None, "tensor"),
            P(("dp", "ctx")),
            P(("dp", "ctx"), None),
            P(None, ("dp", "ctx"), "tensor"),
            P(None, "tensor", ("dp", "ctx")),
            P("dp", "ctx", None),
        ),
        out_specs=(
            P("dp", "ctx", None),
            P("dp", "ctx", None),
            P(("dp", "ctx")),
            P(None, ("dp", "ctx"), "tensor"),
            P("tensor", ("dp", "ctx")),
            P(None, "tensor"),
            P(("dp", "ctx")),
            P(("dp", "ctx"), None),
            P(None, ("dp", "ctx"), "tensor"),
            P(None, "tensor", ("dp", "ctx")),
        ),
        check_vma=False,
    )
```

```python
import functools

import jax
import jax.numpy as jnp
import numpy as np
from jax import lax
from jax.experimental import pallas as pl
from jax.experimental.pallas import tpu as pltpu
from jax.sharding import PartitionSpec as P

BUCKETS = 32
MESH = pl.DeviceIdType.MESH
BF = jnp.bfloat16
F32 = jnp.float32


bucket_edges = np.ceil(16.0 * 8.0 ** (np.arange(1, 16) / 16.0)).astype(np.int32)
bucket_starts = [int(n) for n in range(17)] + [int(n) for n in bucket_edges]


QT = 256
BAND = 128
C0 = float(np.sqrt(2.0 / np.pi))
C1 = 0.044715


def mm(a, b):
    return jnp.dot(a, b, preferred_element_type=F32)


def mm_nt(a, b):
    return lax.dot_general(a, b, (((1,), (1,)), ((), ())), preferred_element_type=F32)


def mm_tn(a, b):
    return lax.dot_general(a, b, (((0,), (0,)), ((), ())), preferred_element_type=F32)


def remote(src, dst, send, recv, device):
    return pltpu.make_async_remote_copy(
        src_ref=src,
        dst_ref=dst,
        send_sem=send,
        recv_sem=recv,
        device_id=device,
        device_id_type=MESH,
    )


def block(start, size, whole=128):
    return pl.ds(pl.multiple_of(start, whole), size)


class Place:
    def __init__(self):
        dp, cx, t = lax.axis_index("dp"), lax.axis_index("ctx"), lax.axis_index("tensor")
        self.dp, self.cx, self.t = dp, cx, t
        self.yy, self.core = lax.div(t, 2), lax.rem(t, 2)
        self.partner = (dp, 1 - cx, t)
        self.sibling = (dp, cx, t + 1 - 2 * self.core)
        self.across = (dp, cx, lax.rem(t + 2, 4))
        self.tensor_peers = [(dp, cx, lax.rem(t + k, 4)) for k in (1, 2, 3)]
        self.z_peers = [(lax.rem(dp + k, 4), cx, t) for k in (1, 2, 3)]
        self.spot = dp + cx * (7 - 2 * dp)
        self.right = self.at_spot(1)
        self.left = self.at_spot(-1)

    def at_spot(self, away):
        spot = lax.rem(self.spot + 8 + away, 8)
        cx = lax.div(spot, 4)
        return (spot + cx * (7 - 2 * spot), cx, self.t)

    def slab(self, away):
        dp, cx, _ = self.at_spot(away)
        return dp * 2 + cx

    def greet(self):
        barrier = pltpu.get_barrier_semaphore()
        peers = self.z_peers + [self.partner] + self.tensor_peers
        for peer in peers:
            pl.semaphore_signal(barrier, inc=1, device_id=peer, device_id_type=MESH)
        pl.semaphore_wait(barrier, len(peers))


class Ring:
    def __init__(self, place, send_sems, recv_sems):
        self.place, self.send_sems, self.recv_sems = place, send_sems, recv_sems

    def copy(self, d, e, s, src, dst):
        at = (d, e, s - 1)
        device = self.place.right if d == 0 else self.place.left
        return remote(src, dst, self.send_sems.at[at], self.recv_sems.at[at], device)


class TensorSum:
    def __init__(self, place, seg, cbuf, ysend, ybuf, kept, c_s, c_r, y_s, y_r, a_s, a_r):
        self.place, self.seg = place, seg
        self.half, self.quarter = seg // 2, seg // 4
        self.cbuf, self.ysend, self.ybuf, self.kept = cbuf, ysend, ybuf, kept
        self.c_s, self.c_r, self.y_s, self.y_r, self.a_s, self.a_r = c_s, c_r, y_s, y_r, a_s, a_r

    def rows(self, m, c, y):
        return block(m * self.seg + c * self.half + y * self.quarter, self.quarter)

    def own_rows(self, m):
        return self.rows(m, self.place.core, self.place.yy)

    def c_copy(self, m, j, src):
        rows = block(m * self.seg + (1 - self.place.core) * self.half, self.half)
        return remote(
            src.at[rows], self.cbuf.at[m, j % 2], self.c_s.at[m, j], self.c_r.at[m, j],
            self.place.sibling,
        )

    def y_copy(self, m, j):
        return remote(
            self.ysend.at[m, j % 2], self.ybuf.at[m, j % 2], self.y_s.at[m, j], self.y_r.at[m, j],
            self.place.across,
        )

    def to_quarters(self, m, j, src):
        self.c_copy(m, j, src).wait_recv()
        yy, core = self.place.yy, self.place.core
        near, far = block(yy * self.quarter, self.quarter), block((1 - yy) * self.quarter, self.quarter)
        other = src[self.rows(m, core, 1 - yy), :].astype(F32)
        self.ysend[m, j % 2] = (other + self.cbuf[m, j % 2, far, :].astype(F32)).astype(BF)
        self.y_copy(m, j).start()
        mine = src[self.rows(m, core, yy), :].astype(F32)
        self.kept[m, j % 2] = mine + self.cbuf[m, j % 2, near, :].astype(F32)

    def total(self, m, j):
        self.y_copy(m, j).wait_recv()
        return self.kept[m, j % 2] + self.ybuf[m, j % 2].astype(F32)

    def a_copy(self, m, j, ref, step, own=None):
        yy, core = self.place.yy, self.place.core
        spot = ref.at[self.rows(m, core, 1 - yy if step == 2 else yy)]
        source = spot if own is None or step == 2 else own
        return remote(
            source, spot, self.a_s.at[m, j, step], self.a_r.at[m, j, step],
            self.place.across if step == 0 else self.place.sibling,
        )

    def a_recv(self, m, j, ref, step):
        yy, core = self.place.yy, self.place.core
        spot = ref.at[
            self.rows(m, core if step == 0 else 1 - core, yy if step == 1 else 1 - yy)
        ]
        return remote(
            spot, spot, self.a_s.at[m, j, step], self.a_r.at[m, j, step], self.place.sibling
        )

    def share(self, m, j, ref, own=None):
        self.a_copy(m, j, ref, 0, own).start()
        self.a_copy(m, j, ref, 1, own).start()

    def pass_on(self, m, j, ref):
        self.a_recv(m, j, ref, 0).wait_recv()
        self.a_copy(m, j, ref, 2).start()

    def shared(self, m, j, ref):
        self.a_recv(m, j, ref, 1).wait_recv()
        self.a_recv(m, j, ref, 2).wait_recv()


def low_lanes(shape):
    return lax.rem(lax.broadcasted_iota(jnp.int32, shape, len(shape) - 1), 128) < 64


def head_lanes(h, base=0):
    return slice(base + h * 128, base + (h + 1) * 128)


def fill_bias(bias_ref, band_ref, heads):
    rows = lax.broadcasted_iota(jnp.int32, (BAND, 2 * BAND), 0)
    cols = lax.broadcasted_iota(jnp.int32, (BAND, 2 * BAND), 1)
    away = rows + BAND - cols
    for h in range(heads):
        tile = jnp.full((BAND, 2 * BAND), bias_ref[0, h], F32)
        for b in range(1, BUCKETS):
            tile = jnp.where(away >= bucket_starts[b], bias_ref[b, h], tile)
        band_ref[h] = tile - bias_ref[BUCKETS - 1, h]


def masked_scores(q_tile, keys, band_ref, scores, h, first, length):
    count = keys.shape[0]
    scores[:, BAND:] = mm_nt(q_tile, keys) * 0.125
    for part in range(QT // BAND):
        spot = (block(part * BAND, BAND), block(first + part * BAND, 2 * BAND))
        scores[spot] = scores[spot] + band_ref[h]
    values = scores[:, BAND:]
    key_pos = lax.broadcasted_iota(jnp.int32, (QT, count), 1)
    query_pos = lax.broadcasted_iota(jnp.int32, (QT, count), 0) + first
    allowed = (key_pos <= query_pos) & (key_pos < length)
    return jnp.where(allowed, values, -1e30), allowed


def bucket_sums(heads, band_sum, whole_sum, dbias):
    rows = lax.broadcasted_iota(jnp.int32, (BAND, 2 * BAND), 0)
    cols = lax.broadcasted_iota(jnp.int32, (BAND, 2 * BAND), 1)
    away = rows + BAND - cols
    bucket = lax.broadcasted_iota(jnp.int32, (BUCKETS, 2 * BAND), 0)
    lanes128 = lax.broadcasted_iota(jnp.int32, (BUCKETS, 128), 1)
    result = jnp.zeros((BUCKETS, 128), F32)
    for h in range(heads):
        tile = band_sum[h]
        sums = jnp.zeros((BUCKETS, 2 * BAND), F32)
        for b in range(BUCKETS - 1):
            inside = (away >= bucket_starts[b]) & (away < bucket_starts[b + 1])
            row = jnp.sum(jnp.where(inside, tile, 0.0), axis=0, keepdims=True)
            sums = jnp.where(bucket == b, row, sums)
        per_bucket = jnp.sum(sums, axis=1, keepdims=True)
        near = jnp.sum(per_bucket, axis=0, keepdims=True)
        total = jnp.sum(whole_sum[h : h + 1, :], axis=1, keepdims=True)
        last = lax.broadcasted_iota(jnp.int32, (BUCKETS, 1), 0) == BUCKETS - 1
        per_bucket = jnp.where(last, total - near, per_bucket)
        result = jnp.where(lanes128 == h, per_bucket, result)
    dbias[...] = result


def norm_back(x, gain, grad):
    scale = lax.rsqrt(jnp.mean(x * x, axis=-1, keepdims=True) + 1e-06)
    unit = x * scale
    pulled = grad * gain
    inner = jnp.mean(pulled * unit, axis=-1, keepdims=True)
    return scale * (pulled - unit * inner), grad * unit


def first_kernel(
    heads,
    len_ref,
    bias_ref,
    tok,
    wsmall,
    w,
    hidden,
    ntwo,
    normed,
    q3,
    kv,
    lse,
    ab3,
    ws,
    gains,
    w_full,
    ws_full,
    bpart,
    cbuf,
    ysend,
    ybuf,
    kept,
    band,
    scores,
    sz_s,
    sz_r,
    sx_s,
    sx_r,
    kv_s,
    kv_r,
    c_s,
    c_r,
    y_s,
    y_r,
    a_s,
    a_r,
    ring_s,
    ring_r,
    local,
):
    place = Place()
    dp, cx, t = place.dp, place.cx, place.t
    seg = tok.shape[0] // 2
    width = tok.shape[1]
    shard = width // 8
    experts = w.shape[0]
    span = kv.shape[2]
    place.greet()
    ring = Ring(place, ring_s, ring_r)
    sums = TensorSum(place, seg, cbuf, ysend, ybuf, kept, c_s, c_r, y_s, y_r, a_s, a_r)

    def small_slab(k, c):
        return lax.rem(dp + 4 - k, 4) * 2 + c

    def sz_copy(k, slab):
        return remote(
            wsmall, ws_full.at[slab], sz_s.at[k - 1], sz_r.at[k - 1], place.z_peers[k - 1]
        )

    def sx_copy(k, c):
        spot = ws_full.at[small_slab(k, c)]
        return remote(wsmall if k == 0 else spot, spot, sx_s.at[k], sx_r.at[k], place.partner)

    small_own = pltpu.make_async_copy(wsmall, ws_full.at[small_slab(0, cx)], local.at[experts])

    def gather(d, e, s, sending):
        away = s - 1 if sending else s
        slab = place.slab(-away if d == 0 else away)
        if s == 4:
            spot = w_full.at[e, d, slab]
        else:
            spot = w_full.at[e, :, slab]
        return ring.copy(d, e, s, w.at[e] if sending and s == 1 else spot, spot)

    def w_own(e):
        return pltpu.make_async_copy(w.at[e], w_full.at[e, :, place.slab(0)], local.at[e])

    steps = [(e, s) for s in (2, 3, 4) for e in range(experts)]

    def pump(count=1):
        for _ in range(count):
            if steps:
                e, s = steps.pop(0)
                for d in range(2):
                    gather(d, e, s - 1, False).wait_recv()
                    gather(d, e, s, True).start()

    small_own.start()
    for k in (1, 3, 2):
        sz_copy(k, small_slab(0, cx)).start()
    sx_copy(0, cx).start()
    for e in range(experts):
        w_own(e).start()
        for d in range(2):
            gather(d, e, 1, True).start()

    @pl.when(cx == 0)
    def _():
        for m in range(2):
            kv[m, seg:, :] = jnp.zeros((seg, span), BF)

    fill_bias(bias_ref, band, heads)
    for k in (1, 3, 2):
        sz_copy(k, small_slab(k, cx)).wait_recv()
        sx_copy(k, cx).start()
    small_own.wait()
    for k in range(4):
        sx_copy(k, 1 - cx).wait_recv()
    total = ws_full[0, shard:, :].astype(F32)
    for i in range(1, 8):
        total = total + ws_full[i, shard:, :].astype(F32)
    gains[...] = total
    for i in range(8):
        ws[i * shard : (i + 1) * shard, :] = ws_full[i, 0:shard, :]

    def project(m):
        def step(i, carry):
            rows = block(m * seg + i * 256, 256)
            x = tok[rows, :].astype(F32)
            scale = lax.rsqrt(jnp.mean(x * x, axis=-1, keepdims=True) + 1e-06)
            x = (x * scale * gains[0:1, :]).astype(BF)
            normed[rows, :] = x
            kv[m, block(cx * seg + i * 256, 256), :] = mm(x, ws[:, 0:span]).astype(BF)
            part = mm(x, ws[:, span:])
            q3[rows, :] = jnp.where(low_lanes(part.shape), part, 0.0).astype(BF)
            return carry

        lax.fori_loop(0, seg // 256, step, 0)

    def kv_copy(m):
        spot = kv.at[m, block(0, seg), :]
        return remote(spot, spot, kv_s.at[m], kv_r.at[m], place.partner)

    for m in range(2):
        project(m)

        @pl.when(cx == 0)
        def _():
            kv_copy(m).start()

    pump(2)

    def attend(m):
        length = len_ref[m]

        def step(i, carry):
            rows = block(m * seg + i * QT, QT)
            first = cx * seg + i * QT
            lanes128 = lax.broadcasted_iota(jnp.int32, (QT, 128), 1)
            tops = jnp.zeros((QT, 128), F32)
            for h in range(heads):
                cut = head_lanes(h)
                values, allowed = masked_scores(
                    q3[rows, cut], kv[m, :, cut], band, scores, h, first, length
                )
                top = jnp.max(values, axis=-1, keepdims=True)
                raised = jnp.where(allowed, jnp.exp(values - top), 0.0)
                mass = jnp.sum(raised, axis=-1, keepdims=True)
                probs = (raised * (1.0 / mass)).astype(BF)
                part = mm(probs, kv[m, :, cut])
                ab3[rows, cut] = jnp.where(low_lanes(part.shape), 0.0, part).astype(BF)
                tops = jnp.where(lanes128 == h, top + jnp.log(mass), tops)
            lse[rows, :] = tops
            bpart[rows, :] = mm_nt(ab3[rows, :], ws[:, span:]).astype(BF)
            return carry

        lax.fori_loop(0, seg // QT, step, 0)

    def second_norm(m):
        rows = sums.own_rows(m)
        x = tok[rows, :].astype(F32) + sums.total(m, 0)
        hidden[m] = x
        scale = lax.rsqrt(jnp.mean(x * x, axis=-1, keepdims=True) + 1e-06)
        ntwo[rows, :] = (x * scale * gains[1:2, :]).astype(BF)
        sums.share(m, 0, ntwo)

    for m in range(2):

        @pl.when(cx == 1)
        def _():
            kv_copy(m).wait_recv()

        attend(m)
        sums.c_copy(m, 0, bpart).start()
        pump()
        sums.to_quarters(m, 0, bpart)
        if m == 1:
            sums.pass_on(0, 0, ntwo)
        pump()
        second_norm(m)
    sums.pass_on(1, 0, ntwo)
    for m in range(2):
        sums.shared(m, 0, ntwo)
    pump(len(steps))

    for e in range(experts):
        w_own(e).wait()
        for d in range(2):
            gather(d, e, 4, False).wait_recv()
    for k in (1, 2, 3):
        sz_copy(k, small_slab(0, cx)).wait_send()
    for k in range(4):
        sx_copy(k, cx).wait_send()
    for e in range(experts):
        for d in range(2):
            for s in (1, 2, 3, 4):
                gather(d, e, s, True).wait_send()
    for m in range(2):
        sums.c_copy(m, 0, bpart).wait_send()
        sums.y_copy(m, 0).wait_send()
        for step in range(3):
            sums.a_copy(m, 0, ntwo, step).wait_send()

        @pl.when(cx == 0)
        def _():
            kv_copy(m).wait_send()


def first_call(lengths, bias, tok, wsmall, w):
    heads = bias.shape[1]
    rows, width = tok.shape
    span = heads * 128
    experts = w.shape[0]
    ff = w.shape[3]
    quarter = rows // 8
    vm = pl.BlockSpec(memory_space=pltpu.VMEM)
    sm = pl.BlockSpec(memory_space=pltpu.SMEM)
    hbm = pl.BlockSpec(memory_space=pl.ANY)
    dma = pltpu.SemaphoreType.DMA
    sds = jax.ShapeDtypeStruct
    return pl.pallas_call(
        functools.partial(first_kernel, heads),
        out_shape=(
            sds((2, quarter, width), F32),
            sds((rows, width), BF),
            sds((rows, width), BF),
            sds((rows, span), BF),
            sds((2, rows, span), BF),
            sds((rows, 128), F32),
            sds((rows, span), BF),
            sds((width, width), BF),
            sds((16, width), F32),
            sds((experts, 2, 8, width // 8, ff), BF),
        ),
        in_specs=[sm, sm, vm, hbm, hbm],
        out_specs=(vm,) * 9 + (hbm,),
        scratch_shapes=[
            pltpu.VMEM((8,) + wsmall.shape, BF),
            pltpu.VMEM((rows, width), BF),
            pltpu.VMEM((2, 1, 2 * quarter, width), BF),
            pltpu.VMEM((2, 1, quarter, width), BF),
            pltpu.VMEM((2, 1, quarter, width), BF),
            pltpu.VMEM((2, 1, quarter, width), F32),
            pltpu.VMEM((heads, BAND, 2 * BAND), F32),
            pltpu.VMEM((QT, rows + BAND), F32),
            dma((3,)),
            dma((3,)),
            dma((4,)),
            dma((4,)),
            dma((2,)),
            dma((2,)),
            dma((2, 1)),
            dma((2, 1)),
            dma((2, 1)),
            dma((2, 1)),
            dma((2, 1, 3)),
            dma((2, 1, 3)),
            dma((2, experts, 4)),
            dma((2, experts, 4)),
            dma((experts + 1,)),
        ],
        compiler_params=pltpu.CompilerParams(
            collective_id=0, has_side_effects=True, vmem_limit_bytes=56 << 20
        ),
    )(lengths, bias, tok, wsmall, w)


def second_kernel(
    heads,
    len_ref,
    bias_ref,
    ids,
    slot_lanes,
    slot_subs,
    cot,
    ntwo,
    q3,
    kv,
    lse,
    ab3,
    ws,
    gains,
    hidden,
    normed_hbm,
    tok_hbm,
    w_full,
    result,
    input_grad,
    w_grad,
    small_grad,
    tiny_out,
    dbias_out,
    wbuf,
    gw,
    first_in,
    second_in,
    gs,
    sx,
    sz,
    sum_grad,
    epart,
    npart,
    ffn,
    probs_ref,
    tok,
    cbuf,
    ysend,
    ybuf,
    kept,
    hgrad,
    bgrad,
    own_out,
    do3,
    grads,
    dkv_acc,
    dkv,
    band,
    scores,
    spread,
    band_sum,
    whole_sum,
    tiny_own,
    tiny_t,
    tiny_x,
    tiny_z,
    dbias_own,
    dbias_x,
    dbias_z,
    load_sem,
    row_sem,
    out_sem,
    ready,
    ring_s,
    ring_r,
    c_s,
    c_r,
    y_s,
    y_r,
    a_s,
    a_r,
    kv_s,
    kv_r,
    sx_s,
    sx_r,
    sz_s,
    sz_r,
    tt_s,
    tt_r,
    tx_s,
    tx_r,
    tz_s,
    tz_r,
    bx_s,
    bx_r,
    bz_s,
    bz_r,
):
    place = Place()
    dp, cx, t = place.dp, place.cx, place.t
    seg = cot.shape[0] // 2
    width = cot.shape[1]
    shard = width // 8
    span = kv.shape[2]
    experts = w_full.shape[0]
    cap = slot_subs.shape[0]
    place.greet()
    ring = Ring(place, ring_s, ring_r)
    sums = TensorSum(place, seg, cbuf, ysend, ybuf, kept, c_s, c_r, y_s, y_r, a_s, a_r)

    def load(e, slot):
        return pltpu.make_async_copy(w_full.at[e], wbuf.at[pl.ds(slot * 2, 2)], load_sem.at[slot])

    def fetch(m):
        return pltpu.make_async_copy(tok_hbm.at[sums.own_rows(m)], tok.at[m], row_sem.at[m])

    load(0, 0).start()
    for m in range(2):
        fetch(m).start()

    router16 = gains[...].astype(BF)

    def upstream_of(rows, m, first):
        spot = lax.broadcasted_iota(jnp.int32, (rows.size, 1), 0) + (cx * seg + first)
        live = (spot < len_ref[m]).astype(F32)
        return live, live * cot[rows, :].astype(F32)

    def chosen_of(rows):
        lanes = lax.broadcasted_iota(jnp.int32, (rows.size, 16), 1)
        return (lanes == ids[rows, :] + 2).astype(F32)

    for m in range(2):

        def gates(i, carry):
            rows = block(m * seg + i * 256, 256)
            logits = mm_nt(ntwo[rows, :], router16)
            lanes = lax.broadcasted_iota(jnp.int32, (256, 16), 1)
            inside = (lanes >= 2) & (lanes < 2 + experts)
            logits = jnp.where(inside, logits, -1e30)
            top = jnp.max(logits, axis=-1, keepdims=True)
            raised = jnp.where(inside, jnp.exp(logits - top), 0.0)
            probs = raised / jnp.sum(raised, axis=-1, keepdims=True)
            probs_ref[rows, :] = probs
            gate = jnp.sum(probs * chosen_of(rows), axis=-1, keepdims=True)
            live, upstream = upstream_of(rows, m, i * 256)
            sum_grad[rows, :] = (gate * upstream).astype(BF)
            epart[rows, :] = jnp.zeros((256, width), BF)
            npart[rows, :] = jnp.zeros((256, width), BF)
            return carry

        lax.fori_loop(0, seg // 256, gates, 0)

    def landing(d, e, s):
        if s == 1:
            return first_in.at[d, e]
        if s == 2:
            return second_in.at[d, e]
        return wbuf.at[e, pl.ds(d * 4 + (s - 3) * 2, 2)]

    def reduce_copy(d, e, s):
        slab = place.slab(5 - s if d == 0 else s - 5)
        src = gw.at[e, d, slab] if s == 1 else gw.at[e, :, slab]
        return ring.copy(d, e, s, src, landing(d, e, s))

    def reduce_first(e):
        for d in range(2):
            reduce_copy(d, e, 1).start()

    def reduce_step(e, s):
        for d in range(2):
            slab = place.slab(5 - s if d == 0 else s - 5)
            reduce_copy(d, e, s - 1).wait_recv()
            came = landing(d, e, s - 1)[...].astype(F32)
            if s == 2:
                gw[e, d, slab] = (gw[e, d, slab].astype(F32) + came).astype(BF)
            else:
                gw[e, :, slab] = (gw[e, :, slab].astype(F32) + came).astype(BF)
            reduce_copy(d, e, s).start()

    def reduce_end(e):
        total = gw[e, :, place.slab(0)].astype(F32)
        for d in range(2):
            reduce_copy(d, e, 4).wait_recv()
            total = total + landing(d, e, 4)[...].astype(F32)
        w_grad[e] = total

    steps = [(experts - 1, 2)] + [(e, s) for s in (3, 4) for e in range(experts)]

    def pump(count=1):
        for _ in range(count):
            if steps:
                reduce_step(*steps.pop(0))

    def weight(slot, which):
        return wbuf[slot * 2 + which].reshape(width, -1)

    picked, slot_grad, activated, raised_grad = (ffn.at[i] for i in range(4))

    def expert_step(e, carry):
        slot = lax.rem(e, 2)
        load(e, slot).wait()

        @pl.when(e + 1 < experts)
        def _():
            load(e + 1, 1 - slot).start()

        def one_micro(m, carry):
            rows = block(m * seg, seg)
            slots = block(m * cap, cap)
            lanes = lax.broadcasted_iota(jnp.int32, (cap, 8), 1)
            column = jnp.sum(
                jnp.where(lanes == m * experts + e, slot_subs[...], 0), axis=1, keepdims=True
            )
            pick = (column == lax.broadcasted_iota(jnp.int32, (cap, seg), 1)).astype(BF)
            row = slot_lanes[pl.ds(m * experts + e, 1), :]
            put = (row == lax.broadcasted_iota(jnp.int32, (seg, cap), 0)).astype(BF)
            chosen_rows = mm(pick, ntwo[rows, :]).astype(BF)
            picked[slots, :] = chosen_rows
            slot_part = mm(pick, sum_grad[rows, :]).astype(BF)
            slot_grad[slots, :] = slot_part
            raised = mm(chosen_rows, weight(slot, 0))
            square = raised * raised
            bent = jnp.tanh(C0 * raised * (1.0 + C1 * square))
            cdf = 0.5 * (1.0 + bent)
            act = (raised * cdf).astype(BF)
            activated[slots, :] = act
            slope = cdf + 0.5 * raised * (1.0 - bent * bent) * (C0 * (1.0 + 3.0 * C1 * square))
            act_grad = mm(slot_part, weight(slot, 1))
            back = (act_grad * slope).astype(BF)
            raised_grad[slots, :] = back
            lowered = mm_nt(act, weight(slot, 1)).astype(BF)
            epart[rows, :] += mm(put, lowered).astype(BF)
            pulled = mm_nt(back, weight(slot, 0)).astype(BF)
            npart[rows, :] += mm(put, pulled).astype(BF)
            return carry

        lax.fori_loop(0, 2, one_micro, 0)

        def weight_part(i, carry):
            lanes = block(i * 384, 384)
            slabs = pl.ds(i * 4, 4)
            part = mm_tn(picked[:, lanes], raised_grad[...]).astype(BF)
            gw[e, 0, slabs] = part.reshape(4, shard, -1)
            part = mm_tn(slot_grad[:, lanes], activated[...]).astype(BF)
            gw[e, 1, slabs] = part.reshape(4, shard, -1)
            return carry

        lax.fori_loop(0, width // 384, weight_part, 0)
        reduce_first(e)

        @pl.when(e > 0)
        def _():
            reduce_step(e - 1, 2)

        return carry

    lax.fori_loop(0, experts, expert_step, 0)

    for peer in (place.right, place.left):
        pl.semaphore_signal(ready, inc=1, device_id=peer, device_id_type=MESH)

    parts = (epart, npart)
    for m in range(2):
        for j in range(2):
            sums.c_copy(m, j, parts[j]).start()

    def fetch_normed(i):
        return pltpu.make_async_copy(normed_hbm.at[pl.ds(i * seg, seg)], ffn.at[i], load_sem.at[i])

    fetch_normed(0).start()
    fetch_normed(1).start()
    for m in range(2):
        for j in range(2):
            sums.to_quarters(m, j, parts[j])
    pump()
    fill_bias(bias_ref, band, heads)
    spread[...] = jnp.zeros(spread.shape, F32)
    band_sum[...] = jnp.zeros(band_sum.shape, F32)
    whole_sum[...] = jnp.zeros(whole_sum.shape, F32)
    tiny_own[...] = jnp.zeros(tiny_own.shape, F32)
    pl.semaphore_wait(ready, 2)
    pump()

    def own_copy(m, j, ref):
        return pltpu.make_async_copy(
            own_out.at[m, j - 1], ref.at[sums.own_rows(m)], out_sem.at[m * 2 + j - 1]
        )

    for m in range(2):
        rows = sums.own_rows(m)
        expert_sum, down = sums.total(m, 0), sums.total(m, 1)
        first = place.core * (seg // 2) + place.yy * (seg // 4)
        live, upstream = upstream_of(rows, m, first)
        probs, chosen = probs_ref[rows, :], chosen_of(rows)
        gate = jnp.sum(probs * chosen, axis=-1, keepdims=True)
        gate_grad = jnp.sum(expert_sum * upstream, axis=-1, keepdims=True)
        logit_grad = (probs * gate_grad * (chosen - gate)).astype(BF)
        x = hidden[m]
        down = down + mm(logit_grad, router16)
        through, gain_terms = norm_back(x, gains[1:2, :], down)
        full = through + upstream
        hgrad[m] = full
        bgrad[rows, :] = full.astype(BF)
        sums.share(m, 0, bgrad)
        own_out[m, 0] = (live * (x + gate * expert_sum)).astype(BF)
        own_copy(m, 1, result).start()
        tiny_own[1:2, :] += jnp.sum(gain_terms, axis=0, keepdims=True)
        tiny_own[...] += mm_tn(logit_grad, ntwo[rows, :])[0:8, :]
    pump()
    for m in range(2):
        sums.pass_on(m, 0, bgrad)
    for m in range(2):
        sums.share(m, 1, result, own_out.at[m, 0])

    def dkv_copy(m, h):
        spot = dkv.at[m, h]
        return remote(spot, spot, kv_s.at[m, h], kv_r.at[m, h], place.partner)

    def attend_back(m):
        length = len_ref[m]

        def lower(i, carry):
            part = mm(bgrad[block(m * seg + i * 256, 256), :], ws[:, span:])
            part = jnp.where(low_lanes(part.shape), 0.0, part)
            do3[block(i * 256, 256), :] = part.astype(BF)
            return carry

        lax.fori_loop(0, seg // 256, lower, 0)
        for h in range(heads):
            cut = head_lanes(h)
            dkv_acc[...] = jnp.zeros(dkv_acc.shape, F32)

            def step(i, carry):
                rows = block(m * seg + i * QT, QT)
                first = cx * seg + i * QT
                q_tile, do_tile = q3[rows, cut], do3[block(i * QT, QT), cut]
                keys = kv[m, :, cut]
                values, allowed = masked_scores(q_tile, keys, band, scores, h, first, length)
                soft = jnp.where(allowed, jnp.exp(values - lse[rows, h : h + 1]), 0.0)
                soft_grad = mm_nt(do_tile, keys)
                delta = jnp.sum(soft * soft_grad, axis=-1, keepdims=True)
                score_grad = (soft * (soft_grad - delta)).astype(BF)
                dkv_acc[...] += mm_tn(soft.astype(BF), do_tile) + 0.125 * mm_tn(score_grad, q_tile)
                part = mm(score_grad, keys) * 0.125
                grads[rows, head_lanes(h, span)] = jnp.where(
                    low_lanes(part.shape), part, 0.0
                ).astype(BF)
                spread[:, BAND:] = score_grad.astype(F32)
                for part in range(QT // BAND):
                    lanes = block(first + part * BAND, 2 * BAND)
                    band_sum[h] += spread[part * BAND : (part + 1) * BAND, lanes]
                whole_sum[h : h + 1, :] += jnp.sum(spread[:, BAND:], axis=0, keepdims=True)
                return carry

            lax.fori_loop(0, seg // QT, step, 0)

            @pl.when(cx == 1)
            def _():
                dkv[m, h] = dkv_acc[0:seg, :].astype(BF)
                dkv_copy(m, h).start()

            grads[pl.ds(m * seg, seg), cut] = dkv_acc[block(cx * seg, seg), :].astype(BF)
            if h % 2 == 1:
                pump()

    def after_attend(m):
        rows = pl.ds(m * seg, seg)

        @pl.when(cx == 0)
        def _():
            for h in range(heads):
                dkv_copy(m, h).wait_recv()
                total = grads[rows, head_lanes(h)].astype(F32) + dkv[m, h].astype(F32)
                grads[rows, head_lanes(h)] = total.astype(BF)

        def lower(i, carry):
            spot = block(m * seg + i * 256, 256)
            npart[spot, :] = mm_nt(grads[spot, :], ws[...]).astype(BF)
            return carry

        lax.fori_loop(0, seg // 256, lower, 0)
        sums.c_copy(m, 2, npart).start()

    for m in range(2):
        sums.shared(m, 0, bgrad)
        attend_back(m)
        if m == 1:
            sums.c_copy(0, 1, npart).wait_send()
            sums.y_copy(0, 0).wait_send()
            after_attend(0)
    sums.c_copy(1, 1, npart).wait_send()
    sums.y_copy(1, 0).wait_send()
    sums.to_quarters(0, 2, npart)
    for m in range(2):
        sums.pass_on(m, 1, result)

    bucket_sums(heads, band_sum, whole_sum, dbias_own)
    bx_copy = remote(dbias_own, dbias_x, bx_s.at[0], bx_r.at[0], place.partner)
    bx_copy.start()

    def out_part(i, carry):
        lanes = block(i * 256, 256)
        gs[lanes, span:] = mm_tn(bgrad[:, lanes], ab3[...]).astype(BF)
        return carry

    lax.fori_loop(0, width // 256, out_part, 0)
    after_attend(1)
    bx_copy.wait_recv()
    dbias_own_sum = dbias_own[...] + dbias_x[...]
    dbias_out[...] = dbias_own_sum

    def bz_copy(k):
        return remote(
            dbias_out, dbias_z.at[k - 1], bz_s.at[k - 1], bz_r.at[k - 1], place.z_peers[k - 1]
        )

    for k in (1, 2, 3):
        bz_copy(k).start()
    fetch_normed(0).wait()
    fetch_normed(1).wait()

    def qkv_part(i, carry):
        lanes = block(i * 256, 256)
        part = mm_tn(ffn[0, :, lanes], grads[0:seg, :])
        part = part + mm_tn(ffn[1, :, lanes], grads[seg:, :])
        gs[lanes, 0:span] = part[:, 0:span].astype(BF)
        both = part[:, span:] + gs[lanes, span:].astype(F32)
        gs[lanes, span:] = both.astype(BF)
        return carry

    lax.fori_loop(0, width // 256, qkv_part, 0)
    sums.to_quarters(1, 2, npart)

    def slab_rows(d, c):
        return block(d * 2 * shard + c * shard, shard, 32)

    def sx_copy(k):
        rows = slab_rows(lax.rem(dp + k, 4), 1 - cx)
        return remote(gs.at[rows, :], sx.at[k], sx_s.at[k], sx_r.at[k], place.partner)

    def sz_copy(k):
        return remote(sx.at[k], sz.at[k - 1], sz_s.at[k - 1], sz_r.at[k - 1], place.z_peers[k - 1])

    order = (2, 1, 3, 0)
    for k in order:
        sx_copy(k).start()

    for m in range(2):
        down = sums.total(m, 2)
        fetch(m).wait()
        through, gain_terms = norm_back(tok[m].astype(F32), gains[0:1, :], down)
        own_out[m, 1] = (through + hgrad[m]).astype(BF)
        sums.share(m, 2, input_grad, own_out.at[m, 1])
        own_copy(m, 2, input_grad).start()
        tiny_own[0:1, :] += jnp.sum(gain_terms, axis=0, keepdims=True)

    def tt_copy(k):
        return remote(
            tiny_own, tiny_t.at[k - 1], tt_s.at[k - 1], tt_r.at[k - 1], place.tensor_peers[k - 1]
        )

    for k in (1, 2, 3):
        tt_copy(k).start()
    pump(len(steps))
    for k in order:
        sx_copy(k).wait_recv()
        rows = slab_rows(lax.rem(dp + k, 4), cx)
        total = gs[rows, :].astype(F32) + sx[k].astype(F32)
        if k == 0:
            small_grad[...] = total
        else:
            sx[k] = total.astype(BF)
            sz_copy(k).start()

    for k in (1, 2, 3):
        tt_copy(k).wait_recv()
    tiny_x[0] = tiny_own[...] + tiny_t[0] + tiny_t[1] + tiny_t[2]
    tx_copy = remote(tiny_x.at[0], tiny_x.at[1], tx_s.at[0], tx_r.at[0], place.partner)
    tx_copy.start()
    for m in range(2):
        sums.pass_on(m, 2, input_grad)
    for e in range(experts):
        reduce_end(e)
    tx_copy.wait_recv()
    tiny_x[2] = tiny_x[0] + tiny_x[1]

    def tz_copy(k):
        return remote(
            tiny_x.at[2], tiny_z.at[k - 1], tz_s.at[k - 1], tz_r.at[k - 1], place.z_peers[k - 1]
        )

    for k in (1, 2, 3):
        tz_copy(k).start()
    total = small_grad[...]
    for k in (1, 2, 3):
        sz_copy(k).wait_recv()
        total = total + sz[k - 1].astype(F32)
    small_grad[...] = total
    total = dbias_own_sum
    for k in (1, 2, 3):
        bz_copy(k).wait_recv()
        total = total + dbias_z[k - 1]
    for k in (1, 2, 3):
        bz_copy(k).wait_send()
    dbias_out[...] = total
    total = tiny_x[2]
    for k in (1, 2, 3):
        tz_copy(k).wait_recv()
        total = total + tiny_z[k - 1]
    tiny_out[...] = total
    for m in range(2):
        sums.shared(m, 1, result)
        sums.shared(m, 2, input_grad)

    for e in range(experts):
        for d in range(2):
            for s in (1, 2, 3, 4):
                reduce_copy(d, e, s).wait_send()
    for k in range(4):
        sx_copy(k).wait_send()
        if k > 0:
            sz_copy(k).wait_send()
            tt_copy(k).wait_send()
            tz_copy(k).wait_send()
    tx_copy.wait_send()
    bx_copy.wait_send()
    for m in range(2):
        sums.c_copy(m, 0, epart).wait_send()
        sums.c_copy(m, 2, npart).wait_send()
        own_copy(m, 1, result).wait()
        own_copy(m, 2, input_grad).wait()
        for j in range(3):
            if j > 0:
                sums.y_copy(m, j).wait_send()
            for step in range(3):
                own = None if j == 0 else own_out.at[m, j - 1]
                sums.a_copy(m, j, (bgrad, result, input_grad)[j], step, own).wait_send()

        @pl.when(cx == 1)
        def _():
            for h in range(heads):
                dkv_copy(m, h).wait_send()


def second_call(
    lengths, bias, ids, slot_lanes, slot_subs, cot, ntwo, q3, kv, lse, ab3, ws, gains, hidden,
    normed, tok, w_full,
):
    heads = bias.shape[1]
    rows, width = cot.shape
    span = q3.shape[1]
    experts, ff = w_full.shape[0], w_full.shape[4]
    seg = rows // 2
    quarter = seg // 4
    shard = width // 8
    slots = 2 * slot_subs.shape[0]
    vm = pl.BlockSpec(memory_space=pltpu.VMEM)
    sm = pl.BlockSpec(memory_space=pltpu.SMEM)
    hbm = pl.BlockSpec(memory_space=pl.ANY)
    dma = pltpu.SemaphoreType.DMA
    sds = jax.ShapeDtypeStruct
    return pl.pallas_call(
        functools.partial(second_kernel, heads),
        out_shape=(
            sds((rows, width), BF),
            sds((rows, width), BF),
            sds((experts, 2, shard, ff), F32),
            sds((shard, width), F32),
            sds((8, width), F32),
            sds((BUCKETS, 128), F32),
        ),
        in_specs=[sm, sm] + [vm] * 12 + [hbm] * 3,
        out_specs=(hbm,) * 2 + (vm,) * 4,
        scratch_shapes=[
            pltpu.VMEM((4, 8, shard, ff), BF),
            pltpu.VMEM((experts, 2, 8, shard, ff), BF),
            pltpu.VMEM((2, experts, shard, ff), BF),
            pltpu.VMEM((2, experts, 2, shard, ff), BF),
            pltpu.VMEM((width, width), BF),
            pltpu.VMEM((4, shard, width), BF),
            pltpu.VMEM((3, shard, width), BF),
            pltpu.VMEM((rows, width), BF),
            pltpu.VMEM((rows, width), BF),
            pltpu.VMEM((rows, width), BF),
            pltpu.VMEM((4, slots, width), BF),
            pltpu.VMEM((rows, 16), F32),
            pltpu.VMEM((2, quarter, width), BF),
            pltpu.VMEM((2, 2, 2 * quarter, width), BF),
            pltpu.VMEM((2, 2, quarter, width), BF),
            pltpu.VMEM((2, 2, quarter, width), BF),
            pltpu.VMEM((2, 2, quarter, width), F32),
            pltpu.VMEM((2, quarter, width), F32),
            pltpu.VMEM((rows, width), BF),
            pltpu.VMEM((2, 2, quarter, width), BF),
            pltpu.VMEM((seg, span), BF),
            pltpu.VMEM((rows, 2 * span), BF),
            pltpu.VMEM((rows, 128), F32),
            pltpu.VMEM((2, heads, seg, 128), BF),
            pltpu.VMEM((heads, BAND, 2 * BAND), F32),
            pltpu.VMEM((QT, rows + BAND), F32),
            pltpu.VMEM((QT, rows + BAND), F32),
            pltpu.VMEM((heads, BAND, 2 * BAND), F32),
            pltpu.VMEM((8, rows), F32),
            pltpu.VMEM((8, width), F32),
            pltpu.VMEM((3, 8, width), F32),
            pltpu.VMEM((3, 8, width), F32),
            pltpu.VMEM((3, 8, width), F32),
            pltpu.VMEM((BUCKETS, 128), F32),
            pltpu.VMEM((BUCKETS, 128), F32),
            pltpu.VMEM((3, BUCKETS, 128), F32),
            dma((2,)),
            dma((2,)),
            dma((4,)),
            pltpu.SemaphoreType.REGULAR,
            dma((2, experts, 4)),
            dma((2, experts, 4)),
            dma((2, 3)),
            dma((2, 3)),
            dma((2, 3)),
            dma((2, 3)),
            dma((2, 3, 3)),
            dma((2, 3, 3)),
            dma((2, heads)),
            dma((2, heads)),
            dma((4,)),
            dma((4,)),
        ]
        + [dma((3,))] * 4
        + [dma((1,))] * 2
        + [dma((3,))] * 2
        + [dma((1,))] * 2
        + [dma((3,))] * 2,
        compiler_params=pltpu.CompilerParams(
            collective_id=1, has_side_effects=True, vmem_limit_bytes=63 << 20
        ),
    )(
        lengths, bias, ids, slot_lanes, slot_subs, cot, ntwo, q3, kv, lse, ab3, ws, gains, hidden,
        normed, tok, w_full,
    )


def body_fast(
    inputs, lengths, expert_ids, slot_rows, attn_gain, qkv_weight, out_weight, position_bias,
    ffn_gain, router_weight, up_weight, down_weight, cotangent,
):
    micro, seg, width = inputs.shape
    rows = micro * seg
    experts = up_weight.shape[0]
    heads = position_bias.shape[1]
    size = qkv_weight.shape[2] // heads
    slab = lax.axis_index("dp") * 2 + lax.axis_index("ctx")
    shard = attn_gain.shape[0]
    by_head = jnp.concatenate(
        [
            qkv_weight[1].reshape(shard, heads, 1, size),
            qkv_weight[2].reshape(shard, heads, 1, size),
        ],
        axis=2,
    ).reshape(shard, -1)
    by_query = jnp.concatenate(
        [
            qkv_weight[0].reshape(shard, heads, 1, size),
            out_weight.T.reshape(shard, heads, 1, size),
        ],
        axis=2,
    ).reshape(shard, -1)
    small = jnp.concatenate(
        [attn_gain[None], ffn_gain[None], router_weight.T, jnp.zeros((10, shard), BF)], axis=0
    )
    small = lax.dynamic_update_slice(jnp.zeros((16, width), BF), small, (0, slab * shard))
    wsmall = jnp.concatenate([jnp.concatenate([by_head, by_query], axis=1), small], axis=0)
    w = jnp.stack([up_weight, jnp.transpose(down_weight, (0, 2, 1))], axis=1)
    tok = inputs.reshape(rows, width)
    hidden, ntwo, normed, q3, kv, lse, ab3, ws, gains, w_full = first_call(
        lengths, position_bias, tok, wsmall, w
    )
    slots = slot_rows[:, 0].reshape(micro * experts, -1)
    result, input_part, w_grad, small_grad, tiny, dbias = second_call(
        lengths, position_bias, expert_ids.reshape(rows, 1), slots, slots.T,
        cotangent.reshape(rows, width), ntwo, q3, kv, lse, ab3, ws, gains, hidden, normed, tok, w_full,
    )
    tiny = lax.dynamic_slice_in_dim(tiny, slab * shard, shard, axis=1)
    parts = small_grad.reshape(shard, 2, heads, 2, size)
    qkv_grad = jnp.stack(
        [parts[:, 1, :, 0], parts[:, 0, :, 0], parts[:, 0, :, 1]], axis=0
    ).reshape(3, shard, heads * size)
    return (
        result.reshape(inputs.shape),
        input_part.reshape(inputs.shape),
        tiny[0],
        qkv_grad,
        parts[:, 1, :, 1].reshape(shard, heads * size).T,
        dbias[:, :heads],
        tiny[1],
        tiny[2 : 2 + experts].T,
        w_grad[:, 0],
        jnp.transpose(w_grad[:, 1], (0, 2, 1)),
    )


def rms_norm(values, gain_vector):
    return (
        values * lax.rsqrt(jnp.mean(values * values, axis=-1, keepdims=True) + 1e-06) * gain_vector
    )


def bucket_of(distance):
    clipped = jnp.maximum(distance, 0)
    edge_values = jnp.asarray(bucket_edges, dtype=jnp.int32)
    beyond = jnp.sum((clipped[..., None] >= edge_values).astype(jnp.int32), axis=-1)
    return jnp.where(clipped < 16, clipped, jnp.minimum(16 + beyond, 31))


def toeplitz(diagonal, query_count, key_count):
    head_count = diagonal.shape[0]
    padded = jnp.pad(diagonal, ((0, 0), (0, 1)))
    row_width = query_count + key_count
    repeated = jnp.broadcast_to(padded[:, None, :], (head_count, query_count, row_width)).reshape(
        head_count, query_count * row_width
    )
    repeated = jnp.pad(repeated, ((0, 0), (0, query_count))).reshape(
        head_count, query_count, row_width + 1
    )[:, :, :key_count]
    return repeated[:, :, ::-1]


def diagonal_sums(gradient):
    head_count, query_count, key_count = gradient.shape
    offset_count = query_count + key_count - 1
    flipped = jnp.pad(gradient[:, :, ::-1], ((0, 0), (0, 0), (0, query_count)))
    skewed = flipped.reshape(head_count, query_count * (offset_count + 1))[
        :, : query_count * offset_count
    ]
    return jnp.sum(skewed.reshape(head_count, query_count, offset_count), axis=1)


def bucket_table(query_first, query_count, key_count):
    offsets = (
        query_first - (key_count - 1) + jnp.arange(query_count + key_count - 1, dtype=jnp.int32)
    )
    return (bucket_of(offsets)[:, None] == jnp.arange(BUCKETS, dtype=jnp.int32)[None, :]).astype(
        jnp.float32
    )


def body(
    inputs,
    lengths,
    expert_ids,
    slot_rows,
    attn_gain,
    qkv_weight,
    out_weight,
    position_bias,
    ffn_gain,
    router_weight,
    up_weight,
    down_weight,
    cotangent,
):
    highest = lax.Precision.HIGHEST
    micro_count, seg_rows, model_width = inputs.shape
    local_heads = position_bias.shape[1]
    head_size = qkv_weight.shape[2] // local_heads
    expert_count = up_weight.shape[0]
    query_first = lax.axis_index("ctx") * seg_rows
    query_pos = query_first + jnp.arange(seg_rows, dtype=jnp.int32)

    def pair_scores(query_heads, query_start, key_heads, length):
        query_count = query_heads.shape[0]
        key_count = key_heads.shape[0]
        scores = (
            jnp.einsum("qhd,khd->hqk", query_heads, key_heads, preferred_element_type=jnp.float32)
            * 0.125
        )
        diagonal = jnp.einsum(
            "rb,bh->hr",
            bucket_table(query_start, query_count, key_count),
            position_bias,
            precision=highest,
        )
        scores = scores + toeplitz(diagonal, query_count, key_count)
        query_place = query_start + jnp.arange(query_count, dtype=jnp.int32)
        key_place = jnp.arange(key_count, dtype=jnp.int32)
        allowed = (key_place[None, :] <= query_place[:, None]) & (key_place[None, :] < length)
        return (scores, allowed)

    def scores_for(query_heads, key_block, length):
        key_count = key_block.shape[0]
        key_heads = key_block.reshape(key_count, local_heads, head_size)
        scores, allowed = pair_scores(query_heads, query_first, key_heads, length)
        return (scores, allowed, key_heads)

    results = []
    input_parts = []
    grad_sums = None
    bias_total = jnp.zeros((local_heads, BUCKETS), jnp.float32)
    for micro_step in range(micro_count):
        forward_gain_one = lax.all_gather(attn_gain, ("dp", "ctx"), axis=0, tiled=True)
        forward_qkv_full = lax.all_gather(qkv_weight, ("dp", "ctx"), axis=1, tiled=True)
        forward_out_full = lax.all_gather(out_weight, ("dp", "ctx"), axis=1, tiled=True)
        forward_gain_two = lax.all_gather(ffn_gain, ("dp", "ctx"), axis=0, tiled=True)
        forward_router_full = lax.all_gather(router_weight, ("dp", "ctx"), axis=0, tiled=True)
        forward_up_full = lax.all_gather(up_weight, ("dp", "ctx"), axis=1, tiled=True)
        forward_down_full = lax.all_gather(down_weight, ("dp", "ctx"), axis=2, tiled=True)
        forward_tokens = inputs[micro_step].astype(jnp.float32)
        forward_length = lengths[micro_step]
        forward_normed = rms_norm(forward_tokens, forward_gain_one.astype(jnp.float32)).astype(
            jnp.bfloat16
        )
        forward_projected = jnp.einsum(
            "td,cde->cte", forward_normed, forward_qkv_full, preferred_element_type=jnp.float32
        ).astype(jnp.bfloat16)
        forward_query_heads = forward_projected[0].reshape(seg_rows, local_heads, head_size)
        row_top = jnp.full((local_heads, seg_rows), -1e30, jnp.float32)
        attend_scores, attend_allowed, attend_key_heads = scores_for(
            forward_query_heads,
            lax.all_gather(forward_projected[1], "ctx", axis=0, tiled=True),
            forward_length,
        )
        value_heads = lax.all_gather(forward_projected[2], "ctx", axis=0, tiled=True).reshape(
            attend_key_heads.shape
        )
        attend_scores = jnp.where(attend_allowed[None], attend_scores, -1e30)
        new_top = jnp.maximum(row_top, jnp.max(attend_scores, axis=-1))
        weights_exp = jnp.where(
            attend_allowed[None], jnp.exp(attend_scores - new_top[:, :, None]), 0.0
        )
        row_total = jnp.sum(weights_exp, axis=-1)
        summed = jnp.einsum(
            "hqk,khd->hqd",
            weights_exp.astype(jnp.bfloat16),
            value_heads,
            preferred_element_type=jnp.float32,
        )
        row_top, row_total, summed = (new_top, row_total, summed)
        forward_attended = summed / row_total[:, :, None]
        forward_log_total = row_top + jnp.log(row_total)
        forward_attended_low = (
            jnp.transpose(forward_attended, (1, 0, 2)).reshape(seg_rows, -1).astype(jnp.bfloat16)
        )
        branch = lax.psum(
            jnp.dot(
                forward_attended_low, forward_out_full, preferred_element_type=jnp.float32
            ).astype(jnp.bfloat16),
            "tensor",
        ).astype(jnp.float32)
        forward_hidden = forward_tokens + branch
        forward_normed_two = rms_norm(forward_hidden, forward_gain_two.astype(jnp.float32)).astype(
            jnp.bfloat16
        )
        logits = jnp.dot(
            forward_normed_two, forward_router_full, preferred_element_type=jnp.float32
        )
        forward_router_probs = jax.nn.softmax(logits, axis=-1)
        forward_chosen = (
            expert_ids[micro_step][:, None] == jnp.arange(expert_count, dtype=jnp.int32)[None, :]
        ).astype(jnp.float32)
        forward_gate_value = jnp.sum(forward_router_probs * forward_chosen, axis=-1)
        forward_slot_table = slot_rows[micro_step, 0]
        padded = jnp.concatenate(
            [forward_normed_two, jnp.zeros((1, model_width), jnp.bfloat16)], axis=0
        )
        forward_picked = padded[forward_slot_table]
        forward_raised = jnp.einsum(
            "ekd,edf->ekf", forward_picked, forward_up_full, preferred_element_type=jnp.float32
        )
        forward_activated = jax.nn.gelu(forward_raised).astype(jnp.bfloat16)
        lowered = jnp.einsum(
            "ekf,efd->ekd", forward_activated, forward_down_full, preferred_element_type=jnp.float32
        )
        spread = (
            jnp.zeros((seg_rows + 1, model_width), jnp.float32)
            .at[forward_slot_table.reshape(-1)]
            .add(lowered.reshape(-1, model_width))[:seg_rows]
        )
        forward_expert_sum = lax.psum(spread.astype(jnp.bfloat16), "tensor").astype(jnp.float32)
        forward_live_rows = (query_pos < forward_length).astype(jnp.float32)[:, None]
        result = (
            forward_live_rows * (forward_hidden + forward_gate_value[:, None] * forward_expert_sum)
        ).astype(jnp.bfloat16)
        forward_kept_state = (
            forward_tokens,
            forward_length,
            forward_normed,
            forward_projected,
            forward_attended,
            forward_log_total,
            forward_attended_low,
            forward_hidden,
            forward_normed_two,
            forward_router_probs,
            forward_chosen,
            forward_gate_value,
            forward_slot_table,
            forward_picked,
            forward_raised,
            forward_activated,
            forward_expert_sum,
            forward_live_rows,
        )
        result, kept_state = (result, forward_kept_state)
        gain_one = lax.all_gather(attn_gain, ("dp", "ctx"), axis=0, tiled=True)
        qkv_full = lax.all_gather(qkv_weight, ("dp", "ctx"), axis=1, tiled=True)
        out_full = lax.all_gather(out_weight, ("dp", "ctx"), axis=1, tiled=True)
        gain_two = lax.all_gather(ffn_gain, ("dp", "ctx"), axis=0, tiled=True)
        router_full = lax.all_gather(router_weight, ("dp", "ctx"), axis=0, tiled=True)
        up_full = lax.all_gather(up_weight, ("dp", "ctx"), axis=1, tiled=True)
        down_full = lax.all_gather(down_weight, ("dp", "ctx"), axis=2, tiled=True)
        (
            tokens,
            backward_length,
            normed,
            projected,
            attended,
            log_total,
            attended_low,
            hidden,
            normed_two,
            router_probs,
            chosen,
            gate_value,
            slot_table,
            picked,
            raised,
            activated,
            expert_sum,
            live_rows,
        ) = kept_state
        upstream = live_rows * cotangent[micro_step].astype(jnp.float32)
        sum_grad = (gate_value[:, None] * upstream).astype(jnp.bfloat16)
        gate_grad = jnp.sum(expert_sum * upstream, axis=-1)
        logit_grad = (router_probs * gate_grad[:, None] * (chosen - gate_value[:, None])).astype(
            jnp.bfloat16
        )
        router_part = jnp.einsum(
            "td,te->de", normed_two, logit_grad, preferred_element_type=jnp.float32
        )
        padded_grad = jnp.concatenate([sum_grad, jnp.zeros((1, model_width), jnp.bfloat16)], axis=0)
        slot_grad = padded_grad[slot_table]
        down_part = jnp.einsum(
            "ekf,ekd->efd", activated, slot_grad, preferred_element_type=jnp.float32
        )
        act_grad = jnp.einsum(
            "ekd,efd->ekf", slot_grad, down_full, preferred_element_type=jnp.float32
        )
        unused_value, gelu_back = jax.vjp(jax.nn.gelu, raised)
        raised_grad = gelu_back(act_grad)[0].astype(jnp.bfloat16)
        up_part = jnp.einsum(
            "ekd,ekf->edf", picked, raised_grad, preferred_element_type=jnp.float32
        )
        picked_grad = jnp.einsum(
            "ekf,edf->ekd", raised_grad, up_full, preferred_element_type=jnp.float32
        )
        spread_grad = (
            jnp.zeros((seg_rows + 1, model_width), jnp.float32)
            .at[slot_table.reshape(-1)]
            .add(picked_grad.reshape(-1, model_width))[:seg_rows]
        )
        normed_two_grad = lax.psum(spread_grad.astype(jnp.bfloat16), "tensor").astype(
            jnp.float32
        ) + jnp.einsum("te,de->td", logit_grad, router_full, preferred_element_type=jnp.float32)
        unused_norm, second_back = jax.vjp(rms_norm, hidden, gain_two.astype(jnp.float32))
        hidden_grad, gain_two_part = second_back(normed_two_grad)
        hidden_grad = hidden_grad + upstream
        branch_grad = hidden_grad.astype(jnp.bfloat16)
        out_part = jnp.einsum(
            "te,td->ed", attended_low, branch_grad, preferred_element_type=jnp.float32
        )
        attended_grad = jnp.einsum(
            "td,ed->te", branch_grad, out_full, preferred_element_type=jnp.float32
        ).astype(jnp.bfloat16)
        grad_heads = attended_grad.reshape(seg_rows, local_heads, head_size)
        row_delta = jnp.sum(
            jnp.transpose(grad_heads.astype(jnp.float32), (1, 0, 2)) * attended, axis=-1
        )
        backward_query_heads = projected[0].reshape(seg_rows, local_heads, head_size)
        bias_zero = jnp.zeros((local_heads, BUCKETS), jnp.float32)
        attend_bias_acc = bias_zero
        bias_acc = attend_bias_acc
        score_scores, score_allowed, score_key_heads = scores_for(
            backward_query_heads,
            lax.all_gather(projected[1], "ctx", axis=0, tiled=True),
            backward_length,
        )
        score_value_heads = lax.all_gather(projected[2], "ctx", axis=0, tiled=True).reshape(
            score_key_heads.shape
        )
        score_key_count = score_key_heads.shape[0]
        soft_weights = jnp.where(
            score_allowed[None], jnp.exp(score_scores - log_total[:, :, None]), 0.0
        )
        weight_grad = jnp.einsum(
            "qhd,khd->hqk", grad_heads, score_value_heads, preferred_element_type=jnp.float32
        )
        score_grad = (soft_weights * (weight_grad - row_delta[:, :, None])).astype(jnp.bfloat16)
        query_acc = jnp.einsum(
            "hqk,khd->qhd", score_grad, score_key_heads, preferred_element_type=jnp.float32
        )
        bias_acc = bias_acc + jnp.dot(
            diagonal_sums(score_grad.astype(jnp.float32)),
            bucket_table(query_first, seg_rows, score_key_count),
            precision=highest,
        )
        (
            (attend_query_acc, attend_bias_acc),
            attend_soft_weights,
            attend_score_grad,
            attend_key_count,
        ) = ((query_acc, bias_acc), soft_weights, score_grad, score_key_count)
        key_term = (
            jnp.einsum(
                "hqk,qhd->khd",
                attend_score_grad,
                backward_query_heads,
                preferred_element_type=jnp.float32,
            )
            * 0.125
        )
        value_term = jnp.einsum(
            "hqk,qhd->khd",
            attend_soft_weights.astype(jnp.bfloat16),
            grad_heads,
            preferred_element_type=jnp.float32,
        )
        grad_term = jnp.stack(
            [key_term.reshape(attend_key_count, -1), value_term.reshape(attend_key_count, -1)],
            axis=1,
        )
        key_value_acc = grad_term
        query_acc, key_value_acc, bias_part = (attend_query_acc, key_value_acc, attend_bias_acc)
        own_grads = lax.psum_scatter(
            key_value_acc.astype(jnp.bfloat16), "ctx", scatter_dimension=0, tiled=True
        ).astype(jnp.float32)
        query_grad = (query_acc * 0.125).reshape(seg_rows, -1).astype(jnp.bfloat16)
        qkv_grad = jnp.stack(
            [
                query_grad,
                own_grads[:, 0].astype(jnp.bfloat16),
                own_grads[:, 1].astype(jnp.bfloat16),
            ],
            axis=0,
        )
        qkv_part = jnp.einsum("td,cte->cde", normed, qkv_grad, preferred_element_type=jnp.float32)
        normed_grad = lax.psum(
            jnp.einsum(
                "cte,cde->td", qkv_grad, qkv_full, preferred_element_type=jnp.float32
            ).astype(jnp.bfloat16),
            "tensor",
        ).astype(jnp.float32)
        unused_first, first_back = jax.vjp(rms_norm, tokens, gain_one.astype(jnp.float32))
        token_grad, gain_one_part = first_back(normed_grad)
        input_part = (token_grad + hidden_grad).astype(jnp.bfloat16)
        weight_parts = (
            gain_one_part,
            qkv_part,
            out_part,
            gain_two_part,
            router_part,
            up_part,
            down_part,
        )
        input_part, weight_parts, bias_part = (input_part, weight_parts, bias_part)
        results.append(result)
        input_parts.append(input_part)
        grad_sums = (
            weight_parts
            if grad_sums is None
            else tuple((old_sum + new_part for old_sum, new_part in zip(grad_sums, weight_parts)))
        )
        bias_total = bias_total + bias_part
    reduced = (
        lax.psum_scatter(grad_sums[0], ("dp", "ctx"), scatter_dimension=0, tiled=True),
        lax.psum_scatter(grad_sums[1], ("dp", "ctx"), scatter_dimension=1, tiled=True),
        lax.psum_scatter(grad_sums[2], ("dp", "ctx"), scatter_dimension=1, tiled=True),
        lax.psum_scatter(grad_sums[3], ("dp", "ctx"), scatter_dimension=0, tiled=True),
        lax.psum_scatter(grad_sums[4], ("dp", "ctx"), scatter_dimension=0, tiled=True),
        lax.psum_scatter(grad_sums[5], ("dp", "ctx"), scatter_dimension=1, tiled=True),
        lax.psum_scatter(grad_sums[6], ("dp", "ctx"), scatter_dimension=2, tiled=True),
    )
    bias_grad_total = lax.psum(bias_total, ("dp", "ctx"))
    return (
        jnp.stack(results, axis=0),
        jnp.stack(input_parts, axis=0),
        reduced[0],
        reduced[1],
        reduced[2],
        jnp.transpose(bias_grad_total),
        reduced[3],
        reduced[4],
        reduced[5],
        reduced[6],
    )


def solution(mesh):
    small = mesh.shape["ctx"] == 2 and mesh.shape["dp"] == 4 and mesh.shape["tensor"] == 4
    return jax.shard_map(
        body_fast if small else body,
        mesh=mesh,
        in_specs=(
            P("dp", "ctx", None),
            P("dp"),
            P("dp", "ctx"),
            P("dp", "ctx", None, None),
            P(("dp", "ctx")),
            P(None, ("dp", "ctx"), "tensor"),
            P("tensor", ("dp", "ctx")),
            P(None, "tensor"),
            P(("dp", "ctx")),
            P(("dp", "ctx"), None),
            P(None, ("dp", "ctx"), "tensor"),
            P(None, "tensor", ("dp", "ctx")),
            P("dp", "ctx", None),
        ),
        out_specs=(
            P("dp", "ctx", None),
            P("dp", "ctx", None),
            P(("dp", "ctx")),
            P(None, ("dp", "ctx"), "tensor"),
            P("tensor", ("dp", "ctx")),
            P(None, "tensor"),
            P(("dp", "ctx")),
            P(("dp", "ctx"), None),
            P(None, ("dp", "ctx"), "tensor"),
            P(None, "tensor", ("dp", "ctx")),
        ),
        check_vma=False,
    )
```

```python
import functools

import jax
import jax.numpy as jnp
import numpy as np
from jax import lax
from jax.experimental import pallas as pl
from jax.experimental.pallas import tpu as pltpu
from jax.sharding import PartitionSpec as P

BUCKETS = 32
MESH = pl.DeviceIdType.MESH
BF = jnp.bfloat16
F32 = jnp.float32


bucket_edges = np.ceil(16.0 * 8.0 ** (np.arange(1, 16) / 16.0)).astype(np.int32)
bucket_starts = [int(n) for n in range(17)] + [int(n) for n in bucket_edges]


QT = 256
BAND = 128
C0 = float(np.sqrt(2.0 / np.pi))
C1 = 0.044715


def mm(a, b):
    return jnp.dot(a, b, preferred_element_type=F32)


def mm_nt(a, b):
    return lax.dot_general(a, b, (((1,), (1,)), ((), ())), preferred_element_type=F32)


def mm_tn(a, b):
    return lax.dot_general(a, b, (((0,), (0,)), ((), ())), preferred_element_type=F32)


def remote(src, dst, send, recv, device):
    return pltpu.make_async_remote_copy(
        src_ref=src,
        dst_ref=dst,
        send_sem=send,
        recv_sem=recv,
        device_id=device,
        device_id_type=MESH,
    )


def block(start, size, whole=128):
    return pl.ds(pl.multiple_of(start, whole), size)


class Place:
    def __init__(self):
        dp, cx, t = lax.axis_index("dp"), lax.axis_index("ctx"), lax.axis_index("tensor")
        self.dp, self.cx, self.t = dp, cx, t
        self.yy, self.core = lax.div(t, 2), lax.rem(t, 2)
        self.partner = (dp, 1 - cx, t)
        self.sibling = (dp, cx, t + 1 - 2 * self.core)
        self.across = (dp, cx, lax.rem(t + 2, 4))
        self.tensor_peers = [(dp, cx, lax.rem(t + k, 4)) for k in (1, 2, 3)]
        self.z_peers = [(lax.rem(dp + k, 4), cx, t) for k in (1, 2, 3)]
        self.spot = dp + cx * (7 - 2 * dp)
        self.right = self.at_spot(1)
        self.left = self.at_spot(-1)

    def at_spot(self, away):
        spot = lax.rem(self.spot + 8 + away, 8)
        cx = lax.div(spot, 4)
        return (spot + cx * (7 - 2 * spot), cx, self.t)

    def slab(self, away):
        dp, cx, _ = self.at_spot(away)
        return dp * 2 + cx

    def greet(self):
        barrier = pltpu.get_barrier_semaphore()
        peers = self.z_peers + [self.partner] + self.tensor_peers
        for peer in peers:
            pl.semaphore_signal(barrier, inc=1, device_id=peer, device_id_type=MESH)
        pl.semaphore_wait(barrier, len(peers))


class Ring:
    def __init__(self, place, send_sems, recv_sems):
        self.place, self.send_sems, self.recv_sems = place, send_sems, recv_sems

    def copy(self, d, e, s, src, dst):
        at = (d, e, s - 1)
        device = self.place.right if d == 0 else self.place.left
        return remote(src, dst, self.send_sems.at[at], self.recv_sems.at[at], device)


class TensorSum:
    def __init__(self, place, seg, cbuf, ysend, ybuf, kept, c_s, c_r, y_s, y_r, a_s, a_r):
        self.place, self.seg = place, seg
        self.slot = (0, 1, 1, 1)
        self.half, self.quarter = seg // 2, seg // 4
        self.cbuf, self.ysend, self.ybuf, self.kept = cbuf, ysend, ybuf, kept
        self.c_s, self.c_r, self.y_s, self.y_r, self.a_s, self.a_r = c_s, c_r, y_s, y_r, a_s, a_r

    def rows(self, m, c, y):
        return block(m * self.seg + c * self.half + y * self.quarter, self.quarter)

    def own_rows(self, m):
        return self.rows(m, self.place.core, self.place.yy)

    def c_copy(self, m, j, src):
        rows = block(m * self.seg + (1 - self.place.core) * self.half, self.half)
        return remote(
            src.at[rows], self.cbuf.at[m, self.slot[j]], self.c_s.at[m, j], self.c_r.at[m, j],
            self.place.sibling,
        )

    def y_copy(self, m, j):
        return remote(
            self.ysend.at[m, self.slot[j]], self.ybuf.at[m, self.slot[j]], self.y_s.at[m, j], self.y_r.at[m, j],
            self.place.across,
        )

    def to_quarters(self, m, j, src):
        self.c_copy(m, j, src).wait_recv()
        yy, core = self.place.yy, self.place.core
        near, far = block(yy * self.quarter, self.quarter), block((1 - yy) * self.quarter, self.quarter)
        other = src[self.rows(m, core, 1 - yy), :].astype(F32)
        self.ysend[m, self.slot[j]] = (other + self.cbuf[m, self.slot[j], far, :].astype(F32)).astype(BF)
        self.y_copy(m, j).start()
        mine = src[self.rows(m, core, yy), :].astype(F32)
        self.kept[m, self.slot[j]] = mine + self.cbuf[m, self.slot[j], near, :].astype(F32)

    def total(self, m, j):
        self.y_copy(m, j).wait_recv()
        return self.kept[m, self.slot[j]] + self.ybuf[m, self.slot[j]].astype(F32)

    def a_copy(self, m, j, ref, step, own=None):
        yy, core = self.place.yy, self.place.core
        spot = ref.at[self.rows(m, core, 1 - yy if step == 2 else yy)]
        source = spot if own is None or step == 2 else own
        return remote(
            source, spot, self.a_s.at[m, j, step], self.a_r.at[m, j, step],
            self.place.across if step == 0 else self.place.sibling,
        )

    def a_recv(self, m, j, ref, step):
        yy, core = self.place.yy, self.place.core
        spot = ref.at[
            self.rows(m, core if step == 0 else 1 - core, yy if step == 1 else 1 - yy)
        ]
        return remote(
            spot, spot, self.a_s.at[m, j, step], self.a_r.at[m, j, step], self.place.sibling
        )

    def share(self, m, j, ref, own=None):
        self.a_copy(m, j, ref, 0, own).start()
        self.a_copy(m, j, ref, 1, own).start()

    def pass_on(self, m, j, ref):
        self.a_recv(m, j, ref, 0).wait_recv()
        self.a_copy(m, j, ref, 2).start()

    def shared(self, m, j, ref):
        self.a_recv(m, j, ref, 1).wait_recv()
        self.a_recv(m, j, ref, 2).wait_recv()


def low_lanes(shape):
    return lax.rem(lax.broadcasted_iota(jnp.int32, shape, len(shape) - 1), 128) < 64


def head_lanes(h, base=0):
    return slice(base + h * 128, base + (h + 1) * 128)


def fill_bias(bias_ref, band_ref, heads):
    rows = lax.broadcasted_iota(jnp.int32, (BAND, 2 * BAND), 0)
    cols = lax.broadcasted_iota(jnp.int32, (BAND, 2 * BAND), 1)
    away = rows + BAND - cols
    for h in range(heads):
        tile = jnp.full((BAND, 2 * BAND), bias_ref[0, h], F32)
        for b in range(1, BUCKETS):
            tile = jnp.where(away >= bucket_starts[b], bias_ref[b, h], tile)
        band_ref[h] = tile - bias_ref[BUCKETS - 1, h]


def masked_scores(q_tile, keys, band_ref, scores, h, first, length):
    count = keys.shape[0]
    scores[:, BAND:] = mm_nt(q_tile, keys) * 0.125
    for part in range(QT // BAND):
        spot = (block(part * BAND, BAND), block(first + part * BAND, 2 * BAND))
        scores[spot] = scores[spot] + band_ref[h]
    values = scores[:, BAND:]
    key_pos = lax.broadcasted_iota(jnp.int32, (QT, count), 1)
    query_pos = lax.broadcasted_iota(jnp.int32, (QT, count), 0) + first
    allowed = (key_pos <= query_pos) & (key_pos < length)
    return jnp.where(allowed, values, -1e30), allowed


def bucket_sums(heads, band_sum, whole_sum, dbias):
    rows = lax.broadcasted_iota(jnp.int32, (BAND, 2 * BAND), 0)
    cols = lax.broadcasted_iota(jnp.int32, (BAND, 2 * BAND), 1)
    away = rows + BAND - cols
    bucket = lax.broadcasted_iota(jnp.int32, (BUCKETS, 2 * BAND), 0)
    lanes128 = lax.broadcasted_iota(jnp.int32, (BUCKETS, 128), 1)
    result = jnp.zeros((BUCKETS, 128), F32)
    for h in range(heads):
        tile = band_sum[h]
        sums = jnp.zeros((BUCKETS, 2 * BAND), F32)
        for b in range(BUCKETS - 1):
            inside = (away >= bucket_starts[b]) & (away < bucket_starts[b + 1])
            row = jnp.sum(jnp.where(inside, tile, 0.0), axis=0, keepdims=True)
            sums = jnp.where(bucket == b, row, sums)
        per_bucket = jnp.sum(sums, axis=1, keepdims=True)
        near = jnp.sum(per_bucket, axis=0, keepdims=True)
        total = jnp.sum(whole_sum[h : h + 1, :], axis=1, keepdims=True)
        last = lax.broadcasted_iota(jnp.int32, (BUCKETS, 1), 0) == BUCKETS - 1
        per_bucket = jnp.where(last, total - near, per_bucket)
        result = jnp.where(lanes128 == h, per_bucket, result)
    dbias[...] = result


def norm_back(x, gain, grad):
    scale = lax.rsqrt(jnp.mean(x * x, axis=-1, keepdims=True) + 1e-06)
    unit = x * scale
    pulled = grad * gain
    inner = jnp.mean(pulled * unit, axis=-1, keepdims=True)
    return scale * (pulled - unit * inner), grad * unit


def layer_kernel(
    heads,
    len_ref,
    bias_ref,
    ids,
    slot_lanes,
    slot_subs,
    tok,
    cot,
    wsmall,
    w,
    result,
    input_grad,
    w_grad,
    small_grad,
    tiny_out,
    dbias_out,
    w_full,
    ws_full,
    ws,
    gains,
    hidden,
    ntwo,
    q3,
    kv,
    lse,
    ab3,
    wbuf,
    gw,
    in_one,
    in_two,
    in_late,
    sx,
    sz,
    sum_grad,
    epart,
    npart,
    ffn,
    probs_ref,
    cbuf,
    ysend,
    ybuf,
    kept,
    hgrad,
    bgrad,
    own_out,
    do3,
    grads,
    dkv_acc,
    dkv,
    band,
    scores,
    spread,
    band_sum,
    whole_sum,
    gg_own,
    gg_in,
    gg_sum,
    tiny_own,
    tiny_t,
    tiny_x,
    tiny_z,
    dbias_own,
    dbias_x,
    dbias_z,
    load_sem,
    out_sem,
    local,
    ready,
    gz_s,
    gz_r,
    gx_s,
    gx_r,
    k_s,
    k_r,
    ag_s,
    ag_r,
    rs_s,
    rs_r,
    c_s,
    c_r,
    y_s,
    y_r,
    a_s,
    a_r,
    kv_s,
    kv_r,
    gg_s,
    gg_r,
    sx_s,
    sx_r,
    sz_s,
    sz_r,
    tt_s,
    tt_r,
    tx_s,
    tx_r,
    tz_s,
    tz_r,
    bx_s,
    bx_r,
    bz_s,
    bz_r,
):
    place = Place()
    dp, cx, t = place.dp, place.cx, place.t
    seg = tok.shape[0] // 2
    width = tok.shape[1]
    shard = width // 8
    experts = w.shape[0]
    span = kv.shape[2]
    cap = slot_subs.shape[0]
    place.greet()
    gather_ring = Ring(place, ag_s, ag_r)
    reduce_ring = Ring(place, rs_s, rs_r)
    sums = TensorSum(place, seg, cbuf, ysend, ybuf, kept, c_s, c_r, y_s, y_r, a_s, a_r)
    bpart = epart

    def small_slab(k, c):
        return lax.rem(dp + 4 - k, 4) * 2 + c

    def gz_copy(k, slab):
        return remote(
            wsmall, ws_full.at[slab], gz_s.at[k - 1], gz_r.at[k - 1], place.z_peers[k - 1]
        )

    def gx_copy(k, c):
        spot = ws_full.at[small_slab(k, c)]
        return remote(wsmall if k == 0 else spot, spot, gx_s.at[k], gx_r.at[k], place.partner)

    small_own = pltpu.make_async_copy(wsmall, ws_full.at[small_slab(0, cx)], local.at[experts])

    def gather(d, e, s, sending):
        away = s - 1 if sending else s
        slab = place.slab(-away if d == 0 else away)
        spot = w_full.at[e, d, slab] if s == 4 else w_full.at[e, :, slab]
        return gather_ring.copy(d, e, s, w.at[e] if sending and s == 1 else spot, spot)

    def w_own(e):
        return pltpu.make_async_copy(w.at[e], w_full.at[e, :, place.slab(0)], local.at[e])

    def gather_step(e, s):
        for d in range(2):
            if s > 1:
                gather(d, e, s - 1, False).wait_recv()
            gather(d, e, s, True).start()

    gathers = [(0, 2), (1, 2), (2, 1), (0, 3), (1, 3), (3, 1), (0, 4), (1, 4)]
    gathers += [(2, 2), (3, 2), (2, 3), (3, 3), (2, 4), (3, 4)]

    def pump_gather(count=1):
        for _ in range(count):
            gather_step(*gathers.pop(0))

    def landing(d, e, s):
        if s == 1:
            return in_one.at[d, e]
        if s == 2:
            return in_two.at[d, e]
        if e < 2:
            return in_late.at[s - 3, d, e]
        return wbuf.at[e, pl.ds(d * 4 + (s - 3) * 2, 2)]

    def reduce_copy(d, e, s):
        slab = place.slab(5 - s if d == 0 else s - 5)
        src = gw.at[e, d, slab] if s == 1 else gw.at[e, :, slab]
        return reduce_ring.copy(d, e, s, src, landing(d, e, s))

    def reduce_step(e, s):
        for d in range(2):
            if s > 1:
                slab = place.slab(5 - s if d == 0 else s - 5)
                reduce_copy(d, e, s - 1).wait_recv()
                came = landing(d, e, s - 1)[...].astype(F32)
                if s == 2:
                    gw[e, d, slab] = (gw[e, d, slab].astype(F32) + came).astype(BF)
                else:
                    gw[e, :, slab] = (gw[e, :, slab].astype(F32) + came).astype(BF)
            reduce_copy(d, e, s).start()

    def reduce_end(e):
        total = gw[e, :, place.slab(0)].astype(F32)
        for d in range(2):
            reduce_copy(d, e, 4).wait_recv()
            total = total + landing(d, e, 4)[...].astype(F32)
        w_grad[e] = total

    late = [(3, 2), (2, 3), (3, 3), (2, 4), (3, 4)]

    def pump_late(count=1):
        for _ in range(count):
            if late:
                reduce_step(*late.pop(0))

    small_own.start()
    for k in (1, 3, 2):
        gz_copy(k, small_slab(0, cx)).start()
    gx_copy(0, cx).start()
    for e in range(2):
        gather_step(e, 1)
    for e in range(experts):
        w_own(e).start()

    @pl.when(cx == 0)
    def _():
        for m in range(2):
            kv[m, seg:, :] = jnp.zeros((seg, span), BF)

    fill_bias(bias_ref, band, heads)
    spread[...] = jnp.zeros(spread.shape, F32)
    band_sum[...] = jnp.zeros(band_sum.shape, F32)
    whole_sum[...] = jnp.zeros(whole_sum.shape, F32)
    tiny_own[...] = jnp.zeros(tiny_own.shape, F32)
    for k in (1, 3, 2):
        gz_copy(k, small_slab(k, cx)).wait_recv()
        gx_copy(k, cx).start()
    small_own.wait()
    for k in range(4):
        gx_copy(k, 1 - cx).wait_recv()
    total = ws_full[0, shard:, :].astype(F32)
    for i in range(1, 8):
        total = total + ws_full[i, shard:, :].astype(F32)
    gains[...] = total
    for i in range(8):
        ws[i * shard : (i + 1) * shard, :] = ws_full[i, 0:shard, :]

    def first_norm(rows):
        x = tok[rows, :].astype(F32)
        scale = lax.rsqrt(jnp.mean(x * x, axis=-1, keepdims=True) + 1e-06)
        return (x * scale * gains[0:1, :]).astype(BF)

    def project(m):
        def step(i, carry):
            rows = block(m * seg + i * 256, 256)
            x = first_norm(rows)
            kv[m, block(cx * seg + i * 256, 256), :] = mm(x, ws[:, 0:span]).astype(BF)
            part = mm(x, ws[:, span:])
            q3[rows, :] = jnp.where(low_lanes(part.shape), part, 0.0).astype(BF)
            return carry

        lax.fori_loop(0, seg // 256, step, 0)

    def k_copy(m):
        spot = kv.at[m, block(0, seg), :]
        return remote(spot, spot, k_s.at[m], k_r.at[m], place.partner)

    for m in range(2):
        project(m)

        @pl.when(cx == 0)
        def _():
            k_copy(m).start()

        pump_gather(1 + m)

    def attend(m):
        length = len_ref[m]

        def step(i, carry):
            rows = block(m * seg + i * QT, QT)
            first = cx * seg + i * QT
            lanes128 = lax.broadcasted_iota(jnp.int32, (QT, 128), 1)
            tops = jnp.zeros((QT, 128), F32)
            for h in range(heads):
                cut = head_lanes(h)
                values, allowed = masked_scores(
                    q3[rows, cut], kv[m, :, cut], band, scores, h, first, length
                )
                top = jnp.max(values, axis=-1, keepdims=True)
                raised = jnp.where(allowed, jnp.exp(values - top), 0.0)
                mass = jnp.sum(raised, axis=-1, keepdims=True)
                probs = (raised * (1.0 / mass)).astype(BF)
                part = mm(probs, kv[m, :, cut])
                ab3[rows, cut] = jnp.where(low_lanes(part.shape), 0.0, part).astype(BF)
                tops = jnp.where(lanes128 == h, top + jnp.log(mass), tops)
            lse[rows, :] = tops
            bpart[rows, :] = mm_nt(ab3[rows, :], ws[:, span:]).astype(BF)
            return carry

        lax.fori_loop(0, seg // QT, step, 0)

    def second_norm(m):
        rows = sums.own_rows(m)
        x = tok[rows, :].astype(F32) + sums.total(m, 3)
        hidden[m] = x
        scale = lax.rsqrt(jnp.mean(x * x, axis=-1, keepdims=True) + 1e-06)
        ntwo[rows, :] = (x * scale * gains[1:2, :]).astype(BF)
        sums.share(m, 3, ntwo)

    for m in range(2):

        @pl.when(cx == 1)
        def _():
            k_copy(m).wait_recv()

        attend(m)
        sums.c_copy(m, 3, bpart).start()
        pump_gather()
        if m == 1:
            second_norm(0)
        sums.to_quarters(m, 3, bpart)
    pump_gather()
    second_norm(1)
    sums.pass_on(0, 3, ntwo)
    pump_gather()
    sums.pass_on(1, 3, ntwo)
    pump_gather()
    for m in range(2):
        sums.shared(m, 3, ntwo)
        sums.c_copy(m, 3, bpart).wait_send()

    router16 = gains[...].astype(BF)

    def upstream_of(rows, m, first):
        spot = lax.broadcasted_iota(jnp.int32, (rows.size, 1), 0) + (cx * seg + first)
        live = (spot < len_ref[m]).astype(F32)
        return live, live * cot[rows, :].astype(F32)

    def chosen_of(rows):
        lanes = lax.broadcasted_iota(jnp.int32, (rows.size, 16), 1)
        return (lanes == ids[rows, :] + 2).astype(F32)

    for m in range(2):

        def gates(i, carry):
            rows = block(m * seg + i * 256, 256)
            logits = mm_nt(ntwo[rows, :], router16)
            lanes = lax.broadcasted_iota(jnp.int32, (256, 16), 1)
            inside = (lanes >= 2) & (lanes < 2 + experts)
            logits = jnp.where(inside, logits, -1e30)
            top = jnp.max(logits, axis=-1, keepdims=True)
            raised = jnp.where(inside, jnp.exp(logits - top), 0.0)
            probs = raised / jnp.sum(raised, axis=-1, keepdims=True)
            probs_ref[rows, :] = probs
            gate = jnp.sum(probs * chosen_of(rows), axis=-1, keepdims=True)
            live, upstream = upstream_of(rows, m, i * 256)
            sum_grad[rows, :] = (gate * upstream).astype(BF)
            epart[rows, :] = jnp.zeros((256, width), BF)
            npart[rows, :] = jnp.zeros((256, width), BF)
            return carry

        lax.fori_loop(0, seg // 256, gates, 0)

    def load(e):
        return pltpu.make_async_copy(
            w_full.at[e], wbuf.at[pl.ds((e % 2) * 2, 2)], load_sem.at[e % 2]
        )

    def arrived(e):
        w_own(e).wait()
        for d in range(2):
            gather(d, e, 4, False).wait_recv()
        load(e).start()

    picked, slot_grad, activated, raised_grad = (ffn.at[i] for i in range(4))

    def expert(e, between):
        slot = e % 2

        def weight(which):
            return wbuf[slot * 2 + which].reshape(width, -1)

        load(e).wait()

        def one_micro(m, carry):
            rows = block(m * seg, seg)
            slots = block(m * cap, cap)
            lanes = lax.broadcasted_iota(jnp.int32, (cap, 8), 1)
            column = jnp.sum(
                jnp.where(lanes == m * experts + e, slot_subs[...], 0), axis=1, keepdims=True
            )
            pick = (column == lax.broadcasted_iota(jnp.int32, (cap, seg), 1)).astype(BF)
            row = slot_lanes[pl.ds(m * experts + e, 1), :]
            put = (row == lax.broadcasted_iota(jnp.int32, (seg, cap), 0)).astype(BF)
            chosen_rows = mm(pick, ntwo[rows, :]).astype(BF)
            picked[slots, :] = chosen_rows
            slot_part = mm(pick, sum_grad[rows, :]).astype(BF)
            slot_grad[slots, :] = slot_part
            raised = mm(chosen_rows, weight(0))
            square = raised * raised
            bent = jnp.tanh(C0 * raised * (1.0 + C1 * square))
            cdf = 0.5 * (1.0 + bent)
            act = (raised * cdf).astype(BF)
            activated[slots, :] = act
            slope = cdf + 0.5 * raised * (1.0 - bent * bent) * (C0 * (1.0 + 3.0 * C1 * square))
            act_grad = mm(slot_part, weight(1))
            back = (act_grad * slope).astype(BF)
            raised_grad[slots, :] = back
            lowered = mm_nt(act, weight(1)).astype(BF)
            epart[rows, :] += mm(put, lowered).astype(BF)
            pulled = mm_nt(back, weight(0)).astype(BF)
            npart[rows, :] += mm(put, pulled).astype(BF)
            return carry

        lax.fori_loop(0, 2, one_micro, 0)
        between()

        def weight_part(i, carry):
            lanes = block(i * 384, 384)
            slabs = pl.ds(i * 4, 4)
            part = mm_tn(picked[:, lanes], raised_grad[...]).astype(BF)
            gw[e, 0, slabs] = part.reshape(4, shard, -1)
            part = mm_tn(slot_grad[:, lanes], activated[...]).astype(BF)
            gw[e, 1, slabs] = part.reshape(4, shard, -1)
            return carry

        lax.fori_loop(0, width // 384, weight_part, 0)
        reduce_step(e, 1)

    pump_gather()
    arrived(0)
    arrived(1)
    expert(0, pump_gather)
    pump_gather()
    expert(1, pump_gather)
    pump_gather(2)
    reduce_step(0, 2)
    arrived(2)
    reduce_step(1, 2)
    reduce_step(0, 3)
    expert(2, lambda: arrived(3))
    reduce_step(1, 3)
    reduce_step(0, 4)

    def last_between():
        reduce_step(1, 4)
        for m in range(2):
            sums.c_copy(m, 1, npart).start()
            sums.c_copy(m, 0, epart).start()

    expert(3, last_between)
    reduce_step(2, 2)

    for peer in (place.right, place.left):
        pl.semaphore_signal(ready, inc=1, device_id=peer, device_id_type=MESH)

    ones = jnp.ones((8, width), BF)
    for m in range(2):

        def gate_terms(i, carry):
            rows = block(m * seg + i * 256, 256)
            live, upstream = upstream_of(rows, m, i * 256)
            terms = epart[rows, :].astype(F32) * upstream
            high = terms.astype(BF)
            rest = (terms - high.astype(F32)).astype(BF)
            gg_own[m, :, block(i * 256, 256)] = mm_nt(ones, high) + mm_nt(ones, rest)
            return carry

        sums.y_copy(m, 3).wait_send()
        sums.to_quarters(m, 1, npart)
        lax.fori_loop(0, seg // 256, gate_terms, 0)

    def gg_copy(k):
        return remote(gg_own, gg_in.at[k - 1], gg_s.at[k - 1], gg_r.at[k - 1], place.tensor_peers[k - 1])

    for k in (1, 2, 3):
        gg_copy(k).start()
    pump_late()
    pl.semaphore_wait(ready, 2)
    for k in (1, 2, 3):
        gg_copy(k).wait_recv()
    gg_sum[...] = gg_own[...] + gg_in[0] + gg_in[1] + gg_in[2]
    own_first = place.core * (seg // 2) + place.yy * (seg // 4)

    def own_copy(m, j, ref):
        return pltpu.make_async_copy(
            own_out.at[m, j - 1], ref.at[sums.own_rows(m)], out_sem.at[m * 2 + j - 1]
        )

    for m in range(2):
        rows = sums.own_rows(m)
        line = gg_sum[m, :, block(own_first, seg // 4)]
        line = jnp.where(lax.broadcasted_iota(jnp.int32, line.shape, 0) == 0, line, 0.0)
        high = line.astype(BF)
        rest = (line - high.astype(F32)).astype(BF)
        ones = jnp.ones((8, 128), BF)
        gate_grad = (mm_tn(high, ones) + mm_tn(rest, ones))[:, 0:1]
        down = sums.total(m, 1)
        live, upstream = upstream_of(rows, m, own_first)
        probs, chosen = probs_ref[rows, :], chosen_of(rows)
        gate = jnp.sum(probs * chosen, axis=-1, keepdims=True)
        logit_grad = (probs * gate_grad * (chosen - gate)).astype(BF)
        down = down + mm(logit_grad, router16)
        through, gain_terms = norm_back(hidden[m], gains[1:2, :], down)
        full = through + upstream
        hgrad[m] = full
        bgrad[rows, :] = full.astype(BF)
        sums.share(m, 0, bgrad)
        tiny_own[1:2, :] += jnp.sum(gain_terms, axis=0, keepdims=True)
        tiny_own[...] += mm_tn(logit_grad, ntwo[rows, :])[0:8, :]
    pump_late()
    for m in range(2):
        sums.pass_on(m, 0, bgrad)
    for m in range(2):
        sums.to_quarters(m, 0, epart)

    def dkv_copy(m, h):
        spot = dkv.at[m, h]
        return remote(spot, spot, kv_s.at[m, h], kv_r.at[m, h], place.partner)

    def attend_back(m):
        length = len_ref[m]

        def lower(i, carry):
            part = mm(bgrad[block(m * seg + i * 256, 256), :], ws[:, span:])
            part = jnp.where(low_lanes(part.shape), 0.0, part)
            do3[block(i * 256, 256), :] = part.astype(BF)
            return carry

        lax.fori_loop(0, seg // 256, lower, 0)
        for h in range(heads):
            cut = head_lanes(h)
            dkv_acc[...] = jnp.zeros(dkv_acc.shape, F32)

            def step(i, carry):
                rows = block(m * seg + i * QT, QT)
                first = cx * seg + i * QT
                q_tile, do_tile = q3[rows, cut], do3[block(i * QT, QT), cut]
                keys = kv[m, :, cut]
                values, allowed = masked_scores(q_tile, keys, band, scores, h, first, length)
                soft = jnp.where(allowed, jnp.exp(values - lse[rows, h : h + 1]), 0.0)
                soft_grad = mm_nt(do_tile, keys)
                delta = jnp.sum(soft * soft_grad, axis=-1, keepdims=True)
                score_grad = (soft * (soft_grad - delta)).astype(BF)
                dkv_acc[...] += mm_tn(soft.astype(BF), do_tile) + 0.125 * mm_tn(score_grad, q_tile)
                part = mm(score_grad, keys) * 0.125
                grads[rows, head_lanes(h, span)] = jnp.where(
                    low_lanes(part.shape), part, 0.0
                ).astype(BF)
                spread[:, BAND:] = score_grad.astype(F32)
                for half in range(QT // BAND):
                    lanes = block(first + half * BAND, 2 * BAND)
                    band_sum[h] += spread[half * BAND : (half + 1) * BAND, lanes]
                whole_sum[h : h + 1, :] += jnp.sum(spread[:, BAND:], axis=0, keepdims=True)
                return carry

            lax.fori_loop(0, seg // QT, step, 0)

            @pl.when(cx == 1)
            def _():
                dkv[m, h] = dkv_acc[0:seg, :].astype(BF)
                dkv_copy(m, h).start()

            grads[pl.ds(m * seg, seg), cut] = dkv_acc[block(cx * seg, seg), :].astype(BF)
            pump_late() if h == 1 else None

    def after_attend(m):
        rows = pl.ds(m * seg, seg)

        @pl.when(cx == 0)
        def _():
            for h in range(heads):
                dkv_copy(m, h).wait_recv()
                total = grads[rows, head_lanes(h)].astype(F32) + dkv[m, h].astype(F32)
                grads[rows, head_lanes(h)] = total.astype(BF)

        def lower(i, carry):
            spot = block(m * seg + i * 256, 256)
            npart[spot, :] = mm_nt(grads[spot, :], ws[...]).astype(BF)
            return carry

        lax.fori_loop(0, seg // 256, lower, 0)
        sums.c_copy(m, 2, npart).start()

    def gs_spot(slab, half):
        return ws_full.at[slab, pl.ds(0, shard), pl.ds(half * span, span)]

    def sx_copy(half, k):
        slab = lax.rem(dp + k, 4) * 2 + 1 - cx
        return remote(
            gs_spot(slab, half), sx.at[half, k], sx_s.at[half, k], sx_r.at[half, k], place.partner
        )

    def sz_copy(half, k):
        return remote(
            sx.at[half, k], sz.at[half, k - 1], sz_s.at[half, k - 1], sz_r.at[half, k - 1],
            place.z_peers[k - 1],
        )

    order = (2, 1, 3, 0)

    def small_part(half):
        def step(i, carry):
            lanes = block(i * 384, 384)
            cols = slice(half * span, (half + 1) * span)
            part = mm_tn(ffn[0, :, lanes], grads[0:seg, cols])
            part = part + mm_tn(ffn[1, :, lanes], grads[seg:, cols])
            if half == 1:
                part = part + mm_tn(bgrad[:, lanes], ab3[...])
            ws_full[pl.ds(i * 4, 4), 0:shard, cols] = part.astype(BF).reshape(4, shard, -1)
            return carry

        lax.fori_loop(0, width // 384, step, 0)
        for k in order:
            sx_copy(half, k).start()

    def small_step(half):
        cols = slice(half * span, (half + 1) * span)
        for k in order:
            sx_copy(half, k).wait_recv()
            slab = lax.rem(dp + k, 4) * 2 + cx
            total = ws_full[slab, 0:shard, cols].astype(F32) + sx[half, k].astype(F32)
            if k == 0:
                small_grad[:, cols] = total
            else:
                sx[half, k] = total.astype(BF)
                sz_copy(half, k).start()

    for m in range(2):
        sums.shared(m, 0, bgrad)
        attend_back(m)
        if m == 0:
            for i in range(2):

                def own_result(i):
                    rows = sums.own_rows(i)
                    expert_sum = sums.total(i, 0)
                    spot = lax.broadcasted_iota(jnp.int32, (seg // 4, 1), 0) + (cx * seg + own_first)
                    live = (spot < len_ref[i]).astype(F32)
                    gate = jnp.sum(probs_ref[rows, :] * chosen_of(rows), axis=-1, keepdims=True)
                    own_out[i, 0] = (live * (hidden[i] + gate * expert_sum)).astype(BF)
                    own_copy(i, 1, result).start()
                    sums.share(i, 1, result, own_out.at[i, 0])

                own_result(i)

    def normed_again(i, carry):
        ffn[lax.div(i, 2), block(lax.rem(i, 2) * 256, 256), :] = first_norm(block(i * 256, 256))
        return carry

    lax.fori_loop(0, 2 * seg // 256, normed_again, 0)
    for k in range(4):
        gx_copy(k, cx).wait_send()
    small_part(1)
    sums.c_copy(0, 1, npart).wait_send()
    sums.y_copy(0, 1).wait_send()
    after_attend(0)
    sums.c_copy(1, 1, npart).wait_send()
    sums.y_copy(1, 1).wait_send()
    sums.to_quarters(0, 2, npart)
    after_attend(1)
    small_part(0)
    sums.to_quarters(1, 2, npart)
    pump_late(len(late))

    for m in range(2):
        down = sums.total(m, 2)
        rows = sums.own_rows(m)
        through, gain_terms = norm_back(tok[rows, :].astype(F32), gains[0:1, :], down)
        own_out[m, 1] = (through + hgrad[m]).astype(BF)
        sums.share(m, 2, input_grad, own_out.at[m, 1])
        own_copy(m, 2, input_grad).start()
        tiny_own[0:1, :] += jnp.sum(gain_terms, axis=0, keepdims=True)

    def tt_copy(k):
        return remote(
            tiny_own, tiny_t.at[k - 1], tt_s.at[k - 1], tt_r.at[k - 1], place.tensor_peers[k - 1]
        )

    for k in (1, 2, 3):
        tt_copy(k).start()
    small_step(1)
    small_step(0)
    for k in (1, 2, 3):
        tt_copy(k).wait_recv()
    tiny_x[0] = tiny_own[...] + tiny_t[0] + tiny_t[1] + tiny_t[2]
    tx_copy = remote(tiny_x.at[0], tiny_x.at[1], tx_s.at[0], tx_r.at[0], place.partner)
    tx_copy.start()
    bucket_sums(heads, band_sum, whole_sum, dbias_own)
    bx_copy = remote(dbias_own, dbias_x, bx_s.at[0], bx_r.at[0], place.partner)
    bx_copy.start()
    for m in range(2):
        sums.pass_on(m, 1, result)
        sums.pass_on(m, 2, input_grad)
    tx_copy.wait_recv()
    tiny_x[2] = tiny_x[0] + tiny_x[1]
    bx_copy.wait_recv()
    dbias_sum = dbias_own[...] + dbias_x[...]
    dbias_out[...] = dbias_sum

    def tz_copy(k):
        return remote(
            tiny_x.at[2], tiny_z.at[k - 1], tz_s.at[k - 1], tz_r.at[k - 1], place.z_peers[k - 1]
        )

    def bz_copy(k):
        return remote(
            dbias_out, dbias_z.at[k - 1], bz_s.at[k - 1], bz_r.at[k - 1], place.z_peers[k - 1]
        )

    for k in (1, 2, 3):
        tz_copy(k).start()
        bz_copy(k).start()
    for e in range(experts):
        reduce_end(e)
    for half in range(2):
        cols = slice(half * span, (half + 1) * span)
        total = small_grad[:, cols]
        for k in (1, 2, 3):
            sz_copy(half, k).wait_recv()
            total = total + sz[half, k - 1].astype(F32)
        small_grad[:, cols] = total
    for k in (1, 2, 3):
        bz_copy(k).wait_recv()
        bz_copy(k).wait_send()
        dbias_sum = dbias_sum + dbias_z[k - 1]
    dbias_out[...] = dbias_sum
    total = tiny_x[2]
    for k in (1, 2, 3):
        tz_copy(k).wait_recv()
        total = total + tiny_z[k - 1]
    tiny_out[...] = total
    for m in range(2):
        sums.shared(m, 1, result)
        sums.shared(m, 2, input_grad)

    for e in range(experts):
        for d in range(2):
            for s in (1, 2, 3, 4):
                gather(d, e, s, True).wait_send()
                reduce_copy(d, e, s).wait_send()
    for k in range(4):
        for half in range(2):
            sx_copy(half, k).wait_send()
            if k > 0:
                sz_copy(half, k).wait_send()
        if k > 0:
            gz_copy(k, small_slab(0, cx)).wait_send()
            gg_copy(k).wait_send()
            tt_copy(k).wait_send()
            tz_copy(k).wait_send()
    tx_copy.wait_send()
    bx_copy.wait_send()
    for m in range(2):
        sums.c_copy(m, 0, epart).wait_send()
        sums.c_copy(m, 2, npart).wait_send()
        own_copy(m, 1, result).wait()
        own_copy(m, 2, input_grad).wait()
        sums.y_copy(m, 0).wait_send()
        sums.y_copy(m, 2).wait_send()
        for j in range(4):
            for step in range(3):
                own = own_out.at[m, j - 1] if j in (1, 2) else None
                ref = (bgrad, result, input_grad, ntwo)[j]
                sums.a_copy(m, j, ref, step, own).wait_send()

        @pl.when(cx == 0)
        def _():
            k_copy(m).wait_send()

        @pl.when(cx == 1)
        def _():
            for h in range(heads):
                dkv_copy(m, h).wait_send()


def layer_call(lengths, bias, ids, slot_lanes, slot_subs, tok, cot, wsmall, w):
    heads = bias.shape[1]
    rows, width = tok.shape
    span = heads * 128
    experts, ff = w.shape[0], w.shape[3]
    seg = rows // 2
    quarter = seg // 4
    shard = width // 8
    slots = 2 * slot_subs.shape[0]
    vm = pl.BlockSpec(memory_space=pltpu.VMEM)
    sm = pl.BlockSpec(memory_space=pltpu.SMEM)
    hbm = pl.BlockSpec(memory_space=pl.ANY)
    dma = pltpu.SemaphoreType.DMA
    sds = jax.ShapeDtypeStruct
    low, full = (lambda *shape: pltpu.VMEM(shape, BF)), (lambda *shape: pltpu.VMEM(shape, F32))

    def pair(*shape):
        return [dma(shape), dma(shape)]

    return pl.pallas_call(
        functools.partial(layer_kernel, heads),
        out_shape=(
            sds((rows, width), BF),
            sds((rows, width), BF),
            sds((experts, 2, shard, ff), F32),
            sds((shard, width), F32),
            sds((8, width), F32),
            sds((BUCKETS, 128), F32),
            sds((experts, 2, 8, shard, ff), BF),
        ),
        in_specs=[sm, sm] + [vm] * 5 + [hbm] * 2,
        out_specs=(hbm,) * 2 + (vm,) * 4 + (hbm,),
        scratch_shapes=[
            low(8, *wsmall.shape),
            low(width, width),
            full(16, width),
            full(2, quarter, width),
            low(rows, width),
            low(rows, span),
            low(2, rows, span),
            full(rows, 128),
            low(rows, span),
            low(4, 8, shard, ff),
            low(experts, 2, 8, shard, ff),
            low(2, experts, shard, ff),
            low(2, experts, 2, shard, ff),
            low(2, 2, 2, 2, shard, ff),
            low(2, 4, shard, span),
            low(2, 3, shard, span),
            low(rows, width),
            low(rows, width),
            low(rows, width),
            low(4, slots, width),
            full(rows, 16),
            low(2, 2, 2 * quarter, width),
            low(2, 2, quarter, width),
            low(2, 2, quarter, width),
            full(2, 2, quarter, width),
            full(2, quarter, width),
            low(rows, width),
            low(2, 2, quarter, width),
            low(seg, span),
            low(rows, 2 * span),
            full(rows, 128),
            low(2, heads, seg, 128),
            full(heads, BAND, 2 * BAND),
            full(QT, rows + BAND),
            full(QT, rows + BAND),
            full(heads, BAND, 2 * BAND),
            full(8, rows),
            full(2, 8, seg),
            full(3, 2, 8, seg),
            full(2, 8, seg),
            full(8, width),
            full(3, 8, width),
            full(3, 8, width),
            full(3, 8, width),
            full(BUCKETS, 128),
            full(BUCKETS, 128),
            full(3, BUCKETS, 128),
            dma((2,)),
            dma((4,)),
            dma((experts + 1,)),
            pltpu.SemaphoreType.REGULAR,
        ]
        + pair(3)
        + pair(4)
        + pair(2)
        + pair(2, experts, 4)
        + pair(2, experts, 4)
        + pair(2, 4)
        + pair(2, 4)
        + pair(2, 4, 3)
        + pair(2, heads)
        + pair(3)
        + pair(2, 4)
        + pair(2, 3)
        + pair(3)
        + pair(1)
        + pair(3)
        + pair(1)
        + pair(3),
        compiler_params=pltpu.CompilerParams(
            collective_id=0, has_side_effects=True, vmem_limit_bytes=63 << 20
        ),
    )(lengths, bias, ids, slot_lanes, slot_subs, tok, cot, wsmall, w)


def body_fast(
    inputs, lengths, expert_ids, slot_rows, attn_gain, qkv_weight, out_weight, position_bias,
    ffn_gain, router_weight, up_weight, down_weight, cotangent,
):
    micro, seg, width = inputs.shape
    rows = micro * seg
    experts = up_weight.shape[0]
    heads = position_bias.shape[1]
    size = qkv_weight.shape[2] // heads
    slab = lax.axis_index("dp") * 2 + lax.axis_index("ctx")
    shard = attn_gain.shape[0]
    by_head = jnp.concatenate(
        [
            qkv_weight[1].reshape(shard, heads, 1, size),
            qkv_weight[2].reshape(shard, heads, 1, size),
        ],
        axis=2,
    ).reshape(shard, -1)
    by_query = jnp.concatenate(
        [
            qkv_weight[0].reshape(shard, heads, 1, size),
            out_weight.T.reshape(shard, heads, 1, size),
        ],
        axis=2,
    ).reshape(shard, -1)
    small = jnp.concatenate(
        [attn_gain[None], ffn_gain[None], router_weight.T, jnp.zeros((10, shard), BF)], axis=0
    )
    small = lax.dynamic_update_slice(jnp.zeros((16, width), BF), small, (0, slab * shard))
    wsmall = jnp.concatenate([jnp.concatenate([by_head, by_query], axis=1), small], axis=0)
    w = jnp.stack([up_weight, jnp.transpose(down_weight, (0, 2, 1))], axis=1)
    tok = inputs.reshape(rows, width)
    slots = slot_rows[:, 0].reshape(micro * experts, -1)
    result, input_part, w_grad, small_grad, tiny, dbias, _ = layer_call(
        lengths, position_bias, expert_ids.reshape(rows, 1), slots, slots.T, tok,
        cotangent.reshape(rows, width), wsmall, w,
    )
    tiny = lax.dynamic_slice_in_dim(tiny, slab * shard, shard, axis=1)
    parts = small_grad.reshape(shard, 2, heads, 2, size)
    qkv_grad = jnp.stack(
        [parts[:, 1, :, 0], parts[:, 0, :, 0], parts[:, 0, :, 1]], axis=0
    ).reshape(3, shard, heads * size)
    return (
        result.reshape(inputs.shape),
        input_part.reshape(inputs.shape),
        tiny[0],
        qkv_grad,
        parts[:, 1, :, 1].reshape(shard, heads * size).T,
        dbias[:, :heads],
        tiny[1],
        tiny[2 : 2 + experts].T,
        w_grad[:, 0],
        jnp.transpose(w_grad[:, 1], (0, 2, 1)),
    )


def rms_norm(values, gain_vector):
    return (
        values * lax.rsqrt(jnp.mean(values * values, axis=-1, keepdims=True) + 1e-06) * gain_vector
    )


def bucket_of(distance):
    clipped = jnp.maximum(distance, 0)
    edge_values = jnp.asarray(bucket_edges, dtype=jnp.int32)
    beyond = jnp.sum((clipped[..., None] >= edge_values).astype(jnp.int32), axis=-1)
    return jnp.where(clipped < 16, clipped, jnp.minimum(16 + beyond, 31))


def toeplitz(diagonal, query_count, key_count):
    head_count = diagonal.shape[0]
    padded = jnp.pad(diagonal, ((0, 0), (0, 1)))
    row_width = query_count + key_count
    repeated = jnp.broadcast_to(padded[:, None, :], (head_count, query_count, row_width)).reshape(
        head_count, query_count * row_width
    )
    repeated = jnp.pad(repeated, ((0, 0), (0, query_count))).reshape(
        head_count, query_count, row_width + 1
    )[:, :, :key_count]
    return repeated[:, :, ::-1]


def diagonal_sums(gradient):
    head_count, query_count, key_count = gradient.shape
    offset_count = query_count + key_count - 1
    flipped = jnp.pad(gradient[:, :, ::-1], ((0, 0), (0, 0), (0, query_count)))
    skewed = flipped.reshape(head_count, query_count * (offset_count + 1))[
        :, : query_count * offset_count
    ]
    return jnp.sum(skewed.reshape(head_count, query_count, offset_count), axis=1)


def bucket_table(query_first, query_count, key_count):
    offsets = (
        query_first - (key_count - 1) + jnp.arange(query_count + key_count - 1, dtype=jnp.int32)
    )
    return (bucket_of(offsets)[:, None] == jnp.arange(BUCKETS, dtype=jnp.int32)[None, :]).astype(
        jnp.float32
    )


def body(
    inputs,
    lengths,
    expert_ids,
    slot_rows,
    attn_gain,
    qkv_weight,
    out_weight,
    position_bias,
    ffn_gain,
    router_weight,
    up_weight,
    down_weight,
    cotangent,
):
    highest = lax.Precision.HIGHEST
    micro_count, seg_rows, model_width = inputs.shape
    local_heads = position_bias.shape[1]
    head_size = qkv_weight.shape[2] // local_heads
    expert_count = up_weight.shape[0]
    query_first = lax.axis_index("ctx") * seg_rows
    query_pos = query_first + jnp.arange(seg_rows, dtype=jnp.int32)

    def pair_scores(query_heads, query_start, key_heads, length):
        query_count = query_heads.shape[0]
        key_count = key_heads.shape[0]
        scores = (
            jnp.einsum("qhd,khd->hqk", query_heads, key_heads, preferred_element_type=jnp.float32)
            * 0.125
        )
        diagonal = jnp.einsum(
            "rb,bh->hr",
            bucket_table(query_start, query_count, key_count),
            position_bias,
            precision=highest,
        )
        scores = scores + toeplitz(diagonal, query_count, key_count)
        query_place = query_start + jnp.arange(query_count, dtype=jnp.int32)
        key_place = jnp.arange(key_count, dtype=jnp.int32)
        allowed = (key_place[None, :] <= query_place[:, None]) & (key_place[None, :] < length)
        return (scores, allowed)

    def scores_for(query_heads, key_block, length):
        key_count = key_block.shape[0]
        key_heads = key_block.reshape(key_count, local_heads, head_size)
        scores, allowed = pair_scores(query_heads, query_first, key_heads, length)
        return (scores, allowed, key_heads)

    results = []
    input_parts = []
    grad_sums = None
    bias_total = jnp.zeros((local_heads, BUCKETS), jnp.float32)
    for micro_step in range(micro_count):
        forward_gain_one = lax.all_gather(attn_gain, ("dp", "ctx"), axis=0, tiled=True)
        forward_qkv_full = lax.all_gather(qkv_weight, ("dp", "ctx"), axis=1, tiled=True)
        forward_out_full = lax.all_gather(out_weight, ("dp", "ctx"), axis=1, tiled=True)
        forward_gain_two = lax.all_gather(ffn_gain, ("dp", "ctx"), axis=0, tiled=True)
        forward_router_full = lax.all_gather(router_weight, ("dp", "ctx"), axis=0, tiled=True)
        forward_up_full = lax.all_gather(up_weight, ("dp", "ctx"), axis=1, tiled=True)
        forward_down_full = lax.all_gather(down_weight, ("dp", "ctx"), axis=2, tiled=True)
        forward_tokens = inputs[micro_step].astype(jnp.float32)
        forward_length = lengths[micro_step]
        forward_normed = rms_norm(forward_tokens, forward_gain_one.astype(jnp.float32)).astype(
            jnp.bfloat16
        )
        forward_projected = jnp.einsum(
            "td,cde->cte", forward_normed, forward_qkv_full, preferred_element_type=jnp.float32
        ).astype(jnp.bfloat16)
        forward_query_heads = forward_projected[0].reshape(seg_rows, local_heads, head_size)
        row_top = jnp.full((local_heads, seg_rows), -1e30, jnp.float32)
        attend_scores, attend_allowed, attend_key_heads = scores_for(
            forward_query_heads,
            lax.all_gather(forward_projected[1], "ctx", axis=0, tiled=True),
            forward_length,
        )
        value_heads = lax.all_gather(forward_projected[2], "ctx", axis=0, tiled=True).reshape(
            attend_key_heads.shape
        )
        attend_scores = jnp.where(attend_allowed[None], attend_scores, -1e30)
        new_top = jnp.maximum(row_top, jnp.max(attend_scores, axis=-1))
        weights_exp = jnp.where(
            attend_allowed[None], jnp.exp(attend_scores - new_top[:, :, None]), 0.0
        )
        row_total = jnp.sum(weights_exp, axis=-1)
        summed = jnp.einsum(
            "hqk,khd->hqd",
            weights_exp.astype(jnp.bfloat16),
            value_heads,
            preferred_element_type=jnp.float32,
        )
        row_top, row_total, summed = (new_top, row_total, summed)
        forward_attended = summed / row_total[:, :, None]
        forward_log_total = row_top + jnp.log(row_total)
        forward_attended_low = (
            jnp.transpose(forward_attended, (1, 0, 2)).reshape(seg_rows, -1).astype(jnp.bfloat16)
        )
        branch = lax.psum(
            jnp.dot(
                forward_attended_low, forward_out_full, preferred_element_type=jnp.float32
            ).astype(jnp.bfloat16),
            "tensor",
        ).astype(jnp.float32)
        forward_hidden = forward_tokens + branch
        forward_normed_two = rms_norm(forward_hidden, forward_gain_two.astype(jnp.float32)).astype(
            jnp.bfloat16
        )
        logits = jnp.dot(
            forward_normed_two, forward_router_full, preferred_element_type=jnp.float32
        )
        forward_router_probs = jax.nn.softmax(logits, axis=-1)
        forward_chosen = (
            expert_ids[micro_step][:, None] == jnp.arange(expert_count, dtype=jnp.int32)[None, :]
        ).astype(jnp.float32)
        forward_gate_value = jnp.sum(forward_router_probs * forward_chosen, axis=-1)
        forward_slot_table = slot_rows[micro_step, 0]
        padded = jnp.concatenate(
            [forward_normed_two, jnp.zeros((1, model_width), jnp.bfloat16)], axis=0
        )
        forward_picked = padded[forward_slot_table]
        forward_raised = jnp.einsum(
            "ekd,edf->ekf", forward_picked, forward_up_full, preferred_element_type=jnp.float32
        )
        forward_activated = jax.nn.gelu(forward_raised).astype(jnp.bfloat16)
        lowered = jnp.einsum(
            "ekf,efd->ekd", forward_activated, forward_down_full, preferred_element_type=jnp.float32
        )
        spread = (
            jnp.zeros((seg_rows + 1, model_width), jnp.float32)
            .at[forward_slot_table.reshape(-1)]
            .add(lowered.reshape(-1, model_width))[:seg_rows]
        )
        forward_expert_sum = lax.psum(spread.astype(jnp.bfloat16), "tensor").astype(jnp.float32)
        forward_live_rows = (query_pos < forward_length).astype(jnp.float32)[:, None]
        result = (
            forward_live_rows * (forward_hidden + forward_gate_value[:, None] * forward_expert_sum)
        ).astype(jnp.bfloat16)
        forward_kept_state = (
            forward_tokens,
            forward_length,
            forward_normed,
            forward_projected,
            forward_attended,
            forward_log_total,
            forward_attended_low,
            forward_hidden,
            forward_normed_two,
            forward_router_probs,
            forward_chosen,
            forward_gate_value,
            forward_slot_table,
            forward_picked,
            forward_raised,
            forward_activated,
            forward_expert_sum,
            forward_live_rows,
        )
        result, kept_state = (result, forward_kept_state)
        gain_one = lax.all_gather(attn_gain, ("dp", "ctx"), axis=0, tiled=True)
        qkv_full = lax.all_gather(qkv_weight, ("dp", "ctx"), axis=1, tiled=True)
        out_full = lax.all_gather(out_weight, ("dp", "ctx"), axis=1, tiled=True)
        gain_two = lax.all_gather(ffn_gain, ("dp", "ctx"), axis=0, tiled=True)
        router_full = lax.all_gather(router_weight, ("dp", "ctx"), axis=0, tiled=True)
        up_full = lax.all_gather(up_weight, ("dp", "ctx"), axis=1, tiled=True)
        down_full = lax.all_gather(down_weight, ("dp", "ctx"), axis=2, tiled=True)
        (
            tokens,
            backward_length,
            normed,
            projected,
            attended,
            log_total,
            attended_low,
            hidden,
            normed_two,
            router_probs,
            chosen,
            gate_value,
            slot_table,
            picked,
            raised,
            activated,
            expert_sum,
            live_rows,
        ) = kept_state
        upstream = live_rows * cotangent[micro_step].astype(jnp.float32)
        sum_grad = (gate_value[:, None] * upstream).astype(jnp.bfloat16)
        gate_grad = jnp.sum(expert_sum * upstream, axis=-1)
        logit_grad = (router_probs * gate_grad[:, None] * (chosen - gate_value[:, None])).astype(
            jnp.bfloat16
        )
        router_part = jnp.einsum(
            "td,te->de", normed_two, logit_grad, preferred_element_type=jnp.float32
        )
        padded_grad = jnp.concatenate([sum_grad, jnp.zeros((1, model_width), jnp.bfloat16)], axis=0)
        slot_grad = padded_grad[slot_table]
        down_part = jnp.einsum(
            "ekf,ekd->efd", activated, slot_grad, preferred_element_type=jnp.float32
        )
        act_grad = jnp.einsum(
            "ekd,efd->ekf", slot_grad, down_full, preferred_element_type=jnp.float32
        )
        unused_value, gelu_back = jax.vjp(jax.nn.gelu, raised)
        raised_grad = gelu_back(act_grad)[0].astype(jnp.bfloat16)
        up_part = jnp.einsum(
            "ekd,ekf->edf", picked, raised_grad, preferred_element_type=jnp.float32
        )
        picked_grad = jnp.einsum(
            "ekf,edf->ekd", raised_grad, up_full, preferred_element_type=jnp.float32
        )
        spread_grad = (
            jnp.zeros((seg_rows + 1, model_width), jnp.float32)
            .at[slot_table.reshape(-1)]
            .add(picked_grad.reshape(-1, model_width))[:seg_rows]
        )
        normed_two_grad = lax.psum(spread_grad.astype(jnp.bfloat16), "tensor").astype(
            jnp.float32
        ) + jnp.einsum("te,de->td", logit_grad, router_full, preferred_element_type=jnp.float32)
        unused_norm, second_back = jax.vjp(rms_norm, hidden, gain_two.astype(jnp.float32))
        hidden_grad, gain_two_part = second_back(normed_two_grad)
        hidden_grad = hidden_grad + upstream
        branch_grad = hidden_grad.astype(jnp.bfloat16)
        out_part = jnp.einsum(
            "te,td->ed", attended_low, branch_grad, preferred_element_type=jnp.float32
        )
        attended_grad = jnp.einsum(
            "td,ed->te", branch_grad, out_full, preferred_element_type=jnp.float32
        ).astype(jnp.bfloat16)
        grad_heads = attended_grad.reshape(seg_rows, local_heads, head_size)
        row_delta = jnp.sum(
            jnp.transpose(grad_heads.astype(jnp.float32), (1, 0, 2)) * attended, axis=-1
        )
        backward_query_heads = projected[0].reshape(seg_rows, local_heads, head_size)
        bias_zero = jnp.zeros((local_heads, BUCKETS), jnp.float32)
        attend_bias_acc = bias_zero
        bias_acc = attend_bias_acc
        score_scores, score_allowed, score_key_heads = scores_for(
            backward_query_heads,
            lax.all_gather(projected[1], "ctx", axis=0, tiled=True),
            backward_length,
        )
        score_value_heads = lax.all_gather(projected[2], "ctx", axis=0, tiled=True).reshape(
            score_key_heads.shape
        )
        score_key_count = score_key_heads.shape[0]
        soft_weights = jnp.where(
            score_allowed[None], jnp.exp(score_scores - log_total[:, :, None]), 0.0
        )
        weight_grad = jnp.einsum(
            "qhd,khd->hqk", grad_heads, score_value_heads, preferred_element_type=jnp.float32
        )
        score_grad = (soft_weights * (weight_grad - row_delta[:, :, None])).astype(jnp.bfloat16)
        query_acc = jnp.einsum(
            "hqk,khd->qhd", score_grad, score_key_heads, preferred_element_type=jnp.float32
        )
        bias_acc = bias_acc + jnp.dot(
            diagonal_sums(score_grad.astype(jnp.float32)),
            bucket_table(query_first, seg_rows, score_key_count),
            precision=highest,
        )
        (
            (attend_query_acc, attend_bias_acc),
            attend_soft_weights,
            attend_score_grad,
            attend_key_count,
        ) = ((query_acc, bias_acc), soft_weights, score_grad, score_key_count)
        key_term = (
            jnp.einsum(
                "hqk,qhd->khd",
                attend_score_grad,
                backward_query_heads,
                preferred_element_type=jnp.float32,
            )
            * 0.125
        )
        value_term = jnp.einsum(
            "hqk,qhd->khd",
            attend_soft_weights.astype(jnp.bfloat16),
            grad_heads,
            preferred_element_type=jnp.float32,
        )
        grad_term = jnp.stack(
            [key_term.reshape(attend_key_count, -1), value_term.reshape(attend_key_count, -1)],
            axis=1,
        )
        key_value_acc = grad_term
        query_acc, key_value_acc, bias_part = (attend_query_acc, key_value_acc, attend_bias_acc)
        own_grads = lax.psum_scatter(
            key_value_acc.astype(jnp.bfloat16), "ctx", scatter_dimension=0, tiled=True
        ).astype(jnp.float32)
        query_grad = (query_acc * 0.125).reshape(seg_rows, -1).astype(jnp.bfloat16)
        qkv_grad = jnp.stack(
            [
                query_grad,
                own_grads[:, 0].astype(jnp.bfloat16),
                own_grads[:, 1].astype(jnp.bfloat16),
            ],
            axis=0,
        )
        qkv_part = jnp.einsum("td,cte->cde", normed, qkv_grad, preferred_element_type=jnp.float32)
        normed_grad = lax.psum(
            jnp.einsum(
                "cte,cde->td", qkv_grad, qkv_full, preferred_element_type=jnp.float32
            ).astype(jnp.bfloat16),
            "tensor",
        ).astype(jnp.float32)
        unused_first, first_back = jax.vjp(rms_norm, tokens, gain_one.astype(jnp.float32))
        token_grad, gain_one_part = first_back(normed_grad)
        input_part = (token_grad + hidden_grad).astype(jnp.bfloat16)
        weight_parts = (
            gain_one_part,
            qkv_part,
            out_part,
            gain_two_part,
            router_part,
            up_part,
            down_part,
        )
        input_part, weight_parts, bias_part = (input_part, weight_parts, bias_part)
        results.append(result)
        input_parts.append(input_part)
        grad_sums = (
            weight_parts
            if grad_sums is None
            else tuple((old_sum + new_part for old_sum, new_part in zip(grad_sums, weight_parts)))
        )
        bias_total = bias_total + bias_part
    reduced = (
        lax.psum_scatter(grad_sums[0], ("dp", "ctx"), scatter_dimension=0, tiled=True),
        lax.psum_scatter(grad_sums[1], ("dp", "ctx"), scatter_dimension=1, tiled=True),
        lax.psum_scatter(grad_sums[2], ("dp", "ctx"), scatter_dimension=1, tiled=True),
        lax.psum_scatter(grad_sums[3], ("dp", "ctx"), scatter_dimension=0, tiled=True),
        lax.psum_scatter(grad_sums[4], ("dp", "ctx"), scatter_dimension=0, tiled=True),
        lax.psum_scatter(grad_sums[5], ("dp", "ctx"), scatter_dimension=1, tiled=True),
        lax.psum_scatter(grad_sums[6], ("dp", "ctx"), scatter_dimension=2, tiled=True),
    )
    bias_grad_total = lax.psum(bias_total, ("dp", "ctx"))
    return (
        jnp.stack(results, axis=0),
        jnp.stack(input_parts, axis=0),
        reduced[0],
        reduced[1],
        reduced[2],
        jnp.transpose(bias_grad_total),
        reduced[3],
        reduced[4],
        reduced[5],
        reduced[6],
    )


def solution(mesh):
    small = mesh.shape["ctx"] == 2 and mesh.shape["dp"] == 4 and mesh.shape["tensor"] == 4
    return jax.shard_map(
        body_fast if small else body,
        mesh=mesh,
        in_specs=(
            P("dp", "ctx", None),
            P("dp"),
            P("dp", "ctx"),
            P("dp", "ctx", None, None),
            P(("dp", "ctx")),
            P(None, ("dp", "ctx"), "tensor"),
            P("tensor", ("dp", "ctx")),
            P(None, "tensor"),
            P(("dp", "ctx")),
            P(("dp", "ctx"), None),
            P(None, ("dp", "ctx"), "tensor"),
            P(None, "tensor", ("dp", "ctx")),
            P("dp", "ctx", None),
        ),
        out_specs=(
            P("dp", "ctx", None),
            P("dp", "ctx", None),
            P(("dp", "ctx")),
            P(None, ("dp", "ctx"), "tensor"),
            P("tensor", ("dp", "ctx")),
            P(None, "tensor"),
            P(("dp", "ctx")),
            P(("dp", "ctx"), None),
            P(None, ("dp", "ctx"), "tensor"),
            P(None, "tensor", ("dp", "ctx")),
        ),
        check_vma=False,
    )
```

```python
import functools

import jax
import jax.numpy as jnp
import numpy as np
from jax import lax
from jax.experimental import pallas as pl
from jax.experimental.pallas import tpu as pltpu
from jax.sharding import PartitionSpec as P

BUCKETS = 32
MESH = pl.DeviceIdType.MESH
BF = jnp.bfloat16
F32 = jnp.float32


bucket_edges = np.ceil(16.0 * 8.0 ** (np.arange(1, 16) / 16.0)).astype(np.int32)
bucket_starts = [int(n) for n in range(17)] + [int(n) for n in bucket_edges]


QT = 256
BAND = 128
C0 = float(np.sqrt(2.0 / np.pi))
C1 = 0.044715


def mm(a, b):
    return jnp.dot(a, b, preferred_element_type=F32)


def mm_nt(a, b):
    return lax.dot_general(a, b, (((1,), (1,)), ((), ())), preferred_element_type=F32)


def mm_tn(a, b):
    return lax.dot_general(a, b, (((0,), (0,)), ((), ())), preferred_element_type=F32)


def remote(src, dst, send, recv, device):
    return pltpu.make_async_remote_copy(
        src_ref=src,
        dst_ref=dst,
        send_sem=send,
        recv_sem=recv,
        device_id=device,
        device_id_type=MESH,
    )


def block(start, size, whole=128):
    return pl.ds(pl.multiple_of(start, whole), size)


class Place:
    def __init__(self):
        dp, cx, t = lax.axis_index("dp"), lax.axis_index("ctx"), lax.axis_index("tensor")
        self.dp, self.cx, self.t = dp, cx, t
        self.yy, self.core = lax.div(t, 2), lax.rem(t, 2)
        self.partner = (dp, 1 - cx, t)
        self.sibling = (dp, cx, t + 1 - 2 * self.core)
        self.across = (dp, cx, lax.rem(t + 2, 4))
        self.tensor_peers = [(dp, cx, lax.rem(t + k, 4)) for k in (1, 2, 3)]
        self.z_peers = [(lax.rem(dp + k, 4), cx, t) for k in (1, 2, 3)]
        self.spot = dp + cx * (7 - 2 * dp)
        self.right = self.at_spot(1)
        self.left = self.at_spot(-1)

    def at_spot(self, away):
        spot = lax.rem(self.spot + 8 + away, 8)
        cx = lax.div(spot, 4)
        return (spot + cx * (7 - 2 * spot), cx, self.t)

    def slab(self, away):
        dp, cx, _ = self.at_spot(away)
        return dp * 2 + cx

    def greet(self):
        barrier = pltpu.get_barrier_semaphore()
        peers = self.z_peers + [self.partner] + self.tensor_peers
        for peer in peers:
            pl.semaphore_signal(barrier, inc=1, device_id=peer, device_id_type=MESH)
        pl.semaphore_wait(barrier, len(peers))


class Ring:
    def __init__(self, place, send_sems, recv_sems):
        self.place, self.send_sems, self.recv_sems = place, send_sems, recv_sems

    def copy(self, d, e, s, src, dst):
        at = (d, e, s - 1)
        device = self.place.right if d == 0 else self.place.left
        return remote(src, dst, self.send_sems.at[at], self.recv_sems.at[at], device)


class TensorSum:
    def __init__(self, place, seg, cbuf, ysend, ybuf, kept, c_s, c_r, y_s, y_r, a_s, a_r):
        self.place, self.seg = place, seg
        self.slot = (0, 1, 1, 1)
        self.half, self.quarter = seg // 2, seg // 4
        self.cbuf, self.ysend, self.ybuf, self.kept = cbuf, ysend, ybuf, kept
        self.c_s, self.c_r, self.y_s, self.y_r, self.a_s, self.a_r = c_s, c_r, y_s, y_r, a_s, a_r

    def rows(self, m, c, y):
        return block(m * self.seg + c * self.half + y * self.quarter, self.quarter)

    def own_rows(self, m):
        return self.rows(m, self.place.core, self.place.yy)

    def c_copy(self, m, j, src):
        rows = block(m * self.seg + (1 - self.place.core) * self.half, self.half)
        return remote(
            src.at[rows], self.cbuf.at[m, self.slot[j]], self.c_s.at[m, j], self.c_r.at[m, j],
            self.place.sibling,
        )

    def y_copy(self, m, j):
        return remote(
            self.ysend.at[m, self.slot[j]], self.ybuf.at[m, self.slot[j]], self.y_s.at[m, j], self.y_r.at[m, j],
            self.place.across,
        )

    def to_quarters(self, m, j, src):
        self.c_copy(m, j, src).wait_recv()
        yy, core = self.place.yy, self.place.core
        near, far = block(yy * self.quarter, self.quarter), block((1 - yy) * self.quarter, self.quarter)
        other = src[self.rows(m, core, 1 - yy), :].astype(F32)
        self.ysend[m, self.slot[j]] = (other + self.cbuf[m, self.slot[j], far, :].astype(F32)).astype(BF)
        self.y_copy(m, j).start()
        mine = src[self.rows(m, core, yy), :].astype(F32)
        self.kept[m, self.slot[j]] = mine + self.cbuf[m, self.slot[j], near, :].astype(F32)

    def total(self, m, j):
        self.y_copy(m, j).wait_recv()
        return self.kept[m, self.slot[j]] + self.ybuf[m, self.slot[j]].astype(F32)

    def a_copy(self, m, j, ref, step, own=None):
        yy, core = self.place.yy, self.place.core
        spot = ref.at[self.rows(m, core, 1 - yy if step == 2 else yy)]
        source = spot if own is None or step == 2 else own
        return remote(
            source, spot, self.a_s.at[m, j, step], self.a_r.at[m, j, step],
            self.place.across if step == 0 else self.place.sibling,
        )

    def a_recv(self, m, j, ref, step):
        yy, core = self.place.yy, self.place.core
        spot = ref.at[
            self.rows(m, core if step == 0 else 1 - core, yy if step == 1 else 1 - yy)
        ]
        return remote(
            spot, spot, self.a_s.at[m, j, step], self.a_r.at[m, j, step], self.place.sibling
        )

    def share(self, m, j, ref, own=None):
        self.a_copy(m, j, ref, 0, own).start()
        self.a_copy(m, j, ref, 1, own).start()

    def pass_on(self, m, j, ref):
        self.a_recv(m, j, ref, 0).wait_recv()
        self.a_copy(m, j, ref, 2).start()

    def shared(self, m, j, ref):
        self.a_recv(m, j, ref, 1).wait_recv()
        self.a_recv(m, j, ref, 2).wait_recv()


def low_lanes(shape):
    return lax.rem(lax.broadcasted_iota(jnp.int32, shape, len(shape) - 1), 128) < 64


def head_lanes(h, base=0):
    return slice(base + h * 128, base + (h + 1) * 128)


def fill_bias(bias_ref, band_ref, heads):
    rows = lax.broadcasted_iota(jnp.int32, (BAND, 2 * BAND), 0)
    cols = lax.broadcasted_iota(jnp.int32, (BAND, 2 * BAND), 1)
    away = rows + BAND - cols

    def one_head(h, carry):
        tile = jnp.full((BAND, 2 * BAND), bias_ref[h, 0], F32)
        for b in range(1, BUCKETS):
            tile = jnp.where(away >= bucket_starts[b], bias_ref[h, b], tile)
        band_ref[h] = tile - bias_ref[h, BUCKETS - 1]
        return carry

    lax.fori_loop(0, heads, one_head, 0)


def masked_scores(q_tile, keys, band_ref, scores, h, first, length):
    count = keys.shape[0]
    scores[:, BAND:] = mm_nt(q_tile, keys) * 0.125
    for part in range(QT // BAND):
        spot = (block(part * BAND, BAND), block(first + part * BAND, 2 * BAND))
        scores[spot] = scores[spot] + band_ref[h]
    values = scores[:, BAND:]
    key_pos = lax.broadcasted_iota(jnp.int32, (QT, count), 1)
    query_pos = lax.broadcasted_iota(jnp.int32, (QT, count), 0) + first
    allowed = (key_pos <= query_pos) & (key_pos < length)
    return jnp.where(allowed, values, -1e30), allowed


def bucket_sums(heads, band_sum, whole_sum, dbias):
    rows = lax.broadcasted_iota(jnp.int32, (BAND, 2 * BAND), 0)
    cols = lax.broadcasted_iota(jnp.int32, (BAND, 2 * BAND), 1)
    away = rows + BAND - cols
    bucket = lax.broadcasted_iota(jnp.int32, (BUCKETS, 2 * BAND), 0)
    lanes128 = lax.broadcasted_iota(jnp.int32, (BUCKETS, 128), 1)

    def one_head(h, carry):
        tile = band_sum[h]
        sums = jnp.zeros((BUCKETS, 2 * BAND), F32)
        for b in range(BUCKETS - 1):
            inside = (away >= bucket_starts[b]) & (away < bucket_starts[b + 1])
            row = jnp.sum(jnp.where(inside, tile, 0.0), axis=0, keepdims=True)
            sums = jnp.where(bucket == b, row, sums)
        per_bucket = jnp.sum(sums, axis=1, keepdims=True)
        near = jnp.sum(per_bucket, axis=0, keepdims=True)
        total = jnp.sum(whole_sum[h, 0:1, :], axis=1, keepdims=True)
        last = lax.broadcasted_iota(jnp.int32, (BUCKETS, 1), 0) == BUCKETS - 1
        per_bucket = jnp.where(last, total - near, per_bucket)
        dbias[...] = jnp.where(lanes128 == h, per_bucket, dbias[...])
        return carry

    dbias[...] = jnp.zeros((BUCKETS, 128), F32)
    lax.fori_loop(0, heads, one_head, 0)


def norm_back(x, gain, grad):
    scale = lax.rsqrt(jnp.mean(x * x, axis=-1, keepdims=True) + 1e-06)
    unit = x * scale
    pulled = grad * gain
    inner = jnp.mean(pulled * unit, axis=-1, keepdims=True)
    return scale * (pulled - unit * inner), grad * unit


def layer_kernel(
    heads,
    len_ref,
    bias_ref,
    slot_lanes,
    tok,
    cot,
    wsmall,
    w,
    result,
    input_grad,
    w_grad,
    small_grad,
    tiny_out,
    dbias_out,
    w_full,
    ws_full,
    ws,
    gains,
    hidden,
    ntwo,
    q3,
    kv,
    lse,
    ab3,
    wbuf,
    gw,
    in_one,
    in_two,
    in_late,
    sx,
    sz,
    sum_grad,
    epart,
    npart,
    ffn,
    probs_ref,
    chosen_ref,
    cbuf,
    ysend,
    ybuf,
    kept,
    hgrad,
    bgrad,
    own_out,
    do3,
    grads,
    dkv_acc,
    dkv,
    band,
    scores,
    spread,
    band_sum,
    whole_sum,
    gg_own,
    gg_in,
    gg_sum,
    tiny_own,
    tiny_t,
    tiny_x,
    tiny_z,
    dbias_own,
    dbias_x,
    dbias_z,
    load_sem,
    out_sem,
    local,
    ready,
    gz_s,
    gz_r,
    gx_s,
    gx_r,
    k_s,
    k_r,
    ag_s,
    ag_r,
    rs_s,
    rs_r,
    c_s,
    c_r,
    y_s,
    y_r,
    a_s,
    a_r,
    kv_s,
    kv_r,
    gg_s,
    gg_r,
    sx_s,
    sx_r,
    sz_s,
    sz_r,
    tt_s,
    tt_r,
    tx_s,
    tx_r,
    tz_s,
    tz_r,
    bx_s,
    bx_r,
    bz_s,
    bz_r,
):
    place = Place()
    dp, cx, t = place.dp, place.cx, place.t
    seg = tok.shape[0] // 2
    width = tok.shape[1]
    shard = width // 8
    experts = w.shape[0]
    span = kv.shape[2]
    cap = slot_lanes.shape[2]
    place.greet()
    gather_ring = Ring(place, ag_s, ag_r)
    reduce_ring = Ring(place, rs_s, rs_r)
    sums = TensorSum(place, seg, cbuf, ysend, ybuf, kept, c_s, c_r, y_s, y_r, a_s, a_r)
    bpart = epart

    def small_slab(k, c):
        return lax.rem(dp + 4 - k, 4) * 2 + c

    def gz_copy(k, slab):
        return remote(
            wsmall, ws_full.at[slab], gz_s.at[k - 1], gz_r.at[k - 1], place.z_peers[k - 1]
        )

    def gx_copy(k, c):
        spot = ws_full.at[small_slab(k, c)]
        return remote(wsmall if k == 0 else spot, spot, gx_s.at[k], gx_r.at[k], place.partner)

    small_own = pltpu.make_async_copy(wsmall, ws_full.at[small_slab(0, cx)], local.at[experts])

    def gather(d, e, s, sending):
        away = s - 1 if sending else s
        slab = place.slab(-away if d == 0 else away)
        spot = w_full.at[e, d, slab] if s == 4 else w_full.at[e, :, slab]
        return gather_ring.copy(d, e, s, w.at[e] if sending and s == 1 else spot, spot)

    def w_own(e):
        return pltpu.make_async_copy(w.at[e], w_full.at[e, :, place.slab(0)], local.at[e])

    def gather_step(e, s):
        for d in range(2):
            if s > 1:
                gather(d, e, s - 1, False).wait_recv()
            gather(d, e, s, True).start()

    def landing(d, e, s):
        if s == 1:
            return in_one.at[d, e]
        if s == 2:
            return in_two.at[d, e]
        if e < 2:
            return in_late.at[s - 3, d, e]
        return wbuf.at[e, pl.ds(d * 4 + (s - 3) * 2, 2)]

    def reduce_copy(d, e, s):
        slab = place.slab(5 - s if d == 0 else s - 5)
        src = gw.at[e, d, slab] if s == 1 else gw.at[e, :, slab]
        return reduce_ring.copy(d, e, s, src, landing(d, e, s))

    def reduce_step(e, s):
        for d in range(2):
            if s > 1:
                slab = place.slab(5 - s if d == 0 else s - 5)
                reduce_copy(d, e, s - 1).wait_recv()
                came = landing(d, e, s - 1)

                def add(i, carry):
                    rows = block(i * 16, 16, 16)
                    if s == 2:
                        total = gw[e, d, slab, rows, :].astype(F32) + came[rows, :].astype(F32)
                        gw[e, d, slab, rows, :] = total.astype(BF)
                    else:
                        total = gw[e, :, slab, rows, :].astype(F32) + came[:, rows, :].astype(F32)
                        gw[e, :, slab, rows, :] = total.astype(BF)
                    return carry

                lax.fori_loop(0, shard // 16, add, 0)
            reduce_copy(d, e, s).start()

    def reduce_end(e):
        for d in range(2):
            reduce_copy(d, e, 4).wait_recv()

        def add(i, carry):
            rows = block(i * 16, 16, 16)
            total = gw[e, :, place.slab(0), rows, :].astype(F32)
            for d in range(2):
                total = total + landing(d, e, 4)[:, rows, :].astype(F32)
            w_grad[e, :, rows, :] = total
            return carry

        lax.fori_loop(0, shard // 16, add, 0)

    late = [(3, 2), (2, 3), (3, 3), (2, 4), (3, 4)]

    def pump_late(count=1):
        for _ in range(count):
            if late:
                reduce_step(*late.pop(0))

    small_own.start()
    for k in (1, 3, 2):
        gz_copy(k, small_slab(0, cx)).start()
    gx_copy(0, cx).start()
    for e in range(2):
        gather_step(e, 1)
    for e in range(experts):
        w_own(e).start()

    @pl.when(cx == 0)
    def _():
        for m in range(2):
            kv[m, seg:, :] = jnp.zeros((seg, span), BF)

    fill_bias(bias_ref, band, heads)
    spread[...] = jnp.zeros(spread.shape, F32)
    band_sum[...] = jnp.zeros(band_sum.shape, F32)
    whole_sum[...] = jnp.zeros(whole_sum.shape, F32)
    tiny_own[...] = jnp.zeros(tiny_own.shape, F32)
    for k in (1, 3, 2):
        gz_copy(k, small_slab(k, cx)).wait_recv()
        gx_copy(k, cx).start()
    small_own.wait()
    for k in range(4):
        gx_copy(k, 1 - cx).wait_recv()
    total = ws_full[0, shard:, :].astype(F32)
    for i in range(1, 8):
        total = total + ws_full[i, shard:, :].astype(F32)
    gains[...] = total
    for i in range(8):
        ws[i * shard : (i + 1) * shard, :] = ws_full[i, 0:shard, :]

    def first_norm(rows):
        x = tok[rows, :].astype(F32)
        scale = lax.rsqrt(jnp.mean(x * x, axis=-1, keepdims=True) + 1e-06)
        return (x * scale * gains[0:1, :]).astype(BF)

    def project(m):
        def step(i, carry):
            rows = block(m * seg + i * 256, 256)
            x = first_norm(rows)
            kv[m, block(cx * seg + i * 256, 256), :] = mm(x, ws[:, 0:span]).astype(BF)
            part = mm(x, ws[:, span:])
            q3[rows, :] = jnp.where(low_lanes(part.shape), part, 0.0).astype(BF)
            return carry

        lax.fori_loop(0, seg // 256, step, 0)

    def k_copy(m):
        spot = kv.at[m, block(0, seg), :]
        return remote(spot, spot, k_s.at[m], k_r.at[m], place.partner)

    for m in range(2):
        project(m)

        @pl.when(cx == 0)
        def _():
            k_copy(m).start()

        if m == 0:
            gather_step(0, 2)
        else:
            gather_step(1, 2)
            gather_step(2, 1)

    def attend(m):
        length = len_ref[m]

        def step(i, carry):
            rows = block(m * seg + i * QT, QT)
            first = cx * seg + i * QT
            lanes128 = lax.broadcasted_iota(jnp.int32, (QT, 128), 1)

            def one_head(h, tops):
                cut = block(h * 128, 128)
                values, allowed = masked_scores(
                    q3[rows, cut], kv[m, :, cut], band, scores, h, first, length
                )
                top = jnp.max(values, axis=-1, keepdims=True)
                raised = jnp.where(allowed, jnp.exp(values - top), 0.0)
                mass = jnp.sum(raised, axis=-1, keepdims=True)
                probs = (raised * (1.0 / mass)).astype(BF)
                part = mm(probs, kv[m, :, cut])
                ab3[rows, cut] = jnp.where(low_lanes(part.shape), 0.0, part).astype(BF)
                return jnp.where(lanes128 == h, top + jnp.log(mass), tops)

            lse[rows, :] = lax.fori_loop(0, heads, one_head, jnp.zeros((QT, 128), F32))
            bpart[rows, :] = mm_nt(ab3[rows, :], ws[:, span:]).astype(BF)
            return carry

        lax.fori_loop(0, seg // QT, step, 0)

    def second_norm(m):
        rows = sums.own_rows(m)
        x = tok[rows, :].astype(F32) + sums.total(m, 3)
        hidden[m] = x
        scale = lax.rsqrt(jnp.mean(x * x, axis=-1, keepdims=True) + 1e-06)
        ntwo[rows, :] = (x * scale * gains[1:2, :]).astype(BF)
        sums.share(m, 3, ntwo)

    for m in range(2):

        @pl.when(cx == 1)
        def _():
            k_copy(m).wait_recv()

        attend(m)
        sums.c_copy(m, 3, bpart).start()
        gather_step(m, 3)
        if m == 1:
            second_norm(0)
        sums.to_quarters(m, 3, bpart)
    gather_step(3, 1)
    second_norm(1)
    sums.pass_on(0, 3, ntwo)
    gather_step(0, 4)
    sums.pass_on(1, 3, ntwo)
    gather_step(1, 4)
    for m in range(2):
        sums.shared(m, 3, ntwo)
        sums.c_copy(m, 3, bpart).wait_send()

    router16 = gains[...].astype(BF)

    def upstream_of(rows, m, first):
        spot = lax.broadcasted_iota(jnp.int32, (rows.size, 1), 0) + (cx * seg + first)
        live = (spot < len_ref[m]).astype(F32)
        return live, live * cot[rows, :].astype(F32)

    def choices(m, carry):
        lanes = lax.broadcasted_iota(jnp.int32, (seg, 16), 1)
        chosen = jnp.zeros((seg, 16), F32)
        for e in range(experts):
            inside = put_of(m, e).astype(F32)
            chosen = jnp.where(lanes == e + 2, jnp.sum(inside, axis=1, keepdims=True), chosen)
        chosen_ref[block(m * seg, seg), :] = chosen
        return carry

    def put_of(m, e):
        row = slot_lanes[m, pl.ds(e, 1), :]
        return row == lax.broadcasted_iota(jnp.int32, (seg, cap), 0)

    lax.fori_loop(0, 2, choices, 0)

    def gates(i, carry):
        rows = block(i * 256, 256)
        m = lax.div(i, seg // 256)
        logits = mm_nt(ntwo[rows, :], router16)
        lanes = lax.broadcasted_iota(jnp.int32, (256, 16), 1)
        inside = (lanes >= 2) & (lanes < 2 + experts)
        logits = jnp.where(inside, logits, -1e30)
        top = jnp.max(logits, axis=-1, keepdims=True)
        raised = jnp.where(inside, jnp.exp(logits - top), 0.0)
        probs = raised / jnp.sum(raised, axis=-1, keepdims=True)
        probs_ref[rows, :] = probs
        gate = jnp.sum(probs * chosen_ref[rows, :], axis=-1, keepdims=True)
        live, upstream = upstream_of(rows, m, lax.rem(i, seg // 256) * 256)
        sum_grad[rows, :] = (gate * upstream).astype(BF)
        epart[rows, :] = jnp.zeros((256, width), BF)
        npart[rows, :] = jnp.zeros((256, width), BF)
        return carry

    lax.fori_loop(0, 2 * seg // 256, gates, 0)

    def load(e):
        slot = lax.rem(e, 2)
        return pltpu.make_async_copy(
            w_full.at[e], wbuf.at[pl.ds(slot * 2, 2)], load_sem.at[slot]
        )

    def arrived(e):
        w_own(e).wait()
        for d in range(2):
            gather(d, e, 4, False).wait_recv()
        load(e).start()

    picked, slot_grad, activated, raised_grad = (ffn.at[i] for i in range(4))

    def start_sums():
        for m in range(2):
            sums.c_copy(m, 1, npart).start()
            sums.c_copy(m, 0, epart).start()

    def g(e, s):
        return lambda: gather_step(e, s)

    def r(e, s):
        return lambda: reduce_step(e, s)

    def here(e):
        return lambda: arrived(e)

    before = ([here(0), here(1)], [], [], [])
    between = ([g(3, 2)], [g(3, 3)], [here(3)], [r(1, 4), start_sums])
    after = (
        [g(2, 3)],
        [g(2, 4), g(3, 4), r(0, 2), here(2), r(1, 2), r(0, 3)],
        [r(1, 3), r(0, 4)],
        [r(2, 2)],
    )

    def act_on(e, plan):
        for i, acts in enumerate(plan):
            if acts:

                @pl.when(e == i)
                def _(acts=acts):
                    for act in acts:
                        act()

    def expert(e, carry):
        slot = lax.rem(e, 2)

        def weight(which):
            return wbuf[slot * 2 + which].reshape(width, -1)

        act_on(e, before)
        load(e).wait()

        def one_micro(m, carry):
            rows = block(m * seg, seg)
            slots = block(m * cap, cap)
            put = put_of(m, e).astype(BF)
            chosen_rows = mm_tn(put, ntwo[rows, :]).astype(BF)
            picked[slots, :] = chosen_rows
            slot_part = mm_tn(put, sum_grad[rows, :]).astype(BF)
            slot_grad[slots, :] = slot_part
            raised = mm(chosen_rows, weight(0))
            square = raised * raised
            bent = jnp.tanh(C0 * raised * (1.0 + C1 * square))
            cdf = 0.5 * (1.0 + bent)
            act = (raised * cdf).astype(BF)
            activated[slots, :] = act
            slope = cdf + 0.5 * raised * (1.0 - bent * bent) * (C0 * (1.0 + 3.0 * C1 * square))
            act_grad = mm(slot_part, weight(1))
            back = (act_grad * slope).astype(BF)
            raised_grad[slots, :] = back
            lowered = mm_nt(act, weight(1)).astype(BF)
            epart[rows, :] += mm(put, lowered).astype(BF)
            pulled = mm_nt(back, weight(0)).astype(BF)
            npart[rows, :] += mm(put, pulled).astype(BF)
            return carry

        lax.fori_loop(0, 2, one_micro, 0)
        act_on(e, between)

        def weight_part(i, carry):
            lanes = block(i * 384, 384)
            slabs = pl.ds(i * 4, 4)
            part = mm_tn(picked[:, lanes], raised_grad[...]).astype(BF)
            gw[e, 0, slabs] = part.reshape(4, shard, -1)
            part = mm_tn(slot_grad[:, lanes], activated[...]).astype(BF)
            gw[e, 1, slabs] = part.reshape(4, shard, -1)
            return carry

        lax.fori_loop(0, width // 384, weight_part, 0)
        reduce_step(e, 1)
        act_on(e, after)
        return carry

    gather_step(2, 2)
    lax.fori_loop(0, experts, expert, 0)

    for peer in (place.right, place.left):
        pl.semaphore_signal(ready, inc=1, device_id=peer, device_id_type=MESH)

    ones = jnp.ones((8, width), BF)
    for m in range(2):

        def gate_terms(i, carry):
            rows = block(m * seg + i * 256, 256)
            live, upstream = upstream_of(rows, m, i * 256)
            terms = epart[rows, :].astype(F32) * upstream
            high = terms.astype(BF)
            rest = (terms - high.astype(F32)).astype(BF)
            gg_own[m, :, block(i * 256, 256)] = mm_nt(ones, high) + mm_nt(ones, rest)
            return carry

        sums.y_copy(m, 3).wait_send()
        sums.to_quarters(m, 1, npart)
        lax.fori_loop(0, seg // 256, gate_terms, 0)

    def gg_copy(k):
        return remote(gg_own, gg_in.at[k - 1], gg_s.at[k - 1], gg_r.at[k - 1], place.tensor_peers[k - 1])

    for k in (1, 2, 3):
        gg_copy(k).start()
    pump_late()
    pl.semaphore_wait(ready, 2)
    for k in (1, 2, 3):
        gg_copy(k).wait_recv()
    gg_sum[...] = gg_own[...] + gg_in[0] + gg_in[1] + gg_in[2]
    own_first = place.core * (seg // 2) + place.yy * (seg // 4)

    def own_copy(m, j, ref):
        return pltpu.make_async_copy(
            own_out.at[m, j - 1], ref.at[sums.own_rows(m)], out_sem.at[m * 2 + j - 1]
        )

    for m in range(2):
        rows = sums.own_rows(m)
        line = gg_sum[m, :, block(own_first, seg // 4)]
        line = jnp.where(lax.broadcasted_iota(jnp.int32, line.shape, 0) == 0, line, 0.0)
        high = line.astype(BF)
        rest = (line - high.astype(F32)).astype(BF)
        ones = jnp.ones((8, 128), BF)
        gate_grad = (mm_tn(high, ones) + mm_tn(rest, ones))[:, 0:1]
        down = sums.total(m, 1)
        live, upstream = upstream_of(rows, m, own_first)
        probs, chosen = probs_ref[rows, :], chosen_ref[rows, :]
        gate = jnp.sum(probs * chosen, axis=-1, keepdims=True)
        logit_grad = (probs * gate_grad * (chosen - gate)).astype(BF)
        down = down + mm(logit_grad, router16)
        through, gain_terms = norm_back(hidden[m], gains[1:2, :], down)
        full = through + upstream
        hgrad[m] = full
        bgrad[rows, :] = full.astype(BF)
        sums.share(m, 0, bgrad)
        tiny_own[1:2, :] += jnp.sum(gain_terms, axis=0, keepdims=True)
        tiny_own[...] += mm_tn(logit_grad, ntwo[rows, :])[0:8, :]
    pump_late()
    for m in range(2):
        sums.pass_on(m, 0, bgrad)
    for m in range(2):
        sums.to_quarters(m, 0, epart)

    def dkv_copy(m, h):
        spot = dkv.at[m, h]
        return remote(spot, spot, kv_s.at[m, h], kv_r.at[m, h], place.partner)

    def attend_back(m):
        length = len_ref[m]

        def lower(i, carry):
            part = mm(bgrad[block(m * seg + i * 256, 256), :], ws[:, span:])
            part = jnp.where(low_lanes(part.shape), 0.0, part)
            do3[block(i * 256, 256), :] = part.astype(BF)
            return carry

        lax.fori_loop(0, seg // 256, lower, 0)

        def one_head(h, carry):
            cut = block(h * 128, 128)
            dkv_acc[...] = jnp.zeros(dkv_acc.shape, F32)

            def step(i, carry):
                rows = block(m * seg + i * QT, QT)
                first = cx * seg + i * QT
                q_tile, do_tile = q3[rows, cut], do3[block(i * QT, QT), cut]
                keys = kv[m, :, cut]
                values, allowed = masked_scores(q_tile, keys, band, scores, h, first, length)
                lanes128 = lax.broadcasted_iota(jnp.int32, (QT, 128), 1)
                mass = jnp.sum(jnp.where(lanes128 == h, lse[rows, :], 0.0), axis=1, keepdims=True)
                soft = jnp.where(allowed, jnp.exp(values - mass), 0.0)
                soft_grad = mm_nt(do_tile, keys)
                delta = jnp.sum(soft * soft_grad, axis=-1, keepdims=True)
                score_grad = (soft * (soft_grad - delta)).astype(BF)
                dkv_acc[...] += mm_tn(soft.astype(BF), do_tile) + 0.125 * mm_tn(score_grad, q_tile)
                part = mm(score_grad, keys) * 0.125
                grads[rows, block(span + h * 128, 128)] = jnp.where(
                    low_lanes(part.shape), part, 0.0
                ).astype(BF)
                spread[:, BAND:] = score_grad.astype(F32)
                for half in range(QT // BAND):
                    lanes = block(first + half * BAND, 2 * BAND)
                    band_sum[h] += spread[half * BAND : (half + 1) * BAND, lanes]
                whole_sum[h, 0:1, :] += jnp.sum(spread[:, BAND:], axis=0, keepdims=True)
                return carry

            lax.fori_loop(0, seg // QT, step, 0)

            @pl.when(cx == 1)
            def _():
                dkv[m, h] = dkv_acc[0:seg, :].astype(BF)
                dkv_copy(m, h).start()

            grads[pl.ds(m * seg, seg), cut] = dkv_acc[block(cx * seg, seg), :].astype(BF)

            @pl.when(h == 1)
            def _():
                pump_late()

            return carry

        lax.fori_loop(0, heads, one_head, 0)

    def after_attend(m):
        rows = pl.ds(m * seg, seg)

        @pl.when(cx == 0)
        def _():
            for h in range(heads):
                dkv_copy(m, h).wait_recv()
                total = grads[rows, head_lanes(h)].astype(F32) + dkv[m, h].astype(F32)
                grads[rows, head_lanes(h)] = total.astype(BF)

        def lower(i, carry):
            spot = block(m * seg + i * 256, 256)
            npart[spot, :] = mm_nt(grads[spot, :], ws[...]).astype(BF)
            return carry

        lax.fori_loop(0, seg // 256, lower, 0)
        sums.c_copy(m, 2, npart).start()

    def gs_spot(slab, half):
        return ws_full.at[slab, pl.ds(0, shard), pl.ds(half * span, span)]

    def sx_copy(half, k):
        slab = lax.rem(dp + k, 4) * 2 + 1 - cx
        return remote(
            gs_spot(slab, half), sx.at[half, k], sx_s.at[half, k], sx_r.at[half, k], place.partner
        )

    def sz_copy(half, k):
        return remote(
            sx.at[half, k], sz.at[half, k - 1], sz_s.at[half, k - 1], sz_r.at[half, k - 1],
            place.z_peers[k - 1],
        )

    order = (2, 1, 3, 0)

    def small_part(half):
        def step(i, carry):
            lanes = block(i * 384, 384)
            cols = slice(half * span, (half + 1) * span)
            part = mm_tn(ffn[0, :, lanes], grads[0:seg, cols])
            part = part + mm_tn(ffn[1, :, lanes], grads[seg:, cols])
            if half == 1:
                part = part + mm_tn(bgrad[:, lanes], ab3[...])
            ws_full[pl.ds(i * 4, 4), 0:shard, cols] = part.astype(BF).reshape(4, shard, -1)
            return carry

        lax.fori_loop(0, width // 384, step, 0)
        for k in order:
            sx_copy(half, k).start()

    def small_step(half):
        cols = slice(half * span, (half + 1) * span)
        for k in order:
            sx_copy(half, k).wait_recv()
            slab = lax.rem(dp + k, 4) * 2 + cx
            total = ws_full[slab, 0:shard, cols].astype(F32) + sx[half, k].astype(F32)
            if k == 0:
                small_grad[:, cols] = total
            else:
                sx[half, k] = total.astype(BF)
                sz_copy(half, k).start()

    for m in range(2):
        sums.shared(m, 0, bgrad)
        attend_back(m)
        if m == 0:
            for i in range(2):

                def own_result(i):
                    rows = sums.own_rows(i)
                    expert_sum = sums.total(i, 0)
                    spot = lax.broadcasted_iota(jnp.int32, (seg // 4, 1), 0) + (cx * seg + own_first)
                    live = (spot < len_ref[i]).astype(F32)
                    gate = jnp.sum(probs_ref[rows, :] * chosen_ref[rows, :], axis=-1, keepdims=True)
                    own_out[i, 0] = (live * (hidden[i] + gate * expert_sum)).astype(BF)
                    own_copy(i, 1, result).start()
                    sums.share(i, 1, result, own_out.at[i, 0])

                own_result(i)

    def normed_again(i, carry):
        ffn[lax.div(i, 2), block(lax.rem(i, 2) * 256, 256), :] = first_norm(block(i * 256, 256))
        return carry

    lax.fori_loop(0, 2 * seg // 256, normed_again, 0)
    for k in range(4):
        gx_copy(k, cx).wait_send()
    small_part(1)
    sums.c_copy(0, 1, npart).wait_send()
    sums.y_copy(0, 1).wait_send()
    after_attend(0)
    sums.c_copy(1, 1, npart).wait_send()
    sums.y_copy(1, 1).wait_send()
    sums.to_quarters(0, 2, npart)
    after_attend(1)
    small_part(0)
    sums.to_quarters(1, 2, npart)
    pump_late(len(late))

    for m in range(2):
        down = sums.total(m, 2)
        rows = sums.own_rows(m)
        through, gain_terms = norm_back(tok[rows, :].astype(F32), gains[0:1, :], down)
        own_out[m, 1] = (through + hgrad[m]).astype(BF)
        sums.share(m, 2, input_grad, own_out.at[m, 1])
        own_copy(m, 2, input_grad).start()
        tiny_own[0:1, :] += jnp.sum(gain_terms, axis=0, keepdims=True)

    def tt_copy(k):
        return remote(
            tiny_own, tiny_t.at[k - 1], tt_s.at[k - 1], tt_r.at[k - 1], place.tensor_peers[k - 1]
        )

    for k in (1, 2, 3):
        tt_copy(k).start()
    small_step(1)
    small_step(0)
    for k in (1, 2, 3):
        tt_copy(k).wait_recv()
    tiny_x[0] = tiny_own[...] + tiny_t[0] + tiny_t[1] + tiny_t[2]
    tx_copy = remote(tiny_x.at[0], tiny_x.at[1], tx_s.at[0], tx_r.at[0], place.partner)
    tx_copy.start()
    bucket_sums(heads, band_sum, whole_sum, dbias_own)
    bx_copy = remote(dbias_own, dbias_x, bx_s.at[0], bx_r.at[0], place.partner)
    bx_copy.start()
    for m in range(2):
        sums.pass_on(m, 1, result)
        sums.pass_on(m, 2, input_grad)
    tx_copy.wait_recv()
    tiny_x[2] = tiny_x[0] + tiny_x[1]
    bx_copy.wait_recv()
    dbias_sum = dbias_own[...] + dbias_x[...]
    dbias_out[...] = dbias_sum

    def tz_copy(k):
        return remote(
            tiny_x.at[2], tiny_z.at[k - 1], tz_s.at[k - 1], tz_r.at[k - 1], place.z_peers[k - 1]
        )

    def bz_copy(k):
        return remote(
            dbias_out, dbias_z.at[k - 1], bz_s.at[k - 1], bz_r.at[k - 1], place.z_peers[k - 1]
        )

    for k in (1, 2, 3):
        tz_copy(k).start()
        bz_copy(k).start()
    for e in range(experts):
        reduce_end(e)
    for half in range(2):
        cols = slice(half * span, (half + 1) * span)
        total = small_grad[:, cols]
        for k in (1, 2, 3):
            sz_copy(half, k).wait_recv()
            total = total + sz[half, k - 1].astype(F32)
        small_grad[:, cols] = total
    for k in (1, 2, 3):
        bz_copy(k).wait_recv()
        bz_copy(k).wait_send()
        dbias_sum = dbias_sum + dbias_z[k - 1]
    dbias_out[...] = dbias_sum
    total = tiny_x[2]
    for k in (1, 2, 3):
        tz_copy(k).wait_recv()
        total = total + tiny_z[k - 1]
    tiny_out[...] = total
    for m in range(2):
        sums.shared(m, 1, result)
        sums.shared(m, 2, input_grad)

    for e in range(experts):
        for d in range(2):
            for s in (1, 2, 3, 4):
                gather(d, e, s, True).wait_send()
                reduce_copy(d, e, s).wait_send()
    for k in range(4):
        for half in range(2):
            sx_copy(half, k).wait_send()
            if k > 0:
                sz_copy(half, k).wait_send()
        if k > 0:
            gz_copy(k, small_slab(0, cx)).wait_send()
            gg_copy(k).wait_send()
            tt_copy(k).wait_send()
            tz_copy(k).wait_send()
    tx_copy.wait_send()
    bx_copy.wait_send()
    for m in range(2):
        sums.c_copy(m, 0, epart).wait_send()
        sums.c_copy(m, 2, npart).wait_send()
        own_copy(m, 1, result).wait()
        own_copy(m, 2, input_grad).wait()
        sums.y_copy(m, 0).wait_send()
        sums.y_copy(m, 2).wait_send()
        for j in range(4):
            for step in range(3):
                own = own_out.at[m, j - 1] if j in (1, 2) else None
                ref = (bgrad, result, input_grad, ntwo)[j]
                sums.a_copy(m, j, ref, step, own).wait_send()

        @pl.when(cx == 0)
        def _():
            k_copy(m).wait_send()

        @pl.when(cx == 1)
        def _():
            for h in range(heads):
                dkv_copy(m, h).wait_send()


def layer_call(lengths, bias, slot_lanes, tok, cot, wsmall, w):
    heads = bias.shape[0]
    rows, width = tok.shape
    span = heads * 128
    experts, ff = w.shape[0], w.shape[3]
    seg = rows // 2
    quarter = seg // 4
    shard = width // 8
    slots = 2 * slot_lanes.shape[2]
    vm = pl.BlockSpec(memory_space=pltpu.VMEM)
    sm = pl.BlockSpec(memory_space=pltpu.SMEM)
    hbm = pl.BlockSpec(memory_space=pl.ANY)
    dma = pltpu.SemaphoreType.DMA
    sds = jax.ShapeDtypeStruct
    low, full = (lambda *shape: pltpu.VMEM(shape, BF)), (lambda *shape: pltpu.VMEM(shape, F32))

    def pair(*shape):
        return [dma(shape), dma(shape)]

    return pl.pallas_call(
        functools.partial(layer_kernel, heads),
        out_shape=(
            sds((rows, width), BF),
            sds((rows, width), BF),
            sds((experts, 2, shard, ff), F32),
            sds((shard, width), F32),
            sds((8, width), F32),
            sds((BUCKETS, 128), F32),
            sds((experts, 2, 8, shard, ff), BF),
        ),
        in_specs=[sm, sm] + [vm] * 3 + [hbm] * 2,
        out_specs=(hbm,) * 2 + (vm,) * 4 + (hbm,),
        scratch_shapes=[
            low(8, *wsmall.shape),
            low(width, width),
            full(16, width),
            full(2, quarter, width),
            low(rows, width),
            low(rows, span),
            low(2, rows, span),
            full(rows, 128),
            low(rows, span),
            low(4, 8, shard, ff),
            low(experts, 2, 8, shard, ff),
            low(2, experts, shard, ff),
            low(2, experts, 2, shard, ff),
            low(2, 2, 2, 2, shard, ff),
            low(2, 4, shard, span),
            low(2, 3, shard, span),
            low(rows, width),
            low(rows, width),
            low(rows, width),
            low(4, slots, width),
            full(rows, 16),
            full(rows, 16),
            low(2, 2, 2 * quarter, width),
            low(2, 2, quarter, width),
            low(2, 2, quarter, width),
            full(2, 2, quarter, width),
            full(2, quarter, width),
            low(rows, width),
            low(2, 2, quarter, width),
            low(seg, span),
            low(rows, 2 * span),
            full(rows, 128),
            low(2, heads, seg, 128),
            full(heads, BAND, 2 * BAND),
            full(QT, rows + BAND),
            full(QT, rows + BAND),
            full(heads, BAND, 2 * BAND),
            full(heads, 8, rows),
            full(2, 8, seg),
            full(3, 2, 8, seg),
            full(2, 8, seg),
            full(8, width),
            full(3, 8, width),
            full(3, 8, width),
            full(3, 8, width),
            full(BUCKETS, 128),
            full(BUCKETS, 128),
            full(3, BUCKETS, 128),
            dma((2,)),
            dma((4,)),
            dma((experts + 1,)),
            pltpu.SemaphoreType.REGULAR,
        ]
        + pair(3)
        + pair(4)
        + pair(2)
        + pair(2, experts, 4)
        + pair(2, experts, 4)
        + pair(2, 4)
        + pair(2, 4)
        + pair(2, 4, 3)
        + pair(2, heads)
        + pair(3)
        + pair(2, 4)
        + pair(2, 3)
        + pair(3)
        + pair(1)
        + pair(3)
        + pair(1)
        + pair(3),
        compiler_params=pltpu.CompilerParams(
            collective_id=0, has_side_effects=True, vmem_limit_bytes=63 << 20
        ),
    )(lengths, bias, slot_lanes, tok, cot, wsmall, w)


def body_fast(
    inputs, lengths, expert_ids, slot_rows, attn_gain, qkv_weight, out_weight, position_bias,
    ffn_gain, router_weight, up_weight, down_weight, cotangent,
):
    micro, seg, width = inputs.shape
    rows = micro * seg
    experts = up_weight.shape[0]
    heads = position_bias.shape[1]
    size = qkv_weight.shape[2] // heads
    slab = lax.axis_index("dp") * 2 + lax.axis_index("ctx")
    shard = attn_gain.shape[0]
    by_head = jnp.concatenate(
        [
            qkv_weight[1].reshape(shard, heads, 1, size),
            qkv_weight[2].reshape(shard, heads, 1, size),
        ],
        axis=2,
    ).reshape(shard, -1)
    by_query = jnp.concatenate(
        [
            qkv_weight[0].reshape(shard, heads, 1, size),
            out_weight.T.reshape(shard, heads, 1, size),
        ],
        axis=2,
    ).reshape(shard, -1)
    small = jnp.concatenate(
        [attn_gain[None], ffn_gain[None], router_weight.T, jnp.zeros((10, shard), BF)], axis=0
    )
    small = lax.dynamic_update_slice(jnp.zeros((16, width), BF), small, (0, slab * shard))
    wsmall = jnp.concatenate([jnp.concatenate([by_head, by_query], axis=1), small], axis=0)
    w = jnp.stack([up_weight, jnp.transpose(down_weight, (0, 2, 1))], axis=1)
    tok = inputs.reshape(rows, width)
    result, input_part, w_grad, small_grad, tiny, dbias, _ = layer_call(
        lengths, position_bias.T, slot_rows.reshape(micro, experts, -1), tok,
        cotangent.reshape(rows, width), wsmall, w,
    )
    tiny = lax.dynamic_slice_in_dim(tiny, slab * shard, shard, axis=1)
    parts = small_grad.reshape(shard, 2, heads, 2, size)
    qkv_grad = jnp.stack(
        [parts[:, 1, :, 0], parts[:, 0, :, 0], parts[:, 0, :, 1]], axis=0
    ).reshape(3, shard, heads * size)
    return (
        result.reshape(inputs.shape),
        input_part.reshape(inputs.shape),
        tiny[0],
        qkv_grad,
        parts[:, 1, :, 1].reshape(shard, heads * size).T,
        dbias[:, :heads],
        tiny[1],
        tiny[2 : 2 + experts].T,
        w_grad[:, 0],
        jnp.transpose(w_grad[:, 1], (0, 2, 1)),
    )


def rms_norm(values, gain_vector):
    return (
        values * lax.rsqrt(jnp.mean(values * values, axis=-1, keepdims=True) + 1e-06) * gain_vector
    )


def bucket_of(distance):
    clipped = jnp.maximum(distance, 0)
    edge_values = jnp.asarray(bucket_edges, dtype=jnp.int32)
    beyond = jnp.sum((clipped[..., None] >= edge_values).astype(jnp.int32), axis=-1)
    return jnp.where(clipped < 16, clipped, jnp.minimum(16 + beyond, 31))


def toeplitz(diagonal, query_count, key_count):
    head_count = diagonal.shape[0]
    padded = jnp.pad(diagonal, ((0, 0), (0, 1)))
    row_width = query_count + key_count
    repeated = jnp.broadcast_to(padded[:, None, :], (head_count, query_count, row_width)).reshape(
        head_count, query_count * row_width
    )
    repeated = jnp.pad(repeated, ((0, 0), (0, query_count))).reshape(
        head_count, query_count, row_width + 1
    )[:, :, :key_count]
    return repeated[:, :, ::-1]


def diagonal_sums(gradient):
    head_count, query_count, key_count = gradient.shape
    offset_count = query_count + key_count - 1
    flipped = jnp.pad(gradient[:, :, ::-1], ((0, 0), (0, 0), (0, query_count)))
    skewed = flipped.reshape(head_count, query_count * (offset_count + 1))[
        :, : query_count * offset_count
    ]
    return jnp.sum(skewed.reshape(head_count, query_count, offset_count), axis=1)


def bucket_table(query_first, query_count, key_count):
    offsets = (
        query_first - (key_count - 1) + jnp.arange(query_count + key_count - 1, dtype=jnp.int32)
    )
    return (bucket_of(offsets)[:, None] == jnp.arange(BUCKETS, dtype=jnp.int32)[None, :]).astype(
        jnp.float32
    )


def body(
    inputs,
    lengths,
    expert_ids,
    slot_rows,
    attn_gain,
    qkv_weight,
    out_weight,
    position_bias,
    ffn_gain,
    router_weight,
    up_weight,
    down_weight,
    cotangent,
):
    highest = lax.Precision.HIGHEST
    micro_count, seg_rows, model_width = inputs.shape
    local_heads = position_bias.shape[1]
    head_size = qkv_weight.shape[2] // local_heads
    expert_count = up_weight.shape[0]
    query_first = lax.axis_index("ctx") * seg_rows
    query_pos = query_first + jnp.arange(seg_rows, dtype=jnp.int32)

    def pair_scores(query_heads, query_start, key_heads, length):
        query_count = query_heads.shape[0]
        key_count = key_heads.shape[0]
        scores = (
            jnp.einsum("qhd,khd->hqk", query_heads, key_heads, preferred_element_type=jnp.float32)
            * 0.125
        )
        diagonal = jnp.einsum(
            "rb,bh->hr",
            bucket_table(query_start, query_count, key_count),
            position_bias,
            precision=highest,
        )
        scores = scores + toeplitz(diagonal, query_count, key_count)
        query_place = query_start + jnp.arange(query_count, dtype=jnp.int32)
        key_place = jnp.arange(key_count, dtype=jnp.int32)
        allowed = (key_place[None, :] <= query_place[:, None]) & (key_place[None, :] < length)
        return (scores, allowed)

    def scores_for(query_heads, key_block, length):
        key_count = key_block.shape[0]
        key_heads = key_block.reshape(key_count, local_heads, head_size)
        scores, allowed = pair_scores(query_heads, query_first, key_heads, length)
        return (scores, allowed, key_heads)

    results = []
    input_parts = []
    grad_sums = None
    bias_total = jnp.zeros((local_heads, BUCKETS), jnp.float32)
    for micro_step in range(micro_count):
        forward_gain_one = lax.all_gather(attn_gain, ("dp", "ctx"), axis=0, tiled=True)
        forward_qkv_full = lax.all_gather(qkv_weight, ("dp", "ctx"), axis=1, tiled=True)
        forward_out_full = lax.all_gather(out_weight, ("dp", "ctx"), axis=1, tiled=True)
        forward_gain_two = lax.all_gather(ffn_gain, ("dp", "ctx"), axis=0, tiled=True)
        forward_router_full = lax.all_gather(router_weight, ("dp", "ctx"), axis=0, tiled=True)
        forward_up_full = lax.all_gather(up_weight, ("dp", "ctx"), axis=1, tiled=True)
        forward_down_full = lax.all_gather(down_weight, ("dp", "ctx"), axis=2, tiled=True)
        forward_tokens = inputs[micro_step].astype(jnp.float32)
        forward_length = lengths[micro_step]
        forward_normed = rms_norm(forward_tokens, forward_gain_one.astype(jnp.float32)).astype(
            jnp.bfloat16
        )
        forward_projected = jnp.einsum(
            "td,cde->cte", forward_normed, forward_qkv_full, preferred_element_type=jnp.float32
        ).astype(jnp.bfloat16)
        forward_query_heads = forward_projected[0].reshape(seg_rows, local_heads, head_size)
        row_top = jnp.full((local_heads, seg_rows), -1e30, jnp.float32)
        attend_scores, attend_allowed, attend_key_heads = scores_for(
            forward_query_heads,
            lax.all_gather(forward_projected[1], "ctx", axis=0, tiled=True),
            forward_length,
        )
        value_heads = lax.all_gather(forward_projected[2], "ctx", axis=0, tiled=True).reshape(
            attend_key_heads.shape
        )
        attend_scores = jnp.where(attend_allowed[None], attend_scores, -1e30)
        new_top = jnp.maximum(row_top, jnp.max(attend_scores, axis=-1))
        weights_exp = jnp.where(
            attend_allowed[None], jnp.exp(attend_scores - new_top[:, :, None]), 0.0
        )
        row_total = jnp.sum(weights_exp, axis=-1)
        summed = jnp.einsum(
            "hqk,khd->hqd",
            weights_exp.astype(jnp.bfloat16),
            value_heads,
            preferred_element_type=jnp.float32,
        )
        row_top, row_total, summed = (new_top, row_total, summed)
        forward_attended = summed / row_total[:, :, None]
        forward_log_total = row_top + jnp.log(row_total)
        forward_attended_low = (
            jnp.transpose(forward_attended, (1, 0, 2)).reshape(seg_rows, -1).astype(jnp.bfloat16)
        )
        branch = lax.psum(
            jnp.dot(
                forward_attended_low, forward_out_full, preferred_element_type=jnp.float32
            ).astype(jnp.bfloat16),
            "tensor",
        ).astype(jnp.float32)
        forward_hidden = forward_tokens + branch
        forward_normed_two = rms_norm(forward_hidden, forward_gain_two.astype(jnp.float32)).astype(
            jnp.bfloat16
        )
        logits = jnp.dot(
            forward_normed_two, forward_router_full, preferred_element_type=jnp.float32
        )
        forward_router_probs = jax.nn.softmax(logits, axis=-1)
        forward_chosen = (
            expert_ids[micro_step][:, None] == jnp.arange(expert_count, dtype=jnp.int32)[None, :]
        ).astype(jnp.float32)
        forward_gate_value = jnp.sum(forward_router_probs * forward_chosen, axis=-1)
        forward_slot_table = slot_rows[micro_step, 0]
        padded = jnp.concatenate(
            [forward_normed_two, jnp.zeros((1, model_width), jnp.bfloat16)], axis=0
        )
        forward_picked = padded[forward_slot_table]
        forward_raised = jnp.einsum(
            "ekd,edf->ekf", forward_picked, forward_up_full, preferred_element_type=jnp.float32
        )
        forward_activated = jax.nn.gelu(forward_raised).astype(jnp.bfloat16)
        lowered = jnp.einsum(
            "ekf,efd->ekd", forward_activated, forward_down_full, preferred_element_type=jnp.float32
        )
        spread = (
            jnp.zeros((seg_rows + 1, model_width), jnp.float32)
            .at[forward_slot_table.reshape(-1)]
            .add(lowered.reshape(-1, model_width))[:seg_rows]
        )
        forward_expert_sum = lax.psum(spread.astype(jnp.bfloat16), "tensor").astype(jnp.float32)
        forward_live_rows = (query_pos < forward_length).astype(jnp.float32)[:, None]
        result = (
            forward_live_rows * (forward_hidden + forward_gate_value[:, None] * forward_expert_sum)
        ).astype(jnp.bfloat16)
        forward_kept_state = (
            forward_tokens,
            forward_length,
            forward_normed,
            forward_projected,
            forward_attended,
            forward_log_total,
            forward_attended_low,
            forward_hidden,
            forward_normed_two,
            forward_router_probs,
            forward_chosen,
            forward_gate_value,
            forward_slot_table,
            forward_picked,
            forward_raised,
            forward_activated,
            forward_expert_sum,
            forward_live_rows,
        )
        result, kept_state = (result, forward_kept_state)
        gain_one = lax.all_gather(attn_gain, ("dp", "ctx"), axis=0, tiled=True)
        qkv_full = lax.all_gather(qkv_weight, ("dp", "ctx"), axis=1, tiled=True)
        out_full = lax.all_gather(out_weight, ("dp", "ctx"), axis=1, tiled=True)
        gain_two = lax.all_gather(ffn_gain, ("dp", "ctx"), axis=0, tiled=True)
        router_full = lax.all_gather(router_weight, ("dp", "ctx"), axis=0, tiled=True)
        up_full = lax.all_gather(up_weight, ("dp", "ctx"), axis=1, tiled=True)
        down_full = lax.all_gather(down_weight, ("dp", "ctx"), axis=2, tiled=True)
        (
            tokens,
            backward_length,
            normed,
            projected,
            attended,
            log_total,
            attended_low,
            hidden,
            normed_two,
            router_probs,
            chosen,
            gate_value,
            slot_table,
            picked,
            raised,
            activated,
            expert_sum,
            live_rows,
        ) = kept_state
        upstream = live_rows * cotangent[micro_step].astype(jnp.float32)
        sum_grad = (gate_value[:, None] * upstream).astype(jnp.bfloat16)
        gate_grad = jnp.sum(expert_sum * upstream, axis=-1)
        logit_grad = (router_probs * gate_grad[:, None] * (chosen - gate_value[:, None])).astype(
            jnp.bfloat16
        )
        router_part = jnp.einsum(
            "td,te->de", normed_two, logit_grad, preferred_element_type=jnp.float32
        )
        padded_grad = jnp.concatenate([sum_grad, jnp.zeros((1, model_width), jnp.bfloat16)], axis=0)
        slot_grad = padded_grad[slot_table]
        down_part = jnp.einsum(
            "ekf,ekd->efd", activated, slot_grad, preferred_element_type=jnp.float32
        )
        act_grad = jnp.einsum(
            "ekd,efd->ekf", slot_grad, down_full, preferred_element_type=jnp.float32
        )
        unused_value, gelu_back = jax.vjp(jax.nn.gelu, raised)
        raised_grad = gelu_back(act_grad)[0].astype(jnp.bfloat16)
        up_part = jnp.einsum(
            "ekd,ekf->edf", picked, raised_grad, preferred_element_type=jnp.float32
        )
        picked_grad = jnp.einsum(
            "ekf,edf->ekd", raised_grad, up_full, preferred_element_type=jnp.float32
        )
        spread_grad = (
            jnp.zeros((seg_rows + 1, model_width), jnp.float32)
            .at[slot_table.reshape(-1)]
            .add(picked_grad.reshape(-1, model_width))[:seg_rows]
        )
        normed_two_grad = lax.psum(spread_grad.astype(jnp.bfloat16), "tensor").astype(
            jnp.float32
        ) + jnp.einsum("te,de->td", logit_grad, router_full, preferred_element_type=jnp.float32)
        unused_norm, second_back = jax.vjp(rms_norm, hidden, gain_two.astype(jnp.float32))
        hidden_grad, gain_two_part = second_back(normed_two_grad)
        hidden_grad = hidden_grad + upstream
        branch_grad = hidden_grad.astype(jnp.bfloat16)
        out_part = jnp.einsum(
            "te,td->ed", attended_low, branch_grad, preferred_element_type=jnp.float32
        )
        attended_grad = jnp.einsum(
            "td,ed->te", branch_grad, out_full, preferred_element_type=jnp.float32
        ).astype(jnp.bfloat16)
        grad_heads = attended_grad.reshape(seg_rows, local_heads, head_size)
        row_delta = jnp.sum(
            jnp.transpose(grad_heads.astype(jnp.float32), (1, 0, 2)) * attended, axis=-1
        )
        backward_query_heads = projected[0].reshape(seg_rows, local_heads, head_size)
        bias_zero = jnp.zeros((local_heads, BUCKETS), jnp.float32)
        attend_bias_acc = bias_zero
        bias_acc = attend_bias_acc
        score_scores, score_allowed, score_key_heads = scores_for(
            backward_query_heads,
            lax.all_gather(projected[1], "ctx", axis=0, tiled=True),
            backward_length,
        )
        score_value_heads = lax.all_gather(projected[2], "ctx", axis=0, tiled=True).reshape(
            score_key_heads.shape
        )
        score_key_count = score_key_heads.shape[0]
        soft_weights = jnp.where(
            score_allowed[None], jnp.exp(score_scores - log_total[:, :, None]), 0.0
        )
        weight_grad = jnp.einsum(
            "qhd,khd->hqk", grad_heads, score_value_heads, preferred_element_type=jnp.float32
        )
        score_grad = (soft_weights * (weight_grad - row_delta[:, :, None])).astype(jnp.bfloat16)
        query_acc = jnp.einsum(
            "hqk,khd->qhd", score_grad, score_key_heads, preferred_element_type=jnp.float32
        )
        bias_acc = bias_acc + jnp.dot(
            diagonal_sums(score_grad.astype(jnp.float32)),
            bucket_table(query_first, seg_rows, score_key_count),
            precision=highest,
        )
        (
            (attend_query_acc, attend_bias_acc),
            attend_soft_weights,
            attend_score_grad,
            attend_key_count,
        ) = ((query_acc, bias_acc), soft_weights, score_grad, score_key_count)
        key_term = (
            jnp.einsum(
                "hqk,qhd->khd",
                attend_score_grad,
                backward_query_heads,
                preferred_element_type=jnp.float32,
            )
            * 0.125
        )
        value_term = jnp.einsum(
            "hqk,qhd->khd",
            attend_soft_weights.astype(jnp.bfloat16),
            grad_heads,
            preferred_element_type=jnp.float32,
        )
        grad_term = jnp.stack(
            [key_term.reshape(attend_key_count, -1), value_term.reshape(attend_key_count, -1)],
            axis=1,
        )
        key_value_acc = grad_term
        query_acc, key_value_acc, bias_part = (attend_query_acc, key_value_acc, attend_bias_acc)
        own_grads = lax.psum_scatter(
            key_value_acc.astype(jnp.bfloat16), "ctx", scatter_dimension=0, tiled=True
        ).astype(jnp.float32)
        query_grad = (query_acc * 0.125).reshape(seg_rows, -1).astype(jnp.bfloat16)
        qkv_grad = jnp.stack(
            [
                query_grad,
                own_grads[:, 0].astype(jnp.bfloat16),
                own_grads[:, 1].astype(jnp.bfloat16),
            ],
            axis=0,
        )
        qkv_part = jnp.einsum("td,cte->cde", normed, qkv_grad, preferred_element_type=jnp.float32)
        normed_grad = lax.psum(
            jnp.einsum(
                "cte,cde->td", qkv_grad, qkv_full, preferred_element_type=jnp.float32
            ).astype(jnp.bfloat16),
            "tensor",
        ).astype(jnp.float32)
        unused_first, first_back = jax.vjp(rms_norm, tokens, gain_one.astype(jnp.float32))
        token_grad, gain_one_part = first_back(normed_grad)
        input_part = (token_grad + hidden_grad).astype(jnp.bfloat16)
        weight_parts = (
            gain_one_part,
            qkv_part,
            out_part,
            gain_two_part,
            router_part,
            up_part,
            down_part,
        )
        input_part, weight_parts, bias_part = (input_part, weight_parts, bias_part)
        results.append(result)
        input_parts.append(input_part)
        grad_sums = (
            weight_parts
            if grad_sums is None
            else tuple((old_sum + new_part for old_sum, new_part in zip(grad_sums, weight_parts)))
        )
        bias_total = bias_total + bias_part
    reduced = (
        lax.psum_scatter(grad_sums[0], ("dp", "ctx"), scatter_dimension=0, tiled=True),
        lax.psum_scatter(grad_sums[1], ("dp", "ctx"), scatter_dimension=1, tiled=True),
        lax.psum_scatter(grad_sums[2], ("dp", "ctx"), scatter_dimension=1, tiled=True),
        lax.psum_scatter(grad_sums[3], ("dp", "ctx"), scatter_dimension=0, tiled=True),
        lax.psum_scatter(grad_sums[4], ("dp", "ctx"), scatter_dimension=0, tiled=True),
        lax.psum_scatter(grad_sums[5], ("dp", "ctx"), scatter_dimension=1, tiled=True),
        lax.psum_scatter(grad_sums[6], ("dp", "ctx"), scatter_dimension=2, tiled=True),
    )
    bias_grad_total = lax.psum(bias_total, ("dp", "ctx"))
    return (
        jnp.stack(results, axis=0),
        jnp.stack(input_parts, axis=0),
        reduced[0],
        reduced[1],
        reduced[2],
        jnp.transpose(bias_grad_total),
        reduced[3],
        reduced[4],
        reduced[5],
        reduced[6],
    )


def solution(mesh):
    small = mesh.shape["ctx"] == 2 and mesh.shape["dp"] == 4 and mesh.shape["tensor"] == 4
    return jax.shard_map(
        body_fast if small else body,
        mesh=mesh,
        in_specs=(
            P("dp", "ctx", None),
            P("dp"),
            P("dp", "ctx"),
            P("dp", "ctx", None, None),
            P(("dp", "ctx")),
            P(None, ("dp", "ctx"), "tensor"),
            P("tensor", ("dp", "ctx")),
            P(None, "tensor"),
            P(("dp", "ctx")),
            P(("dp", "ctx"), None),
            P(None, ("dp", "ctx"), "tensor"),
            P(None, "tensor", ("dp", "ctx")),
            P("dp", "ctx", None),
        ),
        out_specs=(
            P("dp", "ctx", None),
            P("dp", "ctx", None),
            P(("dp", "ctx")),
            P(None, ("dp", "ctx"), "tensor"),
            P("tensor", ("dp", "ctx")),
            P(None, "tensor"),
            P(("dp", "ctx")),
            P(("dp", "ctx"), None),
            P(None, ("dp", "ctx"), "tensor"),
            P(None, "tensor", ("dp", "ctx")),
        ),
        check_vma=False,
    )
```

```python
import functools

import jax
import jax.numpy as jnp
import numpy as np
from jax import lax
from jax.experimental import pallas as pl
from jax.experimental.pallas import tpu as pltpu
from jax.sharding import PartitionSpec as P

BUCKETS = 32
MESH = pl.DeviceIdType.MESH
BF = jnp.bfloat16
F32 = jnp.float32


bucket_edges = np.ceil(16.0 * 8.0 ** (np.arange(1, 16) / 16.0)).astype(np.int32)
bucket_starts = [int(n) for n in range(17)] + [int(n) for n in bucket_edges]


QT = 256
BAND = 128
C0 = float(np.sqrt(2.0 / np.pi))
C1 = 0.044715


def mm(a, b):
    return jnp.dot(a, b, preferred_element_type=F32)


def mm_nt(a, b):
    return lax.dot_general(a, b, (((1,), (1,)), ((), ())), preferred_element_type=F32)


def mm_tn(a, b):
    return lax.dot_general(a, b, (((0,), (0,)), ((), ())), preferred_element_type=F32)


def remote(src, dst, send, recv, device):
    return pltpu.make_async_remote_copy(
        src_ref=src,
        dst_ref=dst,
        send_sem=send,
        recv_sem=recv,
        device_id=device,
        device_id_type=MESH,
    )


def block(start, size, whole=128):
    return pl.ds(pl.multiple_of(start, whole), size)


class Place:
    def __init__(self):
        dp, cx, t = lax.axis_index("dp"), lax.axis_index("ctx"), lax.axis_index("tensor")
        self.dp, self.cx, self.t = dp, cx, t
        self.yy, self.core = lax.div(t, 2), lax.rem(t, 2)
        self.partner = (dp, 1 - cx, t)
        self.sibling = (dp, cx, t + 1 - 2 * self.core)
        self.across = (dp, cx, lax.rem(t + 2, 4))
        self.tensor_peers = [(dp, cx, lax.rem(t + k, 4)) for k in (1, 2, 3)]
        self.z_peers = [(lax.rem(dp + k, 4), cx, t) for k in (1, 2, 3)]
        self.spot = dp + cx * (7 - 2 * dp)
        self.right = self.at_spot(1)
        self.left = self.at_spot(-1)

    def at_spot(self, away):
        spot = lax.rem(self.spot + 8 + away, 8)
        cx = lax.div(spot, 4)
        return (spot + cx * (7 - 2 * spot), cx, self.t)

    def slab(self, away):
        dp, cx, _ = self.at_spot(away)
        return dp * 2 + cx

    def greet(self):
        barrier = pltpu.get_barrier_semaphore()
        peers = self.z_peers + [self.partner] + self.tensor_peers
        for peer in peers:
            pl.semaphore_signal(barrier, inc=1, device_id=peer, device_id_type=MESH)
        pl.semaphore_wait(barrier, len(peers))


class Ring:
    def __init__(self, place, send_sems, recv_sems):
        self.place, self.send_sems, self.recv_sems = place, send_sems, recv_sems

    def copy(self, d, e, s, src, dst):
        at = (d, e, s - 1)
        device = self.place.right if d == 0 else self.place.left
        return remote(src, dst, self.send_sems.at[at], self.recv_sems.at[at], device)


class TensorSum:
    def __init__(self, place, seg, cbuf, ysend, ybuf, kept, c_s, c_r, y_s, y_r, a_s, a_r):
        self.place, self.seg = place, seg
        self.slot = (0, 1, 1, 1)
        self.half, self.quarter = seg // 2, seg // 4
        self.cbuf, self.ysend, self.ybuf, self.kept = cbuf, ysend, ybuf, kept
        self.c_s, self.c_r, self.y_s, self.y_r, self.a_s, self.a_r = c_s, c_r, y_s, y_r, a_s, a_r

    def rows(self, m, c, y):
        return block(m * self.seg + c * self.half + y * self.quarter, self.quarter)

    def own_rows(self, m):
        return self.rows(m, self.place.core, self.place.yy)

    def c_copy(self, m, j, src):
        rows = block(m * self.seg + (1 - self.place.core) * self.half, self.half)
        return remote(
            src.at[rows], self.cbuf.at[m, self.slot[j]], self.c_s.at[m, j], self.c_r.at[m, j],
            self.place.sibling,
        )

    def y_copy(self, m, j):
        return remote(
            self.ysend.at[m, self.slot[j]], self.ybuf.at[m, self.slot[j]], self.y_s.at[m, j], self.y_r.at[m, j],
            self.place.across,
        )

    def to_quarters(self, m, j, src):
        self.c_copy(m, j, src).wait_recv()
        yy, core = self.place.yy, self.place.core
        near, far = block(yy * self.quarter, self.quarter), block((1 - yy) * self.quarter, self.quarter)
        other = src[self.rows(m, core, 1 - yy), :].astype(F32)
        self.ysend[m, self.slot[j]] = (other + self.cbuf[m, self.slot[j], far, :].astype(F32)).astype(BF)
        self.y_copy(m, j).start()
        mine = src[self.rows(m, core, yy), :].astype(F32)
        self.kept[m, self.slot[j]] = mine + self.cbuf[m, self.slot[j], near, :].astype(F32)

    def total(self, m, j):
        self.y_copy(m, j).wait_recv()
        return self.kept[m, self.slot[j]] + self.ybuf[m, self.slot[j]].astype(F32)

    def a_copy(self, m, j, ref, step, own=None):
        yy, core = self.place.yy, self.place.core
        spot = ref.at[self.rows(m, core, 1 - yy if step == 2 else yy)]
        source = spot if own is None or step == 2 else own
        return remote(
            source, spot, self.a_s.at[m, j, step], self.a_r.at[m, j, step],
            self.place.across if step == 0 else self.place.sibling,
        )

    def a_recv(self, m, j, ref, step):
        yy, core = self.place.yy, self.place.core
        spot = ref.at[
            self.rows(m, core if step == 0 else 1 - core, yy if step == 1 else 1 - yy)
        ]
        return remote(
            spot, spot, self.a_s.at[m, j, step], self.a_r.at[m, j, step], self.place.sibling
        )

    def share(self, m, j, ref, own=None):
        self.a_copy(m, j, ref, 0, own).start()
        self.a_copy(m, j, ref, 1, own).start()

    def pass_on(self, m, j, ref):
        self.a_recv(m, j, ref, 0).wait_recv()
        self.a_copy(m, j, ref, 2).start()

    def shared(self, m, j, ref):
        self.a_recv(m, j, ref, 1).wait_recv()
        self.a_recv(m, j, ref, 2).wait_recv()


def low_lanes(shape):
    return lax.rem(lax.broadcasted_iota(jnp.int32, shape, len(shape) - 1), 128) < 64


def head_lanes(h, base=0):
    return slice(base + h * 128, base + (h + 1) * 128)


def fill_bias(bias_ref, band_ref, heads):
    rows = lax.broadcasted_iota(jnp.int32, (BAND, 2 * BAND), 0)
    cols = lax.broadcasted_iota(jnp.int32, (BAND, 2 * BAND), 1)
    away = rows + BAND - cols

    def one_head(h, carry):
        tile = jnp.full((BAND, 2 * BAND), bias_ref[h, 0], F32)
        for b in range(1, BUCKETS):
            tile = jnp.where(away >= bucket_starts[b], bias_ref[h, b], tile)
        band_ref[h] = tile - bias_ref[h, BUCKETS - 1]
        return carry

    lax.fori_loop(0, heads, one_head, 0)


def masked_scores(q_tile, keys, band_ref, scores, h, first, length):
    count = keys.shape[0]
    scores[:, BAND:] = mm_nt(q_tile, keys) * 0.125
    for part in range(QT // BAND):
        spot = (block(part * BAND, BAND), block(first + part * BAND, 2 * BAND))
        scores[spot] = scores[spot] + band_ref[h]
    values = scores[:, BAND:]
    key_pos = lax.broadcasted_iota(jnp.int32, (QT, count), 1)
    query_pos = lax.broadcasted_iota(jnp.int32, (QT, count), 0) + first
    allowed = (key_pos <= query_pos) & (key_pos < length)
    return jnp.where(allowed, values, -1e30), allowed


def bucket_sums(heads, band_sum, whole_sum, dbias):
    rows = lax.broadcasted_iota(jnp.int32, (BAND, 2 * BAND), 0)
    cols = lax.broadcasted_iota(jnp.int32, (BAND, 2 * BAND), 1)
    away = rows + BAND - cols
    bucket = lax.broadcasted_iota(jnp.int32, (BUCKETS, 2 * BAND), 0)
    lanes128 = lax.broadcasted_iota(jnp.int32, (BUCKETS, 128), 1)

    def one_head(h, carry):
        tile = band_sum[h]
        sums = jnp.zeros((BUCKETS, 2 * BAND), F32)
        for b in range(BUCKETS - 1):
            inside = (away >= bucket_starts[b]) & (away < bucket_starts[b + 1])
            row = jnp.sum(jnp.where(inside, tile, 0.0), axis=0, keepdims=True)
            sums = jnp.where(bucket == b, row, sums)
        per_bucket = jnp.sum(sums, axis=1, keepdims=True)
        near = jnp.sum(per_bucket, axis=0, keepdims=True)
        total = jnp.sum(whole_sum[h, 0:1, :], axis=1, keepdims=True)
        last = lax.broadcasted_iota(jnp.int32, (BUCKETS, 1), 0) == BUCKETS - 1
        per_bucket = jnp.where(last, total - near, per_bucket)
        dbias[...] = jnp.where(lanes128 == h, per_bucket, dbias[...])
        return carry

    dbias[...] = jnp.zeros((BUCKETS, 128), F32)
    lax.fori_loop(0, heads, one_head, 0)


def norm_back(x, gain, grad):
    scale = lax.rsqrt(jnp.mean(x * x, axis=-1, keepdims=True) + 1e-06)
    unit = x * scale
    pulled = grad * gain
    inner = jnp.mean(pulled * unit, axis=-1, keepdims=True)
    return scale * (pulled - unit * inner), grad * unit


def layer_kernel(
    heads,
    len_ref,
    bias_ref,
    slot_lanes,
    tok,
    cot,
    qkv,
    out_weight,
    vectors,
    up,
    down_turned,
    result,
    input_grad,
    w_grad,
    qkv_out,
    out_out,
    tiny_out,
    dbias_out,
    w_full,
    wsmall,
    small_grad,
    ws_full,
    ws,
    gains,
    hidden,
    ntwo,
    q3,
    kv,
    lse,
    ab3,
    wbuf,
    gw,
    in_one,
    in_two,
    in_late,
    sx,
    sz,
    sum_grad,
    epart,
    npart,
    ffn,
    probs_ref,
    chosen_ref,
    cbuf,
    ysend,
    ybuf,
    kept,
    hgrad,
    bgrad,
    own_out,
    do3,
    grads,
    dkv_acc,
    dkv,
    band,
    scores,
    spread,
    band_sum,
    whole_sum,
    gg_own,
    gg_in,
    gg_sum,
    tiny_own,
    tiny_t,
    tiny_x,
    tiny_z,
    dbias_own,
    dbias_x,
    dbias_z,
    load_sem,
    out_sem,
    local,
    ready,
    gz_s,
    gz_r,
    gx_s,
    gx_r,
    k_s,
    k_r,
    ag_s,
    ag_r,
    rs_s,
    rs_r,
    c_s,
    c_r,
    y_s,
    y_r,
    a_s,
    a_r,
    kv_s,
    kv_r,
    gg_s,
    gg_r,
    sx_s,
    sx_r,
    sz_s,
    sz_r,
    tt_s,
    tt_r,
    tx_s,
    tx_r,
    tz_s,
    tz_r,
    bx_s,
    bx_r,
    bz_s,
    bz_r,
):
    place = Place()
    dp, cx, t = place.dp, place.cx, place.t
    seg = tok.shape[0] // 2
    width = tok.shape[1]
    shard = width // 8
    experts = up.shape[0]
    span = kv.shape[2]
    cap = slot_lanes.shape[2]
    ahead = low_lanes((shard, 128))

    def packed(base, a, b):
        turned = jnp.where(ahead, a[:, 0:128], pltpu.roll(b[:, 0:128], 64, 1))
        wsmall[0:shard, base : base + 128] = turned.astype(BF)
        turned = jnp.where(ahead, pltpu.roll(a[:, 0:128], 64, 1), b[:, 0:128])
        wsmall[0:shard, base + 128 : base + 256] = turned.astype(BF)
        last = jnp.concatenate([a[:, 128:192], b[:, 128:192]], axis=1)
        wsmall[0:shard, base + 256 : base + 384] = last.astype(BF)

    def unpacked(base):
        one, two, three = (small_grad[:, base + i * 128 : base + i * 128 + 128] for i in range(3))
        first = jnp.where(ahead, one, pltpu.roll(two, 64, 1))
        second = jnp.where(ahead, pltpu.roll(one, 64, 1), two)
        return first, three[:, 0:64], second, pltpu.roll(three, 64, 1)[:, 0:64]

    packed(0, qkv[1].astype(F32), qkv[2].astype(F32))
    packed(span, qkv[0].astype(F32), jnp.transpose(out_weight[...].astype(F32)))
    wsmall[shard:, :] = vectors[...]
    place.greet()
    gather_ring = Ring(place, ag_s, ag_r)
    reduce_ring = Ring(place, rs_s, rs_r)
    sums = TensorSum(place, seg, cbuf, ysend, ybuf, kept, c_s, c_r, y_s, y_r, a_s, a_r)
    bpart = epart
    earlier = bgrad

    def small_slab(k, c):
        return lax.rem(dp + 4 - k, 4) * 2 + c

    def gz_copy(k, slab):
        return remote(
            wsmall, ws_full.at[slab], gz_s.at[k - 1], gz_r.at[k - 1], place.z_peers[k - 1]
        )

    def gx_copy(k, c):
        spot = ws_full.at[small_slab(k, c)]
        return remote(wsmall if k == 0 else spot, spot, gx_s.at[k], gx_r.at[k], place.partner)

    small_own = pltpu.make_async_copy(wsmall, ws_full.at[small_slab(0, cx)], local.at[2 * experts])

    def gather(d, e, s, sending):
        away = s - 1 if sending else s
        slab = place.slab(-away if d == 0 else away)
        if s == 1:
            spots = [w_full.at[e, j, slab] for j in range(2)]
            sources = [up.at[e], down_turned.at[e]] if sending else spots
            return [
                gather_ring.copy(d, e, at, source, spot)
                for at, source, spot in zip((1, 5), sources, spots)
            ]
        spot = w_full.at[e, d, slab] if s == 4 else w_full.at[e, :, slab]
        return [gather_ring.copy(d, e, s, spot, spot)]

    def w_own(e):
        spots = [w_full.at[e, j, place.slab(0)] for j in range(2)]
        return [
            pltpu.make_async_copy(source, spot, local.at[e * 2 + j])
            for j, (source, spot) in enumerate(zip((up.at[e], down_turned.at[e]), spots))
        ]

    def gather_step(e, s):
        for d in range(2):
            if s > 1:
                for copy in gather(d, e, s - 1, False):
                    copy.wait_recv()
            for copy in gather(d, e, s, True):
                copy.start()

    def landing(d, e, s):
        if s == 1:
            return in_one.at[d, e]
        if s == 2:
            return in_two.at[d, e]
        if e < 2:
            return in_late.at[s - 3, d, e]
        return wbuf.at[e, pl.ds(d * 4 + (s - 3) * 2, 2)]

    def reduce_copy(d, e, s):
        slab = place.slab(5 - s if d == 0 else s - 5)
        src = gw.at[e, d, slab] if s == 1 else gw.at[e, :, slab]
        return reduce_ring.copy(d, e, s, src, landing(d, e, s))

    def reduce_step(e, s):
        for d in range(2):
            if s > 1:
                slab = place.slab(5 - s if d == 0 else s - 5)
                reduce_copy(d, e, s - 1).wait_recv()
                came = landing(d, e, s - 1)

                def add(i, carry):
                    rows = block(i * 16, 16, 16)
                    if s == 2:
                        total = gw[e, d, slab, rows, :].astype(F32) + came[rows, :].astype(F32)
                        gw[e, d, slab, rows, :] = total.astype(BF)
                    else:
                        total = gw[e, :, slab, rows, :].astype(F32) + came[:, rows, :].astype(F32)
                        gw[e, :, slab, rows, :] = total.astype(BF)
                    return carry

                lax.fori_loop(0, shard // 16, add, 0)
            reduce_copy(d, e, s).start()

    def reduce_end(e):
        for d in range(2):
            reduce_copy(d, e, 4).wait_recv()

        def add(i, carry):
            rows = block(i * 16, 16, 16)
            total = gw[e, :, place.slab(0), rows, :].astype(F32)
            for d in range(2):
                total = total + landing(d, e, 4)[:, rows, :].astype(F32)
            w_grad[e, :, rows, :] = total
            return carry

        lax.fori_loop(0, shard // 16, add, 0)

    late = [(1, 4), (3, 2), (2, 3), (3, 3), (2, 4), (3, 4)]

    def pump_late(count=1):
        for _ in range(count):
            if late:
                reduce_step(*late.pop(0))

    def tok_copy(m):
        rows = sums.own_rows(m)
        return remote(tok.at[rows], earlier.at[rows], k_s.at[m], k_r.at[m], place.partner)

    @pl.when(cx == 0)
    def _():
        for m in range(2):
            tok_copy(m).start()

    small_own.start()
    for k in (1, 3, 2):
        gz_copy(k, small_slab(0, cx)).start()
    gx_copy(0, cx).start()
    for e in range(2):
        gather_step(e, 1)
    for e in range(experts):
        for copy in w_own(e):
            copy.start()

    @pl.when(cx == 0)
    def _():
        for m in range(2):
            kv[m, seg:, :] = jnp.zeros((seg, span), BF)

    @pl.when(cx == 1)
    def _():
        for m in range(2):
            tok_copy(m).wait_recv()
            sums.share(m, 4, earlier)

    fill_bias(bias_ref, band, heads)
    spread[...] = jnp.zeros(spread.shape, F32)
    band_sum[...] = jnp.zeros(band_sum.shape, F32)
    whole_sum[...] = jnp.zeros(whole_sum.shape, F32)
    tiny_own[...] = jnp.zeros(tiny_own.shape, F32)
    for k in (1, 3, 2):
        gz_copy(k, small_slab(k, cx)).wait_recv()
        gx_copy(k, cx).start()

    @pl.when(cx == 1)
    def _():
        for m in range(2):
            sums.pass_on(m, 4, earlier)

    small_own.wait()
    for k in range(4):
        gx_copy(k, 1 - cx).wait_recv()
    total = ws_full[0, shard:, :].astype(F32)
    for i in range(1, 8):
        total = total + ws_full[i, shard:, :].astype(F32)
    gains[...] = total
    for i in range(8):
        ws[i * shard : (i + 1) * shard, :] = ws_full[i, 0:shard, :]

    def first_norm(source, rows):
        x = source[rows, :].astype(F32)
        scale = lax.rsqrt(jnp.mean(x * x, axis=-1, keepdims=True) + 1e-06)
        return (x * scale * gains[0:1, :]).astype(BF)

    def project(i, carry):
        rows = block(i * 256, 256)
        m, at = lax.div(i, seg // 256), lax.rem(i, seg // 256) * 256
        x = first_norm(tok, rows)
        kv[m, block(cx * seg + at, 256), :] = mm(x, ws[:, 0:span]).astype(BF)
        part = mm(x, ws[:, span:])
        q3[rows, :] = jnp.where(low_lanes(part.shape), part, 0.0).astype(BF)
        return carry

    def project_earlier(i, carry):
        m, at = lax.div(i, seg // 256), lax.rem(i, seg // 256) * 256
        x = first_norm(earlier, block(i * 256, 256))
        kv[m, block(at, 256), :] = mm(x, ws[:, 0:span]).astype(BF)
        return carry

    lax.fori_loop(0, 2 * seg // 256, project, 0)
    gather_step(0, 2)

    @pl.when(cx == 1)
    def _():
        for m in range(2):
            sums.shared(m, 4, earlier)
        lax.fori_loop(0, 2 * seg // 256, project_earlier, 0)

    gather_step(1, 2)
    gather_step(2, 1)

    def attend(m):
        length = len_ref[m]

        def step(i, carry):
            rows = block(m * seg + i * QT, QT)
            first = cx * seg + i * QT
            lanes128 = lax.broadcasted_iota(jnp.int32, (QT, 128), 1)

            def one_head(h, tops):
                cut = block(h * 128, 128)
                values, allowed = masked_scores(
                    q3[rows, cut], kv[m, :, cut], band, scores, h, first, length
                )
                top = jnp.max(values, axis=-1, keepdims=True)
                raised = jnp.where(allowed, jnp.exp(values - top), 0.0)
                mass = jnp.sum(raised, axis=-1, keepdims=True)
                probs = (raised * (1.0 / mass)).astype(BF)
                part = mm(probs, kv[m, :, cut])
                ab3[rows, cut] = jnp.where(low_lanes(part.shape), 0.0, part).astype(BF)
                return jnp.where(lanes128 == h, top + jnp.log(mass), tops)

            lse[rows, :] = lax.fori_loop(0, heads, one_head, jnp.zeros((QT, 128), F32))
            bpart[rows, :] = mm_nt(ab3[rows, :], ws[:, span:]).astype(BF)
            return carry

        lax.fori_loop(0, seg // QT, step, 0)

    def second_norm(m):
        rows = sums.own_rows(m)
        x = tok[rows, :].astype(F32) + sums.total(m, 3)
        hidden[m] = x
        scale = lax.rsqrt(jnp.mean(x * x, axis=-1, keepdims=True) + 1e-06)
        ntwo[rows, :] = (x * scale * gains[1:2, :]).astype(BF)
        sums.share(m, 3, ntwo)

    for m in range(2):
        attend(m)
        sums.c_copy(m, 3, bpart).start()
        gather_step(m, 3)
        if m == 1:
            second_norm(0)
        sums.to_quarters(m, 3, bpart)
    gather_step(3, 1)
    second_norm(1)
    sums.pass_on(0, 3, ntwo)
    gather_step(0, 4)
    sums.pass_on(1, 3, ntwo)
    gather_step(1, 4)
    gather_step(2, 2)
    gather_step(3, 2)
    for m in range(2):
        sums.shared(m, 3, ntwo)
        sums.c_copy(m, 3, bpart).wait_send()

    router16 = gains[...].astype(BF)

    def upstream_of(rows, m, first):
        spot = lax.broadcasted_iota(jnp.int32, (rows.size, 1), 0) + (cx * seg + first)
        live = (spot < len_ref[m]).astype(F32)
        return live, live * cot[rows, :].astype(F32)

    def choices(m, carry):
        lanes = lax.broadcasted_iota(jnp.int32, (seg, 16), 1)
        chosen = jnp.zeros((seg, 16), F32)
        for e in range(experts):
            inside = put_of(m, e).astype(F32)
            chosen = jnp.where(lanes == e + 2, jnp.sum(inside, axis=1, keepdims=True), chosen)
        chosen_ref[block(m * seg, seg), :] = chosen
        return carry

    def put_of(m, e):
        row = slot_lanes[m, pl.ds(e, 1), :]
        return row == lax.broadcasted_iota(jnp.int32, (seg, cap), 0)

    lax.fori_loop(0, 2, choices, 0)

    def gates(i, carry):
        rows = block(i * 256, 256)
        m = lax.div(i, seg // 256)
        logits = mm_nt(ntwo[rows, :], router16)
        lanes = lax.broadcasted_iota(jnp.int32, (256, 16), 1)
        inside = (lanes >= 2) & (lanes < 2 + experts)
        logits = jnp.where(inside, logits, -1e30)
        top = jnp.max(logits, axis=-1, keepdims=True)
        raised = jnp.where(inside, jnp.exp(logits - top), 0.0)
        probs = raised / jnp.sum(raised, axis=-1, keepdims=True)
        probs_ref[rows, :] = probs
        gate = jnp.sum(probs * chosen_ref[rows, :], axis=-1, keepdims=True)
        live, upstream = upstream_of(rows, m, lax.rem(i, seg // 256) * 256)
        sum_grad[rows, :] = (gate * upstream).astype(BF)
        epart[rows, :] = jnp.zeros((256, width), BF)
        npart[rows, :] = jnp.zeros((256, width), BF)
        return carry

    lax.fori_loop(0, 2 * seg // 256, gates, 0)

    def load(e):
        slot = lax.rem(e, 2)
        return pltpu.make_async_copy(
            w_full.at[e], wbuf.at[pl.ds(slot * 2, 2)], load_sem.at[slot]
        )

    def arrived(e):
        for copy in w_own(e):
            copy.wait()
        for d in range(2):
            gather(d, e, 4, False)[0].wait_recv()
        load(e).start()

    picked, slot_grad, activated, raised_grad = (ffn.at[i] for i in range(4))

    def start_sums():
        for m in range(2):
            sums.c_copy(m, 1, npart).start()
            sums.c_copy(m, 0, epart).start()

    def g(e, s):
        return lambda: gather_step(e, s)

    def r(e, s):
        return lambda: reduce_step(e, s)

    def here(e):
        return lambda: arrived(e)

    before = ([here(0), here(1)], [], [], [])
    between = ([g(2, 3)], [g(2, 4)], [here(3)], [start_sums, r(1, 3)])
    after = ([g(3, 3)], [g(3, 4), r(0, 2), here(2)], [r(1, 2), r(0, 3)], [r(0, 4), r(2, 2)])

    def act_on(e, plan):
        for i, acts in enumerate(plan):
            if acts:

                @pl.when(e == i)
                def _(acts=acts):
                    for act in acts:
                        act()

    def expert(e, carry):
        slot = lax.rem(e, 2)

        def weight(which):
            return wbuf[slot * 2 + which].reshape(width, -1)

        act_on(e, before)
        load(e).wait()

        def one_micro(m, carry):
            rows = block(m * seg, seg)
            slots = block(m * cap, cap)
            put = put_of(m, e).astype(BF)
            chosen_rows = mm_tn(put, ntwo[rows, :]).astype(BF)
            picked[slots, :] = chosen_rows
            slot_part = mm_tn(put, sum_grad[rows, :]).astype(BF)
            slot_grad[slots, :] = slot_part
            raised = mm(chosen_rows, weight(0))
            square = raised * raised
            bent = jnp.tanh(C0 * raised * (1.0 + C1 * square))
            cdf = 0.5 * (1.0 + bent)
            act = (raised * cdf).astype(BF)
            activated[slots, :] = act
            slope = cdf + 0.5 * raised * (1.0 - bent * bent) * (C0 * (1.0 + 3.0 * C1 * square))
            act_grad = mm(slot_part, weight(1))
            back = (act_grad * slope).astype(BF)
            raised_grad[slots, :] = back
            lowered = mm_nt(act, weight(1)).astype(BF)
            epart[rows, :] += mm(put, lowered).astype(BF)
            pulled = mm_nt(back, weight(0)).astype(BF)
            npart[rows, :] += mm(put, pulled).astype(BF)
            return carry

        lax.fori_loop(0, 2, one_micro, 0)
        act_on(e, between)

        def weight_part(i, carry):
            lanes = block(i * 384, 384)
            slabs = pl.ds(i * 4, 4)
            part = mm_tn(picked[:, lanes], raised_grad[...]).astype(BF)
            gw[e, 0, slabs] = part.reshape(4, shard, -1)
            part = mm_tn(slot_grad[:, lanes], activated[...]).astype(BF)
            gw[e, 1, slabs] = part.reshape(4, shard, -1)
            return carry

        lax.fori_loop(0, width // 384, weight_part, 0)
        reduce_step(e, 1)
        act_on(e, after)
        return carry

    lax.fori_loop(0, experts, expert, 0)

    for peer in (place.right, place.left):
        pl.semaphore_signal(ready, inc=1, device_id=peer, device_id_type=MESH)

    @pl.when(cx == 1)
    def _():
        for m in range(2):
            for step in range(3):
                sums.a_copy(m, 4, earlier, step).wait_send()

    ones = jnp.ones((8, width), BF)
    for m in range(2):

        def gate_terms(i, carry):
            rows = block(m * seg + i * 256, 256)
            live, upstream = upstream_of(rows, m, i * 256)
            terms = epart[rows, :].astype(F32) * upstream
            high = terms.astype(BF)
            rest = (terms - high.astype(F32)).astype(BF)
            gg_own[m, :, block(i * 256, 256)] = mm_nt(ones, high) + mm_nt(ones, rest)
            return carry

        sums.y_copy(m, 3).wait_send()
        sums.to_quarters(m, 1, npart)
        lax.fori_loop(0, seg // 256, gate_terms, 0)

    def gg_copy(k):
        return remote(gg_own, gg_in.at[k - 1], gg_s.at[k - 1], gg_r.at[k - 1], place.tensor_peers[k - 1])

    for k in (1, 2, 3):
        gg_copy(k).start()
    pump_late(2)
    pl.semaphore_wait(ready, 2)
    for k in (1, 2, 3):
        gg_copy(k).wait_recv()
    gg_sum[...] = gg_own[...] + gg_in[0] + gg_in[1] + gg_in[2]
    own_first = place.core * (seg // 2) + place.yy * (seg // 4)

    def own_copy(m, j, ref):
        return pltpu.make_async_copy(
            own_out.at[m, j - 1], ref.at[sums.own_rows(m)], out_sem.at[m * 2 + j - 1]
        )

    for m in range(2):
        rows = sums.own_rows(m)
        line = gg_sum[m, :, block(own_first, seg // 4)]
        line = jnp.where(lax.broadcasted_iota(jnp.int32, line.shape, 0) == 0, line, 0.0)
        high = line.astype(BF)
        rest = (line - high.astype(F32)).astype(BF)
        ones = jnp.ones((8, 128), BF)
        gate_grad = (mm_tn(high, ones) + mm_tn(rest, ones))[:, 0:1]
        down = sums.total(m, 1)
        live, upstream = upstream_of(rows, m, own_first)
        probs, chosen = probs_ref[rows, :], chosen_ref[rows, :]
        gate = jnp.sum(probs * chosen, axis=-1, keepdims=True)
        logit_grad = (probs * gate_grad * (chosen - gate)).astype(BF)
        down = down + mm(logit_grad, router16)
        through, gain_terms = norm_back(hidden[m], gains[1:2, :], down)
        full = through + upstream
        hgrad[m] = full
        bgrad[rows, :] = full.astype(BF)
        sums.share(m, 0, bgrad)
        tiny_own[1:2, :] += jnp.sum(gain_terms, axis=0, keepdims=True)
        tiny_own[...] += mm_tn(logit_grad, ntwo[rows, :])[0:8, :]
    pump_late()
    for m in range(2):
        sums.pass_on(m, 0, bgrad)
    for m in range(2):
        sums.to_quarters(m, 0, epart)

    def dkv_copy(m, h):
        spot = dkv.at[m, h]
        return remote(spot, spot, kv_s.at[m, h], kv_r.at[m, h], place.partner)

    def attend_back(m):
        length = len_ref[m]

        def lower(i, carry):
            part = mm(bgrad[block(m * seg + i * 256, 256), :], ws[:, span:])
            part = jnp.where(low_lanes(part.shape), 0.0, part)
            do3[block(i * 256, 256), :] = part.astype(BF)
            return carry

        lax.fori_loop(0, seg // 256, lower, 0)

        def one_head(h, carry):
            cut = block(h * 128, 128)
            dkv_acc[...] = jnp.zeros(dkv_acc.shape, F32)

            def step(i, carry):
                rows = block(m * seg + i * QT, QT)
                first = cx * seg + i * QT
                q_tile, do_tile = q3[rows, cut], do3[block(i * QT, QT), cut]
                keys = kv[m, :, cut]
                values, allowed = masked_scores(q_tile, keys, band, scores, h, first, length)
                lanes128 = lax.broadcasted_iota(jnp.int32, (QT, 128), 1)
                mass = jnp.sum(jnp.where(lanes128 == h, lse[rows, :], 0.0), axis=1, keepdims=True)
                soft = jnp.where(allowed, jnp.exp(values - mass), 0.0)
                soft_grad = mm_nt(do_tile, keys)
                delta = jnp.sum(soft * soft_grad, axis=-1, keepdims=True)
                score_grad = (soft * (soft_grad - delta)).astype(BF)
                dkv_acc[...] += mm_tn(soft.astype(BF), do_tile) + 0.125 * mm_tn(score_grad, q_tile)
                part = mm(score_grad, keys) * 0.125
                grads[rows, block(span + h * 128, 128)] = jnp.where(
                    low_lanes(part.shape), part, 0.0
                ).astype(BF)
                spread[:, BAND:] = score_grad.astype(F32)
                for half in range(QT // BAND):
                    lanes = block(first + half * BAND, 2 * BAND)
                    band_sum[h] += spread[half * BAND : (half + 1) * BAND, lanes]
                whole_sum[h, 0:1, :] += jnp.sum(spread[:, BAND:], axis=0, keepdims=True)
                return carry

            lax.fori_loop(0, seg // QT, step, 0)

            @pl.when(cx == 1)
            def _():
                dkv[m, h] = dkv_acc[0:seg, :].astype(BF)
                dkv_copy(m, h).start()

            grads[pl.ds(m * seg, seg), cut] = dkv_acc[block(cx * seg, seg), :].astype(BF)

            if m == 1:

                @pl.when(h == 2)
                def _():
                    pump_late()

            return carry

        lax.fori_loop(0, heads, one_head, 0)

    def after_attend(m):
        rows = pl.ds(m * seg, seg)

        @pl.when(cx == 0)
        def _():
            for h in range(heads):
                dkv_copy(m, h).wait_recv()
                total = grads[rows, head_lanes(h)].astype(F32) + dkv[m, h].astype(F32)
                grads[rows, head_lanes(h)] = total.astype(BF)

        def lower(i, carry):
            spot = block(m * seg + i * 256, 256)
            npart[spot, :] = mm_nt(grads[spot, :], ws[...]).astype(BF)
            return carry

        lax.fori_loop(0, seg // 256, lower, 0)
        sums.c_copy(m, 2, npart).start()

    def gs_spot(slab, half):
        return ws_full.at[slab, pl.ds(0, shard), pl.ds(half * span, span)]

    def sx_copy(half, k):
        slab = lax.rem(dp + k, 4) * 2 + 1 - cx
        return remote(
            gs_spot(slab, half), sx.at[half, k], sx_s.at[half, k], sx_r.at[half, k], place.partner
        )

    def sz_copy(half, k):
        return remote(
            sx.at[half, k], sz.at[half, k - 1], sz_s.at[half, k - 1], sz_r.at[half, k - 1],
            place.z_peers[k - 1],
        )

    order = (2, 1, 3, 0)

    def small_part(half):
        def step(i, carry):
            lanes = block(i * 384, 384)
            cols = slice(half * span, (half + 1) * span)
            part = mm_tn(ffn[0, :, lanes], grads[0:seg, cols])
            part = part + mm_tn(ffn[1, :, lanes], grads[seg:, cols])
            if half == 1:
                part = part + mm_tn(bgrad[:, lanes], ab3[...])
            ws_full[pl.ds(i * 4, 4), 0:shard, cols] = part.astype(BF).reshape(4, shard, -1)
            return carry

        lax.fori_loop(0, width // 384, step, 0)
        for k in order:
            sx_copy(half, k).start()

    def small_step(half):
        cols = slice(half * span, (half + 1) * span)
        for k in order:
            sx_copy(half, k).wait_recv()
            slab = lax.rem(dp + k, 4) * 2 + cx
            total = ws_full[slab, 0:shard, cols].astype(F32) + sx[half, k].astype(F32)
            if k == 0:
                small_grad[:, cols] = total
            else:
                sx[half, k] = total.astype(BF)
                sz_copy(half, k).start()

    for m in range(2):
        sums.shared(m, 0, bgrad)
        attend_back(m)
        if m == 0:
            for i in range(2):

                def own_result(i):
                    rows = sums.own_rows(i)
                    expert_sum = sums.total(i, 0)
                    spot = lax.broadcasted_iota(jnp.int32, (seg // 4, 1), 0) + (cx * seg + own_first)
                    live = (spot < len_ref[i]).astype(F32)
                    gate = jnp.sum(probs_ref[rows, :] * chosen_ref[rows, :], axis=-1, keepdims=True)
                    own_out[i, 0] = (live * (hidden[i] + gate * expert_sum)).astype(BF)
                    own_copy(i, 1, result).start()
                    sums.share(i, 1, result, own_out.at[i, 0])

                own_result(i)

    def normed_again(i, carry):
        ffn[lax.div(i, 2), block(lax.rem(i, 2) * 256, 256), :] = first_norm(tok, block(i * 256, 256))
        return carry

    lax.fori_loop(0, 2 * seg // 256, normed_again, 0)
    for k in range(4):
        gx_copy(k, cx).wait_send()
    small_part(1)
    sums.c_copy(0, 1, npart).wait_send()
    sums.y_copy(0, 1).wait_send()
    after_attend(0)
    sums.c_copy(1, 1, npart).wait_send()
    sums.y_copy(1, 1).wait_send()
    sums.to_quarters(0, 2, npart)
    after_attend(1)
    small_part(0)
    sums.to_quarters(1, 2, npart)
    pump_late(len(late))

    for m in range(2):
        down = sums.total(m, 2)
        rows = sums.own_rows(m)
        through, gain_terms = norm_back(tok[rows, :].astype(F32), gains[0:1, :], down)
        own_out[m, 1] = (through + hgrad[m]).astype(BF)
        sums.share(m, 2, input_grad, own_out.at[m, 1])
        own_copy(m, 2, input_grad).start()
        tiny_own[0:1, :] += jnp.sum(gain_terms, axis=0, keepdims=True)

    def tt_copy(k):
        return remote(
            tiny_own, tiny_t.at[k - 1], tt_s.at[k - 1], tt_r.at[k - 1], place.tensor_peers[k - 1]
        )

    for k in (1, 2, 3):
        tt_copy(k).start()
    small_step(1)
    small_step(0)
    for k in (1, 2, 3):
        tt_copy(k).wait_recv()
    tiny_x[0] = tiny_own[...] + tiny_t[0] + tiny_t[1] + tiny_t[2]
    tx_copy = remote(tiny_x.at[0], tiny_x.at[1], tx_s.at[0], tx_r.at[0], place.partner)
    tx_copy.start()
    bucket_sums(heads, band_sum, whole_sum, dbias_own)
    bx_copy = remote(dbias_own, dbias_x, bx_s.at[0], bx_r.at[0], place.partner)
    bx_copy.start()
    for m in range(2):
        sums.pass_on(m, 1, result)
        sums.pass_on(m, 2, input_grad)
    tx_copy.wait_recv()
    tiny_x[2] = tiny_x[0] + tiny_x[1]
    bx_copy.wait_recv()
    dbias_sum = dbias_own[...] + dbias_x[...]
    dbias_x[...] = dbias_sum

    def tz_copy(k):
        return remote(
            tiny_x.at[2], tiny_z.at[k - 1], tz_s.at[k - 1], tz_r.at[k - 1], place.z_peers[k - 1]
        )

    def bz_copy(k):
        return remote(
            dbias_x, dbias_z.at[k - 1], bz_s.at[k - 1], bz_r.at[k - 1], place.z_peers[k - 1]
        )

    for k in (1, 2, 3):
        tz_copy(k).start()
        bz_copy(k).start()
    for e in range(experts):
        reduce_end(e)
    for half in range(2):
        cols = slice(half * span, (half + 1) * span)
        total = small_grad[:, cols]
        for k in (1, 2, 3):
            sz_copy(half, k).wait_recv()
            total = total + sz[half, k - 1].astype(F32)
        small_grad[:, cols] = total
    first, first_rest, second, second_rest = unpacked(0)
    qkv_out[1, :, 0:128], qkv_out[1, :, 128:192] = first, first_rest
    qkv_out[2, :, 0:128], qkv_out[2, :, 128:192] = second, second_rest
    first, first_rest, second, second_rest = unpacked(span)
    qkv_out[0, :, 0:128], qkv_out[0, :, 128:192] = first, first_rest
    out_out[0:128, :], out_out[128:192, :] = jnp.transpose(second), jnp.transpose(second_rest)
    for k in (1, 2, 3):
        bz_copy(k).wait_recv()
        bz_copy(k).wait_send()
        dbias_sum = dbias_sum + dbias_z[k - 1]
    dbias_out[...] = jnp.transpose(dbias_sum)[0:8, :]
    total = tiny_x[2]
    for k in (1, 2, 3):
        tz_copy(k).wait_recv()
        total = total + tiny_z[k - 1]
    tiny_out[...] = total
    for m in range(2):
        sums.shared(m, 1, result)
        sums.shared(m, 2, input_grad)

    for e in range(experts):
        for d in range(2):
            for s in (1, 2, 3, 4):
                for copy in gather(d, e, s, True):
                    copy.wait_send()
                reduce_copy(d, e, s).wait_send()
    for k in range(4):
        for half in range(2):
            sx_copy(half, k).wait_send()
            if k > 0:
                sz_copy(half, k).wait_send()
        if k > 0:
            gz_copy(k, small_slab(0, cx)).wait_send()
            gg_copy(k).wait_send()
            tt_copy(k).wait_send()
            tz_copy(k).wait_send()
    tx_copy.wait_send()
    bx_copy.wait_send()
    for m in range(2):
        sums.c_copy(m, 0, epart).wait_send()
        sums.c_copy(m, 2, npart).wait_send()
        own_copy(m, 1, result).wait()
        own_copy(m, 2, input_grad).wait()
        sums.y_copy(m, 0).wait_send()
        sums.y_copy(m, 2).wait_send()
        for j in range(4):
            for step in range(3):
                own = own_out.at[m, j - 1] if j in (1, 2) else None
                ref = (bgrad, result, input_grad, ntwo)[j]
                sums.a_copy(m, j, ref, step, own).wait_send()

        @pl.when(cx == 0)
        def _():
            tok_copy(m).wait_send()

        @pl.when(cx == 1)
        def _():
            for h in range(heads):
                dkv_copy(m, h).wait_send()


def layer_call(lengths, bias, slot_lanes, tok, cot, qkv, out_weight, vectors, up, down_turned):
    heads = bias.shape[0]
    rows, width = tok.shape
    span = heads * 128
    experts, ff = up.shape[0], up.shape[2]
    seg = rows // 2
    quarter = seg // 4
    shard = width // 8
    slots = 2 * slot_lanes.shape[2]
    vm = pl.BlockSpec(memory_space=pltpu.VMEM)
    sm = pl.BlockSpec(memory_space=pltpu.SMEM)
    hbm = pl.BlockSpec(memory_space=pl.ANY)
    dma = pltpu.SemaphoreType.DMA
    sds = jax.ShapeDtypeStruct
    low, full = (lambda *shape: pltpu.VMEM(shape, BF)), (lambda *shape: pltpu.VMEM(shape, F32))

    def pair(*shape):
        return [dma(shape), dma(shape)]

    return pl.pallas_call(
        functools.partial(layer_kernel, heads),
        out_shape=(
            sds((rows, width), BF),
            sds((rows, width), BF),
            sds((experts, 2, shard, ff), F32),
            sds(qkv.shape, F32),
            sds(out_weight.shape, F32),
            sds((8, width), F32),
            sds((8, BUCKETS), F32),
            sds((experts, 2, 8, shard, ff), BF),
        ),
        in_specs=[sm, sm] + [vm] * 6 + [hbm] * 2,
        out_specs=(hbm,) * 2 + (vm,) * 5 + (hbm,),
        scratch_shapes=[
            low(shard + 16, width),
            full(shard, width),
            low(8, shard + 16, width),
            low(width, width),
            full(16, width),
            full(2, quarter, width),
            low(rows, width),
            low(rows, span),
            low(2, rows, span),
            full(rows, 128),
            low(rows, span),
            low(4, 8, shard, ff),
            low(experts, 2, 8, shard, ff),
            low(2, experts, shard, ff),
            low(2, experts, 2, shard, ff),
            low(2, 2, 2, 2, shard, ff),
            low(2, 4, shard, span),
            low(2, 3, shard, span),
            low(rows, width),
            low(rows, width),
            low(rows, width),
            low(4, slots, width),
            full(rows, 16),
            full(rows, 16),
            low(2, 2, 2 * quarter, width),
            low(2, 2, quarter, width),
            low(2, 2, quarter, width),
            full(2, 2, quarter, width),
            full(2, quarter, width),
            low(rows, width),
            low(2, 2, quarter, width),
            low(seg, span),
            low(rows, 2 * span),
            full(rows, 128),
            low(2, heads, seg, 128),
            full(heads, BAND, 2 * BAND),
            full(QT, rows + BAND),
            full(QT, rows + BAND),
            full(heads, BAND, 2 * BAND),
            full(heads, 8, rows),
            full(2, 8, seg),
            full(3, 2, 8, seg),
            full(2, 8, seg),
            full(8, width),
            full(3, 8, width),
            full(3, 8, width),
            full(3, 8, width),
            full(BUCKETS, 128),
            full(BUCKETS, 128),
            full(3, BUCKETS, 128),
            dma((2,)),
            dma((4,)),
            dma((2 * experts + 1,)),
            pltpu.SemaphoreType.REGULAR,
        ]
        + pair(3)
        + pair(4)
        + pair(2)
        + pair(2, experts, 5)
        + pair(2, experts, 4)
        + pair(2, 4)
        + pair(2, 4)
        + pair(2, 5, 3)
        + pair(2, heads)
        + pair(3)
        + pair(2, 4)
        + pair(2, 3)
        + pair(3)
        + pair(1)
        + pair(3)
        + pair(1)
        + pair(3),
        compiler_params=pltpu.CompilerParams(
            collective_id=0, has_side_effects=True, vmem_limit_bytes=63 << 20
        ),
    )(lengths, bias, slot_lanes, tok, cot, qkv, out_weight, vectors, up, down_turned)


def body_fast(
    inputs, lengths, expert_ids, slot_rows, attn_gain, qkv_weight, out_weight, position_bias,
    ffn_gain, router_weight, up_weight, down_weight, cotangent,
):
    micro, seg, width = inputs.shape
    rows = micro * seg
    experts = up_weight.shape[0]
    heads = position_bias.shape[1]
    slab = lax.axis_index("dp") * 2 + lax.axis_index("ctx")
    shard = attn_gain.shape[0]
    small = jnp.concatenate(
        [attn_gain[None], ffn_gain[None], router_weight.T, jnp.zeros((10, shard), BF)], axis=0
    )
    small = lax.dynamic_update_slice(jnp.zeros((16, width), BF), small, (0, slab * shard))
    result, input_part, w_grad, qkv_grad, out_grad, tiny, dbias, _ = layer_call(
        lengths, position_bias.T, slot_rows.reshape(micro, experts, -1), inputs.reshape(rows, width),
        cotangent.reshape(rows, width), qkv_weight, out_weight, small, up_weight,
        jnp.transpose(down_weight, (0, 2, 1)),
    )
    tiny = lax.dynamic_slice_in_dim(tiny, slab * shard, shard, axis=1)
    return (
        result.reshape(inputs.shape),
        input_part.reshape(inputs.shape),
        tiny[0],
        qkv_grad,
        out_grad,
        dbias[:heads].T,
        tiny[1],
        tiny[2 : 2 + experts].T,
        w_grad[:, 0],
        jnp.transpose(w_grad[:, 1], (0, 2, 1)),
    )


def rms_norm(values, gain_vector):
    return (
        values * lax.rsqrt(jnp.mean(values * values, axis=-1, keepdims=True) + 1e-06) * gain_vector
    )


def bucket_of(distance):
    clipped = jnp.maximum(distance, 0)
    edge_values = jnp.asarray(bucket_edges, dtype=jnp.int32)
    beyond = jnp.sum((clipped[..., None] >= edge_values).astype(jnp.int32), axis=-1)
    return jnp.where(clipped < 16, clipped, jnp.minimum(16 + beyond, 31))


def toeplitz(diagonal, query_count, key_count):
    head_count = diagonal.shape[0]
    padded = jnp.pad(diagonal, ((0, 0), (0, 1)))
    row_width = query_count + key_count
    repeated = jnp.broadcast_to(padded[:, None, :], (head_count, query_count, row_width)).reshape(
        head_count, query_count * row_width
    )
    repeated = jnp.pad(repeated, ((0, 0), (0, query_count))).reshape(
        head_count, query_count, row_width + 1
    )[:, :, :key_count]
    return repeated[:, :, ::-1]


def diagonal_sums(gradient):
    head_count, query_count, key_count = gradient.shape
    offset_count = query_count + key_count - 1
    flipped = jnp.pad(gradient[:, :, ::-1], ((0, 0), (0, 0), (0, query_count)))
    skewed = flipped.reshape(head_count, query_count * (offset_count + 1))[
        :, : query_count * offset_count
    ]
    return jnp.sum(skewed.reshape(head_count, query_count, offset_count), axis=1)


def bucket_table(query_first, query_count, key_count):
    offsets = (
        query_first - (key_count - 1) + jnp.arange(query_count + key_count - 1, dtype=jnp.int32)
    )
    return (bucket_of(offsets)[:, None] == jnp.arange(BUCKETS, dtype=jnp.int32)[None, :]).astype(
        jnp.float32
    )


def body(
    inputs,
    lengths,
    expert_ids,
    slot_rows,
    attn_gain,
    qkv_weight,
    out_weight,
    position_bias,
    ffn_gain,
    router_weight,
    up_weight,
    down_weight,
    cotangent,
):
    highest = lax.Precision.HIGHEST
    micro_count, seg_rows, model_width = inputs.shape
    local_heads = position_bias.shape[1]
    head_size = qkv_weight.shape[2] // local_heads
    expert_count = up_weight.shape[0]
    query_first = lax.axis_index("ctx") * seg_rows
    query_pos = query_first + jnp.arange(seg_rows, dtype=jnp.int32)

    def pair_scores(query_heads, query_start, key_heads, length):
        query_count = query_heads.shape[0]
        key_count = key_heads.shape[0]
        scores = (
            jnp.einsum("qhd,khd->hqk", query_heads, key_heads, preferred_element_type=jnp.float32)
            * 0.125
        )
        diagonal = jnp.einsum(
            "rb,bh->hr",
            bucket_table(query_start, query_count, key_count),
            position_bias,
            precision=highest,
        )
        scores = scores + toeplitz(diagonal, query_count, key_count)
        query_place = query_start + jnp.arange(query_count, dtype=jnp.int32)
        key_place = jnp.arange(key_count, dtype=jnp.int32)
        allowed = (key_place[None, :] <= query_place[:, None]) & (key_place[None, :] < length)
        return (scores, allowed)

    def scores_for(query_heads, key_block, length):
        key_count = key_block.shape[0]
        key_heads = key_block.reshape(key_count, local_heads, head_size)
        scores, allowed = pair_scores(query_heads, query_first, key_heads, length)
        return (scores, allowed, key_heads)

    results = []
    input_parts = []
    grad_sums = None
    bias_total = jnp.zeros((local_heads, BUCKETS), jnp.float32)
    for micro_step in range(micro_count):
        forward_gain_one = lax.all_gather(attn_gain, ("dp", "ctx"), axis=0, tiled=True)
        forward_qkv_full = lax.all_gather(qkv_weight, ("dp", "ctx"), axis=1, tiled=True)
        forward_out_full = lax.all_gather(out_weight, ("dp", "ctx"), axis=1, tiled=True)
        forward_gain_two = lax.all_gather(ffn_gain, ("dp", "ctx"), axis=0, tiled=True)
        forward_router_full = lax.all_gather(router_weight, ("dp", "ctx"), axis=0, tiled=True)
        forward_up_full = lax.all_gather(up_weight, ("dp", "ctx"), axis=1, tiled=True)
        forward_down_full = lax.all_gather(down_weight, ("dp", "ctx"), axis=2, tiled=True)
        forward_tokens = inputs[micro_step].astype(jnp.float32)
        forward_length = lengths[micro_step]
        forward_normed = rms_norm(forward_tokens, forward_gain_one.astype(jnp.float32)).astype(
            jnp.bfloat16
        )
        forward_projected = jnp.einsum(
            "td,cde->cte", forward_normed, forward_qkv_full, preferred_element_type=jnp.float32
        ).astype(jnp.bfloat16)
        forward_query_heads = forward_projected[0].reshape(seg_rows, local_heads, head_size)
        row_top = jnp.full((local_heads, seg_rows), -1e30, jnp.float32)
        attend_scores, attend_allowed, attend_key_heads = scores_for(
            forward_query_heads,
            lax.all_gather(forward_projected[1], "ctx", axis=0, tiled=True),
            forward_length,
        )
        value_heads = lax.all_gather(forward_projected[2], "ctx", axis=0, tiled=True).reshape(
            attend_key_heads.shape
        )
        attend_scores = jnp.where(attend_allowed[None], attend_scores, -1e30)
        new_top = jnp.maximum(row_top, jnp.max(attend_scores, axis=-1))
        weights_exp = jnp.where(
            attend_allowed[None], jnp.exp(attend_scores - new_top[:, :, None]), 0.0
        )
        row_total = jnp.sum(weights_exp, axis=-1)
        summed = jnp.einsum(
            "hqk,khd->hqd",
            weights_exp.astype(jnp.bfloat16),
            value_heads,
            preferred_element_type=jnp.float32,
        )
        row_top, row_total, summed = (new_top, row_total, summed)
        forward_attended = summed / row_total[:, :, None]
        forward_log_total = row_top + jnp.log(row_total)
        forward_attended_low = (
            jnp.transpose(forward_attended, (1, 0, 2)).reshape(seg_rows, -1).astype(jnp.bfloat16)
        )
        branch = lax.psum(
            jnp.dot(
                forward_attended_low, forward_out_full, preferred_element_type=jnp.float32
            ).astype(jnp.bfloat16),
            "tensor",
        ).astype(jnp.float32)
        forward_hidden = forward_tokens + branch
        forward_normed_two = rms_norm(forward_hidden, forward_gain_two.astype(jnp.float32)).astype(
            jnp.bfloat16
        )
        logits = jnp.dot(
            forward_normed_two, forward_router_full, preferred_element_type=jnp.float32
        )
        forward_router_probs = jax.nn.softmax(logits, axis=-1)
        forward_chosen = (
            expert_ids[micro_step][:, None] == jnp.arange(expert_count, dtype=jnp.int32)[None, :]
        ).astype(jnp.float32)
        forward_gate_value = jnp.sum(forward_router_probs * forward_chosen, axis=-1)
        forward_slot_table = slot_rows[micro_step, 0]
        padded = jnp.concatenate(
            [forward_normed_two, jnp.zeros((1, model_width), jnp.bfloat16)], axis=0
        )
        forward_picked = padded[forward_slot_table]
        forward_raised = jnp.einsum(
            "ekd,edf->ekf", forward_picked, forward_up_full, preferred_element_type=jnp.float32
        )
        forward_activated = jax.nn.gelu(forward_raised).astype(jnp.bfloat16)
        lowered = jnp.einsum(
            "ekf,efd->ekd", forward_activated, forward_down_full, preferred_element_type=jnp.float32
        )
        spread = (
            jnp.zeros((seg_rows + 1, model_width), jnp.float32)
            .at[forward_slot_table.reshape(-1)]
            .add(lowered.reshape(-1, model_width))[:seg_rows]
        )
        forward_expert_sum = lax.psum(spread.astype(jnp.bfloat16), "tensor").astype(jnp.float32)
        forward_live_rows = (query_pos < forward_length).astype(jnp.float32)[:, None]
        result = (
            forward_live_rows * (forward_hidden + forward_gate_value[:, None] * forward_expert_sum)
        ).astype(jnp.bfloat16)
        forward_kept_state = (
            forward_tokens,
            forward_length,
            forward_normed,
            forward_projected,
            forward_attended,
            forward_log_total,
            forward_attended_low,
            forward_hidden,
            forward_normed_two,
            forward_router_probs,
            forward_chosen,
            forward_gate_value,
            forward_slot_table,
            forward_picked,
            forward_raised,
            forward_activated,
            forward_expert_sum,
            forward_live_rows,
        )
        result, kept_state = (result, forward_kept_state)
        gain_one = lax.all_gather(attn_gain, ("dp", "ctx"), axis=0, tiled=True)
        qkv_full = lax.all_gather(qkv_weight, ("dp", "ctx"), axis=1, tiled=True)
        out_full = lax.all_gather(out_weight, ("dp", "ctx"), axis=1, tiled=True)
        gain_two = lax.all_gather(ffn_gain, ("dp", "ctx"), axis=0, tiled=True)
        router_full = lax.all_gather(router_weight, ("dp", "ctx"), axis=0, tiled=True)
        up_full = lax.all_gather(up_weight, ("dp", "ctx"), axis=1, tiled=True)
        down_full = lax.all_gather(down_weight, ("dp", "ctx"), axis=2, tiled=True)
        (
            tokens,
            backward_length,
            normed,
            projected,
            attended,
            log_total,
            attended_low,
            hidden,
            normed_two,
            router_probs,
            chosen,
            gate_value,
            slot_table,
            picked,
            raised,
            activated,
            expert_sum,
            live_rows,
        ) = kept_state
        upstream = live_rows * cotangent[micro_step].astype(jnp.float32)
        sum_grad = (gate_value[:, None] * upstream).astype(jnp.bfloat16)
        gate_grad = jnp.sum(expert_sum * upstream, axis=-1)
        logit_grad = (router_probs * gate_grad[:, None] * (chosen - gate_value[:, None])).astype(
            jnp.bfloat16
        )
        router_part = jnp.einsum(
            "td,te->de", normed_two, logit_grad, preferred_element_type=jnp.float32
        )
        padded_grad = jnp.concatenate([sum_grad, jnp.zeros((1, model_width), jnp.bfloat16)], axis=0)
        slot_grad = padded_grad[slot_table]
        down_part = jnp.einsum(
            "ekf,ekd->efd", activated, slot_grad, preferred_element_type=jnp.float32
        )
        act_grad = jnp.einsum(
            "ekd,efd->ekf", slot_grad, down_full, preferred_element_type=jnp.float32
        )
        unused_value, gelu_back = jax.vjp(jax.nn.gelu, raised)
        raised_grad = gelu_back(act_grad)[0].astype(jnp.bfloat16)
        up_part = jnp.einsum(
            "ekd,ekf->edf", picked, raised_grad, preferred_element_type=jnp.float32
        )
        picked_grad = jnp.einsum(
            "ekf,edf->ekd", raised_grad, up_full, preferred_element_type=jnp.float32
        )
        spread_grad = (
            jnp.zeros((seg_rows + 1, model_width), jnp.float32)
            .at[slot_table.reshape(-1)]
            .add(picked_grad.reshape(-1, model_width))[:seg_rows]
        )
        normed_two_grad = lax.psum(spread_grad.astype(jnp.bfloat16), "tensor").astype(
            jnp.float32
        ) + jnp.einsum("te,de->td", logit_grad, router_full, preferred_element_type=jnp.float32)
        unused_norm, second_back = jax.vjp(rms_norm, hidden, gain_two.astype(jnp.float32))
        hidden_grad, gain_two_part = second_back(normed_two_grad)
        hidden_grad = hidden_grad + upstream
        branch_grad = hidden_grad.astype(jnp.bfloat16)
        out_part = jnp.einsum(
            "te,td->ed", attended_low, branch_grad, preferred_element_type=jnp.float32
        )
        attended_grad = jnp.einsum(
            "td,ed->te", branch_grad, out_full, preferred_element_type=jnp.float32
        ).astype(jnp.bfloat16)
        grad_heads = attended_grad.reshape(seg_rows, local_heads, head_size)
        row_delta = jnp.sum(
            jnp.transpose(grad_heads.astype(jnp.float32), (1, 0, 2)) * attended, axis=-1
        )
        backward_query_heads = projected[0].reshape(seg_rows, local_heads, head_size)
        bias_zero = jnp.zeros((local_heads, BUCKETS), jnp.float32)
        attend_bias_acc = bias_zero
        bias_acc = attend_bias_acc
        score_scores, score_allowed, score_key_heads = scores_for(
            backward_query_heads,
            lax.all_gather(projected[1], "ctx", axis=0, tiled=True),
            backward_length,
        )
        score_value_heads = lax.all_gather(projected[2], "ctx", axis=0, tiled=True).reshape(
            score_key_heads.shape
        )
        score_key_count = score_key_heads.shape[0]
        soft_weights = jnp.where(
            score_allowed[None], jnp.exp(score_scores - log_total[:, :, None]), 0.0
        )
        weight_grad = jnp.einsum(
            "qhd,khd->hqk", grad_heads, score_value_heads, preferred_element_type=jnp.float32
        )
        score_grad = (soft_weights * (weight_grad - row_delta[:, :, None])).astype(jnp.bfloat16)
        query_acc = jnp.einsum(
            "hqk,khd->qhd", score_grad, score_key_heads, preferred_element_type=jnp.float32
        )
        bias_acc = bias_acc + jnp.dot(
            diagonal_sums(score_grad.astype(jnp.float32)),
            bucket_table(query_first, seg_rows, score_key_count),
            precision=highest,
        )
        (
            (attend_query_acc, attend_bias_acc),
            attend_soft_weights,
            attend_score_grad,
            attend_key_count,
        ) = ((query_acc, bias_acc), soft_weights, score_grad, score_key_count)
        key_term = (
            jnp.einsum(
                "hqk,qhd->khd",
                attend_score_grad,
                backward_query_heads,
                preferred_element_type=jnp.float32,
            )
            * 0.125
        )
        value_term = jnp.einsum(
            "hqk,qhd->khd",
            attend_soft_weights.astype(jnp.bfloat16),
            grad_heads,
            preferred_element_type=jnp.float32,
        )
        grad_term = jnp.stack(
            [key_term.reshape(attend_key_count, -1), value_term.reshape(attend_key_count, -1)],
            axis=1,
        )
        key_value_acc = grad_term
        query_acc, key_value_acc, bias_part = (attend_query_acc, key_value_acc, attend_bias_acc)
        own_grads = lax.psum_scatter(
            key_value_acc.astype(jnp.bfloat16), "ctx", scatter_dimension=0, tiled=True
        ).astype(jnp.float32)
        query_grad = (query_acc * 0.125).reshape(seg_rows, -1).astype(jnp.bfloat16)
        qkv_grad = jnp.stack(
            [
                query_grad,
                own_grads[:, 0].astype(jnp.bfloat16),
                own_grads[:, 1].astype(jnp.bfloat16),
            ],
            axis=0,
        )
        qkv_part = jnp.einsum("td,cte->cde", normed, qkv_grad, preferred_element_type=jnp.float32)
        normed_grad = lax.psum(
            jnp.einsum(
                "cte,cde->td", qkv_grad, qkv_full, preferred_element_type=jnp.float32
            ).astype(jnp.bfloat16),
            "tensor",
        ).astype(jnp.float32)
        unused_first, first_back = jax.vjp(rms_norm, tokens, gain_one.astype(jnp.float32))
        token_grad, gain_one_part = first_back(normed_grad)
        input_part = (token_grad + hidden_grad).astype(jnp.bfloat16)
        weight_parts = (
            gain_one_part,
            qkv_part,
            out_part,
            gain_two_part,
            router_part,
            up_part,
            down_part,
        )
        input_part, weight_parts, bias_part = (input_part, weight_parts, bias_part)
        results.append(result)
        input_parts.append(input_part)
        grad_sums = (
            weight_parts
            if grad_sums is None
            else tuple((old_sum + new_part for old_sum, new_part in zip(grad_sums, weight_parts)))
        )
        bias_total = bias_total + bias_part
    reduced = (
        lax.psum_scatter(grad_sums[0], ("dp", "ctx"), scatter_dimension=0, tiled=True),
        lax.psum_scatter(grad_sums[1], ("dp", "ctx"), scatter_dimension=1, tiled=True),
        lax.psum_scatter(grad_sums[2], ("dp", "ctx"), scatter_dimension=1, tiled=True),
        lax.psum_scatter(grad_sums[3], ("dp", "ctx"), scatter_dimension=0, tiled=True),
        lax.psum_scatter(grad_sums[4], ("dp", "ctx"), scatter_dimension=0, tiled=True),
        lax.psum_scatter(grad_sums[5], ("dp", "ctx"), scatter_dimension=1, tiled=True),
        lax.psum_scatter(grad_sums[6], ("dp", "ctx"), scatter_dimension=2, tiled=True),
    )
    bias_grad_total = lax.psum(bias_total, ("dp", "ctx"))
    return (
        jnp.stack(results, axis=0),
        jnp.stack(input_parts, axis=0),
        reduced[0],
        reduced[1],
        reduced[2],
        jnp.transpose(bias_grad_total),
        reduced[3],
        reduced[4],
        reduced[5],
        reduced[6],
    )


def solution(mesh):
    small = mesh.shape["ctx"] == 2 and mesh.shape["dp"] == 4 and mesh.shape["tensor"] == 4
    return jax.shard_map(
        body_fast if small else body,
        mesh=mesh,
        in_specs=(
            P("dp", "ctx", None),
            P("dp"),
            P("dp", "ctx"),
            P("dp", "ctx", None, None),
            P(("dp", "ctx")),
            P(None, ("dp", "ctx"), "tensor"),
            P("tensor", ("dp", "ctx")),
            P(None, "tensor"),
            P(("dp", "ctx")),
            P(("dp", "ctx"), None),
            P(None, ("dp", "ctx"), "tensor"),
            P(None, "tensor", ("dp", "ctx")),
            P("dp", "ctx", None),
        ),
        out_specs=(
            P("dp", "ctx", None),
            P("dp", "ctx", None),
            P(("dp", "ctx")),
            P(None, ("dp", "ctx"), "tensor"),
            P("tensor", ("dp", "ctx")),
            P(None, "tensor"),
            P(("dp", "ctx")),
            P(("dp", "ctx"), None),
            P(None, ("dp", "ctx"), "tensor"),
            P(None, "tensor", ("dp", "ctx")),
        ),
        check_vma=False,
    )
```

```python
import functools

import jax
import jax.numpy as jnp
import numpy as np
from jax import lax
from jax.experimental import pallas as pl
from jax.experimental.pallas import tpu as pltpu
from jax.sharding import PartitionSpec as P

BUCKETS = 32
MESH = pl.DeviceIdType.MESH
BF = jnp.bfloat16
F32 = jnp.float32


bucket_edges = np.ceil(16.0 * 8.0 ** (np.arange(1, 16) / 16.0)).astype(np.int32)
bucket_starts = [int(n) for n in range(17)] + [int(n) for n in bucket_edges]


QT = 256
BAND = 128
C0 = float(np.sqrt(2.0 / np.pi))
C1 = 0.044715


def mm(a, b):
    return jnp.dot(a, b, preferred_element_type=F32)


def mm_nt(a, b):
    return lax.dot_general(a, b, (((1,), (1,)), ((), ())), preferred_element_type=F32)


def mm_tn(a, b):
    return lax.dot_general(a, b, (((0,), (0,)), ((), ())), preferred_element_type=F32)


def remote(src, dst, send, recv, device):
    return pltpu.make_async_remote_copy(
        src_ref=src,
        dst_ref=dst,
        send_sem=send,
        recv_sem=recv,
        device_id=device,
        device_id_type=MESH,
    )


def block(start, size, whole=128):
    return pl.ds(pl.multiple_of(start, whole), size)


class Place:
    def __init__(self):
        dp, cx, t = lax.axis_index("dp"), lax.axis_index("ctx"), lax.axis_index("tensor")
        self.dp, self.cx, self.t = dp, cx, t
        self.yy, self.core = lax.div(t, 2), lax.rem(t, 2)
        self.partner = (dp, 1 - cx, t)
        self.sibling = (dp, cx, t + 1 - 2 * self.core)
        self.across = (dp, cx, lax.rem(t + 2, 4))
        self.tensor_peers = [(dp, cx, lax.rem(t + k, 4)) for k in (1, 2, 3)]
        self.z_peers = [(lax.rem(dp + k, 4), cx, t) for k in (1, 2, 3)]
        self.spot = dp + cx * (7 - 2 * dp)
        self.right = self.at_spot(1)
        self.left = self.at_spot(-1)

    def at_spot(self, away):
        spot = lax.rem(self.spot + 8 + away, 8)
        cx = lax.div(spot, 4)
        return (spot + cx * (7 - 2 * spot), cx, self.t)

    def slab(self, away):
        dp, cx, _ = self.at_spot(away)
        return dp * 2 + cx

    def greet(self):
        barrier = pltpu.get_barrier_semaphore()
        peers = self.z_peers + [self.partner] + self.tensor_peers
        for peer in peers:
            pl.semaphore_signal(barrier, inc=1, device_id=peer, device_id_type=MESH)
        pl.semaphore_wait(barrier, len(peers))


class Ring:
    def __init__(self, place, send_sems, recv_sems):
        self.place, self.send_sems, self.recv_sems = place, send_sems, recv_sems

    def copy(self, d, e, s, src, dst):
        at = (d, e, s - 1)
        device = self.place.right if d == 0 else self.place.left
        return remote(src, dst, self.send_sems.at[at], self.recv_sems.at[at], device)


class TensorSum:
    def __init__(self, place, seg, cbuf, ysend, ybuf, kept, c_s, c_r, y_s, y_r, a_s, a_r):
        self.place, self.seg = place, seg
        self.slot = (0, 1, 1, 1)
        self.half, self.quarter = seg // 2, seg // 4
        self.cbuf, self.ysend, self.ybuf, self.kept = cbuf, ysend, ybuf, kept
        self.c_s, self.c_r, self.y_s, self.y_r, self.a_s, self.a_r = c_s, c_r, y_s, y_r, a_s, a_r

    def rows(self, m, c, y):
        return block(m * self.seg + c * self.half + y * self.quarter, self.quarter)

    def own_rows(self, m):
        return self.rows(m, self.place.core, self.place.yy)

    def c_copy(self, m, j, src):
        rows = block(m * self.seg + (1 - self.place.core) * self.half, self.half)
        return remote(
            src.at[rows], self.cbuf.at[m, self.slot[j]], self.c_s.at[m, j], self.c_r.at[m, j],
            self.place.sibling,
        )

    def y_copy(self, m, j):
        return remote(
            self.ysend.at[m, self.slot[j]], self.ybuf.at[m, self.slot[j]], self.y_s.at[m, j], self.y_r.at[m, j],
            self.place.across,
        )

    def to_quarters(self, m, j, src):
        self.c_copy(m, j, src).wait_recv()
        yy, core = self.place.yy, self.place.core
        near, far = block(yy * self.quarter, self.quarter), block((1 - yy) * self.quarter, self.quarter)
        other = src[self.rows(m, core, 1 - yy), :].astype(F32)
        self.ysend[m, self.slot[j]] = (other + self.cbuf[m, self.slot[j], far, :].astype(F32)).astype(BF)
        self.y_copy(m, j).start()
        mine = src[self.rows(m, core, yy), :].astype(F32)
        self.kept[m, self.slot[j]] = mine + self.cbuf[m, self.slot[j], near, :].astype(F32)

    def total(self, m, j):
        self.y_copy(m, j).wait_recv()
        return self.kept[m, self.slot[j]] + self.ybuf[m, self.slot[j]].astype(F32)

    def a_copy(self, m, j, ref, step, own=None):
        yy, core = self.place.yy, self.place.core
        spot = ref.at[self.rows(m, core, 1 - yy if step == 2 else yy)]
        source = spot if own is None or step == 2 else own
        return remote(
            source, spot, self.a_s.at[m, j, step], self.a_r.at[m, j, step],
            self.place.across if step == 0 else self.place.sibling,
        )

    def a_recv(self, m, j, ref, step):
        yy, core = self.place.yy, self.place.core
        spot = ref.at[
            self.rows(m, core if step == 0 else 1 - core, yy if step == 1 else 1 - yy)
        ]
        return remote(
            spot, spot, self.a_s.at[m, j, step], self.a_r.at[m, j, step], self.place.sibling
        )

    def share(self, m, j, ref, own=None):
        self.a_copy(m, j, ref, 0, own).start()
        self.a_copy(m, j, ref, 1, own).start()

    def pass_on(self, m, j, ref):
        self.a_recv(m, j, ref, 0).wait_recv()
        self.a_copy(m, j, ref, 2).start()

    def shared(self, m, j, ref):
        self.a_recv(m, j, ref, 1).wait_recv()
        self.a_recv(m, j, ref, 2).wait_recv()


def low_lanes(shape):
    return lax.rem(lax.broadcasted_iota(jnp.int32, shape, len(shape) - 1), 128) < 64


def head_lanes(h, base=0):
    return slice(base + h * 128, base + (h + 1) * 128)


def fill_bias(bias_ref, band_ref, heads):
    rows = lax.broadcasted_iota(jnp.int32, (BAND, 2 * BAND), 0)
    cols = lax.broadcasted_iota(jnp.int32, (BAND, 2 * BAND), 1)
    away = rows + BAND - cols

    def one_head(h, carry):
        tile = jnp.full((BAND, 2 * BAND), bias_ref[h, 0], F32)
        for b in range(1, BUCKETS):
            tile = jnp.where(away >= bucket_starts[b], bias_ref[h, b], tile)
        band_ref[h] = tile - bias_ref[h, BUCKETS - 1]
        return carry

    lax.fori_loop(0, heads, one_head, 0)


def masked_scores(q_tile, keys, band_ref, scores, h, first, length):
    count = keys.shape[0]
    scores[:, BAND:] = mm_nt(q_tile, keys) * 0.125
    for part in range(QT // BAND):
        spot = (block(part * BAND, BAND), block(first + part * BAND, 2 * BAND))
        scores[spot] = scores[spot] + band_ref[h]
    values = scores[:, BAND:]
    key_pos = lax.broadcasted_iota(jnp.int32, (QT, count), 1)
    query_pos = lax.broadcasted_iota(jnp.int32, (QT, count), 0) + first
    allowed = (key_pos <= query_pos) & (key_pos < length)
    return jnp.where(allowed, values, -1e30), allowed


def bucket_sums(heads, band_sum, whole_sum, dbias):
    rows = lax.broadcasted_iota(jnp.int32, (BAND, 2 * BAND), 0)
    cols = lax.broadcasted_iota(jnp.int32, (BAND, 2 * BAND), 1)
    away = rows + BAND - cols
    bucket = lax.broadcasted_iota(jnp.int32, (BUCKETS, 2 * BAND), 0)
    lanes128 = lax.broadcasted_iota(jnp.int32, (BUCKETS, 128), 1)

    def one_head(h, carry):
        tile = band_sum[h]
        sums = jnp.zeros((BUCKETS, 2 * BAND), F32)
        for b in range(BUCKETS - 1):
            inside = (away >= bucket_starts[b]) & (away < bucket_starts[b + 1])
            row = jnp.sum(jnp.where(inside, tile, 0.0), axis=0, keepdims=True)
            sums = jnp.where(bucket == b, row, sums)
        per_bucket = jnp.sum(sums, axis=1, keepdims=True)
        near = jnp.sum(per_bucket, axis=0, keepdims=True)
        total = jnp.sum(whole_sum[h, 0:1, :], axis=1, keepdims=True)
        last = lax.broadcasted_iota(jnp.int32, (BUCKETS, 1), 0) == BUCKETS - 1
        per_bucket = jnp.where(last, total - near, per_bucket)
        dbias[...] = jnp.where(lanes128 == h, per_bucket, dbias[...])
        return carry

    dbias[...] = jnp.zeros((BUCKETS, 128), F32)
    lax.fori_loop(0, heads, one_head, 0)


def norm_back(x, gain, grad):
    scale = lax.rsqrt(jnp.mean(x * x, axis=-1, keepdims=True) + 1e-06)
    unit = x * scale
    pulled = grad * gain
    inner = jnp.mean(pulled * unit, axis=-1, keepdims=True)
    return scale * (pulled - unit * inner), grad * unit


def layer_kernel(
    heads,
    len_ref,
    bias_ref,
    slot_lanes,
    tok,
    cot,
    qkv,
    out_weight,
    vectors,
    up,
    down_turned,
    result,
    input_grad,
    up_out,
    down_out,
    qkv_out,
    out_out,
    tiny_out,
    dbias_out,
    w_full,
    wsmall,
    small_grad,
    ws_full,
    ws,
    gains,
    hidden,
    ntwo,
    q3,
    kv,
    lse,
    ab3,
    wbuf,
    gw,
    in_one,
    in_two,
    in_late,
    sx,
    sz,
    sum_grad,
    epart,
    npart,
    ffn,
    probs_ref,
    chosen_ref,
    cbuf,
    ysend,
    ybuf,
    kept,
    hgrad,
    bgrad,
    own_out,
    do3,
    grads,
    dkv_acc,
    dkv,
    band,
    scores,
    spread,
    band_sum,
    whole_sum,
    gg_own,
    gg_in,
    gg_sum,
    tiny_own,
    tiny_t,
    tiny_x,
    tiny_z,
    dbias_own,
    dbias_x,
    dbias_z,
    load_sem,
    out_sem,
    local,
    ready,
    gz_s,
    gz_r,
    gx_s,
    gx_r,
    k_s,
    k_r,
    ag_s,
    ag_r,
    rs_s,
    rs_r,
    c_s,
    c_r,
    y_s,
    y_r,
    a_s,
    a_r,
    kv_s,
    kv_r,
    gg_s,
    gg_r,
    sx_s,
    sx_r,
    sz_s,
    sz_r,
    tt_s,
    tt_r,
    tx_s,
    tx_r,
    tz_s,
    tz_r,
    bx_s,
    bx_r,
    bz_s,
    bz_r,
):
    place = Place()
    dp, cx, t = place.dp, place.cx, place.t
    seg = tok.shape[0] // 2
    width = tok.shape[1]
    shard = width // 8
    experts = up.shape[0]
    span = kv.shape[2]
    cap = slot_lanes.shape[2]
    ahead = low_lanes((shard, 128))

    def packed(base, a, b):
        turned = jnp.where(ahead, a[:, 0:128], pltpu.roll(b[:, 0:128], 64, 1))
        wsmall[0:shard, base : base + 128] = turned.astype(BF)
        turned = jnp.where(ahead, pltpu.roll(a[:, 0:128], 64, 1), b[:, 0:128])
        wsmall[0:shard, base + 128 : base + 256] = turned.astype(BF)
        last = jnp.concatenate([a[:, 128:192], b[:, 128:192]], axis=1)
        wsmall[0:shard, base + 256 : base + 384] = last.astype(BF)

    def unpacked(base):
        one, two, three = (small_grad[:, base + i * 128 : base + i * 128 + 128] for i in range(3))
        first = jnp.where(ahead, one, pltpu.roll(two, 64, 1))
        second = jnp.where(ahead, pltpu.roll(one, 64, 1), two)
        return first, three[:, 0:64], second, pltpu.roll(three, 64, 1)[:, 0:64]

    packed(0, qkv[1].astype(F32), qkv[2].astype(F32))
    packed(span, qkv[0].astype(F32), jnp.transpose(out_weight[...].astype(F32)))
    wsmall[shard:, :] = vectors[...]
    place.greet()
    gather_ring = Ring(place, ag_s, ag_r)
    reduce_ring = Ring(place, rs_s, rs_r)
    sums = TensorSum(place, seg, cbuf, ysend, ybuf, kept, c_s, c_r, y_s, y_r, a_s, a_r)
    bpart = epart
    earlier = bgrad

    def small_slab(k, c):
        return lax.rem(dp + 4 - k, 4) * 2 + c

    def gz_copy(k, slab):
        return remote(
            wsmall, ws_full.at[slab], gz_s.at[k - 1], gz_r.at[k - 1], place.z_peers[k - 1]
        )

    def gx_copy(k, c):
        spot = ws_full.at[small_slab(k, c)]
        return remote(wsmall if k == 0 else spot, spot, gx_s.at[k], gx_r.at[k], place.partner)

    small_own = pltpu.make_async_copy(wsmall, ws_full.at[small_slab(0, cx)], local.at[2 * experts])

    def gather(d, e, s, sending):
        away = s - 1 if sending else s
        slab = place.slab(-away if d == 0 else away)
        if s == 1:
            spots = [w_full.at[e, j, slab] for j in range(2)]
            sources = [up.at[e], down_turned.at[e]] if sending else spots
            return [
                gather_ring.copy(d, e, at, source, spot)
                for at, source, spot in zip((1, 5), sources, spots)
            ]
        spot = w_full.at[e, d, slab] if s == 4 else w_full.at[e, :, slab]
        return [gather_ring.copy(d, e, s, spot, spot)]

    def w_own(e):
        spots = [w_full.at[e, j, place.slab(0)] for j in range(2)]
        return [
            pltpu.make_async_copy(source, spot, local.at[e * 2 + j])
            for j, (source, spot) in enumerate(zip((up.at[e], down_turned.at[e]), spots))
        ]

    def gather_step(e, s):
        for d in range(2):
            if s > 1:
                for copy in gather(d, e, s - 1, False):
                    copy.wait_recv()
            for copy in gather(d, e, s, True):
                copy.start()

    def landing(d, e, s):
        if s == 1:
            return in_one.at[d, e]
        if s == 2:
            return in_two.at[d, e]
        if e < 2:
            return in_late.at[s - 3, d, e]
        return wbuf.at[e, pl.ds(d * 4 + (s - 3) * 2, 2)]

    def reduce_copy(d, e, s):
        slab = place.slab(5 - s if d == 0 else s - 5)
        src = gw.at[e, d, slab] if s == 1 else gw.at[e, :, slab]
        return reduce_ring.copy(d, e, s, src, landing(d, e, s))

    def reduce_step(e, s):
        for d in range(2):
            if s > 1:
                slab = place.slab(5 - s if d == 0 else s - 5)
                reduce_copy(d, e, s - 1).wait_recv()
                came = landing(d, e, s - 1)

                def add(i, carry):
                    rows = block(i * 16, 16, 16)
                    if s == 2:
                        total = gw[e, d, slab, rows, :].astype(F32) + came[rows, :].astype(F32)
                        gw[e, d, slab, rows, :] = total.astype(BF)
                    else:
                        total = gw[e, :, slab, rows, :].astype(F32) + came[:, rows, :].astype(F32)
                        gw[e, :, slab, rows, :] = total.astype(BF)
                    return carry

                lax.fori_loop(0, shard // 16, add, 0)
            reduce_copy(d, e, s).start()

    def reduce_end(e):
        for d in range(2):
            reduce_copy(d, e, 4).wait_recv()

        def add(i, carry):
            rows = block(i * 16, 16, 16)
            total = gw[e, :, place.slab(0), rows, :].astype(F32)
            for d in range(2):
                total = total + landing(d, e, 4)[:, rows, :].astype(F32)
            up_out[e, rows, :] = total[0]
            down_out[e, rows, :] = total[1]
            return carry

        lax.fori_loop(0, shard // 16, add, 0)

    late = [(1, 4), (3, 2), (2, 3), (3, 3), (2, 4), (3, 4)]

    def pump_late(count=1):
        for _ in range(count):
            if late:
                reduce_step(*late.pop(0))

    def tok_copy(m):
        rows = sums.own_rows(m)
        return remote(tok.at[rows], earlier.at[rows], k_s.at[m], k_r.at[m], place.partner)

    @pl.when(cx == 0)
    def _():
        for m in range(2):
            tok_copy(m).start()

    small_own.start()
    for k in (1, 3, 2):
        gz_copy(k, small_slab(0, cx)).start()
    gx_copy(0, cx).start()
    for e in range(2):
        gather_step(e, 1)
    for e in range(experts):
        for copy in w_own(e):
            copy.start()

    @pl.when(cx == 0)
    def _():
        for m in range(2):
            kv[m, seg:, :] = jnp.zeros((seg, span), BF)

    @pl.when(cx == 1)
    def _():
        for m in range(2):
            tok_copy(m).wait_recv()
            sums.share(m, 4, earlier)

    fill_bias(bias_ref, band, heads)
    spread[...] = jnp.zeros(spread.shape, F32)
    band_sum[...] = jnp.zeros(band_sum.shape, F32)
    whole_sum[...] = jnp.zeros(whole_sum.shape, F32)
    tiny_own[...] = jnp.zeros(tiny_own.shape, F32)
    for k in (1, 3, 2):
        gz_copy(k, small_slab(k, cx)).wait_recv()
        gx_copy(k, cx).start()

    @pl.when(cx == 1)
    def _():
        for m in range(2):
            sums.pass_on(m, 4, earlier)

    small_own.wait()
    for k in range(4):
        gx_copy(k, 1 - cx).wait_recv()
    total = ws_full[0, shard:, :].astype(F32)
    for i in range(1, 8):
        total = total + ws_full[i, shard:, :].astype(F32)
    gains[...] = total
    for i in range(8):
        ws[i * shard : (i + 1) * shard, :] = ws_full[i, 0:shard, :]

    def first_norm(source, rows):
        x = source[rows, :].astype(F32)
        scale = lax.rsqrt(jnp.mean(x * x, axis=-1, keepdims=True) + 1e-06)
        return (x * scale * gains[0:1, :]).astype(BF)

    def project(i, carry):
        rows = block(i * 256, 256)
        m, at = lax.div(i, seg // 256), lax.rem(i, seg // 256) * 256
        x = first_norm(tok, rows)
        kv[m, block(cx * seg + at, 256), :] = mm(x, ws[:, 0:span]).astype(BF)
        part = mm(x, ws[:, span:])
        q3[rows, :] = jnp.where(low_lanes(part.shape), part, 0.0).astype(BF)
        return carry

    def project_earlier(i, carry):
        m, at = lax.div(i, seg // 256), lax.rem(i, seg // 256) * 256
        x = first_norm(earlier, block(i * 256, 256))
        kv[m, block(at, 256), :] = mm(x, ws[:, 0:span]).astype(BF)
        return carry

    lax.fori_loop(0, 2 * seg // 256, project, 0)
    gather_step(0, 2)

    @pl.when(cx == 1)
    def _():
        for m in range(2):
            sums.shared(m, 4, earlier)
        lax.fori_loop(0, 2 * seg // 256, project_earlier, 0)

    gather_step(1, 2)
    gather_step(2, 1)

    def attend(m):
        length = len_ref[m]

        def step(i, carry):
            rows = block(m * seg + i * QT, QT)
            first = cx * seg + i * QT
            lanes128 = lax.broadcasted_iota(jnp.int32, (QT, 128), 1)

            def one_head(h, tops):
                cut = block(h * 128, 128)
                values, allowed = masked_scores(
                    q3[rows, cut], kv[m, :, cut], band, scores, h, first, length
                )
                top = jnp.max(values, axis=-1, keepdims=True)
                raised = jnp.where(allowed, jnp.exp(values - top), 0.0)
                mass = jnp.sum(raised, axis=-1, keepdims=True)
                probs = (raised * (1.0 / mass)).astype(BF)
                part = mm(probs, kv[m, :, cut])
                ab3[rows, cut] = jnp.where(low_lanes(part.shape), 0.0, part).astype(BF)
                return jnp.where(lanes128 == h, top + jnp.log(mass), tops)

            lse[rows, :] = lax.fori_loop(0, heads, one_head, jnp.zeros((QT, 128), F32))
            bpart[rows, :] = mm_nt(ab3[rows, :], ws[:, span:]).astype(BF)
            return carry

        lax.fori_loop(0, seg // QT, step, 0)

    def second_norm(m):
        rows = sums.own_rows(m)
        x = tok[rows, :].astype(F32) + sums.total(m, 3)
        hidden[m] = x
        scale = lax.rsqrt(jnp.mean(x * x, axis=-1, keepdims=True) + 1e-06)
        ntwo[rows, :] = (x * scale * gains[1:2, :]).astype(BF)
        sums.share(m, 3, ntwo)

    for m in range(2):
        attend(m)
        sums.c_copy(m, 3, bpart).start()
        gather_step(m, 3)
        if m == 1:
            second_norm(0)
        sums.to_quarters(m, 3, bpart)
    gather_step(2, 2)
    second_norm(1)
    sums.pass_on(0, 3, ntwo)
    gather_step(0, 4)
    sums.pass_on(1, 3, ntwo)
    gather_step(1, 4)
    gather_step(3, 1)
    gather_step(2, 3)
    for m in range(2):
        sums.shared(m, 3, ntwo)
        sums.c_copy(m, 3, bpart).wait_send()

    router16 = gains[...].astype(BF)

    def upstream_of(rows, m, first):
        spot = lax.broadcasted_iota(jnp.int32, (rows.size, 1), 0) + (cx * seg + first)
        live = (spot < len_ref[m]).astype(F32)
        return live, live * cot[rows, :].astype(F32)

    def choices(m, carry):
        lanes = lax.broadcasted_iota(jnp.int32, (seg, 16), 1)
        chosen = jnp.zeros((seg, 16), F32)
        for e in range(experts):
            inside = put_of(m, e).astype(F32)
            chosen = jnp.where(lanes == e + 2, jnp.sum(inside, axis=1, keepdims=True), chosen)
        chosen_ref[block(m * seg, seg), :] = chosen
        return carry

    def put_of(m, e):
        row = slot_lanes[m, pl.ds(e, 1), :]
        return row == lax.broadcasted_iota(jnp.int32, (seg, cap), 0)

    lax.fori_loop(0, 2, choices, 0)

    def gates(i, carry):
        rows = block(i * 256, 256)
        m = lax.div(i, seg // 256)
        logits = mm_nt(ntwo[rows, :], router16)
        lanes = lax.broadcasted_iota(jnp.int32, (256, 16), 1)
        inside = (lanes >= 2) & (lanes < 2 + experts)
        logits = jnp.where(inside, logits, -1e30)
        top = jnp.max(logits, axis=-1, keepdims=True)
        raised = jnp.where(inside, jnp.exp(logits - top), 0.0)
        probs = raised / jnp.sum(raised, axis=-1, keepdims=True)
        probs_ref[rows, :] = probs
        gate = jnp.sum(probs * chosen_ref[rows, :], axis=-1, keepdims=True)
        live, upstream = upstream_of(rows, m, lax.rem(i, seg // 256) * 256)
        sum_grad[rows, :] = (gate * upstream).astype(BF)
        epart[rows, :] = jnp.zeros((256, width), BF)
        npart[rows, :] = jnp.zeros((256, width), BF)
        return carry

    lax.fori_loop(0, 2 * seg // 256, gates, 0)

    def load(e):
        slot = lax.rem(e, 2)
        return pltpu.make_async_copy(
            w_full.at[e], wbuf.at[pl.ds(slot * 2, 2)], load_sem.at[slot]
        )

    def arrived(e):
        for copy in w_own(e):
            copy.wait()
        for d in range(2):
            gather(d, e, 4, False)[0].wait_recv()
        load(e).start()

    picked, slot_grad, activated, raised_grad = (ffn.at[i] for i in range(4))

    def start_sums():
        for m in range(2):
            sums.c_copy(m, 1, npart).start()
            sums.c_copy(m, 0, epart).start()

    def g(e, s):
        return lambda: gather_step(e, s)

    def r(e, s):
        return lambda: reduce_step(e, s)

    def here(e):
        return lambda: arrived(e)

    before = ([here(0), here(1)], [], [], [])
    between = ([g(3, 2)], [g(3, 3), g(3, 4)], [], [start_sums, r(1, 3)])
    after = (
        [g(2, 4)],
        [here(2), r(0, 2)],
        [here(3), r(1, 2), r(0, 3)],
        [r(0, 4), r(2, 2)],
    )

    def act_on(e, plan):
        for i, acts in enumerate(plan):
            if acts:

                @pl.when(e == i)
                def _(acts=acts):
                    for act in acts:
                        act()

    def expert(e, carry):
        slot = lax.rem(e, 2)

        def weight(which):
            return wbuf[slot * 2 + which].reshape(width, -1)

        act_on(e, before)
        load(e).wait()

        def one_micro(m, carry):
            rows = block(m * seg, seg)
            slots = block(m * cap, cap)
            put = put_of(m, e).astype(BF)
            chosen_rows = mm_tn(put, ntwo[rows, :]).astype(BF)
            picked[slots, :] = chosen_rows
            slot_part = mm_tn(put, sum_grad[rows, :]).astype(BF)
            slot_grad[slots, :] = slot_part
            raised = mm(chosen_rows, weight(0))
            square = raised * raised
            bent = jnp.tanh(C0 * raised * (1.0 + C1 * square))
            cdf = 0.5 * (1.0 + bent)
            act = (raised * cdf).astype(BF)
            activated[slots, :] = act
            slope = cdf + 0.5 * raised * (1.0 - bent * bent) * (C0 * (1.0 + 3.0 * C1 * square))
            act_grad = mm(slot_part, weight(1))
            back = (act_grad * slope).astype(BF)
            raised_grad[slots, :] = back
            lowered = mm_nt(act, weight(1)).astype(BF)
            epart[rows, :] += mm(put, lowered).astype(BF)
            pulled = mm_nt(back, weight(0)).astype(BF)
            npart[rows, :] += mm(put, pulled).astype(BF)
            return carry

        lax.fori_loop(0, 2, one_micro, 0)
        act_on(e, between)

        def weight_part(i, carry):
            lanes = block(i * 384, 384)
            slabs = pl.ds(i * 4, 4)
            part = mm_tn(picked[:, lanes], raised_grad[...]).astype(BF)
            gw[e, 0, slabs] = part.reshape(4, shard, -1)
            part = mm_tn(slot_grad[:, lanes], activated[...]).astype(BF)
            gw[e, 1, slabs] = part.reshape(4, shard, -1)
            return carry

        lax.fori_loop(0, width // 384, weight_part, 0)
        reduce_step(e, 1)
        act_on(e, after)
        return carry

    lax.fori_loop(0, experts, expert, 0)

    for peer in (place.right, place.left):
        pl.semaphore_signal(ready, inc=1, device_id=peer, device_id_type=MESH)

    @pl.when(cx == 1)
    def _():
        for m in range(2):
            for step in range(3):
                sums.a_copy(m, 4, earlier, step).wait_send()

    ones = jnp.ones((8, width), BF)
    for m in range(2):

        def gate_terms(i, carry):
            rows = block(m * seg + i * 256, 256)
            live, upstream = upstream_of(rows, m, i * 256)
            terms = epart[rows, :].astype(F32) * upstream
            high = terms.astype(BF)
            rest = (terms - high.astype(F32)).astype(BF)
            gg_own[m, :, block(i * 256, 256)] = mm_nt(ones, high) + mm_nt(ones, rest)
            return carry

        sums.y_copy(m, 3).wait_send()
        sums.to_quarters(m, 1, npart)
        lax.fori_loop(0, seg // 256, gate_terms, 0)

    def gg_copy(k):
        return remote(gg_own, gg_in.at[k - 1], gg_s.at[k - 1], gg_r.at[k - 1], place.tensor_peers[k - 1])

    for k in (1, 2, 3):
        gg_copy(k).start()
    pump_late(2)
    pl.semaphore_wait(ready, 2)
    for k in (1, 2, 3):
        gg_copy(k).wait_recv()
    gg_sum[...] = gg_own[...] + gg_in[0] + gg_in[1] + gg_in[2]
    own_first = place.core * (seg // 2) + place.yy * (seg // 4)

    def own_copy(m, j, ref):
        return pltpu.make_async_copy(
            own_out.at[m, j - 1], ref.at[sums.own_rows(m)], out_sem.at[m * 2 + j - 1]
        )

    for m in range(2):
        rows = sums.own_rows(m)
        line = gg_sum[m, :, block(own_first, seg // 4)]
        line = jnp.where(lax.broadcasted_iota(jnp.int32, line.shape, 0) == 0, line, 0.0)
        high = line.astype(BF)
        rest = (line - high.astype(F32)).astype(BF)
        ones = jnp.ones((8, 128), BF)
        gate_grad = (mm_tn(high, ones) + mm_tn(rest, ones))[:, 0:1]
        down = sums.total(m, 1)
        live, upstream = upstream_of(rows, m, own_first)
        probs, chosen = probs_ref[rows, :], chosen_ref[rows, :]
        gate = jnp.sum(probs * chosen, axis=-1, keepdims=True)
        logit_grad = (probs * gate_grad * (chosen - gate)).astype(BF)
        down = down + mm(logit_grad, router16)
        through, gain_terms = norm_back(hidden[m], gains[1:2, :], down)
        full = through + upstream
        hgrad[m] = full
        bgrad[rows, :] = full.astype(BF)
        sums.share(m, 0, bgrad)
        tiny_own[1:2, :] += jnp.sum(gain_terms, axis=0, keepdims=True)
        tiny_own[...] += mm_tn(logit_grad, ntwo[rows, :])[0:8, :]
    pump_late()
    sums.pass_on(0, 0, bgrad)

    def dkv_copy(m, h):
        spot = dkv.at[m, h]
        return remote(spot, spot, kv_s.at[m, h], kv_r.at[m, h], place.partner)

    def attend_back(m):
        length = len_ref[m]

        def lower(i, carry):
            part = mm(bgrad[block(m * seg + i * 256, 256), :], ws[:, span:])
            part = jnp.where(low_lanes(part.shape), 0.0, part)
            do3[block(i * 256, 256), :] = part.astype(BF)
            return carry

        lax.fori_loop(0, seg // 256, lower, 0)

        def one_head(h, carry):
            cut = block(h * 128, 128)
            dkv_acc[...] = jnp.zeros(dkv_acc.shape, F32)

            def step(i, carry):
                rows = block(m * seg + i * QT, QT)
                first = cx * seg + i * QT
                q_tile, do_tile = q3[rows, cut], do3[block(i * QT, QT), cut]
                keys = kv[m, :, cut]
                values, allowed = masked_scores(q_tile, keys, band, scores, h, first, length)
                lanes128 = lax.broadcasted_iota(jnp.int32, (QT, 128), 1)
                mass = jnp.sum(jnp.where(lanes128 == h, lse[rows, :], 0.0), axis=1, keepdims=True)
                soft = jnp.where(allowed, jnp.exp(values - mass), 0.0)
                soft_grad = mm_nt(do_tile, keys)
                delta = jnp.sum(soft * soft_grad, axis=-1, keepdims=True)
                score_grad = (soft * (soft_grad - delta)).astype(BF)
                dkv_acc[...] += mm_tn(soft.astype(BF), do_tile) + 0.125 * mm_tn(score_grad, q_tile)
                part = mm(score_grad, keys) * 0.125
                grads[rows, block(span + h * 128, 128)] = jnp.where(
                    low_lanes(part.shape), part, 0.0
                ).astype(BF)
                spread[:, BAND:] = score_grad.astype(F32)
                for half in range(QT // BAND):
                    lanes = block(first + half * BAND, 2 * BAND)
                    band_sum[h] += spread[half * BAND : (half + 1) * BAND, lanes]
                whole_sum[h, 0:1, :] += jnp.sum(spread[:, BAND:], axis=0, keepdims=True)
                return carry

            lax.fori_loop(0, seg // QT, step, 0)

            @pl.when(cx == 1)
            def _():
                dkv[m, h] = dkv_acc[0:seg, :].astype(BF)
                dkv_copy(m, h).start()

            grads[pl.ds(m * seg, seg), cut] = dkv_acc[block(cx * seg, seg), :].astype(BF)

            if m == 1:

                @pl.when(h == 2)
                def _():
                    pump_late()

            return carry

        lax.fori_loop(0, heads, one_head, 0)

    def after_attend(m):
        rows = pl.ds(m * seg, seg)

        @pl.when(cx == 0)
        def _():
            for h in range(heads):
                dkv_copy(m, h).wait_recv()
                total = grads[rows, head_lanes(h)].astype(F32) + dkv[m, h].astype(F32)
                grads[rows, head_lanes(h)] = total.astype(BF)

        def lower(i, carry):
            spot = block(m * seg + i * 256, 256)
            npart[spot, :] = mm_nt(grads[spot, :], ws[...]).astype(BF)
            return carry

        lax.fori_loop(0, seg // 256, lower, 0)
        sums.c_copy(m, 2, npart).start()

    def gs_spot(slab, half):
        return ws_full.at[slab, pl.ds(0, shard), pl.ds(half * span, span)]

    def sx_copy(half, k):
        slab = lax.rem(dp + k, 4) * 2 + 1 - cx
        return remote(
            gs_spot(slab, half), sx.at[half, k], sx_s.at[half, k], sx_r.at[half, k], place.partner
        )

    def sz_copy(half, k):
        return remote(
            sx.at[half, k], sz.at[half, k - 1], sz_s.at[half, k - 1], sz_r.at[half, k - 1],
            place.z_peers[k - 1],
        )

    order = (2, 1, 3, 0)

    def small_part(half):
        def step(i, carry):
            lanes = block(i * 384, 384)
            cols = slice(half * span, (half + 1) * span)
            part = mm_tn(ffn[0, :, lanes], grads[0:seg, cols])
            part = part + mm_tn(ffn[1, :, lanes], grads[seg:, cols])
            if half == 1:
                part = part + mm_tn(bgrad[:, lanes], ab3[...])
            ws_full[pl.ds(i * 4, 4), 0:shard, cols] = part.astype(BF).reshape(4, shard, -1)
            return carry

        lax.fori_loop(0, width // 384, step, 0)
        for k in order:
            sx_copy(half, k).start()

    def small_step(half):
        cols = slice(half * span, (half + 1) * span)
        for k in order:
            sx_copy(half, k).wait_recv()
            slab = lax.rem(dp + k, 4) * 2 + cx
            total = ws_full[slab, 0:shard, cols].astype(F32) + sx[half, k].astype(F32)
            if k == 0:
                small_grad[:, cols] = total
            else:
                sx[half, k] = total.astype(BF)
                sz_copy(half, k).start()

    for m in range(2):
        sums.shared(m, 0, bgrad)
        attend_back(m)
        if m == 0:
            sums.pass_on(1, 0, bgrad)
            for i in range(2):
                sums.to_quarters(i, 0, epart)
        if m == 1:
            for i in range(2):

                def own_result(i):
                    rows = sums.own_rows(i)
                    expert_sum = sums.total(i, 0)
                    spot = lax.broadcasted_iota(jnp.int32, (seg // 4, 1), 0) + (cx * seg + own_first)
                    live = (spot < len_ref[i]).astype(F32)
                    gate = jnp.sum(probs_ref[rows, :] * chosen_ref[rows, :], axis=-1, keepdims=True)
                    own_out[i, 0] = (live * (hidden[i] + gate * expert_sum)).astype(BF)
                    own_copy(i, 1, result).start()
                    sums.share(i, 1, result, own_out.at[i, 0])

                own_result(i)

    def normed_again(i, carry):
        ffn[lax.div(i, 2), block(lax.rem(i, 2) * 256, 256), :] = first_norm(tok, block(i * 256, 256))
        return carry

    lax.fori_loop(0, 2 * seg // 256, normed_again, 0)
    for k in range(4):
        gx_copy(k, cx).wait_send()
    small_part(1)
    bucket_sums(heads, band_sum, whole_sum, dbias_own)
    bx_copy = remote(dbias_own, dbias_x, bx_s.at[0], bx_r.at[0], place.partner)
    bx_copy.start()
    sums.c_copy(0, 1, npart).wait_send()
    sums.y_copy(0, 1).wait_send()
    after_attend(0)
    sums.c_copy(1, 1, npart).wait_send()
    sums.y_copy(1, 1).wait_send()
    sums.to_quarters(0, 2, npart)
    after_attend(1)
    small_part(0)
    sums.to_quarters(1, 2, npart)
    pump_late(len(late))

    for m in range(2):
        down = sums.total(m, 2)
        rows = sums.own_rows(m)
        through, gain_terms = norm_back(tok[rows, :].astype(F32), gains[0:1, :], down)
        own_out[m, 1] = (through + hgrad[m]).astype(BF)
        sums.share(m, 2, input_grad, own_out.at[m, 1])
        own_copy(m, 2, input_grad).start()
        tiny_own[0:1, :] += jnp.sum(gain_terms, axis=0, keepdims=True)

    def tt_copy(k):
        return remote(
            tiny_own, tiny_t.at[k - 1], tt_s.at[k - 1], tt_r.at[k - 1], place.tensor_peers[k - 1]
        )

    for k in (1, 2, 3):
        tt_copy(k).start()
    small_step(1)
    bx_copy.wait_recv()
    dbias_sum = dbias_own[...] + dbias_x[...]
    dbias_x[...] = dbias_sum

    def bz_copy(k):
        return remote(
            dbias_x, dbias_z.at[k - 1], bz_s.at[k - 1], bz_r.at[k - 1], place.z_peers[k - 1]
        )

    for k in (1, 2, 3):
        bz_copy(k).start()
    reduce_end(0)
    reduce_end(1)
    small_step(0)
    for k in (1, 2, 3):
        tt_copy(k).wait_recv()
    tiny_x[0] = tiny_own[...] + tiny_t[0] + tiny_t[1] + tiny_t[2]
    tx_copy = remote(tiny_x.at[0], tiny_x.at[1], tx_s.at[0], tx_r.at[0], place.partner)
    tx_copy.start()
    for m in range(2):
        sums.pass_on(m, 1, result)
        sums.pass_on(m, 2, input_grad)
    tx_copy.wait_recv()
    tiny_x[2] = tiny_x[0] + tiny_x[1]

    def tz_copy(k):
        return remote(
            tiny_x.at[2], tiny_z.at[k - 1], tz_s.at[k - 1], tz_r.at[k - 1], place.z_peers[k - 1]
        )

    for k in (1, 2, 3):
        tz_copy(k).start()
    for e in range(2, experts):
        reduce_end(e)
    for half in range(2):
        cols = slice(half * span, (half + 1) * span)
        total = small_grad[:, cols]
        for k in (1, 2, 3):
            sz_copy(half, k).wait_recv()
            total = total + sz[half, k - 1].astype(F32)
        small_grad[:, cols] = total
    first, first_rest, second, second_rest = unpacked(0)
    qkv_out[1, :, 0:128], qkv_out[1, :, 128:192] = first, first_rest
    qkv_out[2, :, 0:128], qkv_out[2, :, 128:192] = second, second_rest
    first, first_rest, second, second_rest = unpacked(span)
    qkv_out[0, :, 0:128], qkv_out[0, :, 128:192] = first, first_rest
    out_out[0:128, :], out_out[128:192, :] = jnp.transpose(second), jnp.transpose(second_rest)
    for k in (1, 2, 3):
        bz_copy(k).wait_recv()
        bz_copy(k).wait_send()
        dbias_sum = dbias_sum + dbias_z[k - 1]
    dbias_out[...] = jnp.transpose(dbias_sum)[0:heads, :]
    total = tiny_x[2]
    for k in (1, 2, 3):
        tz_copy(k).wait_recv()
        total = total + tiny_z[k - 1]
    turn = lax.rem(width - (dp * 2 + cx) * shard, width)
    tiny_out[...] = pltpu.roll(total, turn, 1)[:, 0:shard]
    for m in range(2):
        sums.shared(m, 1, result)
        sums.shared(m, 2, input_grad)

    for e in range(experts):
        for d in range(2):
            for s in (1, 2, 3, 4):
                for copy in gather(d, e, s, True):
                    copy.wait_send()
                reduce_copy(d, e, s).wait_send()
    for k in range(4):
        for half in range(2):
            sx_copy(half, k).wait_send()
            if k > 0:
                sz_copy(half, k).wait_send()
        if k > 0:
            gz_copy(k, small_slab(0, cx)).wait_send()
            gg_copy(k).wait_send()
            tt_copy(k).wait_send()
            tz_copy(k).wait_send()
    tx_copy.wait_send()
    bx_copy.wait_send()
    for m in range(2):
        sums.c_copy(m, 0, epart).wait_send()
        sums.c_copy(m, 2, npart).wait_send()
        own_copy(m, 1, result).wait()
        own_copy(m, 2, input_grad).wait()
        sums.y_copy(m, 0).wait_send()
        sums.y_copy(m, 2).wait_send()
        for j in range(4):
            for step in range(3):
                own = own_out.at[m, j - 1] if j in (1, 2) else None
                ref = (bgrad, result, input_grad, ntwo)[j]
                sums.a_copy(m, j, ref, step, own).wait_send()

        @pl.when(cx == 0)
        def _():
            tok_copy(m).wait_send()

        @pl.when(cx == 1)
        def _():
            for h in range(heads):
                dkv_copy(m, h).wait_send()


def layer_call(lengths, bias, slot_lanes, tok, cot, qkv, out_weight, vectors, up, down_turned):
    heads = bias.shape[0]
    rows, width = tok.shape
    span = heads * 128
    experts, ff = up.shape[0], up.shape[2]
    seg = rows // 2
    quarter = seg // 4
    shard = width // 8
    slots = 2 * slot_lanes.shape[2]
    vm = pl.BlockSpec(memory_space=pltpu.VMEM)
    sm = pl.BlockSpec(memory_space=pltpu.SMEM)
    hbm = pl.BlockSpec(memory_space=pl.ANY)
    dma = pltpu.SemaphoreType.DMA
    sds = jax.ShapeDtypeStruct
    low, full = (lambda *shape: pltpu.VMEM(shape, BF)), (lambda *shape: pltpu.VMEM(shape, F32))

    def pair(*shape):
        return [dma(shape), dma(shape)]

    return pl.pallas_call(
        functools.partial(layer_kernel, heads),
        out_shape=(
            sds((rows, width), BF),
            sds((rows, width), BF),
            sds((experts, shard, ff), F32),
            sds((experts, shard, ff), F32),
            sds(qkv.shape, F32),
            sds(out_weight.shape, F32),
            sds((8, shard), F32),
            sds((heads, BUCKETS), F32),
            sds((experts, 2, 8, shard, ff), BF),
        ),
        in_specs=[sm, sm] + [vm] * 6 + [hbm] * 2,
        out_specs=(hbm,) * 2 + (vm,) * 6 + (hbm,),
        scratch_shapes=[
            low(shard + 16, width),
            full(shard, width),
            low(8, shard + 16, width),
            low(width, width),
            full(16, width),
            full(2, quarter, width),
            low(rows, width),
            low(rows, span),
            low(2, rows, span),
            full(rows, 128),
            low(rows, span),
            low(4, 8, shard, ff),
            low(experts, 2, 8, shard, ff),
            low(2, experts, shard, ff),
            low(2, experts, 2, shard, ff),
            low(2, 2, 2, 2, shard, ff),
            low(2, 4, shard, span),
            low(2, 3, shard, span),
            low(rows, width),
            low(rows, width),
            low(rows, width),
            low(4, slots, width),
            full(rows, 16),
            full(rows, 16),
            low(2, 2, 2 * quarter, width),
            low(2, 2, quarter, width),
            low(2, 2, quarter, width),
            full(2, 2, quarter, width),
            full(2, quarter, width),
            low(rows, width),
            low(2, 2, quarter, width),
            low(seg, span),
            low(rows, 2 * span),
            full(rows, 128),
            low(2, heads, seg, 128),
            full(heads, BAND, 2 * BAND),
            full(QT, rows + BAND),
            full(QT, rows + BAND),
            full(heads, BAND, 2 * BAND),
            full(heads, 8, rows),
            full(2, 8, seg),
            full(3, 2, 8, seg),
            full(2, 8, seg),
            full(8, width),
            full(3, 8, width),
            full(3, 8, width),
            full(3, 8, width),
            full(BUCKETS, 128),
            full(BUCKETS, 128),
            full(3, BUCKETS, 128),
            dma((2,)),
            dma((4,)),
            dma((2 * experts + 1,)),
            pltpu.SemaphoreType.REGULAR,
        ]
        + pair(3)
        + pair(4)
        + pair(2)
        + pair(2, experts, 5)
        + pair(2, experts, 4)
        + pair(2, 4)
        + pair(2, 4)
        + pair(2, 5, 3)
        + pair(2, heads)
        + pair(3)
        + pair(2, 4)
        + pair(2, 3)
        + pair(3)
        + pair(1)
        + pair(3)
        + pair(1)
        + pair(3),
        compiler_params=pltpu.CompilerParams(
            collective_id=0, has_side_effects=True, vmem_limit_bytes=63 << 20
        ),
    )(lengths, bias, slot_lanes, tok, cot, qkv, out_weight, vectors, up, down_turned)


def body_fast(
    inputs, lengths, expert_ids, slot_rows, attn_gain, qkv_weight, out_weight, position_bias,
    ffn_gain, router_weight, up_weight, down_weight, cotangent,
):
    micro, seg, width = inputs.shape
    rows = micro * seg
    experts = up_weight.shape[0]
    slab = lax.axis_index("dp") * 2 + lax.axis_index("ctx")
    shard = attn_gain.shape[0]
    small = jnp.concatenate(
        [attn_gain[None], ffn_gain[None], router_weight.T, jnp.zeros((10, shard), BF)], axis=0
    )
    small = lax.dynamic_update_slice(jnp.zeros((16, width), BF), small, (0, slab * shard))
    result, input_part, up_grad, down_grad, qkv_grad, out_grad, tiny, dbias, _ = layer_call(
        lengths, position_bias.T, slot_rows.reshape(micro, experts, -1), inputs.reshape(rows, width),
        cotangent.reshape(rows, width), qkv_weight, out_weight, small, up_weight,
        jnp.transpose(down_weight, (0, 2, 1)),
    )
    return (
        result.reshape(inputs.shape),
        input_part.reshape(inputs.shape),
        tiny[0],
        qkv_grad,
        out_grad,
        dbias.T,
        tiny[1],
        tiny[2 : 2 + experts].T,
        up_grad,
        jnp.transpose(down_grad, (0, 2, 1)),
    )


def rms_norm(values, gain_vector):
    return (
        values * lax.rsqrt(jnp.mean(values * values, axis=-1, keepdims=True) + 1e-06) * gain_vector
    )


def bucket_of(distance):
    clipped = jnp.maximum(distance, 0)
    edge_values = jnp.asarray(bucket_edges, dtype=jnp.int32)
    beyond = jnp.sum((clipped[..., None] >= edge_values).astype(jnp.int32), axis=-1)
    return jnp.where(clipped < 16, clipped, jnp.minimum(16 + beyond, 31))


def toeplitz(diagonal, query_count, key_count):
    head_count = diagonal.shape[0]
    padded = jnp.pad(diagonal, ((0, 0), (0, 1)))
    row_width = query_count + key_count
    repeated = jnp.broadcast_to(padded[:, None, :], (head_count, query_count, row_width)).reshape(
        head_count, query_count * row_width
    )
    repeated = jnp.pad(repeated, ((0, 0), (0, query_count))).reshape(
        head_count, query_count, row_width + 1
    )[:, :, :key_count]
    return repeated[:, :, ::-1]


def diagonal_sums(gradient):
    head_count, query_count, key_count = gradient.shape
    offset_count = query_count + key_count - 1
    flipped = jnp.pad(gradient[:, :, ::-1], ((0, 0), (0, 0), (0, query_count)))
    skewed = flipped.reshape(head_count, query_count * (offset_count + 1))[
        :, : query_count * offset_count
    ]
    return jnp.sum(skewed.reshape(head_count, query_count, offset_count), axis=1)


def bucket_table(query_first, query_count, key_count):
    offsets = (
        query_first - (key_count - 1) + jnp.arange(query_count + key_count - 1, dtype=jnp.int32)
    )
    return (bucket_of(offsets)[:, None] == jnp.arange(BUCKETS, dtype=jnp.int32)[None, :]).astype(
        jnp.float32
    )


def body(
    inputs,
    lengths,
    expert_ids,
    slot_rows,
    attn_gain,
    qkv_weight,
    out_weight,
    position_bias,
    ffn_gain,
    router_weight,
    up_weight,
    down_weight,
    cotangent,
):
    highest = lax.Precision.HIGHEST
    micro_count, seg_rows, model_width = inputs.shape
    local_heads = position_bias.shape[1]
    head_size = qkv_weight.shape[2] // local_heads
    expert_count = up_weight.shape[0]
    query_first = lax.axis_index("ctx") * seg_rows
    query_pos = query_first + jnp.arange(seg_rows, dtype=jnp.int32)

    def pair_scores(query_heads, query_start, key_heads, length):
        query_count = query_heads.shape[0]
        key_count = key_heads.shape[0]
        scores = (
            jnp.einsum("qhd,khd->hqk", query_heads, key_heads, preferred_element_type=jnp.float32)
            * 0.125
        )
        diagonal = jnp.einsum(
            "rb,bh->hr",
            bucket_table(query_start, query_count, key_count),
            position_bias,
            precision=highest,
        )
        scores = scores + toeplitz(diagonal, query_count, key_count)
        query_place = query_start + jnp.arange(query_count, dtype=jnp.int32)
        key_place = jnp.arange(key_count, dtype=jnp.int32)
        allowed = (key_place[None, :] <= query_place[:, None]) & (key_place[None, :] < length)
        return (scores, allowed)

    def scores_for(query_heads, key_block, length):
        key_count = key_block.shape[0]
        key_heads = key_block.reshape(key_count, local_heads, head_size)
        scores, allowed = pair_scores(query_heads, query_first, key_heads, length)
        return (scores, allowed, key_heads)

    results = []
    input_parts = []
    grad_sums = None
    bias_total = jnp.zeros((local_heads, BUCKETS), jnp.float32)
    for micro_step in range(micro_count):
        forward_gain_one = lax.all_gather(attn_gain, ("dp", "ctx"), axis=0, tiled=True)
        forward_qkv_full = lax.all_gather(qkv_weight, ("dp", "ctx"), axis=1, tiled=True)
        forward_out_full = lax.all_gather(out_weight, ("dp", "ctx"), axis=1, tiled=True)
        forward_gain_two = lax.all_gather(ffn_gain, ("dp", "ctx"), axis=0, tiled=True)
        forward_router_full = lax.all_gather(router_weight, ("dp", "ctx"), axis=0, tiled=True)
        forward_up_full = lax.all_gather(up_weight, ("dp", "ctx"), axis=1, tiled=True)
        forward_down_full = lax.all_gather(down_weight, ("dp", "ctx"), axis=2, tiled=True)
        forward_tokens = inputs[micro_step].astype(jnp.float32)
        forward_length = lengths[micro_step]
        forward_normed = rms_norm(forward_tokens, forward_gain_one.astype(jnp.float32)).astype(
            jnp.bfloat16
        )
        forward_projected = jnp.einsum(
            "td,cde->cte", forward_normed, forward_qkv_full, preferred_element_type=jnp.float32
        ).astype(jnp.bfloat16)
        forward_query_heads = forward_projected[0].reshape(seg_rows, local_heads, head_size)
        row_top = jnp.full((local_heads, seg_rows), -1e30, jnp.float32)
        attend_scores, attend_allowed, attend_key_heads = scores_for(
            forward_query_heads,
            lax.all_gather(forward_projected[1], "ctx", axis=0, tiled=True),
            forward_length,
        )
        value_heads = lax.all_gather(forward_projected[2], "ctx", axis=0, tiled=True).reshape(
            attend_key_heads.shape
        )
        attend_scores = jnp.where(attend_allowed[None], attend_scores, -1e30)
        new_top = jnp.maximum(row_top, jnp.max(attend_scores, axis=-1))
        weights_exp = jnp.where(
            attend_allowed[None], jnp.exp(attend_scores - new_top[:, :, None]), 0.0
        )
        row_total = jnp.sum(weights_exp, axis=-1)
        summed = jnp.einsum(
            "hqk,khd->hqd",
            weights_exp.astype(jnp.bfloat16),
            value_heads,
            preferred_element_type=jnp.float32,
        )
        row_top, row_total, summed = (new_top, row_total, summed)
        forward_attended = summed / row_total[:, :, None]
        forward_log_total = row_top + jnp.log(row_total)
        forward_attended_low = (
            jnp.transpose(forward_attended, (1, 0, 2)).reshape(seg_rows, -1).astype(jnp.bfloat16)
        )
        branch = lax.psum(
            jnp.dot(
                forward_attended_low, forward_out_full, preferred_element_type=jnp.float32
            ).astype(jnp.bfloat16),
            "tensor",
        ).astype(jnp.float32)
        forward_hidden = forward_tokens + branch
        forward_normed_two = rms_norm(forward_hidden, forward_gain_two.astype(jnp.float32)).astype(
            jnp.bfloat16
        )
        logits = jnp.dot(
            forward_normed_two, forward_router_full, preferred_element_type=jnp.float32
        )
        forward_router_probs = jax.nn.softmax(logits, axis=-1)
        forward_chosen = (
            expert_ids[micro_step][:, None] == jnp.arange(expert_count, dtype=jnp.int32)[None, :]
        ).astype(jnp.float32)
        forward_gate_value = jnp.sum(forward_router_probs * forward_chosen, axis=-1)
        forward_slot_table = slot_rows[micro_step, 0]
        padded = jnp.concatenate(
            [forward_normed_two, jnp.zeros((1, model_width), jnp.bfloat16)], axis=0
        )
        forward_picked = padded[forward_slot_table]
        forward_raised = jnp.einsum(
            "ekd,edf->ekf", forward_picked, forward_up_full, preferred_element_type=jnp.float32
        )
        forward_activated = jax.nn.gelu(forward_raised).astype(jnp.bfloat16)
        lowered = jnp.einsum(
            "ekf,efd->ekd", forward_activated, forward_down_full, preferred_element_type=jnp.float32
        )
        spread = (
            jnp.zeros((seg_rows + 1, model_width), jnp.float32)
            .at[forward_slot_table.reshape(-1)]
            .add(lowered.reshape(-1, model_width))[:seg_rows]
        )
        forward_expert_sum = lax.psum(spread.astype(jnp.bfloat16), "tensor").astype(jnp.float32)
        forward_live_rows = (query_pos < forward_length).astype(jnp.float32)[:, None]
        result = (
            forward_live_rows * (forward_hidden + forward_gate_value[:, None] * forward_expert_sum)
        ).astype(jnp.bfloat16)
        forward_kept_state = (
            forward_tokens,
            forward_length,
            forward_normed,
            forward_projected,
            forward_attended,
            forward_log_total,
            forward_attended_low,
            forward_hidden,
            forward_normed_two,
            forward_router_probs,
            forward_chosen,
            forward_gate_value,
            forward_slot_table,
            forward_picked,
            forward_raised,
            forward_activated,
            forward_expert_sum,
            forward_live_rows,
        )
        result, kept_state = (result, forward_kept_state)
        gain_one = lax.all_gather(attn_gain, ("dp", "ctx"), axis=0, tiled=True)
        qkv_full = lax.all_gather(qkv_weight, ("dp", "ctx"), axis=1, tiled=True)
        out_full = lax.all_gather(out_weight, ("dp", "ctx"), axis=1, tiled=True)
        gain_two = lax.all_gather(ffn_gain, ("dp", "ctx"), axis=0, tiled=True)
        router_full = lax.all_gather(router_weight, ("dp", "ctx"), axis=0, tiled=True)
        up_full = lax.all_gather(up_weight, ("dp", "ctx"), axis=1, tiled=True)
        down_full = lax.all_gather(down_weight, ("dp", "ctx"), axis=2, tiled=True)
        (
            tokens,
            backward_length,
            normed,
            projected,
            attended,
            log_total,
            attended_low,
            hidden,
            normed_two,
            router_probs,
            chosen,
            gate_value,
            slot_table,
            picked,
            raised,
            activated,
            expert_sum,
            live_rows,
        ) = kept_state
        upstream = live_rows * cotangent[micro_step].astype(jnp.float32)
        sum_grad = (gate_value[:, None] * upstream).astype(jnp.bfloat16)
        gate_grad = jnp.sum(expert_sum * upstream, axis=-1)
        logit_grad = (router_probs * gate_grad[:, None] * (chosen - gate_value[:, None])).astype(
            jnp.bfloat16
        )
        router_part = jnp.einsum(
            "td,te->de", normed_two, logit_grad, preferred_element_type=jnp.float32
        )
        padded_grad = jnp.concatenate([sum_grad, jnp.zeros((1, model_width), jnp.bfloat16)], axis=0)
        slot_grad = padded_grad[slot_table]
        down_part = jnp.einsum(
            "ekf,ekd->efd", activated, slot_grad, preferred_element_type=jnp.float32
        )
        act_grad = jnp.einsum(
            "ekd,efd->ekf", slot_grad, down_full, preferred_element_type=jnp.float32
        )
        unused_value, gelu_back = jax.vjp(jax.nn.gelu, raised)
        raised_grad = gelu_back(act_grad)[0].astype(jnp.bfloat16)
        up_part = jnp.einsum(
            "ekd,ekf->edf", picked, raised_grad, preferred_element_type=jnp.float32
        )
        picked_grad = jnp.einsum(
            "ekf,edf->ekd", raised_grad, up_full, preferred_element_type=jnp.float32
        )
        spread_grad = (
            jnp.zeros((seg_rows + 1, model_width), jnp.float32)
            .at[slot_table.reshape(-1)]
            .add(picked_grad.reshape(-1, model_width))[:seg_rows]
        )
        normed_two_grad = lax.psum(spread_grad.astype(jnp.bfloat16), "tensor").astype(
            jnp.float32
        ) + jnp.einsum("te,de->td", logit_grad, router_full, preferred_element_type=jnp.float32)
        unused_norm, second_back = jax.vjp(rms_norm, hidden, gain_two.astype(jnp.float32))
        hidden_grad, gain_two_part = second_back(normed_two_grad)
        hidden_grad = hidden_grad + upstream
        branch_grad = hidden_grad.astype(jnp.bfloat16)
        out_part = jnp.einsum(
            "te,td->ed", attended_low, branch_grad, preferred_element_type=jnp.float32
        )
        attended_grad = jnp.einsum(
            "td,ed->te", branch_grad, out_full, preferred_element_type=jnp.float32
        ).astype(jnp.bfloat16)
        grad_heads = attended_grad.reshape(seg_rows, local_heads, head_size)
        row_delta = jnp.sum(
            jnp.transpose(grad_heads.astype(jnp.float32), (1, 0, 2)) * attended, axis=-1
        )
        backward_query_heads = projected[0].reshape(seg_rows, local_heads, head_size)
        bias_zero = jnp.zeros((local_heads, BUCKETS), jnp.float32)
        attend_bias_acc = bias_zero
        bias_acc = attend_bias_acc
        score_scores, score_allowed, score_key_heads = scores_for(
            backward_query_heads,
            lax.all_gather(projected[1], "ctx", axis=0, tiled=True),
            backward_length,
        )
        score_value_heads = lax.all_gather(projected[2], "ctx", axis=0, tiled=True).reshape(
            score_key_heads.shape
        )
        score_key_count = score_key_heads.shape[0]
        soft_weights = jnp.where(
            score_allowed[None], jnp.exp(score_scores - log_total[:, :, None]), 0.0
        )
        weight_grad = jnp.einsum(
            "qhd,khd->hqk", grad_heads, score_value_heads, preferred_element_type=jnp.float32
        )
        score_grad = (soft_weights * (weight_grad - row_delta[:, :, None])).astype(jnp.bfloat16)
        query_acc = jnp.einsum(
            "hqk,khd->qhd", score_grad, score_key_heads, preferred_element_type=jnp.float32
        )
        bias_acc = bias_acc + jnp.dot(
            diagonal_sums(score_grad.astype(jnp.float32)),
            bucket_table(query_first, seg_rows, score_key_count),
            precision=highest,
        )
        (
            (attend_query_acc, attend_bias_acc),
            attend_soft_weights,
            attend_score_grad,
            attend_key_count,
        ) = ((query_acc, bias_acc), soft_weights, score_grad, score_key_count)
        key_term = (
            jnp.einsum(
                "hqk,qhd->khd",
                attend_score_grad,
                backward_query_heads,
                preferred_element_type=jnp.float32,
            )
            * 0.125
        )
        value_term = jnp.einsum(
            "hqk,qhd->khd",
            attend_soft_weights.astype(jnp.bfloat16),
            grad_heads,
            preferred_element_type=jnp.float32,
        )
        grad_term = jnp.stack(
            [key_term.reshape(attend_key_count, -1), value_term.reshape(attend_key_count, -1)],
            axis=1,
        )
        key_value_acc = grad_term
        query_acc, key_value_acc, bias_part = (attend_query_acc, key_value_acc, attend_bias_acc)
        own_grads = lax.psum_scatter(
            key_value_acc.astype(jnp.bfloat16), "ctx", scatter_dimension=0, tiled=True
        ).astype(jnp.float32)
        query_grad = (query_acc * 0.125).reshape(seg_rows, -1).astype(jnp.bfloat16)
        qkv_grad = jnp.stack(
            [
                query_grad,
                own_grads[:, 0].astype(jnp.bfloat16),
                own_grads[:, 1].astype(jnp.bfloat16),
            ],
            axis=0,
        )
        qkv_part = jnp.einsum("td,cte->cde", normed, qkv_grad, preferred_element_type=jnp.float32)
        normed_grad = lax.psum(
            jnp.einsum(
                "cte,cde->td", qkv_grad, qkv_full, preferred_element_type=jnp.float32
            ).astype(jnp.bfloat16),
            "tensor",
        ).astype(jnp.float32)
        unused_first, first_back = jax.vjp(rms_norm, tokens, gain_one.astype(jnp.float32))
        token_grad, gain_one_part = first_back(normed_grad)
        input_part = (token_grad + hidden_grad).astype(jnp.bfloat16)
        weight_parts = (
            gain_one_part,
            qkv_part,
            out_part,
            gain_two_part,
            router_part,
            up_part,
            down_part,
        )
        input_part, weight_parts, bias_part = (input_part, weight_parts, bias_part)
        results.append(result)
        input_parts.append(input_part)
        grad_sums = (
            weight_parts
            if grad_sums is None
            else tuple((old_sum + new_part for old_sum, new_part in zip(grad_sums, weight_parts)))
        )
        bias_total = bias_total + bias_part
    reduced = (
        lax.psum_scatter(grad_sums[0], ("dp", "ctx"), scatter_dimension=0, tiled=True),
        lax.psum_scatter(grad_sums[1], ("dp", "ctx"), scatter_dimension=1, tiled=True),
        lax.psum_scatter(grad_sums[2], ("dp", "ctx"), scatter_dimension=1, tiled=True),
        lax.psum_scatter(grad_sums[3], ("dp", "ctx"), scatter_dimension=0, tiled=True),
        lax.psum_scatter(grad_sums[4], ("dp", "ctx"), scatter_dimension=0, tiled=True),
        lax.psum_scatter(grad_sums[5], ("dp", "ctx"), scatter_dimension=1, tiled=True),
        lax.psum_scatter(grad_sums[6], ("dp", "ctx"), scatter_dimension=2, tiled=True),
    )
    bias_grad_total = lax.psum(bias_total, ("dp", "ctx"))
    return (
        jnp.stack(results, axis=0),
        jnp.stack(input_parts, axis=0),
        reduced[0],
        reduced[1],
        reduced[2],
        jnp.transpose(bias_grad_total),
        reduced[3],
        reduced[4],
        reduced[5],
        reduced[6],
    )


def solution(mesh):
    small = mesh.shape["ctx"] == 2 and mesh.shape["dp"] == 4 and mesh.shape["tensor"] == 4
    return jax.shard_map(
        body_fast if small else body,
        mesh=mesh,
        in_specs=(
            P("dp", "ctx", None),
            P("dp"),
            P("dp", "ctx"),
            P("dp", "ctx", None, None),
            P(("dp", "ctx")),
            P(None, ("dp", "ctx"), "tensor"),
            P("tensor", ("dp", "ctx")),
            P(None, "tensor"),
            P(("dp", "ctx")),
            P(("dp", "ctx"), None),
            P(None, ("dp", "ctx"), "tensor"),
            P(None, "tensor", ("dp", "ctx")),
            P("dp", "ctx", None),
        ),
        out_specs=(
            P("dp", "ctx", None),
            P("dp", "ctx", None),
            P(("dp", "ctx")),
            P(None, ("dp", "ctx"), "tensor"),
            P("tensor", ("dp", "ctx")),
            P(None, "tensor"),
            P(("dp", "ctx")),
            P(("dp", "ctx"), None),
            P(None, ("dp", "ctx"), "tensor"),
            P(None, "tensor", ("dp", "ctx")),
        ),
        check_vma=False,
    )
```
